32 devices in a mesh: ctx: 16 (over z, x, core), head: 2 (over y).
Axes of the slice: x: 2, y: 2, z: 4, core: 2. Of those that a mesh axis runs over, the one named last changes fastest.
Arguments:
- inputs: bfloat16 [5120, 3072], P('ctx', 'head'), may hold values from -6 to 6
- norm_gain: float32 [3072], replicated, may hold values from 0.1 to 1.9
- level_table: bfloat16 [8, 3072], replicated, may hold values from -6 to 6
- w_qkv: bfloat16 [3072, 3, 3072], P(None, None, 'head'), may hold values from -4 to 4
- w_out: bfloat16 [3072, 3072], P('head'), may hold values from -0.21875 to 0.21875
- clip_lengths: int32 [8], replicated, may hold values from 1 to 2560, 5120 in all
- prefix_lengths: int32 [8], replicated, may hold values from 1 to 640
- noise_levels: int32 [8], replicated, may hold values from 0 to 7
- token_rank: int32 [5120], replicated, may hold values from 0 to 15, as said below
Outputs:
- attended: bfloat16 [5120, 3072], P('ctx', 'head')
The draws below stay inside these ranges and needn't reach their ends.
Inputs may be any that keep to these rules, and one draw needn't show every extreme that they name: `clip_lengths`: they sum to 5120; the longest clip has exactly 2560 tokens. `token_rank`: every rank receives exactly 320 tokens. Every block of 320 packed rows gives the same number of tokens to the rank k places after its own index (counted around 16), for each k; no block gives more than 40 tokens to one rank, and that number is reached.
All inputs are finite; a program needn't handle non-finite values.
Results may differ from the reference program's by a relative error of at most 0.009.
Values may be sent and summed in bfloat16 or wider, within the bound.
No kernel may reach another device: no remote copies, remote signals or barrier semaphores. Data moves between devices by JAX's collectives and lax.ppermute only.
A program may use at most 384 MiB of HBM per device.

```python
import math
import jax
import jax.numpy as jnp
import numpy as np
from jax import lax

D = 3072
HEADS = 24
HEAD_DIM = 128
LEVELS = 8
TOK_DEV = 320
TOKENS = 5120
CLIPS = 8
MAXCLIP = 2560
N_CTX = 16


def draw_inputs(key, part):
    key = jax.random.fold_in(key, 5)
    first = jax.random.fold_in(key, 0)
    base = jax.random.normal(first, (TOKENS, D), jnp.float32)
    return jnp.clip(base, -6.0, 6.0).astype(jnp.bfloat16)


def draw_w_qkv(key, part):
    key = jax.random.fold_in(key, 7)
    first, second, third = jax.random.split(key, 3)
    unit = D ** (-0.5)
    base = jnp.clip(jax.random.normal(first, (D, D), jnp.float32), -6.0, 6.0) * unit
    value_part = jnp.clip(jax.random.normal(second, (D, D), jnp.float32), -6.0, 6.0) * unit
    query_part = 2.0 * base
    key_part = jnp.clip(jax.random.normal(third, (D, D), jnp.float32), -6.0, 6.0) * unit
    return jnp.stack([query_part, key_part, value_part], axis=1).astype(jnp.bfloat16)


def draw_token_rank(key, part):
    key = jax.random.fold_in(key, 11)
    ranks = TOKENS // TOK_DEV
    most = 2 * TOK_DEV // ranks
    first, second, third = jax.random.split(key, 3)
    lower = jax.random.randint(first, (ranks // 2,), 0, most + 1)
    lower = lower.at[0].set(most)
    amounts = jnp.stack([lower, most - lower], axis=1).reshape(ranks)
    amounts = jnp.roll(amounts, jax.random.randint(second, (), 0, ranks))
    bounds = jnp.cumsum(amounts)
    slot_offset = jnp.sum((jnp.arange(TOK_DEV)[:, None] >= bounds[None, :]).astype(jnp.int32), axis=1)
    keys = jax.random.split(third, ranks)
    orders = jax.vmap(lambda k: jax.random.permutation(k, TOK_DEV))(keys)
    offsets = slot_offset[orders]
    rank = (jnp.arange(ranks)[:, None] + offsets) % ranks
    return rank.reshape(TOKENS).astype(jnp.int32)


def place_ends(result, rng, smallest, top_value):
    longest = result.shape.index(max(result.shape))
    spots = []
    for shift in (0, 1):
        where = [jax.random.randint(jax.random.fold_in(rng, axis), (), 0, length) for axis, length in enumerate(result.shape)]
        where[longest] = (where[longest] + shift) % result.shape[longest]
        spots.append(tuple(where))
    return result.at[spots[0]].set(smallest).at[spots[1]].set(top_value)


def block_scale(own_key, extent, cuts, smallest, largest):
    loudness, own = 1.0, jax.random.fold_in(own_key, 6)
    for axis_at, shards_of in cuts:
        steps = jnp.exp(jax.random.uniform(jax.random.fold_in(own, axis_at), (shards_of,), jnp.float32, smallest / len(cuts), largest / len(cuts)))
        loudness = loudness * jnp.repeat(steps, extent[axis_at] // shards_of).reshape([-1 if axis == axis_at else 1 for axis in range(len(extent))])
    return loudness


def split_up(amount, total, bound, slope):
    loads = [(1 << 20) // math.isqrt(standing ** slope) + 1 for standing in range(2, amount + 1)]
    spare, given = total - bound - (amount - 1), [1] * (amount - 1)
    while spare > 0:
        candidates = [i for i in range(amount - 1) if given[i] < bound]
        mass, remaining = sum([loads[i] for i in candidates]), spare
        for i in candidates:
            addition = min(bound - given[i], max(1, remaining * loads[i] // mass), spare)
            given[i] = given[i] + addition
            spare = spare - addition
    return np.array([bound] + given)


def ragged(own_key, number_of, total, bound, skew):
    if number_of == 2:
        one = jax.random.randint(own_key, (), max(1, total - bound), min(bound, total - 1) + 1)
        return jnp.stack([one, total - one])
    lengths = jnp.asarray(split_up(number_of, total, bound, skew), jnp.int32)
    couples = (number_of - 1) // 2
    donor, taker = lengths[1:1 + 2 * couples:2], lengths[2:2 + 2 * couples:2]
    room = jnp.minimum(donor - 1, bound - taker)
    passed = jax.random.randint(jax.random.fold_in(own_key, 1), (couples,), 0, 1 << 20) % (room + 1)
    lengths = lengths.at[1:1 + 2 * couples:2].set(donor - passed).at[2:2 + 2 * couples:2].set(taker + passed)
    return lengths[jax.random.permutation(jax.random.fold_in(own_key, 2), number_of)]


def centred(own_key, shape, scale, reach, cuts=(), held_as=jnp.bfloat16):
    values = jax.random.normal(own_key, shape, jnp.float32) * scale
    if len(cuts) > 0:
        values = block_scale(own_key, shape, cuts, -0.22, 0.18) * values
    return jnp.clip(values, min=-reach, max=reach).astype(held_as)


def setup_inputs(seed: int = 0) -> dict:
    arg_keys = jax.random.split(jax.random.key(seed), 10)
    inputs = draw_inputs(jax.random.fold_in(arg_keys[9], 71), 0)
    norm_gain = jnp.clip(1.0 + 0.18 * jax.random.normal(arg_keys[1], (D,), jnp.float32), 0.1, 1.9)
    level_table = centred(arg_keys[2], (LEVELS, D), 1.0, 6.0)
    w_qkv = draw_w_qkv(jax.random.fold_in(arg_keys[9], 71), 0)
    w_out = centred(arg_keys[4], (D, D), (D // 4) ** -0.5, 0.21875, ((0, 2),))
    clip_lengths = ragged(arg_keys[5], CLIPS, TOKENS, MAXCLIP, 2).astype(jnp.int32)
    prefix_lengths = place_ends(jax.random.randint(arg_keys[6], (CLIPS,), 1, MAXCLIP // 4 + 1), jax.random.fold_in(arg_keys[6], 1), 1, (MAXCLIP // 4 + 1) - 1).astype(jnp.int32)
    noise_levels = place_ends(jax.random.randint(arg_keys[7], (CLIPS,), 0, LEVELS), jax.random.fold_in(arg_keys[7], 1), 0, LEVELS - 1).astype(jnp.int32)
    token_rank = draw_token_rank(jax.random.fold_in(arg_keys[9], 71), 0)
    return {"inputs": inputs, "norm_gain": norm_gain, "level_table": level_table, "w_qkv": w_qkv, "w_out": w_out, "clip_lengths": clip_lengths, "prefix_lengths": prefix_lengths, "noise_levels": noise_levels, "token_rank": token_rank}


NEG = -1e+30
EPS = 1e-06

def clip_tables(total_rows, clip_lengths, prefix_lengths, noise_levels):
    rows = jnp.arange(total_rows, dtype=jnp.int32)
    ends = jnp.cumsum(clip_lengths).astype(jnp.int32)
    begins = ends - clip_lengths
    clip_of = lax.optimization_barrier(jnp.sum((rows[:, None] >= ends[None, :]).astype(jnp.int32), axis=1)).astype(jnp.int32)
    member = clip_of[:, None] == jnp.arange(clip_lengths.shape[0], dtype=jnp.int32)[None, :]
    begin_row = lax.optimization_barrier(jnp.sum(jnp.where(member, begins[None, :], 0), axis=1)).astype(jnp.int32)
    lead = jnp.minimum(prefix_lengths, clip_lengths)
    lead_row = lax.optimization_barrier(jnp.sum(jnp.where(member, lead[None, :], 0), axis=1)).astype(jnp.int32)
    level_row = lax.optimization_barrier(jnp.sum(jnp.where(member, noise_levels[None, :], 0), axis=1)).astype(jnp.int32)
    in_prefix = rows - begin_row < lead_row
    return (clip_of, in_prefix, level_row)

def rank_tables(token_rank, ranks, per_rank):
    onehot = (token_rank[:, None] == jnp.arange(ranks, dtype=jnp.int32)[None, :]).astype(jnp.int32)
    earlier = jnp.cumsum(onehot, axis=0) - onehot
    within = lax.optimization_barrier(jnp.sum(earlier * onehot, axis=1)).astype(jnp.int32)
    counts = lax.optimization_barrier(jnp.sum(onehot.reshape(ranks, per_rank, ranks), axis=1)).astype(jnp.int32)
    starts = (jnp.cumsum(counts, axis=0) - counts).astype(jnp.int32)
    return (within, counts, starts)

def normalize(rows, in_prefix, level_row, level_table, norm_gain):
    picks = (level_row[:, None] == jnp.arange(level_table.shape[0], dtype=jnp.int32)[None, :]) & in_prefix[:, None]
    added = jnp.dot(picks.astype(jnp.bfloat16), level_table, preferred_element_type=jnp.float32)
    shifted = rows.astype(jnp.float32) + added
    factor = lax.rsqrt(lax.optimization_barrier(jnp.mean(shifted * shifted, axis=-1, keepdims=True)) + EPS)
    return (shifted * factor * norm_gain.astype(jnp.float32)).astype(jnp.bfloat16)

def reference(inputs, norm_gain, level_table, w_qkv, w_out, clip_lengths, prefix_lengths, noise_levels, token_rank):
    clip_of, in_prefix, level_row = clip_tables(TOKENS, clip_lengths, prefix_lengths, noise_levels)
    normed = normalize(inputs, in_prefix, level_row, level_table, norm_gain)
    qkv = jnp.dot(normed, w_qkv.reshape(D, 3 * D), preferred_element_type=jnp.float32).astype(jnp.bfloat16)
    qkv = qkv.reshape(TOKENS, 3, HEADS, HEAD_DIM)
    queries = jnp.transpose(qkv[:, 0], (1, 0, 2))
    keys = jnp.transpose(qkv[:, 1], (1, 0, 2))
    values = jnp.transpose(qkv[:, 2], (1, 0, 2))
    span = min(TOK_DEV + 2 * MAXCLIP, TOKENS)
    blocks = TOKENS // TOK_DEV
    factor = HEAD_DIM ** (-0.5)

    def one_head(operands):
        q_head, k_head, v_head = operands

        def one_block(index):
            first = (index * TOK_DEV).astype(jnp.int32)
            low = jnp.clip(first - MAXCLIP, 0, TOKENS - span).astype(jnp.int32)
            q_rows = lax.dynamic_slice_in_dim(q_head, first, TOK_DEV, 0)
            k_rows = lax.dynamic_slice_in_dim(k_head, low, span, 0)
            v_rows = lax.dynamic_slice_in_dim(v_head, low, span, 0)
            q_clip = lax.dynamic_slice_in_dim(clip_of, first, TOK_DEV, 0)
            q_pre = lax.dynamic_slice_in_dim(in_prefix, first, TOK_DEV, 0)
            k_clip = lax.dynamic_slice_in_dim(clip_of, low, span, 0)
            k_pre = lax.dynamic_slice_in_dim(in_prefix, low, span, 0)
            scores = jnp.dot(q_rows, k_rows.T, preferred_element_type=jnp.float32) * factor
            allowed = (q_clip[:, None] == k_clip[None, :]) & (jnp.logical_not(q_pre)[:, None] | k_pre[None, :])
            top = lax.optimization_barrier(jnp.max(jnp.where(allowed, scores, NEG), axis=1, keepdims=True))
            weights = jnp.where(allowed, jnp.exp(scores - top), 0.0)
            total = lax.optimization_barrier(jnp.sum(weights, axis=1, keepdims=True))
            summed = jnp.dot(weights.astype(jnp.bfloat16), v_rows, preferred_element_type=jnp.float32)
            return (summed / total).astype(jnp.bfloat16)
        return lax.map(one_block, jnp.arange(blocks, dtype=jnp.int32))
    outcome = lax.map(one_head, (queries, keys, values))
    attention = jnp.transpose(outcome.reshape(HEADS, TOKENS, HEAD_DIM), (1, 0, 2)).reshape(TOKENS, D)
    projected = jnp.dot(attention, w_out, preferred_element_type=jnp.float32).astype(jnp.bfloat16)
    within, counts, starts = rank_tables(token_rank, N_CTX, TOK_DEV)
    place = (token_rank * TOK_DEV + within).astype(jnp.int32)
    return jnp.zeros_like(projected).at[place].set(projected)
```

```python
import jax
import jax.numpy as jnp
from jax import lax
from jax.experimental import pallas as pl
from jax.experimental.pallas import tpu as pltpu
from jax.sharding import PartitionSpec as P

HEAD_DIM = 128


NEG = -1e30
EPS = 1e-06
MAXCLIP = 2560
LOG2E = 1.4426950408889634
VMEM_LIMIT = 48 * 1024 * 1024


def clip_tables(total_rows, clip_lengths, prefix_lengths, noise_levels):
    rows = jnp.arange(total_rows, dtype=jnp.int32)
    ends = jnp.cumsum(clip_lengths)
    begins = ends - clip_lengths
    clip_of = jnp.sum((rows[:, None] >= ends[None, :]).astype(jnp.int32), axis=1)
    member = clip_of[:, None] == jnp.arange(clip_lengths.shape[0], dtype=jnp.int32)[None, :]
    begin_row = jnp.sum(jnp.where(member, begins[None, :], 0), axis=1)
    lead = jnp.minimum(prefix_lengths, clip_lengths)
    lead_row = jnp.sum(jnp.where(member, lead[None, :], 0), axis=1)
    level_row = jnp.sum(jnp.where(member, noise_levels[None, :], 0), axis=1)
    in_prefix = rows - begin_row < lead_row
    return (clip_of, in_prefix, level_row)


def rank_tables(token_rank, ranks, per_rank):
    onehot = (token_rank[:, None] == jnp.arange(ranks, dtype=jnp.int32)[None, :]).astype(jnp.int32)
    earlier = jnp.cumsum(onehot, axis=0) - onehot
    within = jnp.sum(earlier * onehot, axis=1)
    counts = jnp.sum(onehot.reshape(ranks, per_rank, ranks), axis=1)
    starts = jnp.cumsum(counts, axis=0) - counts
    return (within, counts, starts)


def normalize(rows, in_prefix, level_row, level_table, norm_gain):
    picks = (
        level_row[:, None] == jnp.arange(level_table.shape[0], dtype=jnp.int32)[None, :]
    ) & in_prefix[:, None]
    added = jnp.dot(picks.astype(jnp.bfloat16), level_table, preferred_element_type=jnp.float32)
    shifted = rows.astype(jnp.float32) + added
    factor = lax.rsqrt(jnp.mean(shifted * shifted, axis=-1, keepdims=True) + EPS)
    return (shifted * factor * norm_gain).astype(jnp.bfloat16)


def fold_keys(state, queries, query_clip, query_prefix, pairs, key_clip, key_prefix):
    width = queries.shape[1]
    heads_here = width // HEAD_DIM
    factor = HEAD_DIM ** (-0.5)
    allowed_query = jnp.logical_not(query_prefix)

    def absorb(carry, block):
        block_pairs, block_clip, block_prefix = block
        allowed = (query_clip[:, None] == block_clip[None, :]) & (
            allowed_query[:, None] | block_prefix[None, :]
        )
        updated = []
        for head in range(heads_here):
            top, total, summed = carry[head]
            low = head * HEAD_DIM
            q_head = queries[:, low : low + HEAD_DIM]
            k_head = block_pairs[:, low : low + HEAD_DIM]
            v_head = block_pairs[:, width + low : width + low + HEAD_DIM]
            scores = (
                lax.dot_general(
                    q_head, k_head, (((1,), (1,)), ((), ())), preferred_element_type=jnp.float32
                )
                * factor
            )
            masked = jnp.where(allowed, scores, NEG)
            new_top = jnp.maximum(top, jnp.max(masked, axis=1, keepdims=True))
            fade = jnp.exp(top - new_top)
            weights = jnp.where(allowed, jnp.exp(scores - new_top), 0.0)
            total = total * fade + jnp.sum(weights, axis=1, keepdims=True)
            summed = summed * fade + jnp.dot(
                weights.astype(jnp.bfloat16), v_head, preferred_element_type=jnp.float32
            )
            updated.append((new_top, total, summed))
        return (tuple(updated), None)

    count = pairs.shape[0]
    step = 2048 if count > 2048 and count % 2048 == 0 else count
    if step == count:
        result, unused = absorb(state, (pairs, key_clip, key_prefix))
        return result
    stacked = (
        pairs.reshape(count // step, step, pairs.shape[1]),
        key_clip.reshape(count // step, step),
        key_prefix.reshape(count // step, step),
    )
    result, unused = lax.scan(absorb, state, stacked)
    return result


def gathered_body(
    inputs,
    norm_gain,
    level_table,
    w_qkv,
    w_out,
    clip_lengths,
    prefix_lengths,
    noise_levels,
    token_rank,
):
    ranks = lax.axis_size("ctx")
    rank_here = lax.axis_index("ctx")
    per_dev = inputs.shape[0]
    slots = 2 * per_dev // ranks
    local_width = w_qkv.shape[2]
    heads_here = local_width // HEAD_DIM
    total_rows = per_dev * ranks
    clip_of, in_prefix, level_row = clip_tables(
        total_rows, clip_lengths, prefix_lengths, noise_levels
    )
    within, counts, starts = rank_tables(token_rank, ranks, per_dev)
    place = token_rank * per_dev + within
    order = (
        jnp.zeros((total_rows,), jnp.int32).at[place].set(jnp.arange(total_rows, dtype=jnp.int32))
    )
    first = rank_here * per_dev
    own_rank = lax.dynamic_slice_in_dim(token_rank, first, per_dev, 0)
    own_within = lax.dynamic_slice_in_dim(within, first, per_dev, 0)
    send_starts = lax.dynamic_slice_in_dim(starts, rank_here, 1, 0)[0]
    recv_counts = lax.dynamic_slice_in_dim(counts, rank_here, 1, 1)[:, 0]
    recv_starts = lax.dynamic_slice_in_dim(starts, rank_here, 1, 1)[:, 0]
    balanced_rows = lax.dynamic_slice_in_dim(order, first, per_dev, 0)
    target = own_rank * slots + own_within - send_starts[own_rank]
    buffer = jnp.zeros((ranks * slots, inputs.shape[1]), inputs.dtype).at[target].set(inputs)
    received = lax.all_to_all(
        buffer.reshape(ranks, slots, inputs.shape[1]),
        "ctx",
        split_axis=0,
        concat_axis=0,
        tiled=True,
    )
    spots = jnp.arange(slots, dtype=jnp.int32)[None, :]
    index = jnp.where(spots < recv_counts[:, None], recv_starts[:, None] + spots, per_dev).reshape(
        -1
    )
    flat = received.reshape(ranks * slots, received.shape[2])
    rows = jnp.zeros((per_dev, received.shape[2]), received.dtype).at[index].set(flat, mode="drop")
    full_rows = lax.all_gather(rows, "head", axis=1, tiled=True)
    normed = normalize(
        full_rows, in_prefix[balanced_rows], level_row[balanced_rows], level_table, norm_gain
    )
    qkv = jnp.dot(
        normed, w_qkv.reshape(w_qkv.shape[0], 3 * local_width), preferred_element_type=jnp.float32
    ).astype(jnp.bfloat16)
    start_state = tuple(
        (
            (
                jnp.full((per_dev, 1), NEG, jnp.float32),
                jnp.zeros((per_dev, 1), jnp.float32),
                jnp.zeros((per_dev, HEAD_DIM), jnp.float32),
            )
            for head in range(heads_here)
        )
    )
    key_clip = clip_of[order]
    key_prefix = in_prefix[order]
    query_clip = lax.dynamic_slice_in_dim(key_clip, first, per_dev, 0)
    query_prefix = lax.dynamic_slice_in_dim(key_prefix, first, per_dev, 0)
    queries = qkv[:, :local_width]
    pairs = qkv[:, local_width:]
    state = fold_keys(
        start_state,
        queries,
        query_clip,
        query_prefix,
        lax.all_gather(pairs, "ctx", axis=0, tiled=True),
        key_clip,
        key_prefix,
    )
    parts = [state[head][2] / state[head][1] for head in range(heads_here)]
    attention = jnp.concatenate(parts, axis=1).astype(jnp.bfloat16)
    terms = jnp.dot(attention, w_out, preferred_element_type=jnp.float32)
    return lax.psum_scatter(terms.astype(jnp.bfloat16), "head", scatter_dimension=1, tiled=True)


def project_kernel(spot_ref, rows_ref, w_ref, out_ref):
    weights = jnp.concatenate([w_ref[0], w_ref[1], w_ref[2]], axis=1)
    out_ref[0] = jnp.dot(
        rows_ref[...], weights, preferred_element_type=jnp.float32
    ).astype(jnp.bfloat16)


def project_heads(normed, w_parts, spot, first_head, count, group_heads):
    rows, depth = normed.shape
    return pl.pallas_call(
        project_kernel,
        grid_spec=pltpu.PrefetchScalarGridSpec(
            num_scalar_prefetch=1,
            grid=(4, count),
            in_specs=[
                pl.BlockSpec((rows, depth), lambda d, h, spot_ref: (0, 0)),
                pl.BlockSpec(
                    (3, depth, HEAD_DIM),
                    lambda d, h, spot_ref: (
                        0,
                        0,
                        group_heads * jnp.bitwise_xor(spot_ref[0], d) + first_head + h,
                    ),
                ),
            ],
            out_specs=pl.BlockSpec((1, rows, 3 * HEAD_DIM), lambda d, h, spot_ref: (d, 0, h)),
        ),
        out_shape=jax.ShapeDtypeStruct((4, rows, count * 3 * HEAD_DIM), jnp.bfloat16),
        compiler_params=pltpu.CompilerParams(vmem_limit_bytes=VMEM_LIMIT),
        cost_estimate=pl.CostEstimate(
            flops=2 * rows * depth * 12 * HEAD_DIM * count,
            bytes_accessed=2 * depth * 12 * HEAD_DIM * count,
            transcendentals=0,
        ),
    )(spot, normed, w_parts)


def attend_kernel(*refs):
    blocks = refs[:8]
    key_code_ref, low_ref, high_ref, out_ref, q_all, k_all, v_all = refs[8:]
    rows = blocks[0].shape[-2]
    tile = out_ref.shape[0]
    step = pl.program_id(1)

    @pl.when(step == 0)
    def _():
        for index, block in enumerate(blocks):
            spot = slice(index * rows, (index + 1) * rows)
            lead = (0,) if len(block.shape) == 3 else ()
            if index < 4:
                q_all[spot, :] = block[lead + (slice(None), slice(0, HEAD_DIM))]
            k_all[spot, :] = block[lead + (slice(None), slice(HEAD_DIM, 2 * HEAD_DIM))]
            v_all[spot, :] = block[lead + (slice(None), slice(2 * HEAD_DIM, 3 * HEAD_DIM))]

    queries = q_all[pl.ds(pl.multiple_of(step * tile, tile), tile), :]
    scores = lax.dot_general(
        queries, k_all[...], (((1,), (1,)), ((), ())), preferred_element_type=jnp.float32
    )
    code = key_code_ref[...]
    allowed = (code >= low_ref[...]) & (code <= high_ref[...])
    masked = jnp.where(allowed, scores, NEG)
    top = jnp.max(masked, axis=1, keepdims=True)
    weights = jnp.exp2((masked - top) * (HEAD_DIM ** (-0.5) * LOG2E))
    total = jnp.sum(weights, axis=1, keepdims=True)
    summed = jnp.dot(weights.astype(jnp.bfloat16), v_all[...], preferred_element_type=jnp.float32)
    out_ref[...] = (summed / total).astype(jnp.bfloat16)


def attend(own, others, key_code, low, high, count):
    rows = own.shape[1]
    keys, queries, tile = 8 * rows, 4 * rows, 256
    width = 3 * HEAD_DIM
    block = pl.BlockSpec((rows, width), lambda h, t: (0, h))
    column = pl.BlockSpec((tile, 1), lambda h, t: (t, 0))
    return pl.pallas_call(
        attend_kernel,
        grid=(count, queries // tile),
        in_specs=[pl.BlockSpec((1, rows, width), lambda h, t: (0, 0, h))]
        + [block] * 7
        + [pl.BlockSpec((1, keys), lambda h, t: (0, 0)), column, column],
        out_specs=pl.BlockSpec((tile, HEAD_DIM), lambda h, t: (t, h)),
        out_shape=jax.ShapeDtypeStruct((queries, count * HEAD_DIM), jnp.bfloat16),
        scratch_shapes=[
            pltpu.VMEM((queries, HEAD_DIM), jnp.bfloat16),
            pltpu.VMEM((keys, HEAD_DIM), jnp.bfloat16),
            pltpu.VMEM((keys, HEAD_DIM), jnp.bfloat16),
        ],
        compiler_params=pltpu.CompilerParams(vmem_limit_bytes=VMEM_LIMIT),
        cost_estimate=pl.CostEstimate(
            flops=8 * queries * keys * HEAD_DIM * count,
            bytes_accessed=8 * rows * width * 2 * count,
            transcendentals=queries * keys * count,
        ),
    )(own, *others, key_code, low, high)


def place_kernel(base_ref, own_ref, other_ref, place_ref, out_ref):
    rows = out_ref.shape[1]
    half = own_ref.shape[0]
    wanted = base_ref[pl.program_id(0)] + lax.broadcasted_iota(jnp.int32, (rows, 1), 0)
    picks = jnp.where(place_ref[...] == wanted, 1.0, 0.0).astype(jnp.bfloat16)
    out_ref[0] = (
        jnp.dot(picks[:, :half], own_ref[...], preferred_element_type=jnp.float32)
        + jnp.dot(picks[:, half:], other_ref[...], preferred_element_type=jnp.float32)
    ).astype(jnp.bfloat16)


def place_rows(bases, own, other, places, rows):
    slots = bases.shape[0]
    half, width = own.shape
    return pl.pallas_call(
        place_kernel,
        grid_spec=pltpu.PrefetchScalarGridSpec(
            num_scalar_prefetch=1,
            grid=(slots,),
            in_specs=[
                pl.BlockSpec((half, width), lambda d, base_ref: (0, 0)),
                pl.BlockSpec((half, width), lambda d, base_ref: (0, 0)),
                pl.BlockSpec((1, 2 * half), lambda d, base_ref: (0, 0)),
            ],
            out_specs=pl.BlockSpec((1, rows, width), lambda d, base_ref: (d, 0, 0)),
        ),
        out_shape=jax.ShapeDtypeStruct((slots, rows, width), jnp.bfloat16),
        compiler_params=pltpu.CompilerParams(vmem_limit_bytes=VMEM_LIMIT),
        cost_estimate=pl.CostEstimate(
            flops=4 * slots * rows * half * width,
            bytes_accessed=4 * half * width,
            transcendentals=0,
        ),
    )(bases, own, other, places)


def out_kernel(spot_ref, *refs):
    out_ref = refs[-1]
    pieces = (len(refs) - 5) // 4
    total = None
    for d in range(4):
        rows = jnp.concatenate([ref[...] for ref in refs[d * pieces : (d + 1) * pieces]], axis=1)
        term = jnp.dot(rows, refs[4 * pieces + d][...], preferred_element_type=jnp.float32)
        total = term if total is None else total + term
    out_ref[...] = total.astype(out_ref.dtype)


def project_out(attention, w_out, spot, side, dtype):
    rows = attention[0][0].shape[0]
    group = w_out.shape[0] // 4
    columns, tile = w_out.shape[1] // 2, 512
    tiles = columns // tile
    pieces = [piece for slot in attention for piece in slot]

    def w_spec(d):
        return pl.BlockSpec(
            (group, tile),
            lambda t, spot_ref: (jnp.bitwise_xor(spot_ref[0], d), spot_ref[1] * tiles + t),
        )

    return pl.pallas_call(
        out_kernel,
        grid_spec=pltpu.PrefetchScalarGridSpec(
            num_scalar_prefetch=1,
            grid=(tiles,),
            in_specs=[pl.BlockSpec(piece.shape, lambda t, spot_ref: (0, 0)) for piece in pieces]
            + [w_spec(d) for d in range(4)],
            out_specs=pl.BlockSpec((rows, tile), lambda t, spot_ref: (0, t)),
        ),
        out_shape=jax.ShapeDtypeStruct((rows, columns), dtype),
        compiler_params=pltpu.CompilerParams(vmem_limit_bytes=VMEM_LIMIT),
        cost_estimate=pl.CostEstimate(
            flops=2 * rows * columns * 4 * group,
            bytes_accessed=2 * columns * 4 * group,
            transcendentals=0,
        ),
    )(jnp.stack([spot, side]), *pieces, *([w_out] * 4))


def row_facts(rows, clip_lengths, prefix_lengths, noise_levels):
    ends = jnp.cumsum(clip_lengths)
    begins = ends - clip_lengths
    lead = begins + jnp.minimum(prefix_lengths, clip_lengths)
    past = rows[:, None] >= ends[None, :]
    clip = jnp.sum(past.astype(jnp.int32), axis=1)
    inside = (rows[:, None] >= begins[None, :]) & jnp.logical_not(past)
    in_prefix = jnp.any(inside & (rows[:, None] < lead[None, :]), axis=1)
    level = jnp.sum(jnp.where(inside, noise_levels[None, :], 0), axis=1)
    return clip, in_prefix, level


CHUNKS = ((0, 1), (1, 1), (2, 1))


def halved_body(
    inputs,
    norm_gain,
    level_table,
    w_qkv,
    w_out,
    clip_lengths,
    prefix_lengths,
    noise_levels,
    token_rank,
):
    rank_here = lax.axis_index("ctx")
    side = lax.axis_index("head")
    per_dev = inputs.shape[0]
    ranks = 16
    half_rows = 8 * per_dev
    local_width = w_qkv.shape[2]
    group_heads = local_width // HEAD_DIM // 4
    half, block = rank_here // 8, rank_here % 8
    spot = block // 2

    def exchange(array, flip, only=None):
        pairs = [(r, r ^ flip) for r in range(ranks) if only is None or only(r)]
        return lax.ppermute(array, "ctx", pairs)

    begins = jnp.cumsum(clip_lengths) - clip_lengths
    start = jnp.sum(jnp.where(clip_lengths == MAXCLIP, begins, 0))
    early = start <= half_rows // 2

    def packed_row(spots):
        swapped = jnp.where(early, spots < start, spots >= start)
        return spots + half_rows * (half ^ swapped.astype(jnp.int32)), swapped

    own_packed, own_swapped = packed_row(block * per_dev + jnp.arange(per_dev, dtype=jnp.int32))
    moved = lax.cond(
        early,
        lambda x: exchange(x, 8, lambda r: r % 8 < 4),
        lambda x: exchange(x, 8, lambda r: r % 8 >= 4),
        inputs,
    )
    rows = jnp.where(own_swapped[:, None], moved, inputs)
    other = lax.ppermute(rows, "head", [(0, 1), (1, 0)])
    full_rows = jnp.where(
        side == 0,
        jnp.concatenate([rows, other], axis=1),
        jnp.concatenate([other, rows], axis=1),
    )
    unused, own_prefix, own_level = row_facts(
        own_packed, clip_lengths, prefix_lengths, noise_levels
    )
    normed = normalize(full_rows, own_prefix, own_level, level_table, norm_gain)

    flips = jnp.array([0, 2, 4, 6, 1, 3, 5, 7], jnp.int32)
    order = block ^ flips
    spots = (order[:, None] * per_dev + jnp.arange(per_dev, dtype=jnp.int32)[None, :]).reshape(-1)
    packed, swapped = packed_row(spots)
    clip, in_prefix, unused = row_facts(packed, clip_lengths, prefix_lengths, noise_levels)
    code = 2 * clip + jnp.where(in_prefix, 0, 1)
    key_code = code.reshape(1, half_rows)
    high = code[: half_rows // 2].reshape(-1, 1)
    low = (2 * clip[: half_rows // 2]).reshape(-1, 1)

    within, unused, unused = rank_tables(token_rank, ranks, per_dev)
    place = token_rank * per_dev + within
    every_spot = jnp.arange(half_rows, dtype=jnp.int32)
    every_packed, unused = packed_row(every_spot)
    half_place = jnp.where(every_packed >= half_rows, place[half_rows:], place[:half_rows])
    half_place = half_place.reshape(8, per_dev)
    places = jnp.sum(
        jnp.where(
            (order[:, None] == jnp.arange(8, dtype=jnp.int32)[None, :])[:, :, None],
            half_place[None],
            0,
        ),
        axis=1,
    ).reshape(1, half_rows)
    bases = per_dev * (rank_here ^ (2 * jnp.arange(8, dtype=jnp.int32)))

    w_parts = jnp.transpose(w_qkv, (1, 0, 2))
    spot_array = spot.reshape(1)
    attention = [[], [], [], []]
    for first_head, count in CHUNKS:
        mine = project_heads(normed, w_parts, spot_array, first_head, count, group_heads)
        blocks = [mine[0]] + [exchange(mine[d], 2 * d) for d in range(1, 4)]
        pairs = [exchange(part, 1) for part in blocks]
        result = attend(mine, blocks[1:] + pairs, key_code, low, high, count)
        paired = exchange(result, 1)
        across = place_rows(bases[4:], result, paired, places, per_dev)
        arrived = exchange(across, 8)
        staying = place_rows(bases[:4], result, paired, places, per_dev)
        joined = staying + arrived
        attention[0].append(joined[0])
        for d in range(1, 4):
            attention[d].append(exchange(joined[d], 2 * d))

    away = project_out(attention, w_out, spot, 1 - side, jnp.bfloat16)
    away = lax.ppermute(away, "head", [(0, 1), (1, 0)])
    stay = project_out(attention, w_out, spot, side, jnp.float32)
    return (stay + away.astype(jnp.float32)).astype(jnp.bfloat16)


def solution(mesh):
    in_specs = (
        P("ctx", "head"),
        P(),
        P(),
        P(None, None, "head"),
        P("head", None),
        P(),
        P(),
        P(),
        P(),
    )
    out_specs = P("ctx", "head")

    def body(inputs, norm_gain, level_table, w_qkv, *rest):
        ranks, sides = mesh.shape["ctx"], mesh.shape["head"]
        heads_here = w_qkv.shape[2] // HEAD_DIM
        halved = (
            ranks == 16
            and sides == 2
            and ranks * inputs.shape[0] == 2 * MAXCLIP
            and heads_here % 4 == 0
        )
        run = halved_body if halved else gathered_body
        return run(inputs, norm_gain, level_table, w_qkv, *rest)

    return jax.shard_map(body, mesh=mesh, in_specs=in_specs, out_specs=out_specs, check_vma=False)
```

```python
import jax
import jax.numpy as jnp
from jax import lax
from jax.experimental import pallas as pl
from jax.experimental.pallas import tpu as pltpu
from jax.sharding import PartitionSpec as P

HEAD_DIM = 128


NEG = -1e30
EPS = 1e-06
MAXCLIP = 2560
LOG2E = 1.4426950408889634
MIB = 1024 * 1024
COST = 1000000


def clip_tables(total_rows, clip_lengths, prefix_lengths, noise_levels):
    rows = jnp.arange(total_rows, dtype=jnp.int32)
    ends = jnp.cumsum(clip_lengths)
    begins = ends - clip_lengths
    clip_of = jnp.sum((rows[:, None] >= ends[None, :]).astype(jnp.int32), axis=1)
    member = clip_of[:, None] == jnp.arange(clip_lengths.shape[0], dtype=jnp.int32)[None, :]
    begin_row = jnp.sum(jnp.where(member, begins[None, :], 0), axis=1)
    lead = jnp.minimum(prefix_lengths, clip_lengths)
    lead_row = jnp.sum(jnp.where(member, lead[None, :], 0), axis=1)
    level_row = jnp.sum(jnp.where(member, noise_levels[None, :], 0), axis=1)
    in_prefix = rows - begin_row < lead_row
    return (clip_of, in_prefix, level_row)


def rank_tables(token_rank, ranks, per_rank):
    onehot = (token_rank[:, None] == jnp.arange(ranks, dtype=jnp.int32)[None, :]).astype(jnp.int32)
    earlier = jnp.cumsum(onehot, axis=0) - onehot
    within = jnp.sum(earlier * onehot, axis=1)
    counts = jnp.sum(onehot.reshape(ranks, per_rank, ranks), axis=1)
    starts = jnp.cumsum(counts, axis=0) - counts
    return (within, counts, starts)


def normalize(rows, in_prefix, level_row, level_table, norm_gain):
    picks = (
        level_row[:, None] == jnp.arange(level_table.shape[0], dtype=jnp.int32)[None, :]
    ) & in_prefix[:, None]
    added = jnp.dot(picks.astype(jnp.bfloat16), level_table, preferred_element_type=jnp.float32)
    shifted = rows.astype(jnp.float32) + added
    factor = lax.rsqrt(jnp.mean(shifted * shifted, axis=-1, keepdims=True) + EPS)
    return (shifted * factor * norm_gain).astype(jnp.bfloat16)


def fold_keys(state, queries, query_clip, query_prefix, pairs, key_clip, key_prefix):
    width = queries.shape[1]
    heads_here = width // HEAD_DIM
    factor = HEAD_DIM ** (-0.5)
    allowed_query = jnp.logical_not(query_prefix)

    def absorb(carry, block):
        block_pairs, block_clip, block_prefix = block
        allowed = (query_clip[:, None] == block_clip[None, :]) & (
            allowed_query[:, None] | block_prefix[None, :]
        )
        updated = []
        for head in range(heads_here):
            top, total, summed = carry[head]
            low = head * HEAD_DIM
            q_head = queries[:, low : low + HEAD_DIM]
            k_head = block_pairs[:, low : low + HEAD_DIM]
            v_head = block_pairs[:, width + low : width + low + HEAD_DIM]
            scores = (
                lax.dot_general(
                    q_head, k_head, (((1,), (1,)), ((), ())), preferred_element_type=jnp.float32
                )
                * factor
            )
            masked = jnp.where(allowed, scores, NEG)
            new_top = jnp.maximum(top, jnp.max(masked, axis=1, keepdims=True))
            fade = jnp.exp(top - new_top)
            weights = jnp.where(allowed, jnp.exp(scores - new_top), 0.0)
            total = total * fade + jnp.sum(weights, axis=1, keepdims=True)
            summed = summed * fade + jnp.dot(
                weights.astype(jnp.bfloat16), v_head, preferred_element_type=jnp.float32
            )
            updated.append((new_top, total, summed))
        return (tuple(updated), None)

    count = pairs.shape[0]
    step = 2048 if count > 2048 and count % 2048 == 0 else count
    if step == count:
        result, unused = absorb(state, (pairs, key_clip, key_prefix))
        return result
    stacked = (
        pairs.reshape(count // step, step, pairs.shape[1]),
        key_clip.reshape(count // step, step),
        key_prefix.reshape(count // step, step),
    )
    result, unused = lax.scan(absorb, state, stacked)
    return result


def gathered_body(
    inputs,
    norm_gain,
    level_table,
    w_qkv,
    w_out,
    clip_lengths,
    prefix_lengths,
    noise_levels,
    token_rank,
):
    ranks = lax.axis_size("ctx")
    rank_here = lax.axis_index("ctx")
    per_dev = inputs.shape[0]
    slots = 2 * per_dev // ranks
    local_width = w_qkv.shape[2]
    heads_here = local_width // HEAD_DIM
    total_rows = per_dev * ranks
    clip_of, in_prefix, level_row = clip_tables(
        total_rows, clip_lengths, prefix_lengths, noise_levels
    )
    within, counts, starts = rank_tables(token_rank, ranks, per_dev)
    place = token_rank * per_dev + within
    order = (
        jnp.zeros((total_rows,), jnp.int32).at[place].set(jnp.arange(total_rows, dtype=jnp.int32))
    )
    first = rank_here * per_dev
    own_rank = lax.dynamic_slice_in_dim(token_rank, first, per_dev, 0)
    own_within = lax.dynamic_slice_in_dim(within, first, per_dev, 0)
    send_starts = lax.dynamic_slice_in_dim(starts, rank_here, 1, 0)[0]
    recv_counts = lax.dynamic_slice_in_dim(counts, rank_here, 1, 1)[:, 0]
    recv_starts = lax.dynamic_slice_in_dim(starts, rank_here, 1, 1)[:, 0]
    balanced_rows = lax.dynamic_slice_in_dim(order, first, per_dev, 0)
    target = own_rank * slots + own_within - send_starts[own_rank]
    buffer = jnp.zeros((ranks * slots, inputs.shape[1]), inputs.dtype).at[target].set(inputs)
    received = lax.all_to_all(
        buffer.reshape(ranks, slots, inputs.shape[1]),
        "ctx",
        split_axis=0,
        concat_axis=0,
        tiled=True,
    )
    spots = jnp.arange(slots, dtype=jnp.int32)[None, :]
    index = jnp.where(spots < recv_counts[:, None], recv_starts[:, None] + spots, per_dev).reshape(
        -1
    )
    flat = received.reshape(ranks * slots, received.shape[2])
    rows = jnp.zeros((per_dev, received.shape[2]), received.dtype).at[index].set(flat, mode="drop")
    full_rows = lax.all_gather(rows, "head", axis=1, tiled=True)
    normed = normalize(
        full_rows, in_prefix[balanced_rows], level_row[balanced_rows], level_table, norm_gain
    )
    qkv = jnp.dot(
        normed, w_qkv.reshape(w_qkv.shape[0], 3 * local_width), preferred_element_type=jnp.float32
    ).astype(jnp.bfloat16)
    start_state = tuple(
        (
            (
                jnp.full((per_dev, 1), NEG, jnp.float32),
                jnp.zeros((per_dev, 1), jnp.float32),
                jnp.zeros((per_dev, HEAD_DIM), jnp.float32),
            )
            for head in range(heads_here)
        )
    )
    key_clip = clip_of[order]
    key_prefix = in_prefix[order]
    query_clip = lax.dynamic_slice_in_dim(key_clip, first, per_dev, 0)
    query_prefix = lax.dynamic_slice_in_dim(key_prefix, first, per_dev, 0)
    queries = qkv[:, :local_width]
    pairs = qkv[:, local_width:]
    state = fold_keys(
        start_state,
        queries,
        query_clip,
        query_prefix,
        lax.all_gather(pairs, "ctx", axis=0, tiled=True),
        key_clip,
        key_prefix,
    )
    parts = [state[head][2] / state[head][1] for head in range(heads_here)]
    attention = jnp.concatenate(parts, axis=1).astype(jnp.bfloat16)
    terms = jnp.dot(attention, w_out, preferred_element_type=jnp.float32)
    return lax.psum_scatter(terms.astype(jnp.bfloat16), "head", scatter_dimension=1, tiled=True)


def project_kernel(rows_ref, w_ref, *rest):
    out_ref = rest[-1]
    weights = jnp.concatenate([w_ref[0], w_ref[1], w_ref[2]], axis=1)
    out_ref[0] = jnp.dot(
        rows_ref[...], weights, preferred_element_type=jnp.float32
    ).astype(jnp.bfloat16)


def project_heads(normed, w_parts, first_head, count, group_heads, after):
    rows, depth = normed.shape
    return pl.pallas_call(
        project_kernel,
        grid=(4, count),
        in_specs=[
            pl.BlockSpec((rows, depth), lambda m, h: (0, 0)),
            pl.BlockSpec(
                (3, depth, HEAD_DIM), lambda m, h: (0, 0, group_heads * m + first_head + h)
            ),
        ]
        + [pl.BlockSpec(memory_space=pl.ANY)] * len(after),
        out_specs=pl.BlockSpec((1, rows, 3 * HEAD_DIM), lambda m, h: (m, 0, h)),
        out_shape=jax.ShapeDtypeStruct((4, rows, count * 3 * HEAD_DIM), jnp.bfloat16),
        compiler_params=pltpu.CompilerParams(vmem_limit_bytes=20 * MIB),
        cost_estimate=pl.CostEstimate(flops=COST, bytes_accessed=COST, transcendentals=0),
    )(normed, w_parts, *after)


def attend_kernel(own_ref, pair_ref, query_mask_ref, key_mask_ref, *rest):
    out_ref, q_all, k_all, v_all = rest[-4:]
    slots, rows = own_ref.shape[:2]
    tile = out_ref.shape[0]
    step = pl.program_id(1)

    @pl.when((pl.program_id(0) == 0) & (step == 0))
    def _():
        q_all[:, HEAD_DIM:] = query_mask_ref[...]
        k_all[:, HEAD_DIM:] = key_mask_ref[...]

    @pl.when(step == 0)
    def _():
        for index in range(2 * slots):
            spot = slice(index * rows, (index + 1) * rows)
            block = (own_ref if index < slots else pair_ref)[index % slots]
            if index < slots:
                q_all[spot, :HEAD_DIM] = block[:, :HEAD_DIM]
            k_all[spot, :HEAD_DIM] = block[:, HEAD_DIM : 2 * HEAD_DIM]
            v_all[spot, :] = block[:, 2 * HEAD_DIM :]

    queries = q_all[pl.ds(pl.multiple_of(step * tile, tile), tile), :]
    scores = lax.dot_general(
        queries, k_all[...], (((1,), (1,)), ((), ())), preferred_element_type=jnp.float32
    )
    top = jnp.max(scores, axis=1, keepdims=True)
    weights = jnp.exp2((scores - top) * (HEAD_DIM ** (-0.5) * LOG2E))
    total = jnp.sum(weights, axis=1, keepdims=True)
    summed = jnp.dot(weights.astype(jnp.bfloat16), v_all[...], preferred_element_type=jnp.float32)
    out_ref[...] = (summed / total).astype(jnp.bfloat16)


def attend(own, pair, query_mask, key_mask, count, after):
    slots, rows = own.shape[:2]
    keys, queries, tile = 2 * slots * rows, slots * rows, 256
    width = 3 * HEAD_DIM
    block = pl.BlockSpec((slots, rows, width), lambda h, t: (0, 0, h))
    return pl.pallas_call(
        attend_kernel,
        grid=(count, queries // tile),
        in_specs=[
            block,
            block,
            pl.BlockSpec((queries, HEAD_DIM), lambda h, t: (0, 0)),
            pl.BlockSpec((keys, HEAD_DIM), lambda h, t: (0, 0)),
        ]
        + [pl.BlockSpec(memory_space=pl.ANY)] * len(after),
        out_specs=pl.BlockSpec((tile, HEAD_DIM), lambda h, t: (t, h)),
        out_shape=jax.ShapeDtypeStruct((queries, count * HEAD_DIM), jnp.bfloat16),
        scratch_shapes=[
            pltpu.VMEM((queries, 2 * HEAD_DIM), jnp.bfloat16),
            pltpu.VMEM((keys, 2 * HEAD_DIM), jnp.bfloat16),
            pltpu.VMEM((keys, HEAD_DIM), jnp.bfloat16),
        ],
        compiler_params=pltpu.CompilerParams(vmem_limit_bytes=24 * MIB),
        cost_estimate=pl.CostEstimate(flops=COST, bytes_accessed=COST, transcendentals=0),
    )(own, pair, query_mask, key_mask, *after)


def place_kernel(core_ref, own_ref, pair_ref, place_ref, out_ref):
    rows = out_ref.shape[1]
    half = own_ref.shape[0]
    rank = 2 * pl.program_id(0) + core_ref[0]
    wanted = rows * rank + lax.broadcasted_iota(jnp.int32, (rows, 1), 0)
    picks = jnp.where(place_ref[...] == wanted, 1.0, 0.0).astype(jnp.bfloat16)
    out_ref[0] = (
        jnp.dot(picks[:, :half], own_ref[...], preferred_element_type=jnp.float32)
        + jnp.dot(picks[:, half:], pair_ref[...], preferred_element_type=jnp.float32)
    ).astype(jnp.bfloat16)


def place_rows(core, own, pair, places, slots, rows):
    half, width = own.shape
    block = pl.BlockSpec((half, width), lambda n, core_ref: (0, 0))
    return pl.pallas_call(
        place_kernel,
        grid_spec=pltpu.PrefetchScalarGridSpec(
            num_scalar_prefetch=1,
            grid=(slots,),
            in_specs=[block, block, pl.BlockSpec((1, 2 * half), lambda n, core_ref: (0, 0))],
            out_specs=pl.BlockSpec((1, rows, width), lambda n, core_ref: (n, 0, 0)),
        ),
        out_shape=jax.ShapeDtypeStruct((slots, rows, width), jnp.bfloat16),
        compiler_params=pltpu.CompilerParams(vmem_limit_bytes=20 * MIB),
        cost_estimate=pl.CostEstimate(flops=COST, bytes_accessed=COST, transcendentals=0),
    )(core, own, pair, places)


def out_kernel(side_ref, *refs):
    w_ref, out_ref = refs[-2:]
    columns = []
    for m in range(4):
        for ref in refs[:-2]:
            columns.append(ref[m] + ref[4 + m])
    rows = jnp.concatenate(columns, axis=1)
    out_ref[...] = jnp.dot(rows, w_ref[...], preferred_element_type=jnp.float32).astype(
        out_ref.dtype
    )


def project_out(parts, w_out, side, dtype):
    rows = parts[0].shape[1]
    depth = w_out.shape[0]
    columns, tile = w_out.shape[1] // 2, 512
    tiles = columns // tile
    return pl.pallas_call(
        out_kernel,
        grid_spec=pltpu.PrefetchScalarGridSpec(
            num_scalar_prefetch=1,
            grid=(tiles,),
            in_specs=[
                pl.BlockSpec(part.shape, lambda t, side_ref: (0, 0, 0)) for part in parts
            ]
            + [pl.BlockSpec((depth, tile), lambda t, side_ref: (0, side_ref[0] * tiles + t))],
            out_specs=pl.BlockSpec((rows, tile), lambda t, side_ref: (0, t)),
        ),
        out_shape=jax.ShapeDtypeStruct((rows, columns), dtype),
        compiler_params=pltpu.CompilerParams(vmem_limit_bytes=20 * MIB),
        cost_estimate=pl.CostEstimate(flops=COST, bytes_accessed=COST, transcendentals=0),
    )(side.reshape(1), *parts, w_out)


def row_facts(rows, clip_lengths, prefix_lengths, noise_levels):
    ends = jnp.cumsum(clip_lengths)
    begins = ends - clip_lengths
    lead = begins + jnp.minimum(prefix_lengths, clip_lengths)
    past = rows[:, None] >= ends[None, :]
    clip = jnp.sum(past.astype(jnp.int32), axis=1)
    inside = (rows[:, None] >= begins[None, :]) & jnp.logical_not(past)
    in_prefix = jnp.any(inside & (rows[:, None] < lead[None, :]), axis=1)
    level = jnp.sum(jnp.where(inside, noise_levels[None, :], 0), axis=1)
    return clip, in_prefix, level


CHUNKS = ((0, 1), (1, 1), (2, 1))
SWAP_ROWS = (160, 160)


def halved_body(
    inputs,
    norm_gain,
    level_table,
    w_qkv,
    w_out,
    clip_lengths,
    prefix_lengths,
    noise_levels,
    token_rank,
):
    rank_here = lax.axis_index("ctx")
    side = lax.axis_index("head")
    per_dev = inputs.shape[0]
    ranks = 16
    half_rows = 8 * per_dev
    local_width = w_qkv.shape[2]
    group_heads = local_width // HEAD_DIM // 4
    clips = clip_lengths.shape[0]
    half, block, core = rank_here // 8, rank_here % 8, rank_here % 2
    half_groups = [[8 * h + 2 * m + c for m in range(4)] for h in range(2) for c in range(2)]
    core_groups = [[2 * n + c for n in range(8)] for c in range(2)]

    def spread(array, groups):
        return lax.all_to_all(array, "ctx", 0, 0, axis_index_groups=groups, tiled=True)

    def with_pair(array):
        return lax.ppermute(array, "ctx", [(r, r ^ 1) for r in range(ranks)])

    begins = jnp.cumsum(clip_lengths) - clip_lengths
    start = jnp.sum(jnp.where(clip_lengths == MAXCLIP, begins, 0))
    early = start <= half_rows // 2

    def packed_row(spots):
        swapped = jnp.where(early, spots < start, spots >= start)
        return spots + half_rows * (half ^ swapped.astype(jnp.int32)), swapped

    own_packed, own_swapped = packed_row(block * per_dev + jnp.arange(per_dev, dtype=jnp.int32))

    def gather_rows(blocks):
        def run(rows, swapped):
            pairs = [(r, r ^ 8) for r in range(ranks) if r % 8 in blocks]
            bounds = [sum(SWAP_ROWS[:i]) for i in range(len(SWAP_ROWS) + 1)]
            cuts = list(zip(bounds[:-1], bounds[1:]))
            moved = [lax.ppermute(rows[low:high], "ctx", pairs) for low, high in cuts]
            kept = [
                jnp.where(swapped[low:high, None], part, rows[low:high])
                for part, (low, high) in zip(moved, cuts)
            ]
            other = [lax.ppermute(part, "head", [(0, 1), (1, 0)]) for part in kept]
            return tuple(kept), tuple(other)

        return run

    kept, other = lax.cond(
        early, gather_rows(range(4)), gather_rows(range(4, 8)), inputs, own_swapped
    )
    rows, other = jnp.concatenate(kept, axis=0), jnp.concatenate(other, axis=0)
    full_rows = jnp.where(
        side == 0,
        jnp.concatenate([rows, other], axis=1),
        jnp.concatenate([other, rows], axis=1),
    )
    unused, own_prefix, own_level = row_facts(
        own_packed, clip_lengths, prefix_lengths, noise_levels
    )
    normed = normalize(full_rows, own_prefix, own_level, level_table, norm_gain)

    order = jnp.concatenate([2 * jnp.arange(4) + core, 2 * jnp.arange(4) + 1 - core]).astype(
        jnp.int32
    )
    spots = (order[:, None] * per_dev + jnp.arange(per_dev, dtype=jnp.int32)[None, :]).reshape(-1)
    packed, unused = packed_row(spots)
    clip, in_prefix, unused = row_facts(packed, clip_lengths, prefix_lengths, noise_levels)
    column = jnp.arange(HEAD_DIM, dtype=jnp.int32)[None, :]
    same = column == clip[:, None]
    last = column == clips
    own_rows = half_rows // 2
    query_mask = jnp.where(
        same[:own_rows] | (last & in_prefix[:own_rows, None]), 1.0, 0.0
    ).astype(jnp.bfloat16)
    key_mask = jnp.where(
        ((column < clips) & jnp.logical_not(same)) | (last & jnp.logical_not(in_prefix)[:, None]),
        NEG,
        0.0,
    ).astype(jnp.bfloat16)

    within, unused, unused = rank_tables(token_rank, ranks, per_dev)
    place = token_rank * per_dev + within
    every_packed, unused = packed_row(jnp.arange(half_rows, dtype=jnp.int32))
    half_place = jnp.where(every_packed >= half_rows, place[half_rows:], place[:half_rows])
    half_place = half_place.reshape(4, 2, per_dev)
    places = jnp.where(
        core == 0,
        jnp.concatenate([half_place[:, 0], half_place[:, 1]], axis=0),
        jnp.concatenate([half_place[:, 1], half_place[:, 0]], axis=0),
    ).reshape(1, half_rows)

    w_parts = jnp.transpose(w_qkv, (1, 0, 2))
    arrived, after = [], []
    for first_head, count in CHUNKS:
        mine = project_heads(normed, w_parts, first_head, count, group_heads, [])
        arrived.append(spread(mine, half_groups))
    parts = []
    for (first_head, count), own in zip(CHUNKS, arrived):
        result = attend(own, with_pair(own), query_mask, key_mask, count, after)
        placed = place_rows(core.reshape(1), result, with_pair(result), places, 8, per_dev)
        after = [placed]
        parts.append(spread(placed, core_groups))

    away = project_out(parts, w_out, 1 - side, jnp.bfloat16)
    away = lax.ppermute(away, "head", [(0, 1), (1, 0)])
    stay = project_out(parts, w_out, side, jnp.float32)
    return (stay + away.astype(jnp.float32)).astype(jnp.bfloat16)


def solution(mesh):
    in_specs = (
        P("ctx", "head"),
        P(),
        P(),
        P(None, None, "head"),
        P("head", None),
        P(),
        P(),
        P(),
        P(),
    )
    out_specs = P("ctx", "head")

    def body(inputs, norm_gain, level_table, w_qkv, *rest):
        ranks, sides = mesh.shape["ctx"], mesh.shape["head"]
        heads_here = w_qkv.shape[2] // HEAD_DIM
        halved = (
            ranks == 16
            and sides == 2
            and ranks * inputs.shape[0] == 2 * MAXCLIP
            and heads_here % 4 == 0
        )
        run = halved_body if halved else gathered_body
        return run(inputs, norm_gain, level_table, w_qkv, *rest)

    return jax.shard_map(body, mesh=mesh, in_specs=in_specs, out_specs=out_specs, check_vma=False)
```

```python
import jax
import jax.numpy as jnp
from jax import lax
from jax.experimental import pallas as pl
from jax.experimental.pallas import tpu as pltpu
from jax.sharding import PartitionSpec as P

HEAD_DIM = 128


NEG = -1e30
EPS = 1e-06
MAXCLIP = 2560
LOG2E = 1.4426950408889634
MIB = 1024 * 1024
COST = 1000000


def clip_tables(total_rows, clip_lengths, prefix_lengths, noise_levels):
    rows = jnp.arange(total_rows, dtype=jnp.int32)
    ends = jnp.cumsum(clip_lengths)
    begins = ends - clip_lengths
    clip_of = jnp.sum((rows[:, None] >= ends[None, :]).astype(jnp.int32), axis=1)
    member = clip_of[:, None] == jnp.arange(clip_lengths.shape[0], dtype=jnp.int32)[None, :]
    begin_row = jnp.sum(jnp.where(member, begins[None, :], 0), axis=1)
    lead = jnp.minimum(prefix_lengths, clip_lengths)
    lead_row = jnp.sum(jnp.where(member, lead[None, :], 0), axis=1)
    level_row = jnp.sum(jnp.where(member, noise_levels[None, :], 0), axis=1)
    in_prefix = rows - begin_row < lead_row
    return (clip_of, in_prefix, level_row)


def rank_tables(token_rank, ranks, per_rank):
    onehot = (token_rank[:, None] == jnp.arange(ranks, dtype=jnp.int32)[None, :]).astype(jnp.int32)
    earlier = jnp.cumsum(onehot, axis=0) - onehot
    within = jnp.sum(earlier * onehot, axis=1)
    counts = jnp.sum(onehot.reshape(ranks, per_rank, ranks), axis=1)
    starts = jnp.cumsum(counts, axis=0) - counts
    return (within, counts, starts)


def normalize(rows, in_prefix, level_row, level_table, norm_gain):
    picks = (
        level_row[:, None] == jnp.arange(level_table.shape[0], dtype=jnp.int32)[None, :]
    ) & in_prefix[:, None]
    added = jnp.dot(picks.astype(jnp.bfloat16), level_table, preferred_element_type=jnp.float32)
    shifted = rows.astype(jnp.float32) + added
    factor = lax.rsqrt(jnp.mean(shifted * shifted, axis=-1, keepdims=True) + EPS)
    return (shifted * factor * norm_gain).astype(jnp.bfloat16)


def fold_keys(state, queries, query_clip, query_prefix, pairs, key_clip, key_prefix):
    width = queries.shape[1]
    heads_here = width // HEAD_DIM
    factor = HEAD_DIM ** (-0.5)
    allowed_query = jnp.logical_not(query_prefix)

    def absorb(carry, block):
        block_pairs, block_clip, block_prefix = block
        allowed = (query_clip[:, None] == block_clip[None, :]) & (
            allowed_query[:, None] | block_prefix[None, :]
        )
        updated = []
        for head in range(heads_here):
            top, total, summed = carry[head]
            low = head * HEAD_DIM
            q_head = queries[:, low : low + HEAD_DIM]
            k_head = block_pairs[:, low : low + HEAD_DIM]
            v_head = block_pairs[:, width + low : width + low + HEAD_DIM]
            scores = (
                lax.dot_general(
                    q_head, k_head, (((1,), (1,)), ((), ())), preferred_element_type=jnp.float32
                )
                * factor
            )
            masked = jnp.where(allowed, scores, NEG)
            new_top = jnp.maximum(top, jnp.max(masked, axis=1, keepdims=True))
            fade = jnp.exp(top - new_top)
            weights = jnp.where(allowed, jnp.exp(scores - new_top), 0.0)
            total = total * fade + jnp.sum(weights, axis=1, keepdims=True)
            summed = summed * fade + jnp.dot(
                weights.astype(jnp.bfloat16), v_head, preferred_element_type=jnp.float32
            )
            updated.append((new_top, total, summed))
        return (tuple(updated), None)

    count = pairs.shape[0]
    step = 2048 if count > 2048 and count % 2048 == 0 else count
    if step == count:
        result, unused = absorb(state, (pairs, key_clip, key_prefix))
        return result
    stacked = (
        pairs.reshape(count // step, step, pairs.shape[1]),
        key_clip.reshape(count // step, step),
        key_prefix.reshape(count // step, step),
    )
    result, unused = lax.scan(absorb, state, stacked)
    return result


def gathered_body(
    inputs,
    norm_gain,
    level_table,
    w_qkv,
    w_out,
    clip_lengths,
    prefix_lengths,
    noise_levels,
    token_rank,
):
    ranks = lax.axis_size("ctx")
    rank_here = lax.axis_index("ctx")
    per_dev = inputs.shape[0]
    slots = 2 * per_dev // ranks
    local_width = w_qkv.shape[2]
    heads_here = local_width // HEAD_DIM
    total_rows = per_dev * ranks
    clip_of, in_prefix, level_row = clip_tables(
        total_rows, clip_lengths, prefix_lengths, noise_levels
    )
    within, counts, starts = rank_tables(token_rank, ranks, per_dev)
    place = token_rank * per_dev + within
    order = (
        jnp.zeros((total_rows,), jnp.int32).at[place].set(jnp.arange(total_rows, dtype=jnp.int32))
    )
    first = rank_here * per_dev
    own_rank = lax.dynamic_slice_in_dim(token_rank, first, per_dev, 0)
    own_within = lax.dynamic_slice_in_dim(within, first, per_dev, 0)
    send_starts = lax.dynamic_slice_in_dim(starts, rank_here, 1, 0)[0]
    recv_counts = lax.dynamic_slice_in_dim(counts, rank_here, 1, 1)[:, 0]
    recv_starts = lax.dynamic_slice_in_dim(starts, rank_here, 1, 1)[:, 0]
    balanced_rows = lax.dynamic_slice_in_dim(order, first, per_dev, 0)
    target = own_rank * slots + own_within - send_starts[own_rank]
    buffer = jnp.zeros((ranks * slots, inputs.shape[1]), inputs.dtype).at[target].set(inputs)
    received = lax.all_to_all(
        buffer.reshape(ranks, slots, inputs.shape[1]),
        "ctx",
        split_axis=0,
        concat_axis=0,
        tiled=True,
    )
    spots = jnp.arange(slots, dtype=jnp.int32)[None, :]
    index = jnp.where(spots < recv_counts[:, None], recv_starts[:, None] + spots, per_dev).reshape(
        -1
    )
    flat = received.reshape(ranks * slots, received.shape[2])
    rows = jnp.zeros((per_dev, received.shape[2]), received.dtype).at[index].set(flat, mode="drop")
    full_rows = lax.all_gather(rows, "head", axis=1, tiled=True)
    normed = normalize(
        full_rows, in_prefix[balanced_rows], level_row[balanced_rows], level_table, norm_gain
    )
    qkv = jnp.dot(
        normed, w_qkv.reshape(w_qkv.shape[0], 3 * local_width), preferred_element_type=jnp.float32
    ).astype(jnp.bfloat16)
    start_state = tuple(
        (
            (
                jnp.full((per_dev, 1), NEG, jnp.float32),
                jnp.zeros((per_dev, 1), jnp.float32),
                jnp.zeros((per_dev, HEAD_DIM), jnp.float32),
            )
            for head in range(heads_here)
        )
    )
    key_clip = clip_of[order]
    key_prefix = in_prefix[order]
    query_clip = lax.dynamic_slice_in_dim(key_clip, first, per_dev, 0)
    query_prefix = lax.dynamic_slice_in_dim(key_prefix, first, per_dev, 0)
    queries = qkv[:, :local_width]
    pairs = qkv[:, local_width:]
    state = fold_keys(
        start_state,
        queries,
        query_clip,
        query_prefix,
        lax.all_gather(pairs, "ctx", axis=0, tiled=True),
        key_clip,
        key_prefix,
    )
    parts = [state[head][2] / state[head][1] for head in range(heads_here)]
    attention = jnp.concatenate(parts, axis=1).astype(jnp.bfloat16)
    terms = jnp.dot(attention, w_out, preferred_element_type=jnp.float32)
    return lax.psum_scatter(terms.astype(jnp.bfloat16), "head", scatter_dimension=1, tiled=True)


def norm_kernel(side_ref, *refs):
    pieces = (len(refs) - 4) // 2
    picks_ref, level_ref, gain_ref, out_ref = refs[-4:]
    width = out_ref.shape[1] // 2
    spots = [pl.ds(pl.multiple_of(s * width, 128), width) for s in (side_ref[0], 1 - side_ref[0])]
    low = 0
    for piece in range(pieces):
        own_ref, other_ref = refs[piece], refs[pieces + piece]
        rows = slice(low, low + own_ref.shape[0])
        low += own_ref.shape[0]
        picks = picks_ref[rows, :]
        shifted = [
            ref[...].astype(jnp.float32)
            + jnp.dot(picks, level_ref[:, spot], preferred_element_type=jnp.float32)
            for ref, spot in zip((own_ref, other_ref), spots)
        ]
        squares = sum(jnp.sum(part * part, axis=1, keepdims=True) for part in shifted)
        factor = lax.rsqrt(squares / (2 * width) + EPS)
        for part, spot in zip(shifted, spots):
            out_ref[rows, spot] = (part * factor * gain_ref[:, spot]).astype(jnp.bfloat16)


def normalize_rows(kept, other, picks, level_table, norm_gain, side):
    rows = sum(part.shape[0] for part in kept)
    vmem = pl.BlockSpec(memory_space=pltpu.VMEM)
    return pl.pallas_call(
        norm_kernel,
        in_specs=[pl.BlockSpec(memory_space=pltpu.SMEM)] + [vmem] * (2 * len(kept) + 3),
        out_specs=vmem,
        out_shape=jax.ShapeDtypeStruct((rows, 2 * kept[0].shape[1]), jnp.bfloat16),
        compiler_params=pltpu.CompilerParams(vmem_limit_bytes=48 * MIB),
        cost_estimate=pl.CostEstimate(flops=COST, bytes_accessed=COST, transcendentals=0),
    )(side.reshape(1), *kept, *other, picks, level_table, norm_gain.reshape(1, -1))


def project_kernel(rows_ref, first_ref, second_ref, *rest):
    out_ref = rest[-1]
    width = out_ref.shape[2]
    weights = jnp.concatenate(
        [first_ref[0], first_ref[1], first_ref[2], second_ref[0], second_ref[1], second_ref[2]],
        axis=1,
    )
    outcome = jnp.dot(rows_ref[...], weights, preferred_element_type=jnp.float32)
    out_ref[0] = outcome[:, :width].astype(jnp.bfloat16)
    out_ref[1] = outcome[:, width:].astype(jnp.bfloat16)


def project_heads(normed, w_parts, head, group_heads, after):
    rows, depth = normed.shape

    def w_spec(odd):
        return pl.BlockSpec(
            (3, depth, HEAD_DIM), lambda i: (0, 0, group_heads * (2 * i + odd) + head)
        )

    return pl.pallas_call(
        project_kernel,
        grid=(2,),
        in_specs=[pl.BlockSpec((rows, depth), lambda i: (0, 0)), w_spec(0), w_spec(1)]
        + [pl.BlockSpec(memory_space=pl.ANY)] * len(after),
        out_specs=pl.BlockSpec((2, rows, 3 * HEAD_DIM), lambda i: (i, 0, 0)),
        out_shape=jax.ShapeDtypeStruct((4, rows, 3 * HEAD_DIM), jnp.bfloat16),
        compiler_params=pltpu.CompilerParams(vmem_limit_bytes=48 * MIB),
        cost_estimate=pl.CostEstimate(flops=COST, bytes_accessed=COST, transcendentals=0),
    )(normed, w_parts, w_parts, *after)


def attend_kernel(runs_ref, own_ref, pair_ref, order_ref, query_mask_ref, key_mask_ref, *rest):
    out_ref, q_all, k_all, v_all, q_sorted, sorted_out = rest[-6:]
    slots, rows = own_ref.shape[:2]
    queries = q_sorted.shape[0]
    for index in range(2 * slots):
        spot = slice(index * rows, (index + 1) * rows)
        block = (own_ref if index < slots else pair_ref)[index % slots]
        q_all[spot, :HEAD_DIM] = block[:, :HEAD_DIM]
        k_all[spot, :HEAD_DIM] = block[:, HEAD_DIM : 2 * HEAD_DIM]
        v_all[spot, :] = block[:, 2 * HEAD_DIM :]
    q_all[:, HEAD_DIM:] = query_mask_ref[...]
    k_all[:, HEAD_DIM:] = key_mask_ref[...]

    tile = queries // 3
    for step in range(3):
        spot = slice(step * tile, (step + 1) * tile)
        wanted = step * tile + lax.broadcasted_iota(jnp.int32, (tile, 1), 0)
        picks = jnp.where(order_ref[...] == wanted, 1.0, 0.0).astype(jnp.bfloat16)
        q_sorted[spot, :] = jnp.dot(
            picks, q_all[...], preferred_element_type=jnp.float32
        ).astype(jnp.bfloat16)

    tile = queries // ATTEND_TILES
    for step in range(ATTEND_TILES):
        scores = lax.dot_general(
            q_sorted[step * tile : (step + 1) * tile, :],
            k_all[...],
            (((1,), (1,)), ((), ())),
            preferred_element_type=jnp.float32,
        )
        top = jnp.max(scores, axis=1, keepdims=True)
        weights = jnp.exp2((scores - top) * (HEAD_DIM ** (-0.5) * LOG2E))
        total = jnp.sum(weights, axis=1, keepdims=True)
        summed = jnp.dot(
            weights.astype(jnp.bfloat16), v_all[...], preferred_element_type=jnp.float32
        )
        sorted_out[rows + step * tile : rows + (step + 1) * tile, :] = summed / total

    row = lax.broadcasted_iota(jnp.int32, (rows, 1), 0)
    for n in range(out_ref.shape[0]):
        first = sorted_out[pl.ds(rows + runs_ref[3, n], rows), :]
        second = sorted_out[pl.ds(rows + runs_ref[4, n], rows), :]
        in_second = (row >= runs_ref[1, n]) & (row < runs_ref[2, n])
        taken = jnp.where(row < runs_ref[0, n], first, jnp.where(in_second, second, 0.0))
        out_ref[n] = taken.astype(jnp.bfloat16)


def attend(runs, own, pair, order, query_mask, key_mask, after):
    slots, rows = own.shape[:2]
    keys = 2 * slots * rows
    queries = keys // 2 + rows // 2
    vmem = pl.BlockSpec(memory_space=pltpu.VMEM)
    return pl.pallas_call(
        attend_kernel,
        in_specs=[pl.BlockSpec(memory_space=pltpu.SMEM)]
        + [vmem] * 5
        + [pl.BlockSpec(memory_space=pl.ANY)] * len(after),
        out_specs=vmem,
        out_shape=jax.ShapeDtypeStruct((2 * slots, rows, HEAD_DIM), jnp.bfloat16),
        scratch_shapes=[
            pltpu.VMEM((keys, 2 * HEAD_DIM), jnp.bfloat16),
            pltpu.VMEM((keys, 2 * HEAD_DIM), jnp.bfloat16),
            pltpu.VMEM((keys, HEAD_DIM), jnp.bfloat16),
            pltpu.VMEM((queries, 2 * HEAD_DIM), jnp.bfloat16),
            pltpu.VMEM((queries + 2 * rows, HEAD_DIM), jnp.float32),
        ],
        compiler_params=pltpu.CompilerParams(vmem_limit_bytes=48 * MIB),
        cost_estimate=pl.CostEstimate(flops=COST, bytes_accessed=COST, transcendentals=0),
    )(runs, own, pair, order, query_mask, key_mask, *after)


def out_kernel(side_ref, *refs):
    w_ref, out_ref = refs[-2:]
    columns = []
    for m in range(4):
        for ref in refs[:-2]:
            columns.append(ref[m] + ref[4 + m])
    rows = jnp.concatenate(columns, axis=1)
    out_ref[...] = jnp.dot(rows, w_ref[...], preferred_element_type=jnp.float32).astype(
        out_ref.dtype
    )


def project_out(parts, w_out, side, dtype):
    rows = parts[0].shape[1]
    depth = w_out.shape[0]
    columns, tile = w_out.shape[1] // 2, 512
    tiles = columns // tile
    return pl.pallas_call(
        out_kernel,
        grid_spec=pltpu.PrefetchScalarGridSpec(
            num_scalar_prefetch=1,
            grid=(tiles,),
            in_specs=[
                pl.BlockSpec(part.shape, lambda t, side_ref: (0, 0, 0)) for part in parts
            ]
            + [pl.BlockSpec((depth, tile), lambda t, side_ref: (0, side_ref[0] * tiles + t))],
            out_specs=pl.BlockSpec((rows, tile), lambda t, side_ref: (0, t)),
        ),
        out_shape=jax.ShapeDtypeStruct((rows, columns), dtype),
        compiler_params=pltpu.CompilerParams(vmem_limit_bytes=48 * MIB),
        cost_estimate=pl.CostEstimate(flops=COST, bytes_accessed=COST, transcendentals=0),
    )(side.reshape(1), *parts, w_out)


def row_facts(rows, begins, ends, lead, noise_levels):
    past = rows[:, None] >= ends[None, :]
    clip = jnp.sum(past.astype(jnp.int32), axis=1)
    inside = (rows[:, None] >= begins[None, :]) & jnp.logical_not(past)
    in_prefix = jnp.any(inside & (rows[:, None] < lead[None, :]), axis=1)
    level = jnp.sum(jnp.where(inside, noise_levels[None, :], 0), axis=1)
    return clip, in_prefix, level


SWAP_ROWS = (128, 192)
ATTEND_TILES = 3


def halved_body(
    inputs,
    norm_gain,
    level_table,
    w_qkv,
    w_out,
    clip_lengths,
    prefix_lengths,
    noise_levels,
    token_rank,
):
    rank_here = lax.axis_index("ctx")
    side = lax.axis_index("head")
    per_dev = inputs.shape[0]
    ranks = 16
    half_rows = 8 * per_dev
    local_width = w_qkv.shape[2]
    group_heads = local_width // HEAD_DIM // 4
    clips = clip_lengths.shape[0]
    half, block, core = rank_here // 8, rank_here % 8, rank_here % 2
    half_groups = [[8 * h + 2 * m + c for m in range(4)] for h in range(2) for c in range(2)]
    core_groups = [[2 * n + c for n in range(8)] for c in range(2)]

    def spread(array, groups):
        return lax.all_to_all(array, "ctx", 0, 0, axis_index_groups=groups, tiled=True)

    def with_pair(array):
        return lax.ppermute(array, "ctx", [(r, r ^ 1) for r in range(ranks)])

    index = jnp.arange(clips, dtype=jnp.int32)
    begins = jnp.sum(jnp.where(index[None, :] < index[:, None], clip_lengths[None, :], 0), axis=1)
    start = jnp.sum(jnp.where(clip_lengths == MAXCLIP, begins, 0))
    early = start <= half_rows // 2

    def packed_row(spots):
        swapped = jnp.where(early, spots < start, spots >= start)
        return spots + half_rows * (half ^ swapped.astype(jnp.int32)), swapped

    def facts(begins, clip_lengths, prefix_lengths, noise_levels, token_rank):
        ends = begins + clip_lengths
        lead = begins + jnp.minimum(prefix_lengths, clip_lengths)
        local = jnp.arange(per_dev, dtype=jnp.int32)
        own_packed, unused = packed_row(block * per_dev + local)
        unused, own_prefix, own_level = row_facts(own_packed, begins, ends, lead, noise_levels)
        picks = (
            (own_level[:, None] == jnp.arange(level_table.shape[0], dtype=jnp.int32)[None, :])
            & own_prefix[:, None]
        ).astype(jnp.bfloat16)

        order = jnp.concatenate([2 * index[:4] + core, 2 * index[:4] + 1 - core])
        spots = (order[:, None] * per_dev + local[None, :]).reshape(-1)
        packed, unused = packed_row(spots)
        clip, in_prefix, unused = row_facts(packed, begins, ends, lead, noise_levels)
        column = jnp.arange(HEAD_DIM, dtype=jnp.int32)[None, :]
        same = column == clip[:, None]
        last = column == clips
        query_mask = jnp.where(same | (last & in_prefix[:, None]), 1.0, 0.0).astype(jnp.bfloat16)
        key_mask = jnp.where(
            ((column < clips) & jnp.logical_not(same))
            | (last & jnp.logical_not(in_prefix)[:, None]),
            NEG,
            0.0,
        ).astype(jnp.bfloat16)

        rank = jnp.arange(ranks, dtype=jnp.int32)
        onehot = (token_rank[:, None] == rank[None, :]).astype(jnp.int32)
        within = jnp.sum((jnp.cumsum(onehot, axis=0) - onehot) * onehot, axis=1)
        row = jnp.arange(ranks * per_dev, dtype=jnp.int32)
        low = jnp.sum(jnp.where((row < start)[:, None], onehot, 0), axis=0)
        high = jnp.sum(jnp.where((row < start + half_rows)[:, None], onehot, 0), axis=0)
        long_rows = high - low
        earlier = (rank[None, :] < rank[:, None]) & ((rank[None, :] - rank[:, None]) % 2 == 0)
        long_first = jnp.sum(jnp.where(earlier, long_rows[None, :], 0), axis=1)
        rest_first = jnp.sum(jnp.where(earlier, per_dev - long_rows[None, :], 0), axis=1)
        low_of = jnp.sum(onehot * low[None, :], axis=1)
        long_of = jnp.sum(onehot * long_rows[None, :], axis=1)
        long_base = jnp.sum(onehot * (long_first - low)[None, :], axis=1)
        rest_base = jnp.sum(onehot * rest_first[None, :], axis=1)
        in_long = (row >= start) & (row < start + half_rows)
        sorted_at = within + jnp.where(
            in_long, long_base, rest_base - jnp.where(within < low_of, 0, long_of)
        )
        sorted_at = jnp.where(token_rank % 2 == core, sorted_at, -1)
        every_packed, unused = packed_row(jnp.arange(half_rows, dtype=jnp.int32))
        mine = jnp.where(every_packed >= half_rows, sorted_at[half_rows:], sorted_at[:half_rows])
        mine = mine.reshape(4, 2, per_dev)
        query_order = jnp.where(
            core == 0,
            jnp.concatenate([mine[:, 0], mine[:, 1]], axis=0),
            jnp.concatenate([mine[:, 1], mine[:, 0]], axis=0),
        ).reshape(1, half_rows)

        def of_core(values):
            pairs = values.reshape(8, 2)
            return jnp.where(core == 0, pairs[:, 0], pairs[:, 1])

        holds_long = (half == 0) == early
        low, high, long_rows = of_core(low), of_core(high), of_core(long_rows)
        long_first, rest_first = of_core(long_first), of_core(rest_first)
        runs = jnp.stack(
            [
                jnp.where(holds_long, 0, low),
                jnp.where(holds_long, low, high),
                jnp.where(holds_long, high, per_dev),
                jnp.where(holds_long, 0, rest_first),
                jnp.where(holds_long, long_first - low, rest_first - long_rows),
            ]
        )
        runs = runs.at[3:].set(jnp.clip(runs[3:], -per_dev, half_rows // 2 + per_dev // 2))
        return picks, query_mask, key_mask, query_order, runs

    def gather_rows(blocks):
        def run(rows, *tables):
            pairs = [(r, r ^ 8) for r in range(ranks) if r % 8 in blocks]
            unused, swapped = packed_row(block * per_dev + jnp.arange(per_dev, dtype=jnp.int32))
            bounds = [sum(SWAP_ROWS[:i]) for i in range(len(SWAP_ROWS) + 1)]
            cuts = list(zip(bounds[:-1], bounds[1:]))
            moved = [lax.ppermute(rows[low:high], "ctx", pairs) for low, high in cuts]
            kept = [
                jnp.where(swapped[low:high, None], part, rows[low:high])
                for part, (low, high) in zip(moved, cuts)
            ]
            other = [lax.ppermute(part, "head", [(0, 1), (1, 0)]) for part in kept]
            return tuple(kept), tuple(other), facts(*tables)

        return run

    kept, other, (picks, query_mask, key_mask, query_order, runs) = lax.cond(
        early,
        gather_rows(range(4)),
        gather_rows(range(4, 8)),
        inputs,
        begins,
        clip_lengths,
        prefix_lengths,
        noise_levels,
        token_rank,
    )
    normed = normalize_rows(kept, other, picks, level_table, norm_gain, side)

    w_parts = jnp.transpose(w_qkv, (1, 0, 2))
    arrived, parts, after = [], [], []
    for head in range(group_heads):
        mine = project_heads(normed, w_parts, head, group_heads, after)
        arrived.append(spread(mine, half_groups))
        after = [mine, arrived[head - 1]] if head else [mine]
    after = []
    for own in arrived:
        placed = attend(runs, own, with_pair(own), query_order, query_mask, key_mask, after)
        after = [placed]
        parts.append(spread(placed, core_groups))

    away = project_out(parts, w_out, 1 - side, jnp.bfloat16)
    away = lax.ppermute(away, "head", [(0, 1), (1, 0)])
    stay = project_out(parts, w_out, side, jnp.float32)
    return (stay + away.astype(jnp.float32)).astype(jnp.bfloat16)


def solution(mesh):
    in_specs = (
        P("ctx", "head"),
        P(),
        P(),
        P(None, None, "head"),
        P("head", None),
        P(),
        P(),
        P(),
        P(),
    )
    out_specs = P("ctx", "head")

    def body(inputs, norm_gain, level_table, w_qkv, *rest):
        ranks, sides = mesh.shape["ctx"], mesh.shape["head"]
        heads_here = w_qkv.shape[2] // HEAD_DIM
        halved = (
            ranks == 16
            and sides == 2
            and ranks * inputs.shape[0] == 2 * MAXCLIP
            and heads_here % 4 == 0
        )
        run = halved_body if halved else gathered_body
        return run(inputs, norm_gain, level_table, w_qkv, *rest)

    return jax.shard_map(body, mesh=mesh, in_specs=in_specs, out_specs=out_specs, check_vma=False)
```

```python
import functools

import jax
import jax.numpy as jnp
from jax import lax
from jax.experimental import pallas as pl
from jax.experimental.pallas import tpu as pltpu
from jax.sharding import PartitionSpec as P

HEAD_DIM = 128


NEG = -1e30
EPS = 1e-06
MAXCLIP = 2560
LOG2E = 1.4426950408889634
MIB = 1024 * 1024
COST = 1000000


def clip_tables(total_rows, clip_lengths, prefix_lengths, noise_levels):
    rows = jnp.arange(total_rows, dtype=jnp.int32)
    ends = jnp.cumsum(clip_lengths)
    begins = ends - clip_lengths
    clip_of = jnp.sum((rows[:, None] >= ends[None, :]).astype(jnp.int32), axis=1)
    member = clip_of[:, None] == jnp.arange(clip_lengths.shape[0], dtype=jnp.int32)[None, :]
    begin_row = jnp.sum(jnp.where(member, begins[None, :], 0), axis=1)
    lead = jnp.minimum(prefix_lengths, clip_lengths)
    lead_row = jnp.sum(jnp.where(member, lead[None, :], 0), axis=1)
    level_row = jnp.sum(jnp.where(member, noise_levels[None, :], 0), axis=1)
    in_prefix = rows - begin_row < lead_row
    return (clip_of, in_prefix, level_row)


def rank_tables(token_rank, ranks, per_rank):
    onehot = (token_rank[:, None] == jnp.arange(ranks, dtype=jnp.int32)[None, :]).astype(jnp.int32)
    earlier = jnp.cumsum(onehot, axis=0) - onehot
    within = jnp.sum(earlier * onehot, axis=1)
    counts = jnp.sum(onehot.reshape(ranks, per_rank, ranks), axis=1)
    starts = jnp.cumsum(counts, axis=0) - counts
    return (within, counts, starts)


def normalize(rows, in_prefix, level_row, level_table, norm_gain):
    picks = (
        level_row[:, None] == jnp.arange(level_table.shape[0], dtype=jnp.int32)[None, :]
    ) & in_prefix[:, None]
    added = jnp.dot(picks.astype(jnp.bfloat16), level_table, preferred_element_type=jnp.float32)
    shifted = rows.astype(jnp.float32) + added
    factor = lax.rsqrt(jnp.mean(shifted * shifted, axis=-1, keepdims=True) + EPS)
    return (shifted * factor * norm_gain).astype(jnp.bfloat16)


def fold_keys(state, queries, query_clip, query_prefix, pairs, key_clip, key_prefix):
    width = queries.shape[1]
    heads_here = width // HEAD_DIM
    factor = HEAD_DIM ** (-0.5)
    allowed_query = jnp.logical_not(query_prefix)

    def absorb(carry, block):
        block_pairs, block_clip, block_prefix = block
        allowed = (query_clip[:, None] == block_clip[None, :]) & (
            allowed_query[:, None] | block_prefix[None, :]
        )
        updated = []
        for head in range(heads_here):
            top, total, summed = carry[head]
            low = head * HEAD_DIM
            q_head = queries[:, low : low + HEAD_DIM]
            k_head = block_pairs[:, low : low + HEAD_DIM]
            v_head = block_pairs[:, width + low : width + low + HEAD_DIM]
            scores = (
                lax.dot_general(
                    q_head, k_head, (((1,), (1,)), ((), ())), preferred_element_type=jnp.float32
                )
                * factor
            )
            masked = jnp.where(allowed, scores, NEG)
            new_top = jnp.maximum(top, jnp.max(masked, axis=1, keepdims=True))
            fade = jnp.exp(top - new_top)
            weights = jnp.where(allowed, jnp.exp(scores - new_top), 0.0)
            total = total * fade + jnp.sum(weights, axis=1, keepdims=True)
            summed = summed * fade + jnp.dot(
                weights.astype(jnp.bfloat16), v_head, preferred_element_type=jnp.float32
            )
            updated.append((new_top, total, summed))
        return (tuple(updated), None)

    count = pairs.shape[0]
    step = 2048 if count > 2048 and count % 2048 == 0 else count
    if step == count:
        result, unused = absorb(state, (pairs, key_clip, key_prefix))
        return result
    stacked = (
        pairs.reshape(count // step, step, pairs.shape[1]),
        key_clip.reshape(count // step, step),
        key_prefix.reshape(count // step, step),
    )
    result, unused = lax.scan(absorb, state, stacked)
    return result


def gathered_body(
    inputs,
    norm_gain,
    level_table,
    w_qkv,
    w_out,
    clip_lengths,
    prefix_lengths,
    noise_levels,
    token_rank,
):
    ranks = lax.axis_size("ctx")
    rank_here = lax.axis_index("ctx")
    per_dev = inputs.shape[0]
    slots = 2 * per_dev // ranks
    local_width = w_qkv.shape[2]
    heads_here = local_width // HEAD_DIM
    total_rows = per_dev * ranks
    clip_of, in_prefix, level_row = clip_tables(
        total_rows, clip_lengths, prefix_lengths, noise_levels
    )
    within, counts, starts = rank_tables(token_rank, ranks, per_dev)
    place = token_rank * per_dev + within
    order = (
        jnp.zeros((total_rows,), jnp.int32).at[place].set(jnp.arange(total_rows, dtype=jnp.int32))
    )
    first = rank_here * per_dev
    own_rank = lax.dynamic_slice_in_dim(token_rank, first, per_dev, 0)
    own_within = lax.dynamic_slice_in_dim(within, first, per_dev, 0)
    send_starts = lax.dynamic_slice_in_dim(starts, rank_here, 1, 0)[0]
    recv_counts = lax.dynamic_slice_in_dim(counts, rank_here, 1, 1)[:, 0]
    recv_starts = lax.dynamic_slice_in_dim(starts, rank_here, 1, 1)[:, 0]
    balanced_rows = lax.dynamic_slice_in_dim(order, first, per_dev, 0)
    target = own_rank * slots + own_within - send_starts[own_rank]
    buffer = jnp.zeros((ranks * slots, inputs.shape[1]), inputs.dtype).at[target].set(inputs)
    received = lax.all_to_all(
        buffer.reshape(ranks, slots, inputs.shape[1]),
        "ctx",
        split_axis=0,
        concat_axis=0,
        tiled=True,
    )
    spots = jnp.arange(slots, dtype=jnp.int32)[None, :]
    index = jnp.where(spots < recv_counts[:, None], recv_starts[:, None] + spots, per_dev).reshape(
        -1
    )
    flat = received.reshape(ranks * slots, received.shape[2])
    rows = jnp.zeros((per_dev, received.shape[2]), received.dtype).at[index].set(flat, mode="drop")
    full_rows = lax.all_gather(rows, "head", axis=1, tiled=True)
    normed = normalize(
        full_rows, in_prefix[balanced_rows], level_row[balanced_rows], level_table, norm_gain
    )
    qkv = jnp.dot(
        normed, w_qkv.reshape(w_qkv.shape[0], 3 * local_width), preferred_element_type=jnp.float32
    ).astype(jnp.bfloat16)
    start_state = tuple(
        (
            (
                jnp.full((per_dev, 1), NEG, jnp.float32),
                jnp.zeros((per_dev, 1), jnp.float32),
                jnp.zeros((per_dev, HEAD_DIM), jnp.float32),
            )
            for head in range(heads_here)
        )
    )
    key_clip = clip_of[order]
    key_prefix = in_prefix[order]
    query_clip = lax.dynamic_slice_in_dim(key_clip, first, per_dev, 0)
    query_prefix = lax.dynamic_slice_in_dim(key_prefix, first, per_dev, 0)
    queries = qkv[:, :local_width]
    pairs = qkv[:, local_width:]
    state = fold_keys(
        start_state,
        queries,
        query_clip,
        query_prefix,
        lax.all_gather(pairs, "ctx", axis=0, tiled=True),
        key_clip,
        key_prefix,
    )
    parts = [state[head][2] / state[head][1] for head in range(heads_here)]
    attention = jnp.concatenate(parts, axis=1).astype(jnp.bfloat16)
    terms = jnp.dot(attention, w_out, preferred_element_type=jnp.float32)
    return lax.psum_scatter(terms.astype(jnp.bfloat16), "head", scatter_dimension=1, tiled=True)


def packed_rows(place_ref, spots):
    start, early, half = place_ref[0], place_ref[1], place_ref[2]
    total = place_ref[3]
    before = jnp.where(spots < start, early, 1 - early)
    return spots + total * (half + before * (1 - 2 * half))


def clip_flags(rows, bounds_ref):
    begins, ends, leads = bounds_ref[0:1, :], bounds_ref[1:2, :], bounds_ref[2:3, :]
    inside = (rows >= begins) & (rows < ends)
    return inside, inside & (rows < leads)


def mask_kernel(place_ref, bounds_ref, query_ref, key_ref):
    rows = query_ref.shape[0] // 8
    chip, clips = place_ref[4], place_ref[5]
    column = lax.broadcasted_iota(jnp.int32, (1, HEAD_DIM), 1)
    for d in range(4):
        for core in range(2):
            local = lax.broadcasted_iota(jnp.int32, (rows, 1), 0)
            spots = rows * (2 * jnp.bitwise_xor(chip, d) + (core if d < 2 else 1 - core)) + local
            inside, leading = clip_flags(packed_rows(place_ref, spots), bounds_ref)
            spot = slice((2 * d + core) * rows, (2 * d + core + 1) * rows)
            inside = jnp.where(inside, 1.0, 0.0)
            prefix = jnp.sum(jnp.where(leading, 1.0, 0.0), axis=1, keepdims=True)
            query_ref[spot, :] = jnp.where(column == clips, prefix, inside).astype(jnp.bfloat16)
            outside = jnp.where(column < clips, NEG * (1.0 - inside), 0.0)
            key_ref[spot, :] = jnp.where(column == clips, NEG * (1.0 - prefix), outside).astype(
                jnp.bfloat16
            )


def mask_features(place, bounds, keys):
    vmem = pl.BlockSpec(memory_space=pltpu.VMEM)
    shape = jax.ShapeDtypeStruct((keys, HEAD_DIM), jnp.bfloat16)
    return pl.pallas_call(
        mask_kernel,
        in_specs=[pl.BlockSpec(memory_space=pltpu.SMEM), vmem],
        out_specs=(vmem, vmem),
        out_shape=(shape, shape),
        compiler_params=pltpu.CompilerParams(vmem_limit_bytes=32 * MIB),
        cost_estimate=pl.CostEstimate(flops=COST, bytes_accessed=COST, transcendentals=0),
    )(place, bounds)


def norm_kernel(place_ref, *refs):
    pieces = (len(refs) - 5) // 2
    bounds_ref, noise_ref, level_ref, gain_ref, out_ref = refs[-5:]
    width = out_ref.shape[1] // 2
    side, first = place_ref[6], place_ref[7]
    clips, levels = noise_ref.shape[0], level_ref.shape[0]
    spots = [pl.ds(pl.multiple_of(s * width, 128), width) for s in (side, 1 - side)]
    level = lax.broadcasted_iota(jnp.int32, (clips, levels), 1)
    chosen = jnp.where(noise_ref[...] == level, 1.0, 0.0).astype(jnp.bfloat16)
    tables = [
        jnp.dot(chosen, level_ref[:, spot], preferred_element_type=jnp.float32).astype(
            jnp.bfloat16
        )
        for spot in spots
    ]
    low = 0
    for piece in range(pieces):
        own_ref, other_ref = refs[piece], refs[pieces + piece]
        count = own_ref.shape[0]
        rows = slice(low, low + count)
        places = first + low + lax.broadcasted_iota(jnp.int32, (count, 1), 0)
        low += count
        unused, leading = clip_flags(packed_rows(place_ref, places), bounds_ref)
        picks = jnp.where(leading, 1.0, 0.0)[:, :clips].astype(jnp.bfloat16)
        shifted = [
            ref[...].astype(jnp.float32)
            + jnp.dot(picks, table, preferred_element_type=jnp.float32)
            for ref, table in zip((own_ref, other_ref), tables)
        ]
        squares = sum(jnp.sum(part * part, axis=1, keepdims=True) for part in shifted)
        factor = lax.rsqrt(squares / (2 * width) + EPS)
        for part, spot in zip(shifted, spots):
            out_ref[rows, spot] = (part * factor * gain_ref[:, spot]).astype(jnp.bfloat16)


def normalize_rows(place, kept, other, bounds, noise_levels, level_table, norm_gain):
    rows = sum(part.shape[0] for part in kept)
    vmem = pl.BlockSpec(memory_space=pltpu.VMEM)
    return pl.pallas_call(
        norm_kernel,
        in_specs=[pl.BlockSpec(memory_space=pltpu.SMEM)] + [vmem] * (2 * len(kept) + 4),
        out_specs=vmem,
        out_shape=jax.ShapeDtypeStruct((rows, 2 * kept[0].shape[1]), jnp.bfloat16),
        compiler_params=pltpu.CompilerParams(vmem_limit_bytes=48 * MIB),
        cost_estimate=pl.CostEstimate(flops=COST, bytes_accessed=COST, transcendentals=0),
    )(place, *kept, *other, bounds, noise_levels, level_table, norm_gain.reshape(1, -1))


def project_kernel(head, group_heads, place_ref, own_ref, pair_ref, w_ref, *rest):
    first_ref, second_ref, w_all, sems = rest[-4:]
    chip, core = place_ref[4], place_ref[8]
    pieces = (((0, 0), (0, 1)), ((1, 0), (1, 1)), ((0, 2), (1, 2)))
    copies = []
    for index, piece in enumerate(pieces):
        for position, (slot, part) in enumerate(piece):
            target = jnp.bitwise_xor(chip, jnp.bitwise_xor(3 * core, slot))
            column = pl.multiple_of((group_heads * target + head) * HEAD_DIM, HEAD_DIM)
            copies.append(
                pltpu.make_async_copy(
                    w_ref.at[part, :, pl.ds(column, HEAD_DIM)],
                    w_all.at[index, :, position * HEAD_DIM : (position + 1) * HEAD_DIM],
                    sems.at[index, position],
                )
            )
    for copy in copies:
        copy.start()
    rows = jnp.concatenate([own_ref[...], pair_ref[...]], axis=0)
    for index, piece in enumerate(pieces):
        copies[2 * index].wait()
        copies[2 * index + 1].wait()
        outcome = jnp.dot(rows, w_all[index], preferred_element_type=jnp.float32).astype(
            jnp.bfloat16
        )
        for position, (slot, part) in enumerate(piece):
            (first_ref, second_ref)[slot][:, part * HEAD_DIM : (part + 1) * HEAD_DIM] = outcome[
                :, position * HEAD_DIM : (position + 1) * HEAD_DIM
            ]


def project_heads(place, own, pair, w_parts, head, group_heads, after):
    rows, depth = own.shape
    vmem, hbm = pl.BlockSpec(memory_space=pltpu.VMEM), pl.BlockSpec(memory_space=pl.ANY)
    shape = jax.ShapeDtypeStruct((2 * rows, 3 * HEAD_DIM), jnp.bfloat16)
    return pl.pallas_call(
        functools.partial(project_kernel, head, group_heads),
        in_specs=[pl.BlockSpec(memory_space=pltpu.SMEM), vmem, vmem, hbm] + [hbm] * len(after),
        out_specs=(vmem, vmem),
        out_shape=(shape, shape),
        scratch_shapes=[
            pltpu.VMEM((3, depth, 2 * HEAD_DIM), jnp.bfloat16),
            pltpu.SemaphoreType.DMA((3, 2)),
        ],
        compiler_params=pltpu.CompilerParams(vmem_limit_bytes=48 * MIB),
        cost_estimate=pl.CostEstimate(flops=COST, bytes_accessed=COST, transcendentals=0),
    )(place, own, pair, w_parts, *after)


def attend_kernel(place_ref, runs_ref, *refs):
    mine, near, far, pair_first, pair_far, pair_near = refs[:6]
    order_ref, query_mask_ref, key_mask_ref = refs[6:9]
    stay_ref, cross_ref, q_all, k_all, v_all, sorted_out = refs[-6:]
    chip_rows = mine.shape[0]
    rows = chip_rows // 2
    queries = sorted_out.shape[0] - 2 * rows

    def hold(sources):
        for index, source in enumerate(sources):
            spot = slice(index * chip_rows, (index + 1) * chip_rows)
            q_all[spot, :HEAD_DIM] = source[:, :HEAD_DIM]
            k_all[spot, :HEAD_DIM] = source[:, HEAD_DIM : 2 * HEAD_DIM]
            v_all[spot, :HEAD_DIM] = source[:, 2 * HEAD_DIM :]

    @pl.when(place_ref[8] == 0)
    def _():
        hold((mine, near, pair_near, pair_far))

    @pl.when(place_ref[8] == 1)
    def _():
        hold((pair_first, pair_near, near, far))

    q_all[:, HEAD_DIM:] = query_mask_ref[...]
    k_all[:, HEAD_DIM:] = key_mask_ref[...]
    v_all[:, HEAD_DIM:] = jnp.ones((4 * chip_rows, HEAD_DIM), jnp.bfloat16)
    tile = queries // ATTEND_TILES

    def score(step):
        wanted = step * tile + lax.broadcasted_iota(jnp.int32, (tile, 1), 0)
        picks = jnp.where(order_ref[...] == wanted, 1.0, 0.0).astype(jnp.bfloat16)
        sorted_queries = jnp.dot(picks, q_all[...], preferred_element_type=jnp.float32)
        return lax.dot_general(
            sorted_queries.astype(jnp.bfloat16),
            k_all[...],
            (((1,), (1,)), ((), ())),
            preferred_element_type=jnp.float32,
        )

    coming = score(0)
    for step in range(ATTEND_TILES):
        scores = coming
        if step + 1 < ATTEND_TILES:
            coming = score(step + 1)
        top = jnp.max(scores, axis=1, keepdims=True)
        weights = jnp.exp2((scores - top) * (HEAD_DIM ** (-0.5) * LOG2E))
        summed = jnp.dot(
            weights.astype(jnp.bfloat16), v_all[...], preferred_element_type=jnp.float32
        )
        sorted_out[rows + step * tile : rows + (step + 1) * tile, :] = (
            summed[:, :HEAD_DIM] / summed[:, HEAD_DIM:]
        )

    row = lax.broadcasted_iota(jnp.int32, (rows, 1), 0)
    for n in range(8):
        first = sorted_out[pl.ds(rows + runs_ref[3, n], rows), :]
        second = sorted_out[pl.ds(rows + runs_ref[4, n], rows), :]
        in_second = (row >= runs_ref[1, n]) & (row < runs_ref[2, n])
        taken = jnp.where(row < runs_ref[0, n], first, jnp.where(in_second, second, 0.0))
        (stay_ref, cross_ref)[n // 4][n % 4] = taken.astype(jnp.bfloat16)


def attend(place, runs, blocks, order, query_mask, key_mask, after):
    chip_rows = blocks[0].shape[0]
    rows, keys = chip_rows // 2, 4 * chip_rows
    queries = keys // 2 + rows // 2
    vmem, smem = pl.BlockSpec(memory_space=pltpu.VMEM), pl.BlockSpec(memory_space=pltpu.SMEM)
    shape = jax.ShapeDtypeStruct((4, rows, HEAD_DIM), jnp.bfloat16)
    return pl.pallas_call(
        attend_kernel,
        in_specs=[smem, smem]
        + [vmem] * (len(blocks) + 3)
        + [pl.BlockSpec(memory_space=pl.ANY)] * len(after),
        out_specs=(vmem, vmem),
        out_shape=(shape, shape),
        scratch_shapes=[
            pltpu.VMEM((keys, 2 * HEAD_DIM), jnp.bfloat16),
            pltpu.VMEM((keys, 2 * HEAD_DIM), jnp.bfloat16),
            pltpu.VMEM((keys, 2 * HEAD_DIM), jnp.bfloat16),
            pltpu.VMEM((queries + 2 * rows, HEAD_DIM), jnp.float32),
        ],
        compiler_params=pltpu.CompilerParams(vmem_limit_bytes=48 * MIB),
        cost_estimate=pl.CostEstimate(flops=COST, bytes_accessed=COST, transcendentals=0),
    )(place, runs, *blocks, order, query_mask, key_mask, *after)


def out_kernel(pieces, spot_ref, *refs):
    out_ref = refs[-1]
    columns, low = [], 0
    for count in pieces:
        columns += [ref[...].reshape(ref.shape[-2:]) for ref in refs[low : low + count]]
        low += count
    weights = jnp.concatenate([ref[...] for ref in refs[low : low + 4]], axis=0)
    rows = jnp.concatenate(columns, axis=1)
    out_ref[...] = jnp.dot(rows, weights, preferred_element_type=jnp.float32).astype(out_ref.dtype)


def project_out(spots, attention, w_out, dtype):
    rows = attention[0][0].shape[-2]
    group = w_out.shape[0] // 4
    columns, tile = w_out.shape[1] // 2, 512
    tiles = columns // tile
    pieces = [piece for slot in attention for piece in slot]

    def whole(piece):
        return pl.BlockSpec(piece.shape, lambda t, spot_ref: (0,) * piece.ndim)

    def w_spec(d):
        return pl.BlockSpec(
            (group, tile),
            lambda t, spot_ref: (jnp.bitwise_xor(spot_ref[0], d), spot_ref[1] * tiles + t),
        )

    return pl.pallas_call(
        functools.partial(out_kernel, [len(slot) for slot in attention]),
        grid_spec=pltpu.PrefetchScalarGridSpec(
            num_scalar_prefetch=1,
            grid=(tiles,),
            in_specs=[whole(piece) for piece in pieces] + [w_spec(d) for d in range(4)],
            out_specs=pl.BlockSpec((rows, tile), lambda t, spot_ref: (0, t)),
        ),
        out_shape=jax.ShapeDtypeStruct((rows, columns), dtype),
        compiler_params=pltpu.CompilerParams(vmem_limit_bytes=48 * MIB),
        cost_estimate=pl.CostEstimate(flops=COST, bytes_accessed=COST, transcendentals=0),
    )(spots, *pieces, *([w_out] * 4))


SWAP_ROWS = (80, 112, 128)
ATTEND_TILES = 5


def halved_body(
    inputs,
    norm_gain,
    level_table,
    w_qkv,
    w_out,
    clip_lengths,
    prefix_lengths,
    noise_levels,
    token_rank,
):
    rank_here = lax.axis_index("ctx")
    side = lax.axis_index("head")
    per_dev = inputs.shape[0]
    ranks = 16
    half_rows = 8 * per_dev
    group_heads = w_qkv.shape[2] // HEAD_DIM // 4
    clips = clip_lengths.shape[0]
    half, block, core = rank_here // 8, rank_here % 8, rank_here % 2
    chip = block // 2

    def exchange(array, flip, only=lambda r: True):
        pairs = [(r, r ^ flip) for r in range(ranks) if only(r)]
        return lax.ppermute(array, "ctx", pairs)

    index = jnp.arange(clips, dtype=jnp.int32)
    begins = jnp.sum(jnp.where(index[None, :] < index[:, None], clip_lengths[None, :], 0), axis=1)
    start = jnp.sum(jnp.where(clip_lengths == MAXCLIP, begins, 0))
    early = start <= half_rows // 2
    place = jnp.stack(
        [
            start,
            early.astype(jnp.int32),
            half,
            jnp.int32(half_rows),
            chip,
            jnp.int32(clips),
            side,
            block * per_dev,
            core,
        ]
    )
    ends = begins + clip_lengths
    leads = begins + jnp.minimum(prefix_lengths, clip_lengths)
    bounds = jnp.pad(jnp.stack([begins, ends, leads]), ((0, 5), (0, HEAD_DIM - clips)))

    def sort_tables(token_rank, start, early):
        rank = jnp.arange(ranks, dtype=jnp.int32)
        onehot = (token_rank[:, None] == rank[None, :]).astype(jnp.int32)
        within = jnp.sum((jnp.cumsum(onehot, axis=0) - onehot) * onehot, axis=1)
        row = jnp.arange(ranks * per_dev, dtype=jnp.int32)
        low = jnp.sum(jnp.where((row < start)[:, None], onehot, 0), axis=0)
        high = jnp.sum(jnp.where((row < start + half_rows)[:, None], onehot, 0), axis=0)
        long_rows = high - low
        earlier = (rank[None, :] < rank[:, None]) & ((rank[None, :] - rank[:, None]) % 2 == 0)
        long_first = jnp.sum(jnp.where(earlier, long_rows[None, :], 0), axis=1)
        rest_first = jnp.sum(jnp.where(earlier, per_dev - long_rows[None, :], 0), axis=1)
        low_of = jnp.sum(onehot * low[None, :], axis=1)
        long_of = jnp.sum(onehot * long_rows[None, :], axis=1)
        long_base = jnp.sum(onehot * (long_first - low)[None, :], axis=1)
        rest_base = jnp.sum(onehot * rest_first[None, :], axis=1)
        in_long = (row >= start) & (row < start + half_rows)
        sorted_at = within + jnp.where(
            in_long, long_base, rest_base - jnp.where(within < low_of, 0, long_of)
        )
        sorted_at = jnp.where(token_rank % 2 == core, sorted_at, -1)
        spots = jnp.arange(half_rows, dtype=jnp.int32)
        swapped = jnp.where(early, spots < start, spots >= start)
        swapped = jnp.where(half == 1, jnp.logical_not(swapped), swapped)
        mine = jnp.where(swapped, sorted_at[half_rows:], sorted_at[:half_rows])
        mine = mine.reshape(4, 2, per_dev)
        mine = jnp.where(chip % 2 == 1, mine.reshape(2, 2, 2, per_dev)[:, ::-1].reshape(4, 2, per_dev), mine)
        mine = jnp.where(chip // 2 == 1, jnp.concatenate([mine[2:], mine[:2]], axis=0), mine)
        query_order = jnp.concatenate([mine[:2], mine[2:, ::-1]], axis=0).reshape(1, half_rows)

        holds_long = (half == 0) == early
        targets = rank_here ^ (2 * jnp.arange(8, dtype=jnp.int32))
        pick = targets[:, None] == rank[None, :]

        def of_targets(values):
            return jnp.sum(jnp.where(pick, values[None, :], 0), axis=1)

        low, long_rows = of_targets(low), of_targets(long_rows)
        high = low + long_rows
        long_first, rest_first = of_targets(long_first), of_targets(rest_first)
        furthest = half_rows // 2 + per_dev // 2
        runs = jnp.stack(
            [
                jnp.where(holds_long, 0, low),
                jnp.where(holds_long, low, high),
                jnp.where(holds_long, high, per_dev),
                jnp.clip(jnp.where(holds_long, 0, rest_first), -per_dev, furthest),
                jnp.clip(
                    jnp.where(holds_long, long_first - low, rest_first - long_rows),
                    -per_dev,
                    furthest,
                ),
            ]
        )
        return query_order, runs

    def gather_rows(blocks):
        def run(rows, place, bounds, token_rank, start, early):
            spots = block * per_dev + jnp.arange(per_dev, dtype=jnp.int32)
            swapped = jnp.where(early, spots < start, spots >= start)
            cuts = [sum(SWAP_ROWS[:i]) for i in range(len(SWAP_ROWS) + 1)]
            cuts = list(zip(cuts[:-1], cuts[1:]))
            moved = [exchange(rows[a:b], 8, lambda r: r % 8 in blocks) for a, b in cuts]
            kept = [
                jnp.where(swapped[a:b, None], part, rows[a:b])
                for part, (a, b) in zip(moved, cuts)
            ]
            other = [lax.ppermute(part, "head", [(0, 1), (1, 0)]) for part in kept]
            return (
                tuple(kept),
                tuple(other),
                mask_features(place, bounds, half_rows),
                sort_tables(token_rank, start, early),
            )

        return run

    kept, other, (query_mask, key_mask), (query_order, runs) = lax.cond(
        early,
        gather_rows(range(4)),
        gather_rows(range(4, 8)),
        inputs,
        place,
        bounds,
        token_rank,
        start,
        early,
    )
    normed = normalize_rows(
        place, kept, other, bounds, noise_levels.reshape(-1, 1), level_table, norm_gain
    )
    pair = exchange(normed, 1)

    w_parts = jnp.transpose(w_qkv, (1, 0, 2))
    blocks, after = [], []
    for head in range(group_heads):
        first, second = project_heads(place, normed, pair, w_parts, head, group_heads, after)
        near = lax.ppermute(
            second, "ctx", [(r, r ^ (2 if r % 2 == 0 else 4)) for r in range(ranks)]
        )
        far = exchange(first, 6, lambda r: r % 2 == 1)
        pair_first = exchange(first, 1, lambda r: r % 2 == 0)
        pair_far = exchange(far, 1, lambda r: r % 2 == 1)
        pair_near = exchange(near, 1)
        blocks.append([first, near, far, pair_first, pair_far, pair_near])
        after = [second] + (blocks[head - 1][1:3] if head else [])

    placed, crossed, after = [], [], [second, *blocks[1][1:3]]
    for head in range(group_heads):
        stay, cross = attend(
            place, runs, blocks[head], query_order, query_mask, key_mask, after
        )
        crossed.append(exchange(cross, 8))
        placed.append(stay + crossed[head])
        after = [cross] + (crossed[head - 1 : head] if head else blocks[-1][1:3])

    early_heads = placed[: group_heads - 1]
    attention = []
    for d in range(4):
        pieces = [
            jnp.concatenate([part[d] for part in early_heads], axis=1),
            placed[group_heads - 1][d],
        ]
        attention.append([exchange(piece, 2 * d) if d else piece for piece in pieces])

    spots = jnp.stack([chip, 1 - side])
    away = project_out(spots, attention, w_out, jnp.bfloat16)
    away = lax.ppermute(away, "head", [(0, 1), (1, 0)])
    stay = project_out(jnp.stack([chip, side]), attention, w_out, jnp.float32)
    return (stay + away.astype(jnp.float32)).astype(jnp.bfloat16)


def solution(mesh):
    in_specs = (
        P("ctx", "head"),
        P(),
        P(),
        P(None, None, "head"),
        P("head", None),
        P(),
        P(),
        P(),
        P(),
    )
    out_specs = P("ctx", "head")

    def body(inputs, norm_gain, level_table, w_qkv, *rest):
        ranks, sides = mesh.shape["ctx"], mesh.shape["head"]
        heads_here = w_qkv.shape[2] // HEAD_DIM
        halved = (
            ranks == 16
            and sides == 2
            and ranks * inputs.shape[0] == 2 * MAXCLIP
            and heads_here % 4 == 0
        )
        run = halved_body if halved else gathered_body
        return run(inputs, norm_gain, level_table, w_qkv, *rest)

    return jax.shard_map(body, mesh=mesh, in_specs=in_specs, out_specs=out_specs, check_vma=False)
```

```python
import functools

import jax
import jax.numpy as jnp
from jax import lax
from jax.experimental import pallas as pl
from jax.experimental.pallas import tpu as pltpu
from jax.sharding import PartitionSpec as P

HEAD_DIM = 128


NEG = -1e30
EPS = 1e-06
MAXCLIP = 2560
LOG2E = 1.4426950408889634
MIB = 1024 * 1024
COST = 1000000
LONG_COST = 10000000000


def clip_tables(total_rows, clip_lengths, prefix_lengths, noise_levels):
    rows = jnp.arange(total_rows, dtype=jnp.int32)
    ends = jnp.cumsum(clip_lengths)
    begins = ends - clip_lengths
    clip_of = jnp.sum((rows[:, None] >= ends[None, :]).astype(jnp.int32), axis=1)
    member = clip_of[:, None] == jnp.arange(clip_lengths.shape[0], dtype=jnp.int32)[None, :]
    begin_row = jnp.sum(jnp.where(member, begins[None, :], 0), axis=1)
    lead = jnp.minimum(prefix_lengths, clip_lengths)
    lead_row = jnp.sum(jnp.where(member, lead[None, :], 0), axis=1)
    level_row = jnp.sum(jnp.where(member, noise_levels[None, :], 0), axis=1)
    in_prefix = rows - begin_row < lead_row
    return (clip_of, in_prefix, level_row)


def rank_tables(token_rank, ranks, per_rank):
    onehot = (token_rank[:, None] == jnp.arange(ranks, dtype=jnp.int32)[None, :]).astype(jnp.int32)
    earlier = jnp.cumsum(onehot, axis=0) - onehot
    within = jnp.sum(earlier * onehot, axis=1)
    counts = jnp.sum(onehot.reshape(ranks, per_rank, ranks), axis=1)
    starts = jnp.cumsum(counts, axis=0) - counts
    return (within, counts, starts)


def normalize(rows, in_prefix, level_row, level_table, norm_gain):
    picks = (
        level_row[:, None] == jnp.arange(level_table.shape[0], dtype=jnp.int32)[None, :]
    ) & in_prefix[:, None]
    added = jnp.dot(picks.astype(jnp.bfloat16), level_table, preferred_element_type=jnp.float32)
    shifted = rows.astype(jnp.float32) + added
    factor = lax.rsqrt(jnp.mean(shifted * shifted, axis=-1, keepdims=True) + EPS)
    return (shifted * factor * norm_gain).astype(jnp.bfloat16)


def fold_keys(state, queries, query_clip, query_prefix, pairs, key_clip, key_prefix):
    width = queries.shape[1]
    heads_here = width // HEAD_DIM
    factor = HEAD_DIM ** (-0.5)
    allowed_query = jnp.logical_not(query_prefix)

    def absorb(carry, block):
        block_pairs, block_clip, block_prefix = block
        allowed = (query_clip[:, None] == block_clip[None, :]) & (
            allowed_query[:, None] | block_prefix[None, :]
        )
        updated = []
        for head in range(heads_here):
            top, total, summed = carry[head]
            low = head * HEAD_DIM
            q_head = queries[:, low : low + HEAD_DIM]
            k_head = block_pairs[:, low : low + HEAD_DIM]
            v_head = block_pairs[:, width + low : width + low + HEAD_DIM]
            scores = (
                lax.dot_general(
                    q_head, k_head, (((1,), (1,)), ((), ())), preferred_element_type=jnp.float32
                )
                * factor
            )
            masked = jnp.where(allowed, scores, NEG)
            new_top = jnp.maximum(top, jnp.max(masked, axis=1, keepdims=True))
            fade = jnp.exp(top - new_top)
            weights = jnp.where(allowed, jnp.exp(scores - new_top), 0.0)
            total = total * fade + jnp.sum(weights, axis=1, keepdims=True)
            summed = summed * fade + jnp.dot(
                weights.astype(jnp.bfloat16), v_head, preferred_element_type=jnp.float32
            )
            updated.append((new_top, total, summed))
        return (tuple(updated), None)

    count = pairs.shape[0]
    step = 2048 if count > 2048 and count % 2048 == 0 else count
    if step == count:
        result, unused = absorb(state, (pairs, key_clip, key_prefix))
        return result
    stacked = (
        pairs.reshape(count // step, step, pairs.shape[1]),
        key_clip.reshape(count // step, step),
        key_prefix.reshape(count // step, step),
    )
    result, unused = lax.scan(absorb, state, stacked)
    return result


def gathered_body(
    inputs,
    norm_gain,
    level_table,
    w_qkv,
    w_out,
    clip_lengths,
    prefix_lengths,
    noise_levels,
    token_rank,
):
    ranks = lax.axis_size("ctx")
    rank_here = lax.axis_index("ctx")
    per_dev = inputs.shape[0]
    slots = 2 * per_dev // ranks
    local_width = w_qkv.shape[2]
    heads_here = local_width // HEAD_DIM
    total_rows = per_dev * ranks
    clip_of, in_prefix, level_row = clip_tables(
        total_rows, clip_lengths, prefix_lengths, noise_levels
    )
    within, counts, starts = rank_tables(token_rank, ranks, per_dev)
    place = token_rank * per_dev + within
    order = (
        jnp.zeros((total_rows,), jnp.int32).at[place].set(jnp.arange(total_rows, dtype=jnp.int32))
    )
    first = rank_here * per_dev
    own_rank = lax.dynamic_slice_in_dim(token_rank, first, per_dev, 0)
    own_within = lax.dynamic_slice_in_dim(within, first, per_dev, 0)
    send_starts = lax.dynamic_slice_in_dim(starts, rank_here, 1, 0)[0]
    recv_counts = lax.dynamic_slice_in_dim(counts, rank_here, 1, 1)[:, 0]
    recv_starts = lax.dynamic_slice_in_dim(starts, rank_here, 1, 1)[:, 0]
    balanced_rows = lax.dynamic_slice_in_dim(order, first, per_dev, 0)
    target = own_rank * slots + own_within - send_starts[own_rank]
    buffer = jnp.zeros((ranks * slots, inputs.shape[1]), inputs.dtype).at[target].set(inputs)
    received = lax.all_to_all(
        buffer.reshape(ranks, slots, inputs.shape[1]),
        "ctx",
        split_axis=0,
        concat_axis=0,
        tiled=True,
    )
    spots = jnp.arange(slots, dtype=jnp.int32)[None, :]
    index = jnp.where(spots < recv_counts[:, None], recv_starts[:, None] + spots, per_dev).reshape(
        -1
    )
    flat = received.reshape(ranks * slots, received.shape[2])
    rows = jnp.zeros((per_dev, received.shape[2]), received.dtype).at[index].set(flat, mode="drop")
    full_rows = lax.all_gather(rows, "head", axis=1, tiled=True)
    normed = normalize(
        full_rows, in_prefix[balanced_rows], level_row[balanced_rows], level_table, norm_gain
    )
    qkv = jnp.dot(
        normed, w_qkv.reshape(w_qkv.shape[0], 3 * local_width), preferred_element_type=jnp.float32
    ).astype(jnp.bfloat16)
    start_state = tuple(
        (
            (
                jnp.full((per_dev, 1), NEG, jnp.float32),
                jnp.zeros((per_dev, 1), jnp.float32),
                jnp.zeros((per_dev, HEAD_DIM), jnp.float32),
            )
            for head in range(heads_here)
        )
    )
    key_clip = clip_of[order]
    key_prefix = in_prefix[order]
    query_clip = lax.dynamic_slice_in_dim(key_clip, first, per_dev, 0)
    query_prefix = lax.dynamic_slice_in_dim(key_prefix, first, per_dev, 0)
    queries = qkv[:, :local_width]
    pairs = qkv[:, local_width:]
    state = fold_keys(
        start_state,
        queries,
        query_clip,
        query_prefix,
        lax.all_gather(pairs, "ctx", axis=0, tiled=True),
        key_clip,
        key_prefix,
    )
    parts = [state[head][2] / state[head][1] for head in range(heads_here)]
    attention = jnp.concatenate(parts, axis=1).astype(jnp.bfloat16)
    terms = jnp.dot(attention, w_out, preferred_element_type=jnp.float32)
    return lax.psum_scatter(terms.astype(jnp.bfloat16), "head", scatter_dimension=1, tiled=True)


def packed_rows(place_ref, spots):
    start, early, half = place_ref[0], place_ref[1], place_ref[2]
    total = place_ref[3]
    before = jnp.where(spots < start, early, 1 - early)
    return spots + total * (half + before * (1 - 2 * half))


def clip_flags(rows, bounds_ref):
    begins, ends, leads = bounds_ref[0:1, :], bounds_ref[1:2, :], bounds_ref[2:3, :]
    inside = (rows >= begins) & (rows < ends)
    return inside, inside & (rows < leads)


def mask_kernel(place_ref, bounds_ref, query_ref, key_ref):
    rows = query_ref.shape[0] // 8
    chip, clips = place_ref[4], place_ref[5]
    column = lax.broadcasted_iota(jnp.int32, (1, HEAD_DIM), 1)
    for d in range(4):
        for core in range(2):
            local = lax.broadcasted_iota(jnp.int32, (rows, 1), 0)
            spots = rows * (2 * jnp.bitwise_xor(chip, d) + (core if d < 2 else 1 - core)) + local
            inside, leading = clip_flags(packed_rows(place_ref, spots), bounds_ref)
            spot = slice((2 * d + core) * rows, (2 * d + core + 1) * rows)
            inside = jnp.where(inside, 1.0, 0.0)
            prefix = jnp.sum(jnp.where(leading, 1.0, 0.0), axis=1, keepdims=True)
            query_ref[spot, :] = jnp.where(column == clips, prefix, inside).astype(jnp.bfloat16)
            outside = jnp.where(column < clips, NEG * (1.0 - inside), 0.0)
            key_ref[spot, :] = jnp.where(column == clips, NEG * (1.0 - prefix), outside).astype(
                jnp.bfloat16
            )


def mask_features(place, bounds, keys):
    vmem = pl.BlockSpec(memory_space=pltpu.VMEM)
    shape = jax.ShapeDtypeStruct((keys, HEAD_DIM), jnp.bfloat16)
    return pl.pallas_call(
        mask_kernel,
        in_specs=[pl.BlockSpec(memory_space=pltpu.SMEM), vmem],
        out_specs=(vmem, vmem),
        out_shape=(shape, shape),
        compiler_params=pltpu.CompilerParams(vmem_limit_bytes=32 * MIB),
        cost_estimate=pl.CostEstimate(flops=COST, bytes_accessed=COST, transcendentals=0),
    )(place, bounds)


def select_kernel(low, place_ref, own_ref, moved_ref, *rest):
    out_ref = rest[-1]
    count = out_ref.shape[0]
    spots = place_ref[7] + low + lax.broadcasted_iota(jnp.int32, (count, 1), 0)
    swapped = jnp.where(spots < place_ref[0], place_ref[1], 1 - place_ref[1])
    out_ref[...] = jnp.where(swapped == 1, moved_ref[...], own_ref[low : low + count, :])


def select_rows(place, rows, moved, low, after):
    vmem = pl.BlockSpec(memory_space=pltpu.VMEM)
    return pl.pallas_call(
        functools.partial(select_kernel, low),
        in_specs=[pl.BlockSpec(memory_space=pltpu.SMEM), vmem, vmem]
        + [pl.BlockSpec(memory_space=pl.ANY)] * len(after),
        out_specs=vmem,
        out_shape=jax.ShapeDtypeStruct(moved.shape, moved.dtype),
        compiler_params=pltpu.CompilerParams(vmem_limit_bytes=16 * MIB),
        cost_estimate=pl.CostEstimate(flops=COST, bytes_accessed=COST, transcendentals=0),
    )(place, rows, moved, *after)


def weight_copies(place_ref, head, group_heads, w_ref, out_ref, sems):
    copies = []
    for slot in range(2):
        target = jnp.bitwise_xor(place_ref[4], jnp.bitwise_xor(3 * place_ref[8], slot))
        column = pl.multiple_of((group_heads * target + head) * HEAD_DIM, HEAD_DIM)
        for part in range(3):
            to = 3 * slot + part
            copies.append(
                pltpu.make_async_copy(
                    w_ref.at[part, :, pl.ds(column, HEAD_DIM)],
                    out_ref.at[:, to * HEAD_DIM : (to + 1) * HEAD_DIM],
                    sems.at[to],
                )
            )
    return copies


def norm_kernel(group_heads, place_ref, *refs):
    pieces = (len(refs) - 8) // 2
    bounds_ref, noise_ref, level_ref, gain_ref, w_ref, out_ref, next_ref, sems = refs[-8:]
    copies = weight_copies(place_ref, 0, group_heads, w_ref, next_ref, sems)
    for copy in copies:
        copy.start()
    width = out_ref.shape[1] // 2
    side, first = place_ref[6], place_ref[7]
    clips, levels = noise_ref.shape[0], level_ref.shape[0]
    spots = [pl.ds(pl.multiple_of(s * width, 128), width) for s in (side, 1 - side)]
    level = lax.broadcasted_iota(jnp.int32, (clips, levels), 1)
    chosen = jnp.where(noise_ref[...] == level, 1.0, 0.0).astype(jnp.bfloat16)
    tables = [
        jnp.dot(chosen, level_ref[:, spot], preferred_element_type=jnp.float32).astype(
            jnp.bfloat16
        )
        for spot in spots
    ]
    low = 0
    for piece in range(pieces):
        own_ref, other_ref = refs[piece], refs[pieces + piece]
        count = own_ref.shape[0]
        rows = slice(low, low + count)
        places = first + low + lax.broadcasted_iota(jnp.int32, (count, 1), 0)
        low += count
        unused, leading = clip_flags(packed_rows(place_ref, places), bounds_ref)
        picks = jnp.where(leading, 1.0, 0.0)[:, :clips].astype(jnp.bfloat16)
        shifted = [
            ref[...].astype(jnp.float32)
            + jnp.dot(picks, table, preferred_element_type=jnp.float32)
            for ref, table in zip((own_ref, other_ref), tables)
        ]
        squares = sum(jnp.sum(part * part, axis=1, keepdims=True) for part in shifted)
        factor = lax.rsqrt(squares / (2 * width) + EPS)
        for part, spot in zip(shifted, spots):
            out_ref[rows, spot] = (part * factor * gain_ref[:, spot]).astype(jnp.bfloat16)
    for copy in copies:
        copy.wait()


def normalize_rows(
    place, kept, other, bounds, noise_levels, level_table, norm_gain, w_parts, group_heads
):
    rows, depth = sum(part.shape[0] for part in kept), 2 * kept[0].shape[1]
    vmem = pl.BlockSpec(memory_space=pltpu.VMEM)
    return pl.pallas_call(
        functools.partial(norm_kernel, group_heads),
        in_specs=[pl.BlockSpec(memory_space=pltpu.SMEM)]
        + [vmem] * (2 * len(kept) + 4)
        + [pl.BlockSpec(memory_space=pl.ANY)],
        out_specs=(vmem, vmem),
        out_shape=(
            jax.ShapeDtypeStruct((rows, depth), jnp.bfloat16),
            jax.ShapeDtypeStruct((depth, 6 * HEAD_DIM), jnp.bfloat16),
        ),
        scratch_shapes=[pltpu.SemaphoreType.DMA((6,))],
        compiler_params=pltpu.CompilerParams(vmem_limit_bytes=24 * MIB),
        cost_estimate=pl.CostEstimate(flops=COST, bytes_accessed=COST, transcendentals=0),
    )(place, *kept, *other, bounds, noise_levels, level_table, norm_gain.reshape(1, -1), w_parts)


def project_kernel(next_head, group_heads, place_ref, own_ref, pair_ref, weights_ref, w_ref, *rest):
    copies = []
    if next_head is None:
        first_ref, second_ref = rest[-2:]
    else:
        first_ref, second_ref, next_ref, sems = rest[-4:]
        copies = weight_copies(place_ref, next_head, group_heads, w_ref, next_ref, sems)
    for copy in copies:
        copy.start()
    rows = jnp.concatenate([own_ref[...], pair_ref[...]], axis=0)
    outcome = jnp.dot(rows, weights_ref[...], preferred_element_type=jnp.float32)
    first_ref[...] = outcome[:, : 3 * HEAD_DIM].astype(jnp.bfloat16)
    second_ref[...] = outcome[:, 3 * HEAD_DIM :].astype(jnp.bfloat16)
    for copy in copies:
        copy.wait()


def project_heads(place, own, pair, weights, w_parts, next_head, group_heads, after):
    rows, depth = own.shape
    vmem, hbm = pl.BlockSpec(memory_space=pltpu.VMEM), pl.BlockSpec(memory_space=pl.ANY)
    shape = jax.ShapeDtypeStruct((2 * rows, 3 * HEAD_DIM), jnp.bfloat16)
    more = next_head is not None
    return pl.pallas_call(
        functools.partial(project_kernel, next_head, group_heads),
        in_specs=[pl.BlockSpec(memory_space=pltpu.SMEM), vmem, vmem, vmem, hbm]
        + [hbm] * len(after),
        out_specs=(vmem, vmem) + (vmem,) * more,
        out_shape=(shape, shape)
        + (jax.ShapeDtypeStruct(weights.shape, weights.dtype),) * more,
        scratch_shapes=[pltpu.SemaphoreType.DMA((6,))] * more,
        compiler_params=pltpu.CompilerParams(vmem_limit_bytes=24 * MIB),
        cost_estimate=pl.CostEstimate(flops=COST, bytes_accessed=COST, transcendentals=0),
    )(place, own, pair, weights, w_parts, *after)


def attend_kernel(fetch, place_ref, runs_ref, *refs):
    copies = []
    if fetch:
        w_ref, sorted_ref, sems = refs[9], refs[-6], refs[-1]
        refs = refs[:-6] + refs[-5:-1]
        group = w_ref.shape[0] // 4
        for d in range(4):
            target = jnp.bitwise_xor(place_ref[4], d)
            copies.append(
                pltpu.make_async_copy(
                    w_ref.at[pl.ds(pl.multiple_of(group * target, group), group), :],
                    sorted_ref.at[group * d : group * (d + 1), :],
                    sems.at[d],
                )
            )
    for copy in copies:
        copy.start()
    mine, near, far, pair_first, pair_far, pair_near = refs[:6]
    order_ref, query_mask_ref, key_mask_ref = refs[6:9]
    stay_ref, cross_ref, q_all, k_all, v_all, sorted_out = refs[-6:]
    chip_rows = mine.shape[0]
    rows = chip_rows // 2
    queries = sorted_out.shape[0] - 2 * rows

    def hold(sources):
        for index, source in enumerate(sources):
            spot = slice(index * chip_rows, (index + 1) * chip_rows)
            q_all[spot, :HEAD_DIM] = source[:, :HEAD_DIM]
            k_all[spot, :HEAD_DIM] = source[:, HEAD_DIM : 2 * HEAD_DIM]
            v_all[spot, :HEAD_DIM] = source[:, 2 * HEAD_DIM :]

    @pl.when(place_ref[8] == 0)
    def _():
        hold((mine, near, pair_near, pair_far))

    @pl.when(place_ref[8] == 1)
    def _():
        hold((pair_first, pair_near, near, far))

    q_all[:, HEAD_DIM:] = query_mask_ref[...]
    k_all[:, HEAD_DIM:] = key_mask_ref[...]
    v_all[:, HEAD_DIM:] = jnp.ones((4 * chip_rows, HEAD_DIM), jnp.bfloat16)
    tile = queries // ATTEND_TILES

    def score(step):
        wanted = step * tile + lax.broadcasted_iota(jnp.int32, (tile, 1), 0)
        picks = jnp.where(order_ref[...] == wanted, 1.0, 0.0).astype(jnp.bfloat16)
        sorted_queries = jnp.dot(picks, q_all[...], preferred_element_type=jnp.float32)
        return lax.dot_general(
            sorted_queries.astype(jnp.bfloat16),
            k_all[...],
            (((1,), (1,)), ((), ())),
            preferred_element_type=jnp.float32,
        )

    coming = score(0)
    for step in range(ATTEND_TILES):
        scores = coming
        if step + 1 < ATTEND_TILES:
            coming = score(step + 1)
        top = jnp.max(scores, axis=1, keepdims=True)
        weights = jnp.exp2((scores - top) * (HEAD_DIM ** (-0.5) * LOG2E))
        summed = jnp.dot(
            weights.astype(jnp.bfloat16), v_all[...], preferred_element_type=jnp.float32
        )
        sorted_out[rows + step * tile : rows + (step + 1) * tile, :] = (
            summed[:, :HEAD_DIM] / summed[:, HEAD_DIM:]
        )

    row = lax.broadcasted_iota(jnp.int32, (rows, 1), 0)
    for n in range(8):
        first = sorted_out[pl.ds(rows + runs_ref[3, n], rows), :]
        second = sorted_out[pl.ds(rows + runs_ref[4, n], rows), :]
        in_second = (row >= runs_ref[1, n]) & (row < runs_ref[2, n])
        taken = jnp.where(row < runs_ref[0, n], first, jnp.where(in_second, second, 0.0))
        (stay_ref, cross_ref)[n // 4][n % 4] = taken.astype(jnp.bfloat16)
    for copy in copies:
        copy.wait()


def attend(place, runs, blocks, order, query_mask, key_mask, w_out, after):
    chip_rows = blocks[0].shape[0]
    rows, keys = chip_rows // 2, 4 * chip_rows
    queries = keys // 2 + rows // 2
    vmem, smem = pl.BlockSpec(memory_space=pltpu.VMEM), pl.BlockSpec(memory_space=pltpu.SMEM)
    hbm = pl.BlockSpec(memory_space=pl.ANY)
    shape = jax.ShapeDtypeStruct((4, rows, HEAD_DIM), jnp.bfloat16)
    fetch = w_out is not None
    extra = (w_out,) * fetch
    return pl.pallas_call(
        functools.partial(attend_kernel, fetch),
        in_specs=[smem, smem] + [vmem] * (len(blocks) + 3) + [hbm] * (fetch + len(after)),
        out_specs=(vmem, vmem) + (vmem,) * fetch,
        out_shape=(shape, shape)
        + tuple(jax.ShapeDtypeStruct(array.shape, array.dtype) for array in extra),
        scratch_shapes=[
            pltpu.VMEM((keys, 2 * HEAD_DIM), jnp.bfloat16),
            pltpu.VMEM((keys, 2 * HEAD_DIM), jnp.bfloat16),
            pltpu.VMEM((keys, 2 * HEAD_DIM), jnp.bfloat16),
            pltpu.VMEM((queries + 2 * rows, HEAD_DIM), jnp.float32),
        ]
        + [pltpu.SemaphoreType.DMA((4,))] * fetch,
        compiler_params=pltpu.CompilerParams(vmem_limit_bytes=36 * MIB),
        cost_estimate=pl.CostEstimate(
            flops=LONG_COST, bytes_accessed=COST, transcendentals=0
        ),
    )(place, runs, *blocks, order, query_mask, key_mask, *extra, *after)


def join_kernel(heads, *refs):
    outs = refs[-4:]
    for d in range(4):
        parts = [refs[2 * h][d] + refs[2 * h + 1][d] for h in range(heads)]
        outs[d][...] = jnp.concatenate(parts, axis=1)


def join_halves(stays, arrivals, after):
    heads, (slots, rows, width) = len(stays), stays[0].shape
    vmem = pl.BlockSpec(memory_space=pltpu.VMEM)
    pairs = [part for both in zip(stays, arrivals) for part in both]
    shape = jax.ShapeDtypeStruct((rows, heads * width), jnp.bfloat16)
    return pl.pallas_call(
        functools.partial(join_kernel, heads),
        in_specs=[vmem] * len(pairs) + [pl.BlockSpec(memory_space=pl.ANY)] * len(after),
        out_specs=(vmem,) * slots,
        out_shape=(shape,) * slots,
        compiler_params=pltpu.CompilerParams(vmem_limit_bytes=16 * MIB),
        cost_estimate=pl.CostEstimate(flops=COST, bytes_accessed=COST, transcendentals=0),
    )(*pairs, *after)


def out_kernel(side_ref, *refs):
    w_ref, out_ref = refs[-2:]
    columns = out_ref.shape[1]
    rows = jnp.concatenate([ref[...] for ref in refs[:-2]], axis=1)
    spot = pl.ds(pl.multiple_of(side_ref[0] * columns, HEAD_DIM), columns)
    out_ref[...] = jnp.dot(rows, w_ref[:, spot], preferred_element_type=jnp.float32).astype(
        out_ref.dtype
    )


def project_out(side, pieces, w_sorted, dtype):
    rows = pieces[0].shape[0]
    vmem = pl.BlockSpec(memory_space=pltpu.VMEM)
    return pl.pallas_call(
        out_kernel,
        in_specs=[pl.BlockSpec(memory_space=pltpu.SMEM)] + [vmem] * (len(pieces) + 1),
        out_specs=vmem,
        out_shape=jax.ShapeDtypeStruct((rows, w_sorted.shape[1] // 2), dtype),
        compiler_params=pltpu.CompilerParams(vmem_limit_bytes=32 * MIB),
        cost_estimate=pl.CostEstimate(flops=COST, bytes_accessed=COST, transcendentals=0),
    )(side.reshape(1), *pieces, w_sorted)


SWAP_ROWS = (128, 112, 80)
ATTEND_TILES = 3


def halved_body(
    inputs,
    norm_gain,
    level_table,
    w_qkv,
    w_out,
    clip_lengths,
    prefix_lengths,
    noise_levels,
    token_rank,
):
    rank_here = lax.axis_index("ctx")
    side = lax.axis_index("head")
    per_dev = inputs.shape[0]
    ranks = 16
    half_rows = 8 * per_dev
    group_heads = w_qkv.shape[2] // HEAD_DIM // 4
    clips = clip_lengths.shape[0]
    half, block, core = rank_here // 8, rank_here % 8, rank_here % 2
    chip = block // 2

    def exchange(array, flip, only=lambda r: True):
        pairs = [(r, r ^ flip) for r in range(ranks) if only(r)]
        return lax.ppermute(array, "ctx", pairs)

    index = jnp.arange(clips, dtype=jnp.int32)
    begins = jnp.sum(jnp.where(index[None, :] < index[:, None], clip_lengths[None, :], 0), axis=1)
    start = jnp.sum(jnp.where(clip_lengths == MAXCLIP, begins, 0))
    early = start <= half_rows // 2
    def tables(begins, start, early, clip_lengths, prefix_lengths):
        place = jnp.stack(
            [
                start,
                early.astype(jnp.int32),
                half,
                jnp.int32(half_rows),
                chip,
                jnp.int32(clips),
                side,
                block * per_dev,
                core,
            ]
        )
        ends = begins + clip_lengths
        leads = begins + jnp.minimum(prefix_lengths, clip_lengths)
        bounds = jnp.pad(jnp.stack([begins, ends, leads]), ((0, 5), (0, HEAD_DIM - clips)))
        return place, bounds

    def sort_tables(token_rank, start, early):
        rank = jnp.arange(ranks, dtype=jnp.int32)
        onehot = (token_rank[:, None] == rank[None, :]).astype(jnp.int32)
        within = jnp.sum((jnp.cumsum(onehot, axis=0) - onehot) * onehot, axis=1)
        row = jnp.arange(ranks * per_dev, dtype=jnp.int32)
        low = jnp.sum(jnp.where((row < start)[:, None], onehot, 0), axis=0)
        high = jnp.sum(jnp.where((row < start + half_rows)[:, None], onehot, 0), axis=0)
        long_rows = high - low
        earlier = (rank[None, :] < rank[:, None]) & ((rank[None, :] - rank[:, None]) % 2 == 0)
        long_first = jnp.sum(jnp.where(earlier, long_rows[None, :], 0), axis=1)
        rest_first = jnp.sum(jnp.where(earlier, per_dev - long_rows[None, :], 0), axis=1)
        low_of = jnp.sum(onehot * low[None, :], axis=1)
        long_of = jnp.sum(onehot * long_rows[None, :], axis=1)
        long_base = jnp.sum(onehot * (long_first - low)[None, :], axis=1)
        rest_base = jnp.sum(onehot * rest_first[None, :], axis=1)
        in_long = (row >= start) & (row < start + half_rows)
        sorted_at = within + jnp.where(
            in_long, long_base, rest_base - jnp.where(within < low_of, 0, long_of)
        )
        sorted_at = jnp.where(token_rank % 2 == core, sorted_at, -1)
        spots = jnp.arange(half_rows, dtype=jnp.int32)
        swapped = jnp.where(early, spots < start, spots >= start)
        swapped = jnp.where(half == 1, jnp.logical_not(swapped), swapped)
        mine = jnp.where(swapped, sorted_at[half_rows:], sorted_at[:half_rows])
        mine = mine.reshape(4, 2, per_dev)
        mine = jnp.where(chip % 2 == 1, mine.reshape(2, 2, 2, per_dev)[:, ::-1].reshape(4, 2, per_dev), mine)
        mine = jnp.where(chip // 2 == 1, jnp.concatenate([mine[2:], mine[:2]], axis=0), mine)
        query_order = jnp.concatenate([mine[:2], mine[2:, ::-1]], axis=0).reshape(1, half_rows)

        holds_long = (half == 0) == early
        targets = rank_here ^ (2 * jnp.arange(8, dtype=jnp.int32))
        pick = targets[:, None] == rank[None, :]

        def of_targets(values):
            return jnp.sum(jnp.where(pick, values[None, :], 0), axis=1)

        low, long_rows = of_targets(low), of_targets(long_rows)
        high = low + long_rows
        long_first, rest_first = of_targets(long_first), of_targets(rest_first)
        furthest = half_rows // 2 + per_dev // 2
        runs = jnp.stack(
            [
                jnp.where(holds_long, 0, low),
                jnp.where(holds_long, low, high),
                jnp.where(holds_long, high, per_dev),
                jnp.clip(jnp.where(holds_long, 0, rest_first), -per_dev, furthest),
                jnp.clip(
                    jnp.where(holds_long, long_first - low, rest_first - long_rows),
                    -per_dev,
                    furthest,
                ),
            ]
        )
        return query_order, runs

    def gather_rows(blocks):
        def run(rows, begins, start, early, clip_lengths, prefix_lengths, token_rank):
            place, bounds = tables(begins, start, early, clip_lengths, prefix_lengths)
            cuts = [sum(SWAP_ROWS[:i]) for i in range(len(SWAP_ROWS) + 1)]
            cuts = list(zip(cuts[:-1], cuts[1:]))
            moved = [exchange(rows[a:b], 8, lambda r: r % 8 in blocks) for a, b in cuts]
            kept = []
            for part, (a, b) in zip(moved, cuts):
                kept.append(select_rows(place, rows, part, a, kept[-1:]))
            other = [lax.ppermute(part, "head", [(0, 1), (1, 0)]) for part in kept]
            return (
                tuple(kept),
                tuple(other),
                mask_features(place, bounds, half_rows),
                sort_tables(token_rank, start, early),
                place,
                bounds,
            )

        return run

    kept, other, (query_mask, key_mask), (query_order, runs), place, bounds = lax.cond(
        early,
        gather_rows(range(4)),
        gather_rows(range(4, 8)),
        inputs,
        begins,
        start,
        early,
        clip_lengths,
        prefix_lengths,
        token_rank,
    )
    w_parts = jnp.transpose(w_qkv, (1, 0, 2))
    normed, weights = normalize_rows(
        place,
        kept,
        other,
        bounds,
        noise_levels.reshape(-1, 1),
        level_table,
        norm_gain,
        w_parts,
        group_heads,
    )
    pair = exchange(normed, 1)

    blocks, after = [], []
    for head in range(group_heads):
        next_head = head + 1 if head + 1 < group_heads else None
        first, second, *more = project_heads(
            place, normed, pair, weights, w_parts, next_head, group_heads, after
        )
        weights = more[0] if more else None
        near = lax.ppermute(
            second, "ctx", [(r, r ^ (2 if r % 2 == 0 else 4)) for r in range(ranks)]
        )
        far = exchange(first, 6, lambda r: r % 2 == 1)
        pair_first = exchange(first, 1, lambda r: r % 2 == 0)
        pair_far = exchange(far, 1, lambda r: r % 2 == 1)
        pair_near = exchange(near, 1)
        blocks.append([first, near, far, pair_first, pair_far, pair_near])
        after = [pair_first] + (blocks[head - 1][1:3] if head else [])

    stays, arrivals, after = [], [], [second, *blocks[1][1:3]]
    for head in range(group_heads):
        last = head + 1 == group_heads
        stay, cross, *w_sorted = attend(
            place,
            runs,
            blocks[head],
            query_order,
            query_mask,
            key_mask,
            w_out if last else None,
            after,
        )
        stays.append(stay)
        arrivals.append(exchange(cross, 8))
        after = [cross] + (arrivals[head - 1 : head] if head else blocks[-1][1:3])

    pieces = [[], [], [], []]
    for heads, after in ((slice(0, -1), [cross]), (slice(-1, None), [])):
        joined = join_halves(stays[heads], arrivals[heads], after)
        for d in range(4):
            pieces[d].append(exchange(joined[d], 2 * d) if d else joined[d])
    pieces = [piece for slot in pieces for piece in slot]

    away = project_out(1 - side, pieces, w_sorted[0], jnp.bfloat16)
    away = lax.ppermute(away, "head", [(0, 1), (1, 0)])
    stay = project_out(side, pieces, w_sorted[0], jnp.float32)
    return (stay + away.astype(jnp.float32)).astype(jnp.bfloat16)


def solution(mesh):
    in_specs = (
        P("ctx", "head"),
        P(),
        P(),
        P(None, None, "head"),
        P("head", None),
        P(),
        P(),
        P(),
        P(),
    )
    out_specs = P("ctx", "head")

    def body(inputs, norm_gain, level_table, w_qkv, *rest):
        ranks, sides = mesh.shape["ctx"], mesh.shape["head"]
        heads_here = w_qkv.shape[2] // HEAD_DIM
        halved = (
            ranks == 16
            and sides == 2
            and ranks * inputs.shape[0] == 2 * MAXCLIP
            and heads_here % 4 == 0
        )
        run = halved_body if halved else gathered_body
        return run(inputs, norm_gain, level_table, w_qkv, *rest)

    return jax.shard_map(body, mesh=mesh, in_specs=in_specs, out_specs=out_specs, check_vma=False)
```

```python
import functools

import jax
import jax.numpy as jnp
from jax import lax
from jax.experimental import pallas as pl
from jax.experimental.pallas import tpu as pltpu
from jax.sharding import PartitionSpec as P

HEAD_DIM = 128


NEG = -1e30
EPS = 1e-06
MAXCLIP = 2560
LOG2E = 1.4426950408889634
MIB = 1024 * 1024
COST = 1000000
LONG_COST = 10000000000


def clip_tables(total_rows, clip_lengths, prefix_lengths, noise_levels):
    rows = jnp.arange(total_rows, dtype=jnp.int32)
    ends = jnp.cumsum(clip_lengths)
    begins = ends - clip_lengths
    clip_of = jnp.sum((rows[:, None] >= ends[None, :]).astype(jnp.int32), axis=1)
    member = clip_of[:, None] == jnp.arange(clip_lengths.shape[0], dtype=jnp.int32)[None, :]
    begin_row = jnp.sum(jnp.where(member, begins[None, :], 0), axis=1)
    lead = jnp.minimum(prefix_lengths, clip_lengths)
    lead_row = jnp.sum(jnp.where(member, lead[None, :], 0), axis=1)
    level_row = jnp.sum(jnp.where(member, noise_levels[None, :], 0), axis=1)
    in_prefix = rows - begin_row < lead_row
    return (clip_of, in_prefix, level_row)


def rank_tables(token_rank, ranks, per_rank):
    onehot = (token_rank[:, None] == jnp.arange(ranks, dtype=jnp.int32)[None, :]).astype(jnp.int32)
    earlier = jnp.cumsum(onehot, axis=0) - onehot
    within = jnp.sum(earlier * onehot, axis=1)
    counts = jnp.sum(onehot.reshape(ranks, per_rank, ranks), axis=1)
    starts = jnp.cumsum(counts, axis=0) - counts
    return (within, counts, starts)


def normalize(rows, in_prefix, level_row, level_table, norm_gain):
    picks = (
        level_row[:, None] == jnp.arange(level_table.shape[0], dtype=jnp.int32)[None, :]
    ) & in_prefix[:, None]
    added = jnp.dot(picks.astype(jnp.bfloat16), level_table, preferred_element_type=jnp.float32)
    shifted = rows.astype(jnp.float32) + added
    factor = lax.rsqrt(jnp.mean(shifted * shifted, axis=-1, keepdims=True) + EPS)
    return (shifted * factor * norm_gain).astype(jnp.bfloat16)


def fold_keys(state, queries, query_clip, query_prefix, pairs, key_clip, key_prefix):
    width = queries.shape[1]
    heads_here = width // HEAD_DIM
    factor = HEAD_DIM ** (-0.5)
    allowed_query = jnp.logical_not(query_prefix)

    def absorb(carry, block):
        block_pairs, block_clip, block_prefix = block
        allowed = (query_clip[:, None] == block_clip[None, :]) & (
            allowed_query[:, None] | block_prefix[None, :]
        )
        updated = []
        for head in range(heads_here):
            top, total, summed = carry[head]
            low = head * HEAD_DIM
            q_head = queries[:, low : low + HEAD_DIM]
            k_head = block_pairs[:, low : low + HEAD_DIM]
            v_head = block_pairs[:, width + low : width + low + HEAD_DIM]
            scores = (
                lax.dot_general(
                    q_head, k_head, (((1,), (1,)), ((), ())), preferred_element_type=jnp.float32
                )
                * factor
            )
            masked = jnp.where(allowed, scores, NEG)
            new_top = jnp.maximum(top, jnp.max(masked, axis=1, keepdims=True))
            fade = jnp.exp(top - new_top)
            weights = jnp.where(allowed, jnp.exp(scores - new_top), 0.0)
            total = total * fade + jnp.sum(weights, axis=1, keepdims=True)
            summed = summed * fade + jnp.dot(
                weights.astype(jnp.bfloat16), v_head, preferred_element_type=jnp.float32
            )
            updated.append((new_top, total, summed))
        return (tuple(updated), None)

    count = pairs.shape[0]
    step = 2048 if count > 2048 and count % 2048 == 0 else count
    if step == count:
        result, unused = absorb(state, (pairs, key_clip, key_prefix))
        return result
    stacked = (
        pairs.reshape(count // step, step, pairs.shape[1]),
        key_clip.reshape(count // step, step),
        key_prefix.reshape(count // step, step),
    )
    result, unused = lax.scan(absorb, state, stacked)
    return result


def gathered_body(
    inputs,
    norm_gain,
    level_table,
    w_qkv,
    w_out,
    clip_lengths,
    prefix_lengths,
    noise_levels,
    token_rank,
):
    ranks = lax.axis_size("ctx")
    rank_here = lax.axis_index("ctx")
    per_dev = inputs.shape[0]
    slots = 2 * per_dev // ranks
    local_width = w_qkv.shape[2]
    heads_here = local_width // HEAD_DIM
    total_rows = per_dev * ranks
    clip_of, in_prefix, level_row = clip_tables(
        total_rows, clip_lengths, prefix_lengths, noise_levels
    )
    within, counts, starts = rank_tables(token_rank, ranks, per_dev)
    place = token_rank * per_dev + within
    order = (
        jnp.zeros((total_rows,), jnp.int32).at[place].set(jnp.arange(total_rows, dtype=jnp.int32))
    )
    first = rank_here * per_dev
    own_rank = lax.dynamic_slice_in_dim(token_rank, first, per_dev, 0)
    own_within = lax.dynamic_slice_in_dim(within, first, per_dev, 0)
    send_starts = lax.dynamic_slice_in_dim(starts, rank_here, 1, 0)[0]
    recv_counts = lax.dynamic_slice_in_dim(counts, rank_here, 1, 1)[:, 0]
    recv_starts = lax.dynamic_slice_in_dim(starts, rank_here, 1, 1)[:, 0]
    balanced_rows = lax.dynamic_slice_in_dim(order, first, per_dev, 0)
    target = own_rank * slots + own_within - send_starts[own_rank]
    buffer = jnp.zeros((ranks * slots, inputs.shape[1]), inputs.dtype).at[target].set(inputs)
    received = lax.all_to_all(
        buffer.reshape(ranks, slots, inputs.shape[1]),
        "ctx",
        split_axis=0,
        concat_axis=0,
        tiled=True,
    )
    spots = jnp.arange(slots, dtype=jnp.int32)[None, :]
    index = jnp.where(spots < recv_counts[:, None], recv_starts[:, None] + spots, per_dev).reshape(
        -1
    )
    flat = received.reshape(ranks * slots, received.shape[2])
    rows = jnp.zeros((per_dev, received.shape[2]), received.dtype).at[index].set(flat, mode="drop")
    full_rows = lax.all_gather(rows, "head", axis=1, tiled=True)
    normed = normalize(
        full_rows, in_prefix[balanced_rows], level_row[balanced_rows], level_table, norm_gain
    )
    qkv = jnp.dot(
        normed, w_qkv.reshape(w_qkv.shape[0], 3 * local_width), preferred_element_type=jnp.float32
    ).astype(jnp.bfloat16)
    start_state = tuple(
        (
            (
                jnp.full((per_dev, 1), NEG, jnp.float32),
                jnp.zeros((per_dev, 1), jnp.float32),
                jnp.zeros((per_dev, HEAD_DIM), jnp.float32),
            )
            for head in range(heads_here)
        )
    )
    key_clip = clip_of[order]
    key_prefix = in_prefix[order]
    query_clip = lax.dynamic_slice_in_dim(key_clip, first, per_dev, 0)
    query_prefix = lax.dynamic_slice_in_dim(key_prefix, first, per_dev, 0)
    queries = qkv[:, :local_width]
    pairs = qkv[:, local_width:]
    state = fold_keys(
        start_state,
        queries,
        query_clip,
        query_prefix,
        lax.all_gather(pairs, "ctx", axis=0, tiled=True),
        key_clip,
        key_prefix,
    )
    parts = [state[head][2] / state[head][1] for head in range(heads_here)]
    attention = jnp.concatenate(parts, axis=1).astype(jnp.bfloat16)
    terms = jnp.dot(attention, w_out, preferred_element_type=jnp.float32)
    return lax.psum_scatter(terms.astype(jnp.bfloat16), "head", scatter_dimension=1, tiled=True)


def packed_rows(place_ref, spots):
    start, early, half = place_ref[0], place_ref[1], place_ref[2]
    total = place_ref[3]
    before = jnp.where(spots < start, early, 1 - early)
    return spots + total * (half + before * (1 - 2 * half))


def clip_flags(rows, bounds_ref):
    begins, ends, leads = bounds_ref[0:1, :], bounds_ref[1:2, :], bounds_ref[2:3, :]
    inside = (rows >= begins) & (rows < ends)
    return inside, inside & (rows < leads)


def count_earlier(hot):
    ranks, rows, lanes = hot.shape
    flat = hot.reshape(ranks * rows, lanes).astype(jnp.bfloat16)

    def numbers(shape, axis):
        return lax.broadcasted_iota(jnp.int32, shape, axis)

    def group(index):
        return sum(jnp.where(index >= rows * k, 1, 0) for k in range(1, ranks))

    def ones(flags):
        return jnp.where(flags, 1.0, 0.0).astype(jnp.bfloat16)

    total = ranks * rows
    in_row = ones(numbers((lanes, lanes), 0) < numbers((lanes, lanes), 1))
    below, across = numbers((total, 1), 0), numbers((1, total), 1)
    in_rank = ones((group(below) == group(across)) & (across < below))
    row_sums = jnp.dot(
        flat, jnp.ones((lanes, lanes), jnp.bfloat16), preferred_element_type=jnp.float32
    )
    earlier = jnp.dot(flat, in_row, preferred_element_type=jnp.float32) + jnp.dot(
        in_rank, row_sums.astype(jnp.bfloat16), preferred_element_type=jnp.float32
    )
    return earlier.reshape(ranks, rows, lanes)


def table_kernel(ranks, place_ref, bounds_ref, rank_ref, *refs):
    order_ref, runs_ref, query_ref, key_ref, held = refs
    start, early, half, half_rows = (place_ref[k] for k in range(4))
    chip, clips, core, rank_here = (place_ref[k] for k in (4, 5, 8, 9))
    holds_long = half != early
    tokens = rank_ref[...]
    rows, lanes = tokens.shape
    per_dev = rows * lanes // ranks

    token = lanes * lax.broadcasted_iota(jnp.int32, tokens.shape, 0) + lax.broadcasted_iota(
        jnp.int32, tokens.shape, 1
    )
    hots = [jnp.where(tokens == rank, 1.0, 0.0) for rank in range(ranks)]
    earlier = count_earlier(jnp.stack(hots))
    within = sum(hots[rank] * earlier[rank] for rank in range(ranks))
    before = jnp.where(token < start, 1.0, 0.0)
    upto = jnp.where(token < start + half_rows, 1.0, 0.0)
    target = jnp.bitwise_xor(rank_here, 2 * lax.broadcasted_iota(jnp.int32, (1, lanes), 1))
    long_first, rest_first = [0.0, 0.0], [0.0, 0.0]
    long_base = rest_base = low_of = long_of = 0.0
    runs = [0.0] * 5
    for rank, hot in enumerate(hots):
        low = jnp.sum(hot * before, keepdims=True)
        high = jnp.sum(hot * upto, keepdims=True)
        parity = rank % 2
        first, rest = long_first[parity], rest_first[parity]
        long_base += hot * (first - low)
        rest_base += hot * rest
        low_of += hot * low
        long_of += hot * (high - low)
        here = jnp.where(target == rank, 1.0, 0.0)
        values = (
            jnp.where(holds_long, 0.0, low),
            jnp.where(holds_long, low, high),
            jnp.where(holds_long, high, float(per_dev)),
            jnp.where(holds_long, 0.0, rest),
            jnp.where(holds_long, first - low, rest - (high - low)),
        )
        runs = [run + here * value for run, value in zip(runs, values)]
        long_first[parity] = first + (high - low)
        rest_first[parity] = rest + (per_dev - (high - low))
    furthest = rows * lanes // 4 + per_dev // 2
    for index, run in enumerate(runs):
        run = run.astype(jnp.int32)
        runs_ref[index : index + 1, :] = (
            run if index < 3 else jnp.clip(run, -per_dev, furthest)
        )
    sorted_at = within + jnp.where(
        upto - before == 1.0, long_base, rest_base - jnp.where(within < low_of, 0.0, long_of)
    )
    held[...] = jnp.where(jnp.bitwise_and(tokens, 1) == core, sorted_at.astype(jnp.int32), -1)
    half_lines = rows // 2
    spots = lanes * lax.broadcasted_iota(
        jnp.int32, (half_lines, lanes), 0
    ) + lax.broadcasted_iota(jnp.int32, (half_lines, lanes), 1)
    later = packed_rows(place_ref, spots) >= half_rows
    held[:half_lines, :] = jnp.where(later, held[half_lines:, :], held[:half_lines, :])
    lines = half_lines // 4
    for d in range(4):
        line = lines * jnp.bitwise_xor(chip, d)
        order_ref[lines * d : lines * (d + 1), :] = held[pl.ds(line, lines), :]

    column = lax.broadcasted_iota(jnp.int32, (1, HEAD_DIM), 1)
    chip_rows = query_ref.shape[0] // 4
    for d in range(4):
        local = lax.broadcasted_iota(jnp.int32, (chip_rows, 1), 0)
        spots = chip_rows * jnp.bitwise_xor(chip, d) + local
        inside, leading = clip_flags(packed_rows(place_ref, spots), bounds_ref)
        spot = slice(d * chip_rows, (d + 1) * chip_rows)
        inside = jnp.where(inside, 1.0, 0.0)
        prefix = jnp.sum(jnp.where(leading, 1.0, 0.0), axis=1, keepdims=True)
        query_ref[spot, :] = jnp.where(column == clips, prefix, inside).astype(jnp.bfloat16)
        outside = jnp.where(column < clips, NEG * (1.0 - inside), 0.0)
        key_ref[spot, :] = jnp.where(column == clips, NEG * (1.0 - prefix), outside).astype(
            jnp.bfloat16
        )


def make_tables(place, bounds, token_rank, ranks, keys):
    vmem = pl.BlockSpec(memory_space=pltpu.VMEM)
    tokens = token_rank.reshape(-1, HEAD_DIM)
    features = jax.ShapeDtypeStruct((keys, HEAD_DIM), jnp.bfloat16)
    return pl.pallas_call(
        functools.partial(table_kernel, ranks),
        in_specs=[pl.BlockSpec(memory_space=pltpu.SMEM), vmem, vmem],
        out_specs=(vmem,) * 4,
        out_shape=(
            jax.ShapeDtypeStruct((tokens.shape[0] // 2, HEAD_DIM), jnp.int32),
            jax.ShapeDtypeStruct((8, HEAD_DIM), jnp.int32),
            features,
            features,
        ),
        scratch_shapes=[pltpu.VMEM(tokens.shape, jnp.int32)],
        compiler_params=pltpu.CompilerParams(vmem_limit_bytes=38 * MIB),
        cost_estimate=pl.CostEstimate(flops=COST, bytes_accessed=COST, transcendentals=0),
    )(place, bounds, tokens)


def select_kernel(low, place_ref, own_ref, moved_ref, *rest):
    out_ref = rest[-1]
    count = out_ref.shape[0]
    spots = place_ref[7] + low + lax.broadcasted_iota(jnp.int32, (count, 1), 0)
    swapped = jnp.where(spots < place_ref[0], place_ref[1], 1 - place_ref[1])
    out_ref[...] = jnp.where(swapped == 1, moved_ref[...], own_ref[low : low + count, :])


def select_rows(place, rows, moved, low, after):
    vmem = pl.BlockSpec(memory_space=pltpu.VMEM)
    return pl.pallas_call(
        functools.partial(select_kernel, low),
        in_specs=[pl.BlockSpec(memory_space=pltpu.SMEM), vmem, vmem]
        + [pl.BlockSpec(memory_space=pl.ANY)] * len(after),
        out_specs=vmem,
        out_shape=jax.ShapeDtypeStruct(moved.shape, moved.dtype),
        compiler_params=pltpu.CompilerParams(vmem_limit_bytes=16 * MIB),
        cost_estimate=pl.CostEstimate(flops=COST, bytes_accessed=COST, transcendentals=0),
    )(place, rows, moved, *after)


def head_of(chip, index, group_heads):
    return 2 * group_heads * (chip // 2) + 2 * index + chip % 2


def weight_copies(place_ref, index, group_heads, w_ref, out_ref, sems):
    pair = jnp.bitwise_xor(place_ref[4] // 2, place_ref[8])
    first = head_of(2 * pair, index, group_heads)
    columns = pl.ds(pl.multiple_of(first * HEAD_DIM, HEAD_DIM), 2 * HEAD_DIM)
    return [
        pltpu.make_async_copy(
            w_ref.at[part, :, columns],
            out_ref.at[:, 2 * part * HEAD_DIM : 2 * (part + 1) * HEAD_DIM],
            sems.at[part],
        )
        for part in range(3)
    ]


def norm_kernel(group_heads, place_ref, *refs):
    pieces = (len(refs) - 8) // 2
    bounds_ref, noise_ref, level_ref, gain_ref, w_ref, out_ref, next_ref, sems = refs[-8:]
    copies = weight_copies(place_ref, 0, group_heads, w_ref, next_ref, sems)
    for copy in copies:
        copy.start()
    width = out_ref.shape[1] // 2
    side, first = place_ref[6], place_ref[7]
    clips, levels = noise_ref.shape[0], level_ref.shape[0]
    spots = [pl.ds(pl.multiple_of(s * width, 128), width) for s in (side, 1 - side)]
    level = lax.broadcasted_iota(jnp.int32, (clips, levels), 1)
    chosen = jnp.where(noise_ref[...] == level, 1.0, 0.0).astype(jnp.bfloat16)
    tables = [
        jnp.dot(chosen, level_ref[:, spot], preferred_element_type=jnp.float32).astype(
            jnp.bfloat16
        )
        for spot in spots
    ]
    low = 0
    for piece in range(pieces):
        own_ref, other_ref = refs[piece], refs[pieces + piece]
        count = own_ref.shape[0]
        rows = slice(low, low + count)
        places = first + low + lax.broadcasted_iota(jnp.int32, (count, 1), 0)
        low += count
        unused, leading = clip_flags(packed_rows(place_ref, places), bounds_ref)
        picks = jnp.where(leading, 1.0, 0.0)[:, :clips].astype(jnp.bfloat16)
        shifted = [
            ref[...].astype(jnp.float32)
            + jnp.dot(picks, table, preferred_element_type=jnp.float32)
            for ref, table in zip((own_ref, other_ref), tables)
        ]
        squares = sum(jnp.sum(part * part, axis=1, keepdims=True) for part in shifted)
        factor = lax.rsqrt(squares / (2 * width) + EPS)
        for part, spot in zip(shifted, spots):
            out_ref[rows, spot] = (part * factor * gain_ref[:, spot]).astype(jnp.bfloat16)
    for copy in copies:
        copy.wait()


def normalize_rows(
    place, kept, other, bounds, noise_levels, level_table, norm_gain, w_parts, group_heads
):
    rows, depth = sum(part.shape[0] for part in kept), 2 * kept[0].shape[1]
    vmem = pl.BlockSpec(memory_space=pltpu.VMEM)
    return pl.pallas_call(
        functools.partial(norm_kernel, group_heads),
        in_specs=[pl.BlockSpec(memory_space=pltpu.SMEM)]
        + [vmem] * (2 * len(kept) + 4)
        + [pl.BlockSpec(memory_space=pltpu.HBM)],
        out_specs=(vmem, vmem),
        out_shape=(
            jax.ShapeDtypeStruct((rows, depth), jnp.bfloat16),
            jax.ShapeDtypeStruct((depth, 6 * HEAD_DIM), jnp.bfloat16),
        ),
        scratch_shapes=[pltpu.SemaphoreType.DMA((3,))],
        compiler_params=pltpu.CompilerParams(vmem_limit_bytes=38 * MIB),
        cost_estimate=pl.CostEstimate(flops=COST, bytes_accessed=COST, transcendentals=0),
    )(place, *kept, *other, bounds, noise_levels, level_table, norm_gain.reshape(1, -1), w_parts)


def project_kernel(next_head, group_heads, place_ref, own_ref, pair_ref, weights_ref, w_ref, *rest):
    copies = []
    if next_head is None:
        first_ref, second_ref = rest[-2:]
    else:
        first_ref, second_ref, next_ref, sems = rest[-4:]
        copies = weight_copies(place_ref, next_head, group_heads, w_ref, next_ref, sems)
    for copy in copies:
        copy.start()
    rows = jnp.concatenate([own_ref[...], pair_ref[...]], axis=0)
    outcome = jnp.dot(rows, weights_ref[...], preferred_element_type=jnp.float32)
    outcome = outcome.astype(jnp.bfloat16)

    count = own_ref.shape[0]

    def store(even_ref, odd_ref):
        for index, core in enumerate((place_ref[8], 1 - place_ref[8])):
            rows = pl.ds(pl.multiple_of(core * count, count), count)
            half = outcome[index * count : (index + 1) * count]
            for part in range(3):
                to = slice(part * HEAD_DIM, (part + 1) * HEAD_DIM)
                even_ref[rows, to] = half[:, 2 * part * HEAD_DIM : (2 * part + 1) * HEAD_DIM]
                odd_ref[rows, to] = half[:, (2 * part + 1) * HEAD_DIM : 2 * (part + 1) * HEAD_DIM]

    same = place_ref[4] % 2 == place_ref[8]

    @pl.when(same)
    def _():
        store(first_ref, second_ref)

    @pl.when(jnp.logical_not(same))
    def _():
        store(second_ref, first_ref)

    for copy in copies:
        copy.wait()


def project_heads(place, own, pair, weights, w_parts, next_head, group_heads, after):
    rows, depth = own.shape
    vmem, hbm = pl.BlockSpec(memory_space=pltpu.VMEM), pl.BlockSpec(memory_space=pl.ANY)
    shape = jax.ShapeDtypeStruct((2 * rows, 3 * HEAD_DIM), jnp.bfloat16)
    more = next_head is not None
    return pl.pallas_call(
        functools.partial(project_kernel, next_head, group_heads),
        in_specs=[
            pl.BlockSpec(memory_space=pltpu.SMEM),
            vmem,
            vmem,
            vmem,
            pl.BlockSpec(memory_space=pltpu.HBM),
        ]
        + [hbm] * len(after),
        out_specs=(vmem, vmem) + (vmem,) * more,
        out_shape=(shape, shape)
        + (jax.ShapeDtypeStruct(weights.shape, weights.dtype),) * more,
        scratch_shapes=[pltpu.SemaphoreType.DMA((3,))] * more,
        compiler_params=pltpu.CompilerParams(vmem_limit_bytes=38 * MIB),
        cost_estimate=pl.CostEstimate(flops=COST, bytes_accessed=COST, transcendentals=0),
    )(place, own, pair, weights, w_parts, *after)


def attend_kernel(fetch, place_ref, runs_ref, *refs):
    copies = []
    if fetch:
        w_ref, sorted_ref, sems = refs[9], refs[-6], refs[-1]
        refs = refs[:-6] + refs[-5:-1]
        heads = w_ref.shape[0] // HEAD_DIM // 4
        for d in range(4):
            for index in range(heads):
                head = head_of(jnp.bitwise_xor(place_ref[4], d), index, heads)
                to = (heads * d + index) * HEAD_DIM
                copies.append(
                    pltpu.make_async_copy(
                        w_ref.at[pl.ds(pl.multiple_of(head * HEAD_DIM, HEAD_DIM), HEAD_DIM), :],
                        sorted_ref.at[to : to + HEAD_DIM, :],
                        sems.at[heads * d + index],
                    )
                )
    for copy in copies:
        copy.start()
    mine, near, far, pair_first, pair_far, pair_near = refs[:6]
    order_ref, query_mask_ref, key_mask_ref = refs[6:9]
    stay_ref, cross_ref, q_all, k_all, v_all, sorted_out = refs[-6:]
    chip_rows = mine.shape[0]
    rows = chip_rows // 2
    queries = sorted_out.shape[0] - 2 * rows

    def hold(sources):
        for index, source in enumerate(sources):
            spot = slice(index * chip_rows, (index + 1) * chip_rows)
            q_all[spot, :HEAD_DIM] = source[:, :HEAD_DIM]
            k_all[spot, :HEAD_DIM] = source[:, HEAD_DIM : 2 * HEAD_DIM]
            v_all[spot, :HEAD_DIM] = source[:, 2 * HEAD_DIM :]

    @pl.when(place_ref[8] == 0)
    def _():
        hold((mine, near, pair_near, pair_far))

    @pl.when(place_ref[8] == 1)
    def _():
        hold((pair_first, pair_near, near, far))

    q_all[:, HEAD_DIM:] = query_mask_ref[...]
    k_all[:, HEAD_DIM:] = key_mask_ref[...]
    v_all[:, HEAD_DIM:] = jnp.ones((4 * chip_rows, HEAD_DIM), jnp.bfloat16)
    tile = queries // ATTEND_TILES

    def score(step):
        wanted = step * tile + lax.broadcasted_iota(jnp.int32, (tile, 1), 0)
        picks = jnp.concatenate(
            [
                jnp.where(order_ref[line : line + 1, :] == wanted, 1.0, 0.0).astype(jnp.bfloat16)
                for line in range(order_ref.shape[0])
            ],
            axis=1,
        )
        sorted_queries = jnp.dot(picks, q_all[...], preferred_element_type=jnp.float32)
        return lax.dot_general(
            sorted_queries.astype(jnp.bfloat16),
            k_all[...],
            (((1,), (1,)), ((), ())),
            preferred_element_type=jnp.float32,
        )

    coming = score(0)
    for step in range(ATTEND_TILES):
        scores = coming
        if step + 1 < ATTEND_TILES:
            coming = score(step + 1)
        top = jnp.max(scores, axis=1, keepdims=True)
        weights = jnp.exp2((scores - top) * (HEAD_DIM ** (-0.5) * LOG2E))
        summed = jnp.dot(
            weights.astype(jnp.bfloat16), v_all[...], preferred_element_type=jnp.float32
        )
        sorted_out[rows + step * tile : rows + (step + 1) * tile, :] = (
            summed[:, :HEAD_DIM] / summed[:, HEAD_DIM:]
        )

    row = lax.broadcasted_iota(jnp.int32, (rows, 1), 0)
    for n in range(8):
        first = sorted_out[pl.ds(rows + runs_ref[3, n], rows), :]
        second = sorted_out[pl.ds(rows + runs_ref[4, n], rows), :]
        in_second = (row >= runs_ref[1, n]) & (row < runs_ref[2, n])
        taken = jnp.where(row < runs_ref[0, n], first, jnp.where(in_second, second, 0.0))
        (stay_ref, cross_ref)[n // 4][n % 4] = taken.astype(jnp.bfloat16)
    for copy in copies:
        copy.wait()


def attend(place, runs, blocks, order, query_mask, key_mask, w_out, after):
    chip_rows = blocks[0].shape[0]
    rows, keys = chip_rows // 2, 4 * chip_rows
    queries = keys // 2 + rows // 2
    vmem, smem = pl.BlockSpec(memory_space=pltpu.VMEM), pl.BlockSpec(memory_space=pltpu.SMEM)
    hbm = pl.BlockSpec(memory_space=pl.ANY)
    shape = jax.ShapeDtypeStruct((4, rows, HEAD_DIM), jnp.bfloat16)
    fetch = w_out is not None
    extra = (w_out,) * fetch
    return pl.pallas_call(
        functools.partial(attend_kernel, fetch),
        in_specs=[smem, smem]
        + [vmem] * (len(blocks) + 3)
        + [pl.BlockSpec(memory_space=pltpu.HBM)] * fetch
        + [hbm] * len(after),
        out_specs=(vmem, vmem) + (vmem,) * fetch,
        out_shape=(shape, shape)
        + tuple(jax.ShapeDtypeStruct(array.shape, array.dtype) for array in extra),
        scratch_shapes=[
            pltpu.VMEM((keys, 2 * HEAD_DIM), jnp.bfloat16),
            pltpu.VMEM((keys, 2 * HEAD_DIM), jnp.bfloat16),
            pltpu.VMEM((keys, 2 * HEAD_DIM), jnp.bfloat16),
            pltpu.VMEM((queries + 2 * rows, HEAD_DIM), jnp.float32),
        ]
        + [pltpu.SemaphoreType.DMA((array.shape[0] // HEAD_DIM,)) for array in extra],
        compiler_params=pltpu.CompilerParams(vmem_limit_bytes=26 * MIB),
        cost_estimate=pl.CostEstimate(
            flops=LONG_COST, bytes_accessed=COST, transcendentals=0
        ),
    )(place, runs, *blocks, order, query_mask, key_mask, *extra, *after)


def join_kernel(heads, *refs):
    outs = refs[-4:]
    for d in range(4):
        parts = [refs[2 * h][d] + refs[2 * h + 1][d] for h in range(heads)]
        outs[d][...] = jnp.concatenate(parts, axis=1)


def join_halves(stays, arrivals, after):
    heads, (slots, rows, width) = len(stays), stays[0].shape
    vmem = pl.BlockSpec(memory_space=pltpu.VMEM)
    pairs = [part for both in zip(stays, arrivals) for part in both]
    shape = jax.ShapeDtypeStruct((rows, heads * width), jnp.bfloat16)
    return pl.pallas_call(
        functools.partial(join_kernel, heads),
        in_specs=[vmem] * len(pairs) + [pl.BlockSpec(memory_space=pl.ANY)] * len(after),
        out_specs=(vmem,) * slots,
        out_shape=(shape,) * slots,
        compiler_params=pltpu.CompilerParams(vmem_limit_bytes=16 * MIB),
        cost_estimate=pl.CostEstimate(flops=COST, bytes_accessed=COST, transcendentals=0),
    )(*pairs, *after)


def out_kernel(side_ref, *refs):
    w_ref, out_ref = refs[-2:]
    columns = out_ref.shape[1]
    rows = jnp.concatenate([ref[...] for ref in refs[:-2]], axis=1)
    spot = pl.ds(pl.multiple_of(side_ref[0] * columns, HEAD_DIM), columns)
    out_ref[...] = jnp.dot(rows, w_ref[:, spot], preferred_element_type=jnp.float32).astype(
        out_ref.dtype
    )


def project_out(side, pieces, w_sorted, dtype):
    rows = pieces[0].shape[0]
    vmem = pl.BlockSpec(memory_space=pltpu.VMEM)
    return pl.pallas_call(
        out_kernel,
        in_specs=[pl.BlockSpec(memory_space=pltpu.SMEM)] + [vmem] * (len(pieces) + 1),
        out_specs=vmem,
        out_shape=jax.ShapeDtypeStruct((rows, w_sorted.shape[1] // 2), dtype),
        compiler_params=pltpu.CompilerParams(vmem_limit_bytes=12 * MIB),
        cost_estimate=pl.CostEstimate(flops=COST, bytes_accessed=COST, transcendentals=0),
    )(side.reshape(1), *pieces, w_sorted)


SWAP_ROWS = (128, 112, 80)
ATTEND_TILES = 3


def halved_body(
    inputs,
    norm_gain,
    level_table,
    w_qkv,
    w_out,
    clip_lengths,
    prefix_lengths,
    noise_levels,
    token_rank,
):
    rank_here = lax.axis_index("ctx")
    side = lax.axis_index("head")
    per_dev = inputs.shape[0]
    ranks = 16
    half_rows = 8 * per_dev
    group_heads = w_qkv.shape[2] // HEAD_DIM // 4
    clips = clip_lengths.shape[0]
    half, block, core = rank_here // 8, rank_here % 8, rank_here % 2
    chip = block // 2

    def exchange(array, flip, only=lambda r: True):
        pairs = [(r, r ^ flip) for r in range(ranks) if only(r)]
        return lax.ppermute(array, "ctx", pairs)

    index = jnp.arange(clips, dtype=jnp.int32)
    begins = jnp.sum(jnp.where(index[None, :] < index[:, None], clip_lengths[None, :], 0), axis=1)
    start = jnp.sum(jnp.where(clip_lengths == MAXCLIP, begins, 0))
    early = start <= half_rows // 2
    def tables(begins, start, early, clip_lengths, prefix_lengths):
        place = jnp.stack(
            [
                start,
                early.astype(jnp.int32),
                half,
                jnp.int32(half_rows),
                chip,
                jnp.int32(clips),
                side,
                block * per_dev,
                core,
                rank_here,
            ]
        )
        ends = begins + clip_lengths
        leads = begins + jnp.minimum(prefix_lengths, clip_lengths)
        bounds = jnp.pad(jnp.stack([begins, ends, leads]), ((0, 5), (0, HEAD_DIM - clips)))
        return place, bounds

    def gather_rows(blocks):
        def run(rows, begins, start, early, clip_lengths, prefix_lengths):
            place, bounds = tables(begins, start, early, clip_lengths, prefix_lengths)
            cuts = [sum(SWAP_ROWS[:i]) for i in range(len(SWAP_ROWS) + 1)]
            cuts = list(zip(cuts[:-1], cuts[1:]))
            moved = [exchange(rows[a:b], 8, lambda r: r % 8 in blocks) for a, b in cuts]
            kept = []
            for part, (a, b) in zip(moved, cuts):
                kept.append(select_rows(place, rows, part, a, kept[-1:]))
            other = [lax.ppermute(part, "head", [(0, 1), (1, 0)]) for part in kept]
            return tuple(kept), tuple(other), place, bounds

        return run

    kept, other, place, bounds = lax.cond(
        early,
        gather_rows(range(4)),
        gather_rows(range(4, 8)),
        inputs,
        begins,
        start,
        early,
        clip_lengths,
        prefix_lengths,
    )
    w_parts = jnp.transpose(w_qkv, (1, 0, 2))
    normed, weights = normalize_rows(
        place,
        kept,
        other,
        bounds,
        noise_levels.reshape(-1, 1),
        level_table,
        norm_gain,
        w_parts,
        group_heads,
    )
    pair = exchange(normed, 1)
    query_order, runs, query_mask, key_mask = make_tables(
        place, bounds, token_rank, ranks, half_rows
    )

    def project(head, weights, after):
        next_head = head + 1 if head + 1 < group_heads else None
        first, second, *more = project_heads(
            place, normed, pair, weights, w_parts, next_head, group_heads, after
        )
        near = lax.ppermute(
            second, "ctx", [(r, r ^ (2 if r % 2 == 0 else 4)) for r in range(ranks)]
        )
        far = exchange(first, 6, lambda r: r % 2 == 1)
        pair_first = exchange(first, 1, lambda r: r % 2 == 0)
        pair_far = exchange(far, 1, lambda r: r % 2 == 1)
        pair_near = exchange(near, 1)
        return [first, near, far, pair_first, pair_far, pair_near], more[0] if more else None

    blocks = []
    for head in range(group_heads):
        after = ([blocks[-1][3]] if blocks else []) + (blocks[-2][1:3] if head > 1 else [])
        block, weights = project(head, weights, after)
        blocks.append(block)
    stays, arrivals, after = [], [], [blocks[-1][0], *blocks[1][1:3]]
    for head in range(group_heads):
        last = head + 1 == group_heads
        stay, cross, *w_sorted = attend(
            place,
            runs,
            blocks[head],
            query_order,
            query_mask,
            key_mask,
            w_out if last else None,
            after,
        )
        stays.append(stay)
        arrivals.append(exchange(cross, 8))
        after = [cross] + (arrivals[head - 1 : head] if head else blocks[-1][1:3])

    pieces = [[], [], [], []]
    for heads, after in ((slice(0, -1), [cross]), (slice(-1, None), [])):
        joined = join_halves(stays[heads], arrivals[heads], after)
        for d in range(4):
            pieces[d].append(exchange(joined[d], 2 * d) if d else joined[d])
    pieces = [piece for slot in pieces for piece in slot]

    away = project_out(1 - side, pieces, w_sorted[0], jnp.bfloat16)
    away = lax.ppermute(away, "head", [(0, 1), (1, 0)])
    stay = project_out(side, pieces, w_sorted[0], jnp.float32)
    return (stay + away.astype(jnp.float32)).astype(jnp.bfloat16)


def solution(mesh):
    in_specs = (
        P("ctx", "head"),
        P(),
        P(),
        P(None, None, "head"),
        P("head", None),
        P(),
        P(),
        P(),
        P(),
    )
    out_specs = P("ctx", "head")

    def body(inputs, norm_gain, level_table, w_qkv, *rest):
        ranks, sides = mesh.shape["ctx"], mesh.shape["head"]
        heads_here = w_qkv.shape[2] // HEAD_DIM
        halved = (
            ranks == 16
            and sides == 2
            and ranks * inputs.shape[0] == 2 * MAXCLIP
            and heads_here % 4 == 0
        )
        run = halved_body if halved else gathered_body
        return run(inputs, norm_gain, level_table, w_qkv, *rest)

    return jax.shard_map(body, mesh=mesh, in_specs=in_specs, out_specs=out_specs, check_vma=False)
```

```python
import functools

import jax
import jax.numpy as jnp
from jax import lax
from jax.experimental import pallas as pl
from jax.experimental.pallas import tpu as pltpu
from jax.sharding import PartitionSpec as P

HEAD_DIM = 128


NEG = -1e30
EPS = 1e-06
MAXCLIP = 2560
LOG2E = 1.4426950408889634
MIB = 1024 * 1024
COST = 1000000
LONG_COST = 10000000000


def clip_tables(total_rows, clip_lengths, prefix_lengths, noise_levels):
    rows = jnp.arange(total_rows, dtype=jnp.int32)
    ends = jnp.cumsum(clip_lengths)
    begins = ends - clip_lengths
    clip_of = jnp.sum((rows[:, None] >= ends[None, :]).astype(jnp.int32), axis=1)
    member = clip_of[:, None] == jnp.arange(clip_lengths.shape[0], dtype=jnp.int32)[None, :]
    begin_row = jnp.sum(jnp.where(member, begins[None, :], 0), axis=1)
    lead = jnp.minimum(prefix_lengths, clip_lengths)
    lead_row = jnp.sum(jnp.where(member, lead[None, :], 0), axis=1)
    level_row = jnp.sum(jnp.where(member, noise_levels[None, :], 0), axis=1)
    in_prefix = rows - begin_row < lead_row
    return (clip_of, in_prefix, level_row)


def rank_tables(token_rank, ranks, per_rank):
    onehot = (token_rank[:, None] == jnp.arange(ranks, dtype=jnp.int32)[None, :]).astype(jnp.int32)
    earlier = jnp.cumsum(onehot, axis=0) - onehot
    within = jnp.sum(earlier * onehot, axis=1)
    counts = jnp.sum(onehot.reshape(ranks, per_rank, ranks), axis=1)
    starts = jnp.cumsum(counts, axis=0) - counts
    return (within, counts, starts)


def normalize(rows, in_prefix, level_row, level_table, norm_gain):
    picks = (
        level_row[:, None] == jnp.arange(level_table.shape[0], dtype=jnp.int32)[None, :]
    ) & in_prefix[:, None]
    added = jnp.dot(picks.astype(jnp.bfloat16), level_table, preferred_element_type=jnp.float32)
    shifted = rows.astype(jnp.float32) + added
    factor = lax.rsqrt(jnp.mean(shifted * shifted, axis=-1, keepdims=True) + EPS)
    return (shifted * factor * norm_gain).astype(jnp.bfloat16)


def fold_keys(state, queries, query_clip, query_prefix, pairs, key_clip, key_prefix):
    width = queries.shape[1]
    heads_here = width // HEAD_DIM
    factor = HEAD_DIM ** (-0.5)
    allowed_query = jnp.logical_not(query_prefix)

    def absorb(carry, block):
        block_pairs, block_clip, block_prefix = block
        allowed = (query_clip[:, None] == block_clip[None, :]) & (
            allowed_query[:, None] | block_prefix[None, :]
        )
        updated = []
        for head in range(heads_here):
            top, total, summed = carry[head]
            low = head * HEAD_DIM
            q_head = queries[:, low : low + HEAD_DIM]
            k_head = block_pairs[:, low : low + HEAD_DIM]
            v_head = block_pairs[:, width + low : width + low + HEAD_DIM]
            scores = (
                lax.dot_general(
                    q_head, k_head, (((1,), (1,)), ((), ())), preferred_element_type=jnp.float32
                )
                * factor
            )
            masked = jnp.where(allowed, scores, NEG)
            new_top = jnp.maximum(top, jnp.max(masked, axis=1, keepdims=True))
            fade = jnp.exp(top - new_top)
            weights = jnp.where(allowed, jnp.exp(scores - new_top), 0.0)
            total = total * fade + jnp.sum(weights, axis=1, keepdims=True)
            summed = summed * fade + jnp.dot(
                weights.astype(jnp.bfloat16), v_head, preferred_element_type=jnp.float32
            )
            updated.append((new_top, total, summed))
        return (tuple(updated), None)

    count = pairs.shape[0]
    step = 2048 if count > 2048 and count % 2048 == 0 else count
    if step == count:
        result, unused = absorb(state, (pairs, key_clip, key_prefix))
        return result
    stacked = (
        pairs.reshape(count // step, step, pairs.shape[1]),
        key_clip.reshape(count // step, step),
        key_prefix.reshape(count // step, step),
    )
    result, unused = lax.scan(absorb, state, stacked)
    return result


def gathered_body(
    inputs,
    norm_gain,
    level_table,
    w_qkv,
    w_out,
    clip_lengths,
    prefix_lengths,
    noise_levels,
    token_rank,
):
    ranks = lax.axis_size("ctx")
    rank_here = lax.axis_index("ctx")
    per_dev = inputs.shape[0]
    slots = 2 * per_dev // ranks
    local_width = w_qkv.shape[2]
    heads_here = local_width // HEAD_DIM
    total_rows = per_dev * ranks
    clip_of, in_prefix, level_row = clip_tables(
        total_rows, clip_lengths, prefix_lengths, noise_levels
    )
    within, counts, starts = rank_tables(token_rank, ranks, per_dev)
    place = token_rank * per_dev + within
    order = (
        jnp.zeros((total_rows,), jnp.int32).at[place].set(jnp.arange(total_rows, dtype=jnp.int32))
    )
    first = rank_here * per_dev
    own_rank = lax.dynamic_slice_in_dim(token_rank, first, per_dev, 0)
    own_within = lax.dynamic_slice_in_dim(within, first, per_dev, 0)
    send_starts = lax.dynamic_slice_in_dim(starts, rank_here, 1, 0)[0]
    recv_counts = lax.dynamic_slice_in_dim(counts, rank_here, 1, 1)[:, 0]
    recv_starts = lax.dynamic_slice_in_dim(starts, rank_here, 1, 1)[:, 0]
    balanced_rows = lax.dynamic_slice_in_dim(order, first, per_dev, 0)
    target = own_rank * slots + own_within - send_starts[own_rank]
    buffer = jnp.zeros((ranks * slots, inputs.shape[1]), inputs.dtype).at[target].set(inputs)
    received = lax.all_to_all(
        buffer.reshape(ranks, slots, inputs.shape[1]),
        "ctx",
        split_axis=0,
        concat_axis=0,
        tiled=True,
    )
    spots = jnp.arange(slots, dtype=jnp.int32)[None, :]
    index = jnp.where(spots < recv_counts[:, None], recv_starts[:, None] + spots, per_dev).reshape(
        -1
    )
    flat = received.reshape(ranks * slots, received.shape[2])
    rows = jnp.zeros((per_dev, received.shape[2]), received.dtype).at[index].set(flat, mode="drop")
    full_rows = lax.all_gather(rows, "head", axis=1, tiled=True)
    normed = normalize(
        full_rows, in_prefix[balanced_rows], level_row[balanced_rows], level_table, norm_gain
    )
    qkv = jnp.dot(
        normed, w_qkv.reshape(w_qkv.shape[0], 3 * local_width), preferred_element_type=jnp.float32
    ).astype(jnp.bfloat16)
    start_state = tuple(
        (
            (
                jnp.full((per_dev, 1), NEG, jnp.float32),
                jnp.zeros((per_dev, 1), jnp.float32),
                jnp.zeros((per_dev, HEAD_DIM), jnp.float32),
            )
            for head in range(heads_here)
        )
    )
    key_clip = clip_of[order]
    key_prefix = in_prefix[order]
    query_clip = lax.dynamic_slice_in_dim(key_clip, first, per_dev, 0)
    query_prefix = lax.dynamic_slice_in_dim(key_prefix, first, per_dev, 0)
    queries = qkv[:, :local_width]
    pairs = qkv[:, local_width:]
    state = fold_keys(
        start_state,
        queries,
        query_clip,
        query_prefix,
        lax.all_gather(pairs, "ctx", axis=0, tiled=True),
        key_clip,
        key_prefix,
    )
    parts = [state[head][2] / state[head][1] for head in range(heads_here)]
    attention = jnp.concatenate(parts, axis=1).astype(jnp.bfloat16)
    terms = jnp.dot(attention, w_out, preferred_element_type=jnp.float32)
    return lax.psum_scatter(terms.astype(jnp.bfloat16), "head", scatter_dimension=1, tiled=True)


def packed_rows(place_ref, spots):
    start, early, half = place_ref[0], place_ref[1], place_ref[2]
    total = place_ref[3]
    before = jnp.where(spots < start, early, 1 - early)
    return spots + total * (half + before * (1 - 2 * half))


def clip_flags(rows, bounds_ref):
    begins, ends, leads = bounds_ref[0:1, :], bounds_ref[1:2, :], bounds_ref[2:3, :]
    inside = (rows >= begins) & (rows < ends)
    return inside, inside & (rows < leads)


def count_earlier(hot):
    ranks, rows, lanes = hot.shape
    flat = hot.reshape(ranks * rows, lanes).astype(jnp.bfloat16)

    def numbers(shape, axis):
        return lax.broadcasted_iota(jnp.int32, shape, axis)

    def group(index):
        return sum(jnp.where(index >= rows * k, 1, 0) for k in range(1, ranks))

    def ones(flags):
        return jnp.where(flags, 1.0, 0.0).astype(jnp.bfloat16)

    total = ranks * rows
    in_row = ones(numbers((lanes, lanes), 0) < numbers((lanes, lanes), 1))
    below, across = numbers((total, 1), 0), numbers((1, total), 1)
    in_rank = ones((group(below) == group(across)) & (across < below))
    row_sums = jnp.dot(
        flat, jnp.ones((lanes, lanes), jnp.bfloat16), preferred_element_type=jnp.float32
    )
    earlier = jnp.dot(flat, in_row, preferred_element_type=jnp.float32) + jnp.dot(
        in_rank, row_sums.astype(jnp.bfloat16), preferred_element_type=jnp.float32
    )
    return earlier.reshape(ranks, rows, lanes)


def table_kernel(ranks, place_ref, bounds_ref, rank_ref, *refs):
    order_ref, runs_ref, query_ref, key_ref, held = refs
    start, early, half, half_rows = (place_ref[k] for k in range(4))
    chip, clips, core, rank_here = (place_ref[k] for k in (4, 5, 8, 9))
    holds_long = half != early
    tokens = rank_ref[...]
    rows, lanes = tokens.shape
    per_dev = rows * lanes // ranks

    token = lanes * lax.broadcasted_iota(jnp.int32, tokens.shape, 0) + lax.broadcasted_iota(
        jnp.int32, tokens.shape, 1
    )
    hots = [jnp.where(tokens == rank, 1.0, 0.0) for rank in range(ranks)]
    earlier = count_earlier(jnp.stack(hots))
    within = sum(hots[rank] * earlier[rank] for rank in range(ranks))
    before = jnp.where(token < start, 1.0, 0.0)
    upto = jnp.where(token < start + half_rows, 1.0, 0.0)
    target = jnp.bitwise_xor(rank_here, 2 * lax.broadcasted_iota(jnp.int32, (1, lanes), 1))
    long_first, rest_first = [0.0, 0.0], [0.0, 0.0]
    long_base = rest_base = low_of = long_of = 0.0
    runs = [0.0] * 5
    for rank, hot in enumerate(hots):
        low = jnp.sum(hot * before, keepdims=True)
        high = jnp.sum(hot * upto, keepdims=True)
        parity = rank % 2
        first, rest = long_first[parity], rest_first[parity]
        long_base += hot * (first - low)
        rest_base += hot * rest
        low_of += hot * low
        long_of += hot * (high - low)
        here = jnp.where(target == rank, 1.0, 0.0)
        values = (
            jnp.where(holds_long, 0.0, low),
            jnp.where(holds_long, low, high),
            jnp.where(holds_long, high, float(per_dev)),
            jnp.where(holds_long, 0.0, rest),
            jnp.where(holds_long, first - low, rest - (high - low)),
        )
        runs = [run + here * value for run, value in zip(runs, values)]
        long_first[parity] = first + (high - low)
        rest_first[parity] = rest + (per_dev - (high - low))
    furthest = rows * lanes // 4 + per_dev // 2
    for index, run in enumerate(runs):
        run = run.astype(jnp.int32)
        runs_ref[index : index + 1, :] = (
            run if index < 3 else jnp.clip(run, -per_dev, furthest)
        )
    sorted_at = within + jnp.where(
        upto - before == 1.0, long_base, rest_base - jnp.where(within < low_of, 0.0, long_of)
    )
    held[...] = jnp.where(jnp.bitwise_and(tokens, 1) == core, sorted_at.astype(jnp.int32), -1)
    half_lines = rows // 2
    spots = lanes * lax.broadcasted_iota(
        jnp.int32, (half_lines, lanes), 0
    ) + lax.broadcasted_iota(jnp.int32, (half_lines, lanes), 1)
    later = packed_rows(place_ref, spots) >= half_rows
    held[:half_lines, :] = jnp.where(later, held[half_lines:, :], held[:half_lines, :])
    lines = half_lines // 4
    for d in range(4):
        line = lines * jnp.bitwise_xor(chip, d)
        order_ref[lines * d : lines * (d + 1), :] = held[pl.ds(line, lines), :]

    column = lax.broadcasted_iota(jnp.int32, (1, HEAD_DIM), 1)
    chip_rows = query_ref.shape[0] // 4
    for d in range(4):
        local = lax.broadcasted_iota(jnp.int32, (chip_rows, 1), 0)
        spots = chip_rows * jnp.bitwise_xor(chip, d) + local
        inside, leading = clip_flags(packed_rows(place_ref, spots), bounds_ref)
        spot = slice(d * chip_rows, (d + 1) * chip_rows)
        inside = jnp.where(inside, 1.0, 0.0)
        prefix = jnp.sum(jnp.where(leading, 1.0, 0.0), axis=1, keepdims=True)
        query_ref[spot, :] = jnp.where(column == clips, prefix, inside).astype(jnp.bfloat16)
        outside = jnp.where(column < clips, NEG * (1.0 - inside), 0.0)
        key_ref[spot, :] = jnp.where(column == clips, NEG * (1.0 - prefix), outside).astype(
            jnp.bfloat16
        )


def make_tables(place, bounds, token_rank, ranks, keys):
    vmem = pl.BlockSpec(memory_space=pltpu.VMEM)
    tokens = token_rank.reshape(-1, HEAD_DIM)
    features = jax.ShapeDtypeStruct((keys, HEAD_DIM), jnp.bfloat16)
    return pl.pallas_call(
        functools.partial(table_kernel, ranks),
        in_specs=[pl.BlockSpec(memory_space=pltpu.SMEM), vmem, vmem],
        out_specs=(vmem,) * 4,
        out_shape=(
            jax.ShapeDtypeStruct((tokens.shape[0] // 2, HEAD_DIM), jnp.int32),
            jax.ShapeDtypeStruct((8, HEAD_DIM), jnp.int32),
            features,
            features,
        ),
        scratch_shapes=[pltpu.VMEM(tokens.shape, jnp.int32)],
        compiler_params=pltpu.CompilerParams(vmem_limit_bytes=30 * MIB),
        cost_estimate=pl.CostEstimate(flops=COST, bytes_accessed=COST, transcendentals=0),
    )(place, bounds, tokens)


def select_kernel(low, place_ref, own_ref, moved_ref, *rest):
    out_ref = rest[-1]
    spots = place_ref[7] + low + lax.broadcasted_iota(jnp.int32, (out_ref.shape[0], 1), 0)
    swapped = jnp.where(spots < place_ref[0], place_ref[1], 1 - place_ref[1])
    out_ref[...] = jnp.where(swapped == 1, moved_ref[...], own_ref[...])


def select_rows(place, own, moved, low, after):
    vmem = pl.BlockSpec(memory_space=pltpu.VMEM)
    return pl.pallas_call(
        functools.partial(select_kernel, low),
        in_specs=[pl.BlockSpec(memory_space=pltpu.SMEM), vmem, vmem]
        + [pl.BlockSpec(memory_space=pl.ANY)] * len(after),
        out_specs=vmem,
        out_shape=jax.ShapeDtypeStruct(moved.shape, moved.dtype),
        compiler_params=pltpu.CompilerParams(vmem_limit_bytes=8 * MIB),
        cost_estimate=pl.CostEstimate(flops=COST, bytes_accessed=COST, transcendentals=0),
    )(place, own, moved, *after)


def head_of(chip, index, group_heads):
    return 2 * group_heads * (chip // 2) + 2 * index + chip % 2


def weight_copies(place_ref, indices, group_heads, w_ref, out_ref, sems):
    pair = jnp.bitwise_xor(place_ref[4] // 2, place_ref[8])
    depth = out_ref.shape[0] // COPY_PIECES
    copies = []
    for position, index in enumerate(indices):
        first = head_of(2 * pair, index, group_heads)
        columns = pl.ds(pl.multiple_of(first * HEAD_DIM, HEAD_DIM), 2 * HEAD_DIM)
        for part in range(3):
            to = 3 * position + part
            for piece in range(COPY_PIECES):
                rows = slice(piece * depth, (piece + 1) * depth)
                copies.append(
                    pltpu.make_async_copy(
                        w_ref.at[part, rows, columns],
                        out_ref.at[rows, 2 * to * HEAD_DIM : 2 * (to + 1) * HEAD_DIM],
                        sems.at[to, piece],
                    )
                )
    return copies


def norm_kernel(indices, group_heads, place_ref, *refs):
    pieces = (len(refs) - 8) // 2
    bounds_ref, noise_ref, level_ref, gain_ref, w_ref, out_ref, next_ref, sems = refs[-8:]
    copies = weight_copies(place_ref, indices, group_heads, w_ref, next_ref, sems)
    for copy in copies:
        copy.start()
    width = out_ref.shape[1] // 2
    side, first = place_ref[6], place_ref[7]
    clips, levels = noise_ref.shape[0], level_ref.shape[0]
    spots = [pl.ds(pl.multiple_of(s * width, 128), width) for s in (side, 1 - side)]
    level = lax.broadcasted_iota(jnp.int32, (clips, levels), 1)
    chosen = jnp.where(noise_ref[...] == level, 1.0, 0.0).astype(jnp.bfloat16)
    tables = [
        jnp.dot(chosen, level_ref[:, spot], preferred_element_type=jnp.float32).astype(
            jnp.bfloat16
        )
        for spot in spots
    ]
    low = 0
    for piece in range(pieces):
        own_ref, other_ref = refs[piece], refs[pieces + piece]
        count = own_ref.shape[0]
        rows = slice(low, low + count)
        places = first + low + lax.broadcasted_iota(jnp.int32, (count, 1), 0)
        low += count
        unused, leading = clip_flags(packed_rows(place_ref, places), bounds_ref)
        picks = jnp.where(leading, 1.0, 0.0)[:, :clips].astype(jnp.bfloat16)
        shifted = [
            ref[...].astype(jnp.float32)
            + jnp.dot(picks, table, preferred_element_type=jnp.float32)
            for ref, table in zip((own_ref, other_ref), tables)
        ]
        squares = sum(jnp.sum(part * part, axis=1, keepdims=True) for part in shifted)
        factor = lax.rsqrt(squares / (2 * width) + EPS)
        for part, spot in zip(shifted, spots):
            out_ref[rows, spot] = (part * factor * gain_ref[:, spot]).astype(jnp.bfloat16)
    for copy in copies:
        copy.wait()


def normalize_rows(
    place, kept, other, bounds, noise_levels, level_table, norm_gain, w_parts, indices, group_heads
):
    rows, depth = sum(part.shape[0] for part in kept), 2 * kept[0].shape[1]
    vmem = pl.BlockSpec(memory_space=pltpu.VMEM)
    return pl.pallas_call(
        functools.partial(norm_kernel, indices, group_heads),
        in_specs=[pl.BlockSpec(memory_space=pltpu.SMEM)]
        + [vmem] * (2 * len(kept) + 4)
        + [pl.BlockSpec(memory_space=pltpu.HBM)],
        out_specs=(vmem, vmem),
        out_shape=(
            jax.ShapeDtypeStruct((rows, depth), jnp.bfloat16),
            jax.ShapeDtypeStruct((depth, 6 * len(indices) * HEAD_DIM), jnp.bfloat16),
        ),
        scratch_shapes=[pltpu.SemaphoreType.DMA((3 * len(indices), COPY_PIECES))],
        compiler_params=pltpu.CompilerParams(vmem_limit_bytes=30 * MIB),
        cost_estimate=pl.CostEstimate(flops=COST, bytes_accessed=COST, transcendentals=0),
    )(place, *kept, *other, bounds, noise_levels, level_table, norm_gain.reshape(1, -1), w_parts)


def project_kernel(upcoming, group_heads, place_ref, own_ref, pair_ref, weights_ref, w_ref, *rest):
    copies = []
    if upcoming:
        first_ref, second_ref, next_ref, sems = rest[-4:]
        copies = weight_copies(place_ref, upcoming, group_heads, w_ref, next_ref, sems)
    else:
        first_ref, second_ref = rest[-2:]
    for copy in copies:
        copy.start()
    rows = jnp.concatenate([own_ref[...], pair_ref[...]], axis=0)
    count, width = own_ref.shape[0], 6 * HEAD_DIM
    same = place_ref[4] % 2 == place_ref[8]

    def store(outcome, base, even_ref, odd_ref):
        for index, core in enumerate((place_ref[8], 1 - place_ref[8])):
            spot = pl.ds(pl.multiple_of(core * count, count), count)
            half = outcome[index * count : (index + 1) * count]
            for part in range(3):
                to = slice(base + part * HEAD_DIM, base + (part + 1) * HEAD_DIM)
                even_ref[spot, to] = half[:, 2 * part * HEAD_DIM : (2 * part + 1) * HEAD_DIM]
                odd_ref[spot, to] = half[:, (2 * part + 1) * HEAD_DIM : 2 * (part + 1) * HEAD_DIM]

    for head in range(weights_ref.shape[1] // width):
        outcome = jnp.dot(
            rows,
            weights_ref[:, head * width : (head + 1) * width],
            preferred_element_type=jnp.float32,
        ).astype(jnp.bfloat16)
        base = head * width // 2

        @pl.when(same)
        def _():
            store(outcome, base, first_ref, second_ref)

        @pl.when(jnp.logical_not(same))
        def _():
            store(outcome, base, second_ref, first_ref)

    for copy in copies:
        copy.wait()


def project_heads(place, own, pair, weights, w_parts, upcoming, group_heads, after):
    rows, depth = own.shape
    vmem, hbm = pl.BlockSpec(memory_space=pltpu.VMEM), pl.BlockSpec(memory_space=pl.ANY)
    shape = jax.ShapeDtypeStruct((2 * rows, weights.shape[1] // 2), jnp.bfloat16)
    more = len(upcoming) > 0
    return pl.pallas_call(
        functools.partial(project_kernel, upcoming, group_heads),
        in_specs=[pl.BlockSpec(memory_space=pltpu.SMEM), vmem, vmem, vmem, hbm]
        + [hbm] * len(after),
        out_specs=(vmem, vmem) + (vmem,) * more,
        out_shape=(shape, shape)
        + (jax.ShapeDtypeStruct((depth, 6 * len(upcoming) * HEAD_DIM), weights.dtype),) * more,
        scratch_shapes=[pltpu.SemaphoreType.DMA((3 * len(upcoming), COPY_PIECES))] * more,
        compiler_params=pltpu.CompilerParams(vmem_limit_bytes=30 * MIB),
        cost_estimate=pl.CostEstimate(flops=COST, bytes_accessed=COST, transcendentals=0),
    )(place, own, pair, weights, w_parts, *after)


def attend_kernel(base, place_ref, runs_ref, *refs):
    mine, near, far, pair_first, pair_far, pair_near = refs[:6]
    order_ref, query_mask_ref, key_mask_ref = refs[6:9]
    stay_ref, cross_ref, q_all, k_all, v_all, sorted_out = refs[-6:]
    chip_rows = mine.shape[0]
    rows = chip_rows // 2
    queries = sorted_out.shape[0] - 2 * rows

    def hold(sources):
        for index, source in enumerate(sources):
            spot = slice(index * chip_rows, (index + 1) * chip_rows)
            for part, held in enumerate((q_all, k_all, v_all)):
                low = base + part * HEAD_DIM
                held[spot, :HEAD_DIM] = source[:, low : low + HEAD_DIM]

    @pl.when(place_ref[8] == 0)
    def _():
        hold((mine, near, pair_near, pair_far))

    @pl.when(place_ref[8] == 1)
    def _():
        hold((pair_first, pair_near, near, far))

    q_all[:, HEAD_DIM:] = query_mask_ref[...]
    k_all[:, HEAD_DIM:] = key_mask_ref[...]
    v_all[:, HEAD_DIM:] = jnp.ones((4 * chip_rows, HEAD_DIM), jnp.bfloat16)
    tile = queries // ATTEND_TILES

    def score(step):
        wanted = step * tile + lax.broadcasted_iota(jnp.int32, (tile, 1), 0)
        picks = jnp.concatenate(
            [
                jnp.where(order_ref[line : line + 1, :] == wanted, 1.0, 0.0).astype(jnp.bfloat16)
                for line in range(order_ref.shape[0])
            ],
            axis=1,
        )
        sorted_queries = jnp.dot(picks, q_all[...], preferred_element_type=jnp.float32)
        return lax.dot_general(
            sorted_queries.astype(jnp.bfloat16),
            k_all[...],
            (((1,), (1,)), ((), ())),
            preferred_element_type=jnp.float32,
        )

    coming = score(0)
    for step in range(ATTEND_TILES):
        scores = coming
        if step + 1 < ATTEND_TILES:
            coming = score(step + 1)
        top = jnp.max(scores, axis=1, keepdims=True)
        weights = jnp.exp2((scores - top) * (HEAD_DIM ** (-0.5) * LOG2E))
        summed = jnp.dot(
            weights.astype(jnp.bfloat16), v_all[...], preferred_element_type=jnp.float32
        )
        sorted_out[rows + step * tile : rows + (step + 1) * tile, :] = (
            summed[:, :HEAD_DIM] / summed[:, HEAD_DIM:]
        )

    row = lax.broadcasted_iota(jnp.int32, (rows, 1), 0)
    for n in range(8):
        first = sorted_out[pl.ds(rows + runs_ref[3, n], rows), :]
        second = sorted_out[pl.ds(rows + runs_ref[4, n], rows), :]
        in_second = (row >= runs_ref[1, n]) & (row < runs_ref[2, n])
        taken = jnp.where(row < runs_ref[0, n], first, jnp.where(in_second, second, 0.0))
        (stay_ref, cross_ref)[n // 4][n % 4] = taken.astype(jnp.bfloat16)


def attend(place, runs, blocks, position, order, query_mask, key_mask, after):
    chip_rows = blocks[0].shape[0]
    rows, keys = chip_rows // 2, 4 * chip_rows
    queries = keys // 2 + rows // 2
    vmem, smem = pl.BlockSpec(memory_space=pltpu.VMEM), pl.BlockSpec(memory_space=pltpu.SMEM)
    shape = jax.ShapeDtypeStruct((4, rows, HEAD_DIM), jnp.bfloat16)
    return pl.pallas_call(
        functools.partial(attend_kernel, 3 * position * HEAD_DIM),
        in_specs=[smem, smem]
        + [vmem] * (len(blocks) + 3)
        + [pl.BlockSpec(memory_space=pl.ANY)] * len(after),
        out_specs=(vmem, vmem),
        out_shape=(shape, shape),
        scratch_shapes=[
            pltpu.VMEM((keys, 2 * HEAD_DIM), jnp.bfloat16),
            pltpu.VMEM((keys, 2 * HEAD_DIM), jnp.bfloat16),
            pltpu.VMEM((keys, 2 * HEAD_DIM), jnp.bfloat16),
            pltpu.VMEM((queries + 2 * rows, HEAD_DIM), jnp.float32),
        ],
        compiler_params=pltpu.CompilerParams(vmem_limit_bytes=32 * MIB),
        cost_estimate=pl.CostEstimate(
            flops=LONG_COST, bytes_accessed=COST, transcendentals=0
        ),
    )(place, runs, *blocks, order, query_mask, key_mask, *after)


def join_kernel(heads, *refs):
    outs = refs[-4:]
    for d in range(4):
        parts = [refs[2 * h][d] + refs[2 * h + 1][d] for h in range(heads)]
        outs[d][...] = jnp.concatenate(parts, axis=1)


def join_halves(stays, arrivals, after, cost):
    heads, (slots, rows, width) = len(stays), stays[0].shape
    vmem = pl.BlockSpec(memory_space=pltpu.VMEM)
    pairs = [part for both in zip(stays, arrivals) for part in both]
    shape = jax.ShapeDtypeStruct((rows, heads * width), jnp.bfloat16)
    return pl.pallas_call(
        functools.partial(join_kernel, heads),
        in_specs=[vmem] * len(pairs) + [pl.BlockSpec(memory_space=pl.ANY)] * len(after),
        out_specs=(vmem,) * slots,
        out_shape=(shape,) * slots,
        compiler_params=pltpu.CompilerParams(vmem_limit_bytes=16 * MIB),
        cost_estimate=pl.CostEstimate(flops=cost, bytes_accessed=COST, transcendentals=0),
    )(*pairs, *after)


def own_weights(place_ref, w_ref, indices, side):
    columns = w_ref.shape[1] // 2
    spot = pl.ds(pl.multiple_of(side * columns, HEAD_DIM), columns)
    heads = w_ref.shape[0] // HEAD_DIM // 4
    blocks = []
    for d in range(4):
        for index in indices:
            head = head_of(jnp.bitwise_xor(place_ref[4], d), index, heads)
            blocks.append(w_ref[pl.ds(pl.multiple_of(head * HEAD_DIM, HEAD_DIM), HEAD_DIM), spot])
    return jnp.concatenate(blocks, axis=0)


def out_first_kernel(indices, away, place_ref, *refs):
    w_ref, out_ref = refs[-2:]
    rows = jnp.concatenate([ref[...] for ref in refs[:-2]], axis=1)
    side = 1 - place_ref[6] if away else place_ref[6]
    out_ref[...] = jnp.dot(
        rows, own_weights(place_ref, w_ref, indices, side), preferred_element_type=jnp.float32
    ).astype(out_ref.dtype)


def out_rows_kernel(*refs):
    refs[-1][...] = jnp.concatenate([ref[...] for ref in refs[:-1]], axis=1)


def out_middle_kernel(indices, place_ref, total_ref, rows_ref, far_ref, w_ref, out_ref):
    weights = own_weights(place_ref, w_ref, indices, place_ref[6])
    product = jnp.dot(rows_ref[...], weights, preferred_element_type=jnp.float32)
    out_ref[...] = total_ref[...] + far_ref[...].astype(jnp.float32) + product


def out_last_kernel(place_ref, total_ref, rows_ref, held_ref, pair_ref, out_ref):
    chip = place_ref[4]

    def run(near_ref, far_ref):
        blocks = []
        for d in range(4):
            head = jnp.bitwise_xor(chip, d) % 2
            spot = pl.ds(pl.multiple_of(head * HEAD_DIM, HEAD_DIM), HEAD_DIM)
            blocks.append((near_ref if d < 2 else far_ref)[spot, :])
        product = jnp.dot(
            rows_ref[...], jnp.concatenate(blocks, axis=0), preferred_element_type=jnp.float32
        )
        out_ref[...] = (total_ref[...] + product).astype(jnp.bfloat16)

    @pl.when(chip // 2 == place_ref[8])
    def _():
        run(held_ref, pair_ref)

    @pl.when(chip // 2 != place_ref[8])
    def _():
        run(pair_ref, held_ref)


def out_call(kernel, scalars, arrays, shapes):
    vmem = pl.BlockSpec(memory_space=pltpu.VMEM)
    return pl.pallas_call(
        kernel,
        in_specs=[pl.BlockSpec(memory_space=pltpu.SMEM)] * len(scalars) + [vmem] * len(arrays),
        out_specs=(vmem,) * len(shapes),
        out_shape=tuple(jax.ShapeDtypeStruct(shape, dtype) for shape, dtype in shapes),
        compiler_params=pltpu.CompilerParams(vmem_limit_bytes=16 * MIB),
        cost_estimate=pl.CostEstimate(flops=COST, bytes_accessed=COST, transcendentals=0),
    )(*scalars, *arrays)


SWAP_ROWS = (128, 112, 80)
ATTEND_TILES = 2
HEAD_CHUNKS = ((0,), (1, 2))
COPY_PIECES = 4


def halved_body(
    inputs,
    norm_gain,
    level_table,
    w_qkv,
    w_out,
    clip_lengths,
    prefix_lengths,
    noise_levels,
    token_rank,
):
    rank_here = lax.axis_index("ctx")
    side = lax.axis_index("head")
    per_dev = inputs.shape[0]
    ranks = 16
    half_rows = 8 * per_dev
    group_heads = w_qkv.shape[2] // HEAD_DIM // 4
    clips = clip_lengths.shape[0]
    half, block, core = rank_here // 8, rank_here % 8, rank_here % 2
    chip = block // 2

    def exchange(array, flip, only=lambda r: True):
        pairs = [(r, r ^ flip) for r in range(ranks) if only(r)]
        return lax.ppermute(array, "ctx", pairs)

    index = jnp.arange(clips, dtype=jnp.int32)
    ahead = (index[None, :] < index[:, None]) & (clip_lengths == MAXCLIP)[:, None]
    start = jnp.sum(jnp.where(ahead, clip_lengths[None, :], 0))
    early = start <= half_rows // 2
    def tables(start, early, clip_lengths, prefix_lengths):
        earlier = index[None, :] < index[:, None]
        begins = jnp.sum(jnp.where(earlier, clip_lengths[None, :], 0), axis=1)
        place = jnp.stack(
            [
                start,
                early.astype(jnp.int32),
                half,
                jnp.int32(half_rows),
                chip,
                jnp.int32(clips),
                side,
                block * per_dev,
                core,
                rank_here,
            ]
        )
        ends = begins + clip_lengths
        leads = begins + jnp.minimum(prefix_lengths, clip_lengths)
        bounds = jnp.pad(jnp.stack([begins, ends, leads]), ((0, 5), (0, HEAD_DIM - clips)))
        return place, bounds

    def gather_rows(blocks):
        def run(rows, start, early, clip_lengths, prefix_lengths, noise_levels, w_out):
            place, bounds = tables(start, early, clip_lengths, prefix_lengths)
            cuts = [sum(SWAP_ROWS[:i]) for i in range(len(SWAP_ROWS) + 1)]
            cuts = list(zip(cuts[:-1], cuts[1:]))
            parts = [rows[a:b] for a, b in cuts]
            moved = [exchange(part, 8, lambda r: r % 8 in blocks) for part in parts]
            kept = []
            for part, new, (a, b) in zip(parts, moved, cuts):
                kept.append(select_rows(place, part, new, a, kept[-1:]))
            other = [lax.ppermute(part, "head", [(0, 1), (1, 0)]) for part in kept]
            columns, last = w_out.shape[1] // 2, 2 * (group_heads - 1) * HEAD_DIM
            corner = (core * w_out.shape[0] // 2 + last, (1 - side) * columns)
            sent = lax.dynamic_slice(w_out, corner, (2 * HEAD_DIM, columns))
            return tuple(kept), tuple(other), place, bounds, noise_levels.reshape(-1, 1), sent

        return run

    kept, other, place, bounds, noise_column, sent = lax.cond(
        early,
        gather_rows(range(4)),
        gather_rows(range(4, 8)),
        inputs,
        start,
        early,
        clip_lengths,
        prefix_lengths,
        noise_levels,
        w_out,
    )
    swap_sides = [(0, 1), (1, 0)]
    far_held = lax.ppermute(sent, "head", swap_sides)
    w_parts = jnp.transpose(w_qkv, (1, 0, 2))
    normed, weights = normalize_rows(
        place,
        kept,
        other,
        bounds,
        noise_column,
        level_table,
        norm_gain,
        w_parts,
        HEAD_CHUNKS[0],
        group_heads,
    )
    pair = exchange(normed, 1)
    query_order, runs, query_mask, key_mask = make_tables(
        place, bounds, token_rank, ranks, half_rows
    )

    def project(upcoming, weights, after):
        first, second, *more = project_heads(
            place, normed, pair, weights, w_parts, upcoming, group_heads, after
        )
        near = lax.ppermute(
            second, "ctx", [(r, r ^ (2 if r % 2 == 0 else 4)) for r in range(ranks)]
        )
        far = exchange(first, 6, lambda r: r % 2 == 1)
        pair_first = exchange(first, 1, lambda r: r % 2 == 0)
        return [first, near, far, pair_first], more[0] if more else None

    def share(block, after):
        first, near, far, pair_first = block
        near, far, *unused = lax.optimization_barrier((near, far, *after))
        pair_far = exchange(far, 1, lambda r: r % 2 == 1)
        return [first, near, far, pair_first, pair_far, exchange(near, 1)]

    blocks, after = [], []
    for upcoming in (*HEAD_CHUNKS[1:], ()):
        block, weights = project(upcoming, weights, after)
        blocks.append(block)
        after = [block[3]]
    stays, arrivals, after = [], [], [blocks[-1][0]]
    for block, heads in zip(blocks, HEAD_CHUNKS):
        block = share(block, after)
        for position, head in enumerate(heads):
            stay, cross = attend(
                place, runs, block, position, query_order, query_mask, key_mask, after
            )
            stays.append(stay)
            arrivals.append(exchange(cross, 8))
            after = [cross] + (arrivals[head - 1 : head] if head else [])
    far_pair = exchange(lax.optimization_barrier((far_held, cross))[0], 1)

    def to_owners(heads, after, cost):
        joined = join_halves(stays[heads], arrivals[heads], after, cost)
        return [exchange(part, 2 * d) if d else part for d, part in enumerate(joined)]

    first_heads, last_head = list(range(group_heads - 1)), [group_heads - 1]
    columns = inputs.shape[1]
    pieces = to_owners(slice(0, -1), [cross], COST)
    (away,) = out_call(
        functools.partial(out_first_kernel, first_heads, True),
        [place],
        [*pieces, w_out],
        [((per_dev, columns), jnp.bfloat16)],
    )
    first_far = lax.ppermute(away, "head", swap_sides)
    (total,) = out_call(
        functools.partial(out_first_kernel, first_heads, False),
        [place],
        [*pieces, w_out],
        [((per_dev, columns), jnp.float32)],
    )
    pieces = to_owners(slice(-1, None), [], LONG_COST)
    (last_rows,) = out_call(
        out_rows_kernel,
        [],
        pieces,
        [((per_dev, sum(piece.shape[1] for piece in pieces)), jnp.bfloat16)],
    )
    last_far = lax.ppermute(last_rows, "head", swap_sides)
    (total,) = out_call(
        functools.partial(out_middle_kernel, last_head),
        [place],
        [total, last_rows, first_far, w_out],
        [((per_dev, columns), jnp.float32)],
    )
    (attended,) = out_call(
        out_last_kernel,
        [place],
        [total, last_far, far_held, far_pair],
        [((per_dev, columns), jnp.bfloat16)],
    )
    return attended


def solution(mesh):
    in_specs = (
        P("ctx", "head"),
        P(),
        P(),
        P(None, None, "head"),
        P("head", None),
        P(),
        P(),
        P(),
        P(),
    )
    out_specs = P("ctx", "head")

    def body(inputs, norm_gain, level_table, w_qkv, *rest):
        ranks, sides = mesh.shape["ctx"], mesh.shape["head"]
        heads_here = w_qkv.shape[2] // HEAD_DIM
        halved = (
            ranks == 16
            and sides == 2
            and ranks * inputs.shape[0] == 2 * MAXCLIP
            and heads_here == 4 * sum(len(heads) for heads in HEAD_CHUNKS)
        )
        run = halved_body if halved else gathered_body
        return run(inputs, norm_gain, level_table, w_qkv, *rest)

    return jax.shard_map(body, mesh=mesh, in_specs=in_specs, out_specs=out_specs, check_vma=False)
```

```python
import functools

import jax
import jax.numpy as jnp
from jax import lax
from jax.experimental import pallas as pl
from jax.experimental.pallas import tpu as pltpu
from jax.sharding import PartitionSpec as P

HEAD_DIM = 128


NEG = -1e30
EPS = 1e-06
MAXCLIP = 2560
LOG2E = 1.4426950408889634
MIB = 1024 * 1024
COST = 1000000
LONG_COST = 200000000000


def clip_tables(total_rows, clip_lengths, prefix_lengths, noise_levels):
    rows = jnp.arange(total_rows, dtype=jnp.int32)
    ends = jnp.cumsum(clip_lengths)
    begins = ends - clip_lengths
    clip_of = jnp.sum((rows[:, None] >= ends[None, :]).astype(jnp.int32), axis=1)
    member = clip_of[:, None] == jnp.arange(clip_lengths.shape[0], dtype=jnp.int32)[None, :]
    begin_row = jnp.sum(jnp.where(member, begins[None, :], 0), axis=1)
    lead = jnp.minimum(prefix_lengths, clip_lengths)
    lead_row = jnp.sum(jnp.where(member, lead[None, :], 0), axis=1)
    level_row = jnp.sum(jnp.where(member, noise_levels[None, :], 0), axis=1)
    in_prefix = rows - begin_row < lead_row
    return (clip_of, in_prefix, level_row)


def rank_tables(token_rank, ranks, per_rank):
    onehot = (token_rank[:, None] == jnp.arange(ranks, dtype=jnp.int32)[None, :]).astype(jnp.int32)
    earlier = jnp.cumsum(onehot, axis=0) - onehot
    within = jnp.sum(earlier * onehot, axis=1)
    counts = jnp.sum(onehot.reshape(ranks, per_rank, ranks), axis=1)
    starts = jnp.cumsum(counts, axis=0) - counts
    return (within, counts, starts)


def normalize(rows, in_prefix, level_row, level_table, norm_gain):
    picks = (
        level_row[:, None] == jnp.arange(level_table.shape[0], dtype=jnp.int32)[None, :]
    ) & in_prefix[:, None]
    added = jnp.dot(picks.astype(jnp.bfloat16), level_table, preferred_element_type=jnp.float32)
    shifted = rows.astype(jnp.float32) + added
    factor = lax.rsqrt(jnp.mean(shifted * shifted, axis=-1, keepdims=True) + EPS)
    return (shifted * factor * norm_gain).astype(jnp.bfloat16)


def fold_keys(state, queries, query_clip, query_prefix, pairs, key_clip, key_prefix):
    width = queries.shape[1]
    heads_here = width // HEAD_DIM
    factor = HEAD_DIM ** (-0.5)
    allowed_query = jnp.logical_not(query_prefix)

    def absorb(carry, block):
        block_pairs, block_clip, block_prefix = block
        allowed = (query_clip[:, None] == block_clip[None, :]) & (
            allowed_query[:, None] | block_prefix[None, :]
        )
        updated = []
        for head in range(heads_here):
            top, total, summed = carry[head]
            low = head * HEAD_DIM
            q_head = queries[:, low : low + HEAD_DIM]
            k_head = block_pairs[:, low : low + HEAD_DIM]
            v_head = block_pairs[:, width + low : width + low + HEAD_DIM]
            scores = (
                lax.dot_general(
                    q_head, k_head, (((1,), (1,)), ((), ())), preferred_element_type=jnp.float32
                )
                * factor
            )
            masked = jnp.where(allowed, scores, NEG)
            new_top = jnp.maximum(top, jnp.max(masked, axis=1, keepdims=True))
            fade = jnp.exp(top - new_top)
            weights = jnp.where(allowed, jnp.exp(scores - new_top), 0.0)
            total = total * fade + jnp.sum(weights, axis=1, keepdims=True)
            summed = summed * fade + jnp.dot(
                weights.astype(jnp.bfloat16), v_head, preferred_element_type=jnp.float32
            )
            updated.append((new_top, total, summed))
        return (tuple(updated), None)

    count = pairs.shape[0]
    step = 2048 if count > 2048 and count % 2048 == 0 else count
    if step == count:
        result, unused = absorb(state, (pairs, key_clip, key_prefix))
        return result
    stacked = (
        pairs.reshape(count // step, step, pairs.shape[1]),
        key_clip.reshape(count // step, step),
        key_prefix.reshape(count // step, step),
    )
    result, unused = lax.scan(absorb, state, stacked)
    return result


def gathered_body(
    inputs,
    norm_gain,
    level_table,
    w_qkv,
    w_out,
    clip_lengths,
    prefix_lengths,
    noise_levels,
    token_rank,
):
    ranks = lax.axis_size("ctx")
    rank_here = lax.axis_index("ctx")
    per_dev = inputs.shape[0]
    slots = 2 * per_dev // ranks
    local_width = w_qkv.shape[2]
    heads_here = local_width // HEAD_DIM
    total_rows = per_dev * ranks
    clip_of, in_prefix, level_row = clip_tables(
        total_rows, clip_lengths, prefix_lengths, noise_levels
    )
    within, counts, starts = rank_tables(token_rank, ranks, per_dev)
    place = token_rank * per_dev + within
    order = (
        jnp.zeros((total_rows,), jnp.int32).at[place].set(jnp.arange(total_rows, dtype=jnp.int32))
    )
    first = rank_here * per_dev
    own_rank = lax.dynamic_slice_in_dim(token_rank, first, per_dev, 0)
    own_within = lax.dynamic_slice_in_dim(within, first, per_dev, 0)
    send_starts = lax.dynamic_slice_in_dim(starts, rank_here, 1, 0)[0]
    recv_counts = lax.dynamic_slice_in_dim(counts, rank_here, 1, 1)[:, 0]
    recv_starts = lax.dynamic_slice_in_dim(starts, rank_here, 1, 1)[:, 0]
    balanced_rows = lax.dynamic_slice_in_dim(order, first, per_dev, 0)
    target = own_rank * slots + own_within - send_starts[own_rank]
    buffer = jnp.zeros((ranks * slots, inputs.shape[1]), inputs.dtype).at[target].set(inputs)
    received = lax.all_to_all(
        buffer.reshape(ranks, slots, inputs.shape[1]),
        "ctx",
        split_axis=0,
        concat_axis=0,
        tiled=True,
    )
    spots = jnp.arange(slots, dtype=jnp.int32)[None, :]
    index = jnp.where(spots < recv_counts[:, None], recv_starts[:, None] + spots, per_dev).reshape(
        -1
    )
    flat = received.reshape(ranks * slots, received.shape[2])
    rows = jnp.zeros((per_dev, received.shape[2]), received.dtype).at[index].set(flat, mode="drop")
    full_rows = lax.all_gather(rows, "head", axis=1, tiled=True)
    normed = normalize(
        full_rows, in_prefix[balanced_rows], level_row[balanced_rows], level_table, norm_gain
    )
    qkv = jnp.dot(
        normed, w_qkv.reshape(w_qkv.shape[0], 3 * local_width), preferred_element_type=jnp.float32
    ).astype(jnp.bfloat16)
    start_state = tuple(
        (
            (
                jnp.full((per_dev, 1), NEG, jnp.float32),
                jnp.zeros((per_dev, 1), jnp.float32),
                jnp.zeros((per_dev, HEAD_DIM), jnp.float32),
            )
            for head in range(heads_here)
        )
    )
    key_clip = clip_of[order]
    key_prefix = in_prefix[order]
    query_clip = lax.dynamic_slice_in_dim(key_clip, first, per_dev, 0)
    query_prefix = lax.dynamic_slice_in_dim(key_prefix, first, per_dev, 0)
    queries = qkv[:, :local_width]
    pairs = qkv[:, local_width:]
    state = fold_keys(
        start_state,
        queries,
        query_clip,
        query_prefix,
        lax.all_gather(pairs, "ctx", axis=0, tiled=True),
        key_clip,
        key_prefix,
    )
    parts = [state[head][2] / state[head][1] for head in range(heads_here)]
    attention = jnp.concatenate(parts, axis=1).astype(jnp.bfloat16)
    terms = jnp.dot(attention, w_out, preferred_element_type=jnp.float32)
    return lax.psum_scatter(terms.astype(jnp.bfloat16), "head", scatter_dimension=1, tiled=True)


def packed_rows(place_ref, spots):
    start, early, half = place_ref[0], place_ref[1], place_ref[2]
    total = place_ref[3]
    before = jnp.where(spots < start, early, 1 - early)
    return spots + total * (half + before * (1 - 2 * half))


def clip_flags(rows, bounds_ref):
    begins, ends, leads = bounds_ref[0:1, :], bounds_ref[1:2, :], bounds_ref[2:3, :]
    inside = (rows >= begins) & (rows < ends)
    return inside, inside & (rows < leads)


def count_earlier(hot):
    ranks, rows, lanes = hot.shape
    flat = hot.reshape(ranks * rows, lanes).astype(jnp.bfloat16)

    def numbers(shape, axis):
        return lax.broadcasted_iota(jnp.int32, shape, axis)

    def group(index):
        return sum(jnp.where(index >= rows * k, 1, 0) for k in range(1, ranks))

    def ones(flags):
        return jnp.where(flags, 1.0, 0.0).astype(jnp.bfloat16)

    total = ranks * rows
    in_row = ones(numbers((lanes, lanes), 0) < numbers((lanes, lanes), 1))
    below, across = numbers((total, 1), 0), numbers((1, total), 1)
    in_rank = ones((group(below) == group(across)) & (across < below))
    row_sums = jnp.dot(
        flat, jnp.ones((lanes, lanes), jnp.bfloat16), preferred_element_type=jnp.float32
    )
    earlier = jnp.dot(flat, in_row, preferred_element_type=jnp.float32) + jnp.dot(
        in_rank, row_sums.astype(jnp.bfloat16), preferred_element_type=jnp.float32
    )
    return earlier.reshape(ranks, rows, lanes)


def table_kernel(ranks, place_ref, bounds_ref, rank_ref, *refs):
    order_ref, runs_ref, query_ref, key_ref, held = refs
    start, early, half, half_rows = (place_ref[k] for k in range(4))
    chip, clips, core, rank_here = (place_ref[k] for k in (4, 5, 8, 9))
    holds_long = half != early
    tokens = rank_ref[...]
    rows, lanes = tokens.shape
    per_dev = rows * lanes // ranks

    token = lanes * lax.broadcasted_iota(jnp.int32, tokens.shape, 0) + lax.broadcasted_iota(
        jnp.int32, tokens.shape, 1
    )
    hots = [jnp.where(tokens == rank, 1.0, 0.0) for rank in range(ranks)]
    earlier = count_earlier(jnp.stack(hots))
    within = sum(hots[rank] * earlier[rank] for rank in range(ranks))
    before = jnp.where(token < start, 1.0, 0.0)
    upto = jnp.where(token < start + half_rows, 1.0, 0.0)
    target = jnp.bitwise_xor(rank_here, 2 * lax.broadcasted_iota(jnp.int32, (1, lanes), 1))
    long_first, rest_first = [0.0, 0.0], [0.0, 0.0]
    long_base = rest_base = low_of = long_of = 0.0
    runs = [0.0] * 5
    for rank, hot in enumerate(hots):
        low = jnp.sum(hot * before, keepdims=True)
        high = jnp.sum(hot * upto, keepdims=True)
        parity = rank % 2
        first, rest = long_first[parity], rest_first[parity]
        long_base += hot * (first - low)
        rest_base += hot * rest
        low_of += hot * low
        long_of += hot * (high - low)
        here = jnp.where(target == rank, 1.0, 0.0)
        values = (
            jnp.where(holds_long, 0.0, low),
            jnp.where(holds_long, low, high),
            jnp.where(holds_long, high, float(per_dev)),
            jnp.where(holds_long, 0.0, rest),
            jnp.where(holds_long, first - low, rest - (high - low)),
        )
        runs = [run + here * value for run, value in zip(runs, values)]
        long_first[parity] = first + (high - low)
        rest_first[parity] = rest + (per_dev - (high - low))
    furthest = rows * lanes // 4 + per_dev // 2
    for index, run in enumerate(runs):
        run = run.astype(jnp.int32)
        runs_ref[index : index + 1, :] = (
            run if index < 3 else jnp.clip(run, -per_dev, furthest)
        )
    sorted_at = within + jnp.where(
        upto - before == 1.0, long_base, rest_base - jnp.where(within < low_of, 0.0, long_of)
    )
    held[...] = jnp.where(jnp.bitwise_and(tokens, 1) == core, sorted_at.astype(jnp.int32), -1)
    half_lines = rows // 2
    spots = lanes * lax.broadcasted_iota(
        jnp.int32, (half_lines, lanes), 0
    ) + lax.broadcasted_iota(jnp.int32, (half_lines, lanes), 1)
    later = packed_rows(place_ref, spots) >= half_rows
    held[:half_lines, :] = jnp.where(later, held[half_lines:, :], held[:half_lines, :])
    lines = half_lines // 4
    for d in range(4):
        line = lines * jnp.bitwise_xor(chip, d)
        order_ref[lines * d : lines * (d + 1), :] = held[pl.ds(line, lines), :]

    column = lax.broadcasted_iota(jnp.int32, (1, HEAD_DIM), 1)
    chip_rows = query_ref.shape[0] // 4
    for d in range(4):
        local = lax.broadcasted_iota(jnp.int32, (chip_rows, 1), 0)
        spots = chip_rows * jnp.bitwise_xor(chip, d) + local
        inside, leading = clip_flags(packed_rows(place_ref, spots), bounds_ref)
        spot = slice(d * chip_rows, (d + 1) * chip_rows)
        inside = jnp.where(inside, 1.0, 0.0)
        prefix = jnp.sum(jnp.where(leading, 1.0, 0.0), axis=1, keepdims=True)
        query_ref[spot, :] = jnp.where(column == clips, prefix, inside).astype(jnp.bfloat16)
        outside = jnp.where(column < clips, NEG * (1.0 - inside), 0.0)
        key_ref[spot, :] = jnp.where(column == clips, NEG * (1.0 - prefix), outside).astype(
            jnp.bfloat16
        )


def make_tables(place, bounds, token_rank, ranks, keys):
    vmem = pl.BlockSpec(memory_space=pltpu.VMEM)
    tokens = token_rank.reshape(-1, HEAD_DIM)
    features = jax.ShapeDtypeStruct((keys, HEAD_DIM), jnp.bfloat16)
    return pl.pallas_call(
        functools.partial(table_kernel, ranks),
        in_specs=[pl.BlockSpec(memory_space=pltpu.SMEM), vmem, vmem],
        out_specs=(vmem,) * 4,
        out_shape=(
            jax.ShapeDtypeStruct((tokens.shape[0] // 2, HEAD_DIM), jnp.int32),
            jax.ShapeDtypeStruct((8, HEAD_DIM), jnp.int32),
            features,
            features,
        ),
        scratch_shapes=[pltpu.VMEM(tokens.shape, jnp.int32)],
        compiler_params=pltpu.CompilerParams(vmem_limit_bytes=26 * MIB),
        cost_estimate=pl.CostEstimate(flops=COST, bytes_accessed=COST, transcendentals=0),
    )(place, bounds, tokens)


def select_kernel(low, place_ref, own_ref, moved_ref, *rest):
    out_ref = rest[-1]
    spots = place_ref[7] + low + lax.broadcasted_iota(jnp.int32, (out_ref.shape[0], 1), 0)
    swapped = jnp.where(spots < place_ref[0], place_ref[1], 1 - place_ref[1])
    out_ref[...] = jnp.where(swapped == 1, moved_ref[...], own_ref[...])


def select_rows(place, own, moved, low, after):
    vmem = pl.BlockSpec(memory_space=pltpu.VMEM)
    return pl.pallas_call(
        functools.partial(select_kernel, low),
        in_specs=[pl.BlockSpec(memory_space=pltpu.SMEM), vmem, vmem]
        + [pl.BlockSpec(memory_space=pl.ANY)] * len(after),
        out_specs=vmem,
        out_shape=jax.ShapeDtypeStruct(moved.shape, moved.dtype),
        compiler_params=pltpu.CompilerParams(vmem_limit_bytes=8 * MIB),
        cost_estimate=pl.CostEstimate(flops=COST, bytes_accessed=COST, transcendentals=0),
    )(place, own, moved, *after)


def head_of(chip, index, group_heads):
    return 2 * group_heads * (chip // 2) + 2 * index + chip % 2


def weight_copies(place_ref, w_ref, out_ref, sems):
    columns = out_ref.shape[2]
    pair = jnp.bitwise_xor(place_ref[4] // 2, place_ref[8])
    spot = pl.ds(pl.multiple_of(pair * columns, HEAD_DIM), columns)
    depth = out_ref.shape[1] // COPY_PIECES
    copies = []
    for part in range(3):
        for piece in range(COPY_PIECES):
            rows = slice(piece * depth, (piece + 1) * depth)
            copies.append(
                pltpu.make_async_copy(
                    w_ref.at[part, rows, spot], out_ref.at[part, rows, :], sems.at[part, piece]
                )
            )
    return copies


def norm_kernel(place_ref, *refs):
    pieces = (len(refs) - 8) // 2
    bounds_ref, noise_ref, level_ref, gain_ref, w_ref, out_ref, next_ref, sems = refs[-8:]
    copies = weight_copies(place_ref, w_ref, next_ref, sems)
    for copy in copies:
        copy.start()
    width = out_ref.shape[1] // 2
    side, first = place_ref[6], place_ref[7]
    clips, levels = noise_ref.shape[0], level_ref.shape[0]
    spots = [pl.ds(pl.multiple_of(s * width, 128), width) for s in (side, 1 - side)]
    level = lax.broadcasted_iota(jnp.int32, (clips, levels), 1)
    chosen = jnp.where(noise_ref[...] == level, 1.0, 0.0).astype(jnp.bfloat16)
    tables = [
        jnp.dot(chosen, level_ref[:, spot], preferred_element_type=jnp.float32).astype(
            jnp.bfloat16
        )
        for spot in spots
    ]
    low = 0
    for piece in range(pieces):
        own_ref, other_ref = refs[piece], refs[pieces + piece]
        count = own_ref.shape[0]
        rows = slice(low, low + count)
        places = first + low + lax.broadcasted_iota(jnp.int32, (count, 1), 0)
        low += count
        unused, leading = clip_flags(packed_rows(place_ref, places), bounds_ref)
        picks = jnp.where(leading, 1.0, 0.0)[:, :clips].astype(jnp.bfloat16)
        shifted = [
            ref[...].astype(jnp.float32)
            + jnp.dot(picks, table, preferred_element_type=jnp.float32)
            for ref, table in zip((own_ref, other_ref), tables)
        ]
        squares = sum(jnp.sum(part * part, axis=1, keepdims=True) for part in shifted)
        factor = lax.rsqrt(squares / (2 * width) + EPS)
        for part, spot in zip(shifted, spots):
            out_ref[rows, spot] = (part * factor * gain_ref[:, spot]).astype(jnp.bfloat16)
    for copy in copies:
        copy.wait()


def normalize_rows(
    place, kept, other, bounds, noise_levels, level_table, norm_gain, w_parts
):
    rows, depth = sum(part.shape[0] for part in kept), 2 * kept[0].shape[1]
    vmem = pl.BlockSpec(memory_space=pltpu.VMEM)
    return pl.pallas_call(
        norm_kernel,
        in_specs=[pl.BlockSpec(memory_space=pltpu.SMEM)]
        + [vmem] * (2 * len(kept) + 4)
        + [pl.BlockSpec(memory_space=pltpu.HBM)],
        out_specs=(vmem, vmem),
        out_shape=(
            jax.ShapeDtypeStruct((rows, depth), jnp.bfloat16),
            jax.ShapeDtypeStruct((3, depth, w_parts.shape[2] // 2), jnp.bfloat16),
        ),
        scratch_shapes=[pltpu.SemaphoreType.DMA((3, COPY_PIECES))],
        compiler_params=pltpu.CompilerParams(vmem_limit_bytes=26 * MIB),
        cost_estimate=pl.CostEstimate(flops=COST, bytes_accessed=COST, transcendentals=0),
    )(place, *kept, *other, bounds, noise_levels, level_table, norm_gain.reshape(1, -1), w_parts)


def project_kernel(indices, place_ref, own_ref, pair_ref, weights_ref, *rest):
    first_ref, second_ref = rest[-2:]
    rows = jnp.concatenate([own_ref[...], pair_ref[...]], axis=0)
    count = own_ref.shape[0]
    same = place_ref[4] % 2 == place_ref[8]

    def store(outcome, base, even_ref, odd_ref):
        for index, core in enumerate((place_ref[8], 1 - place_ref[8])):
            spot = pl.ds(pl.multiple_of(core * count, count), count)
            half = outcome[index * count : (index + 1) * count]
            for part in range(3):
                to = slice(base + part * HEAD_DIM, base + (part + 1) * HEAD_DIM)
                even_ref[spot, to] = half[:, 2 * part * HEAD_DIM : (2 * part + 1) * HEAD_DIM]
                odd_ref[spot, to] = half[:, (2 * part + 1) * HEAD_DIM : 2 * (part + 1) * HEAD_DIM]

    for position, index in enumerate(indices):
        spot = slice(2 * index * HEAD_DIM, 2 * (index + 1) * HEAD_DIM)
        weights = jnp.concatenate([weights_ref[part, :, spot] for part in range(3)], axis=1)
        outcome = jnp.dot(rows, weights, preferred_element_type=jnp.float32).astype(jnp.bfloat16)
        base = 3 * position * HEAD_DIM

        @pl.when(same)
        def _():
            store(outcome, base, first_ref, second_ref)

        @pl.when(jnp.logical_not(same))
        def _():
            store(outcome, base, second_ref, first_ref)


def project_heads(place, own, pair, weights, indices, after):
    rows = own.shape[0]
    vmem = pl.BlockSpec(memory_space=pltpu.VMEM)
    shape = jax.ShapeDtypeStruct((2 * rows, 3 * len(indices) * HEAD_DIM), jnp.bfloat16)
    return pl.pallas_call(
        functools.partial(project_kernel, indices),
        in_specs=[pl.BlockSpec(memory_space=pltpu.SMEM), vmem, vmem, vmem]
        + [pl.BlockSpec(memory_space=pl.ANY)] * len(after),
        out_specs=(vmem, vmem),
        out_shape=(shape, shape),
        compiler_params=pltpu.CompilerParams(vmem_limit_bytes=26 * MIB),
        cost_estimate=pl.CostEstimate(flops=COST, bytes_accessed=COST, transcendentals=0),
    )(place, own, pair, weights, *after)


def attend_kernel(base, place_ref, runs_ref, *refs):
    mine, near, far, pair_first, pair_far, pair_near = refs[:6]
    order_ref, query_mask_ref, key_mask_ref = refs[6:9]
    stay_ref, cross_ref, q_all, k_all, v_all, sorted_out = refs[-6:]
    chip_rows = mine.shape[0]
    rows = chip_rows // 2
    queries = sorted_out.shape[0] - 2 * rows

    def hold(sources):
        for index, source in enumerate(sources):
            spot = slice(index * chip_rows, (index + 1) * chip_rows)
            for part, held in enumerate((q_all, k_all, v_all)):
                low = base + part * HEAD_DIM
                held[spot, :HEAD_DIM] = source[:, low : low + HEAD_DIM]

    @pl.when(place_ref[8] == 0)
    def _():
        hold((mine, near, pair_near, pair_far))

    @pl.when(place_ref[8] == 1)
    def _():
        hold((pair_first, pair_near, near, far))

    q_all[:, HEAD_DIM:] = query_mask_ref[...]
    k_all[:, HEAD_DIM:] = key_mask_ref[...]
    v_all[:, HEAD_DIM:] = jnp.ones((4 * chip_rows, HEAD_DIM), jnp.bfloat16)
    tile = queries // ATTEND_TILES

    def score(step):
        wanted = step * tile + lax.broadcasted_iota(jnp.int32, (tile, 1), 0)
        picks = jnp.concatenate(
            [
                jnp.where(order_ref[line : line + 1, :] == wanted, 1.0, 0.0).astype(jnp.bfloat16)
                for line in range(order_ref.shape[0])
            ],
            axis=1,
        )
        sorted_queries = jnp.dot(picks, q_all[...], preferred_element_type=jnp.float32)
        return lax.dot_general(
            sorted_queries.astype(jnp.bfloat16),
            k_all[...],
            (((1,), (1,)), ((), ())),
            preferred_element_type=jnp.float32,
        )

    coming = score(0)
    for step in range(ATTEND_TILES):
        scores = coming
        if step + 1 < ATTEND_TILES:
            coming = score(step + 1)
        top = jnp.max(scores, axis=1, keepdims=True)
        weights = jnp.exp2((scores - top) * (HEAD_DIM ** (-0.5) * LOG2E))
        summed = jnp.dot(
            weights.astype(jnp.bfloat16), v_all[...], preferred_element_type=jnp.float32
        )
        sorted_out[rows + step * tile : rows + (step + 1) * tile, :] = (
            summed[:, :HEAD_DIM] / summed[:, HEAD_DIM:]
        )

    row = lax.broadcasted_iota(jnp.int32, (rows, 1), 0)
    for n in range(8):
        first = sorted_out[pl.ds(rows + runs_ref[3, n], rows), :]
        second = sorted_out[pl.ds(rows + runs_ref[4, n], rows), :]
        in_second = (row >= runs_ref[1, n]) & (row < runs_ref[2, n])
        taken = jnp.where(row < runs_ref[0, n], first, jnp.where(in_second, second, 0.0))
        (stay_ref, cross_ref)[n // 4][n % 4] = taken.astype(jnp.bfloat16)


def attend(place, runs, blocks, position, order, query_mask, key_mask, after):
    chip_rows = blocks[0].shape[0]
    rows, keys = chip_rows // 2, 4 * chip_rows
    queries = keys // 2 + rows // 2
    vmem, smem = pl.BlockSpec(memory_space=pltpu.VMEM), pl.BlockSpec(memory_space=pltpu.SMEM)
    shape = jax.ShapeDtypeStruct((4, rows, HEAD_DIM), jnp.bfloat16)
    return pl.pallas_call(
        functools.partial(attend_kernel, 3 * position * HEAD_DIM),
        in_specs=[smem, smem]
        + [vmem] * (len(blocks) + 3)
        + [pl.BlockSpec(memory_space=pl.ANY)] * len(after),
        out_specs=(vmem, vmem),
        out_shape=(shape, shape),
        scratch_shapes=[
            pltpu.VMEM((keys, 2 * HEAD_DIM), jnp.bfloat16),
            pltpu.VMEM((keys, 2 * HEAD_DIM), jnp.bfloat16),
            pltpu.VMEM((keys, 2 * HEAD_DIM), jnp.bfloat16),
            pltpu.VMEM((queries + 2 * rows, HEAD_DIM), jnp.float32),
        ],
        compiler_params=pltpu.CompilerParams(vmem_limit_bytes=32 * MIB),
        cost_estimate=pl.CostEstimate(
            flops=COST, bytes_accessed=COST, transcendentals=0
        ),
    )(place, runs, *blocks, order, query_mask, key_mask, *after)


def join_kernel(heads, *refs):
    outs = refs[-4:]
    for d in range(4):
        parts = [refs[2 * h][d] + refs[2 * h + 1][d] for h in range(heads)]
        outs[d][...] = jnp.concatenate(parts, axis=1)


def join_halves(stays, arrivals, after, cost):
    heads, (slots, rows, width) = len(stays), stays[0].shape
    vmem = pl.BlockSpec(memory_space=pltpu.VMEM)
    pairs = [part for both in zip(stays, arrivals) for part in both]
    shape = jax.ShapeDtypeStruct((rows, heads * width), jnp.bfloat16)
    return pl.pallas_call(
        functools.partial(join_kernel, heads),
        in_specs=[vmem] * len(pairs) + [pl.BlockSpec(memory_space=pl.ANY)] * len(after),
        out_specs=(vmem,) * slots,
        out_shape=(shape,) * slots,
        compiler_params=pltpu.CompilerParams(vmem_limit_bytes=16 * MIB),
        cost_estimate=pl.CostEstimate(flops=cost, bytes_accessed=COST, transcendentals=0),
    )(*pairs, *after)


def own_weights(place_ref, w_ref, indices):
    columns = w_ref.shape[1] // 2
    spot = pl.ds(pl.multiple_of(place_ref[6] * columns, HEAD_DIM), columns)
    heads = w_ref.shape[0] // HEAD_DIM // 4
    blocks = []
    for d in range(4):
        for index in indices:
            head = head_of(jnp.bitwise_xor(place_ref[4], d), index, heads)
            blocks.append(w_ref[pl.ds(pl.multiple_of(head * HEAD_DIM, HEAD_DIM), HEAD_DIM), spot])
    return jnp.concatenate(blocks, axis=0)


def add_far_product(place_ref, rows_ref, held_ref, pair_ref, indices, store):
    chip = place_ref[4]

    def run(near_ref, far_ref):
        blocks = []
        for d in range(4):
            for index in indices:
                head = 2 * index + jnp.bitwise_xor(chip, d) % 2
                spot = pl.ds(pl.multiple_of(head * HEAD_DIM, HEAD_DIM), HEAD_DIM)
                blocks.append((near_ref if d < 2 else far_ref)[spot, :])
        weights = jnp.concatenate(blocks, axis=0)
        store(jnp.dot(rows_ref[...], weights, preferred_element_type=jnp.float32))

    @pl.when(chip // 2 == place_ref[8])
    def _():
        run(held_ref, pair_ref)

    @pl.when(chip // 2 != place_ref[8])
    def _():
        run(pair_ref, held_ref)


def out_rows_kernel(*refs):
    refs[-1][...] = jnp.concatenate([ref[...] for ref in refs[:-1]], axis=1)


def out_own_kernel(indices, place_ref, *refs):
    w_ref, out_ref = refs[-2:]
    product = jnp.dot(
        refs[0][...], own_weights(place_ref, w_ref, indices), preferred_element_type=jnp.float32
    )
    out_ref[...] = product if len(refs) == 3 else refs[1][...] + product


def out_far_kernel(indices, place_ref, total_ref, rows_ref, held_ref, pair_ref, out_ref):
    def store(product):
        out_ref[...] = (total_ref[...] + product).astype(out_ref.dtype)

    add_far_product(place_ref, rows_ref, held_ref, pair_ref, indices, store)


def out_call(kernel, scalars, arrays, shapes):
    vmem = pl.BlockSpec(memory_space=pltpu.VMEM)
    return pl.pallas_call(
        kernel,
        in_specs=[pl.BlockSpec(memory_space=pltpu.SMEM)] * len(scalars) + [vmem] * len(arrays),
        out_specs=(vmem,) * len(shapes),
        out_shape=tuple(jax.ShapeDtypeStruct(shape, dtype) for shape, dtype in shapes),
        compiler_params=pltpu.CompilerParams(vmem_limit_bytes=16 * MIB),
        cost_estimate=pl.CostEstimate(flops=COST, bytes_accessed=COST, transcendentals=0),
    )(*scalars, *arrays)


SWAP_ROWS = (128, 112, 80)
ATTEND_TILES = 3
HEAD_CHUNKS = ((0,), (1, 2))
COPY_PIECES = 4


def halved_body(
    inputs,
    norm_gain,
    level_table,
    w_qkv,
    w_out,
    clip_lengths,
    prefix_lengths,
    noise_levels,
    token_rank,
):
    rank_here = lax.axis_index("ctx")
    side = lax.axis_index("head")
    per_dev = inputs.shape[0]
    ranks = 16
    half_rows = 8 * per_dev
    group_heads = w_qkv.shape[2] // HEAD_DIM // 4
    clips = clip_lengths.shape[0]
    half, block, core = rank_here // 8, rank_here % 8, rank_here % 2
    chip = block // 2

    def exchange(array, flip, only=lambda r: True):
        pairs = [(r, r ^ flip) for r in range(ranks) if only(r)]
        return lax.ppermute(array, "ctx", pairs)

    index = jnp.arange(clips, dtype=jnp.int32)
    ahead = (index[None, :] < index[:, None]) & (clip_lengths == MAXCLIP)[:, None]
    start = jnp.sum(jnp.where(ahead, clip_lengths[None, :], 0))
    early = start <= half_rows // 2
    def tables(start, early, clip_lengths, prefix_lengths):
        earlier = index[None, :] < index[:, None]
        begins = jnp.sum(jnp.where(earlier, clip_lengths[None, :], 0), axis=1)
        place = jnp.stack(
            [
                start,
                early.astype(jnp.int32),
                half,
                jnp.int32(half_rows),
                chip,
                jnp.int32(clips),
                side,
                block * per_dev,
                core,
                rank_here,
            ]
        )
        ends = begins + clip_lengths
        leads = begins + jnp.minimum(prefix_lengths, clip_lengths)
        bounds = jnp.pad(jnp.stack([begins, ends, leads]), ((0, 5), (0, HEAD_DIM - clips)))
        return place, bounds

    def gather_rows(blocks):
        def run(rows, start, early, clip_lengths, prefix_lengths, noise_levels, w_out):
            place, bounds = tables(start, early, clip_lengths, prefix_lengths)
            cuts = [sum(SWAP_ROWS[:i]) for i in range(len(SWAP_ROWS) + 1)]
            cuts = list(zip(cuts[:-1], cuts[1:]))
            parts = [rows[a:b] for a, b in cuts]
            moved = [exchange(part, 8, lambda r: r % 8 in blocks) for part in parts]
            kept = []
            for part, new, (a, b) in zip(parts, moved, cuts):
                kept.append(select_rows(place, part, new, a, kept[-1:]))
            other = [lax.ppermute(part, "head", [(0, 1), (1, 0)]) for part in kept]
            depth, columns = w_out.shape[0] // 2, w_out.shape[1] // 2
            sent = lax.dynamic_slice(
                w_out, (core * depth, (1 - side) * columns), (depth, columns)
            )
            return tuple(kept), tuple(other), place, bounds, noise_levels.reshape(-1, 1), sent

        return run

    kept, other, place, bounds, noise_column, sent = lax.cond(
        early,
        gather_rows(range(4)),
        gather_rows(range(4, 8)),
        inputs,
        start,
        early,
        clip_lengths,
        prefix_lengths,
        noise_levels,
        w_out,
    )
    swap_sides = [(0, 1), (1, 0)]
    far_held = lax.ppermute(sent, "head", swap_sides)
    w_parts = jnp.transpose(w_qkv, (1, 0, 2))
    normed, weights = normalize_rows(
        place,
        kept,
        other,
        bounds,
        noise_column,
        level_table,
        norm_gain,
        w_parts,
    )
    pair = exchange(normed, 1)
    query_order, runs, query_mask, key_mask = make_tables(
        place, bounds, token_rank, ranks, half_rows
    )

    def project(indices, after):
        first, second = project_heads(place, normed, pair, weights, indices, after)
        near = lax.ppermute(
            second, "ctx", [(r, r ^ (2 if r % 2 == 0 else 4)) for r in range(ranks)]
        )
        far = exchange(first, 6, lambda r: r % 2 == 1)
        pair_first = exchange(first, 1, lambda r: r % 2 == 0)
        return [first, near, far, pair_first]

    def share(block, after):
        first, near, far, pair_first = block
        near, far, *unused = lax.optimization_barrier((near, far, *after))
        pair_far = exchange(far, 1, lambda r: r % 2 == 1)
        return [first, near, far, pair_first, pair_far, exchange(near, 1)]

    blocks, after = [], []
    for heads in HEAD_CHUNKS:
        blocks.append(project(heads, after))
        after = [blocks[-1][3]]
    stays, arrivals, after = [], [], [blocks[-1][0]]
    for block, heads in zip(blocks, HEAD_CHUNKS):
        block = share(block, after)
        for position, head in enumerate(heads):
            stay, cross = attend(
                place, runs, block, position, query_order, query_mask, key_mask, after
            )
            stays.append(stay)
            arrivals.append(exchange(cross, 8))
            after = [cross] + (arrivals[head - 1 : head] if head else [])

    def to_owners(heads, after, cost):
        joined = join_halves(stays[heads], arrivals[heads], after, cost)
        return [exchange(part, 2 * d) if d else part for d, part in enumerate(joined)]

    first_heads, last_head = list(range(group_heads - 1)), [group_heads - 1]
    columns = inputs.shape[1]

    def across(heads, after, cost):
        pieces = to_owners(heads, after, cost)
        width = sum(piece.shape[1] for piece in pieces)
        (rows,) = out_call(out_rows_kernel, [], pieces, [((per_dev, width), jnp.bfloat16)])
        return rows, lax.ppermute(rows, "head", swap_sides)

    def add(kernel, heads, arrays, dtype=jnp.float32):
        (total,) = out_call(
            functools.partial(kernel, heads), [place], arrays, [((per_dev, columns), dtype)]
        )
        return total

    rows, far_rows = across(slice(0, -1), [cross], COST)
    far_pair = exchange(lax.optimization_barrier((far_held, rows))[0], 1)
    total = add(out_own_kernel, first_heads, [rows, w_out])
    last_rows, last_far = across(slice(-1, None), [], LONG_COST)
    total = add(out_own_kernel, last_head, [last_rows, total, w_out])
    total = add(out_far_kernel, first_heads, [total, far_rows, far_held, far_pair])
    return add(out_far_kernel, last_head, [total, last_far, far_held, far_pair], jnp.bfloat16)


def solution(mesh):
    in_specs = (
        P("ctx", "head"),
        P(),
        P(),
        P(None, None, "head"),
        P("head", None),
        P(),
        P(),
        P(),
        P(),
    )
    out_specs = P("ctx", "head")

    def body(inputs, norm_gain, level_table, w_qkv, *rest):
        ranks, sides = mesh.shape["ctx"], mesh.shape["head"]
        heads_here = w_qkv.shape[2] // HEAD_DIM
        halved = (
            ranks == 16
            and sides == 2
            and ranks * inputs.shape[0] == 2 * MAXCLIP
            and heads_here == 4 * sum(len(heads) for heads in HEAD_CHUNKS)
        )
        run = halved_body if halved else gathered_body
        return run(inputs, norm_gain, level_table, w_qkv, *rest)

    return jax.shard_map(body, mesh=mesh, in_specs=in_specs, out_specs=out_specs, check_vma=False)
```

```python
import functools

import jax
import jax.numpy as jnp
from jax import lax
from jax.experimental import pallas as pl
from jax.experimental.pallas import tpu as pltpu
from jax.sharding import PartitionSpec as P

HEAD_DIM = 128


NEG = -1e30
EPS = 1e-06
MAXCLIP = 2560
LOG2E = 1.4426950408889634
MIB = 1024 * 1024
COST = 1000000
LONG_COST = 200000000000


def clip_tables(total_rows, clip_lengths, prefix_lengths, noise_levels):
    rows = jnp.arange(total_rows, dtype=jnp.int32)
    ends = jnp.cumsum(clip_lengths)
    begins = ends - clip_lengths
    clip_of = jnp.sum((rows[:, None] >= ends[None, :]).astype(jnp.int32), axis=1)
    member = clip_of[:, None] == jnp.arange(clip_lengths.shape[0], dtype=jnp.int32)[None, :]
    begin_row = jnp.sum(jnp.where(member, begins[None, :], 0), axis=1)
    lead = jnp.minimum(prefix_lengths, clip_lengths)
    lead_row = jnp.sum(jnp.where(member, lead[None, :], 0), axis=1)
    level_row = jnp.sum(jnp.where(member, noise_levels[None, :], 0), axis=1)
    in_prefix = rows - begin_row < lead_row
    return (clip_of, in_prefix, level_row)


def rank_tables(token_rank, ranks, per_rank):
    onehot = (token_rank[:, None] == jnp.arange(ranks, dtype=jnp.int32)[None, :]).astype(jnp.int32)
    earlier = jnp.cumsum(onehot, axis=0) - onehot
    within = jnp.sum(earlier * onehot, axis=1)
    counts = jnp.sum(onehot.reshape(ranks, per_rank, ranks), axis=1)
    starts = jnp.cumsum(counts, axis=0) - counts
    return (within, counts, starts)


def normalize(rows, in_prefix, level_row, level_table, norm_gain):
    picks = (
        level_row[:, None] == jnp.arange(level_table.shape[0], dtype=jnp.int32)[None, :]
    ) & in_prefix[:, None]
    added = jnp.dot(picks.astype(jnp.bfloat16), level_table, preferred_element_type=jnp.float32)
    shifted = rows.astype(jnp.float32) + added
    factor = lax.rsqrt(jnp.mean(shifted * shifted, axis=-1, keepdims=True) + EPS)
    return (shifted * factor * norm_gain).astype(jnp.bfloat16)


def fold_keys(state, queries, query_clip, query_prefix, pairs, key_clip, key_prefix):
    width = queries.shape[1]
    heads_here = width // HEAD_DIM
    factor = HEAD_DIM ** (-0.5)
    allowed_query = jnp.logical_not(query_prefix)

    def absorb(carry, block):
        block_pairs, block_clip, block_prefix = block
        allowed = (query_clip[:, None] == block_clip[None, :]) & (
            allowed_query[:, None] | block_prefix[None, :]
        )
        updated = []
        for head in range(heads_here):
            top, total, summed = carry[head]
            low = head * HEAD_DIM
            q_head = queries[:, low : low + HEAD_DIM]
            k_head = block_pairs[:, low : low + HEAD_DIM]
            v_head = block_pairs[:, width + low : width + low + HEAD_DIM]
            scores = (
                lax.dot_general(
                    q_head, k_head, (((1,), (1,)), ((), ())), preferred_element_type=jnp.float32
                )
                * factor
            )
            masked = jnp.where(allowed, scores, NEG)
            new_top = jnp.maximum(top, jnp.max(masked, axis=1, keepdims=True))
            fade = jnp.exp(top - new_top)
            weights = jnp.where(allowed, jnp.exp(scores - new_top), 0.0)
            total = total * fade + jnp.sum(weights, axis=1, keepdims=True)
            summed = summed * fade + jnp.dot(
                weights.astype(jnp.bfloat16), v_head, preferred_element_type=jnp.float32
            )
            updated.append((new_top, total, summed))
        return (tuple(updated), None)

    count = pairs.shape[0]
    step = 2048 if count > 2048 and count % 2048 == 0 else count
    if step == count:
        result, unused = absorb(state, (pairs, key_clip, key_prefix))
        return result
    stacked = (
        pairs.reshape(count // step, step, pairs.shape[1]),
        key_clip.reshape(count // step, step),
        key_prefix.reshape(count // step, step),
    )
    result, unused = lax.scan(absorb, state, stacked)
    return result


def gathered_body(
    inputs,
    norm_gain,
    level_table,
    w_qkv,
    w_out,
    clip_lengths,
    prefix_lengths,
    noise_levels,
    token_rank,
):
    ranks = lax.axis_size("ctx")
    rank_here = lax.axis_index("ctx")
    per_dev = inputs.shape[0]
    slots = 2 * per_dev // ranks
    local_width = w_qkv.shape[2]
    heads_here = local_width // HEAD_DIM
    total_rows = per_dev * ranks
    clip_of, in_prefix, level_row = clip_tables(
        total_rows, clip_lengths, prefix_lengths, noise_levels
    )
    within, counts, starts = rank_tables(token_rank, ranks, per_dev)
    place = token_rank * per_dev + within
    order = (
        jnp.zeros((total_rows,), jnp.int32).at[place].set(jnp.arange(total_rows, dtype=jnp.int32))
    )
    first = rank_here * per_dev
    own_rank = lax.dynamic_slice_in_dim(token_rank, first, per_dev, 0)
    own_within = lax.dynamic_slice_in_dim(within, first, per_dev, 0)
    send_starts = lax.dynamic_slice_in_dim(starts, rank_here, 1, 0)[0]
    recv_counts = lax.dynamic_slice_in_dim(counts, rank_here, 1, 1)[:, 0]
    recv_starts = lax.dynamic_slice_in_dim(starts, rank_here, 1, 1)[:, 0]
    balanced_rows = lax.dynamic_slice_in_dim(order, first, per_dev, 0)
    target = own_rank * slots + own_within - send_starts[own_rank]
    buffer = jnp.zeros((ranks * slots, inputs.shape[1]), inputs.dtype).at[target].set(inputs)
    received = lax.all_to_all(
        buffer.reshape(ranks, slots, inputs.shape[1]),
        "ctx",
        split_axis=0,
        concat_axis=0,
        tiled=True,
    )
    spots = jnp.arange(slots, dtype=jnp.int32)[None, :]
    index = jnp.where(spots < recv_counts[:, None], recv_starts[:, None] + spots, per_dev).reshape(
        -1
    )
    flat = received.reshape(ranks * slots, received.shape[2])
    rows = jnp.zeros((per_dev, received.shape[2]), received.dtype).at[index].set(flat, mode="drop")
    full_rows = lax.all_gather(rows, "head", axis=1, tiled=True)
    normed = normalize(
        full_rows, in_prefix[balanced_rows], level_row[balanced_rows], level_table, norm_gain
    )
    qkv = jnp.dot(
        normed, w_qkv.reshape(w_qkv.shape[0], 3 * local_width), preferred_element_type=jnp.float32
    ).astype(jnp.bfloat16)
    start_state = tuple(
        (
            (
                jnp.full((per_dev, 1), NEG, jnp.float32),
                jnp.zeros((per_dev, 1), jnp.float32),
                jnp.zeros((per_dev, HEAD_DIM), jnp.float32),
            )
            for head in range(heads_here)
        )
    )
    key_clip = clip_of[order]
    key_prefix = in_prefix[order]
    query_clip = lax.dynamic_slice_in_dim(key_clip, first, per_dev, 0)
    query_prefix = lax.dynamic_slice_in_dim(key_prefix, first, per_dev, 0)
    queries = qkv[:, :local_width]
    pairs = qkv[:, local_width:]
    state = fold_keys(
        start_state,
        queries,
        query_clip,
        query_prefix,
        lax.all_gather(pairs, "ctx", axis=0, tiled=True),
        key_clip,
        key_prefix,
    )
    parts = [state[head][2] / state[head][1] for head in range(heads_here)]
    attention = jnp.concatenate(parts, axis=1).astype(jnp.bfloat16)
    terms = jnp.dot(attention, w_out, preferred_element_type=jnp.float32)
    return lax.psum_scatter(terms.astype(jnp.bfloat16), "head", scatter_dimension=1, tiled=True)


def packed_rows(place_ref, spots):
    start, early, half = place_ref[0], place_ref[1], place_ref[2]
    total = place_ref[3]
    before = jnp.where(spots < start, early, 1 - early)
    return spots + total * (half + before * (1 - 2 * half))


def clip_flags(rows, bounds_ref):
    begins, ends, leads = bounds_ref[0:1, :], bounds_ref[1:2, :], bounds_ref[2:3, :]
    inside = (rows >= begins) & (rows < ends)
    return inside, inside & (rows < leads)


def count_earlier(hot):
    ranks, rows, lanes = hot.shape
    flat = hot.reshape(ranks * rows, lanes).astype(jnp.bfloat16)

    def numbers(shape, axis):
        return lax.broadcasted_iota(jnp.int32, shape, axis)

    def group(index):
        return sum(jnp.where(index >= rows * k, 1, 0) for k in range(1, ranks))

    def ones(flags):
        return jnp.where(flags, 1.0, 0.0).astype(jnp.bfloat16)

    total = ranks * rows
    in_row = ones(numbers((lanes, lanes), 0) < numbers((lanes, lanes), 1))
    below, across = numbers((total, 1), 0), numbers((1, total), 1)
    in_rank = ones((group(below) == group(across)) & (across < below))
    row_sums = jnp.dot(
        flat, jnp.ones((lanes, lanes), jnp.bfloat16), preferred_element_type=jnp.float32
    )
    earlier = jnp.dot(flat, in_row, preferred_element_type=jnp.float32) + jnp.dot(
        in_rank, row_sums.astype(jnp.bfloat16), preferred_element_type=jnp.float32
    )
    return earlier.reshape(ranks, rows, lanes)


def table_kernel(ranks, place_ref, bounds_ref, rank_ref, *refs):
    order_ref, runs_ref, query_ref, key_ref, held = refs
    start, early, half, half_rows = (place_ref[k] for k in range(4))
    chip, clips, core, rank_here = (place_ref[k] for k in (4, 5, 8, 9))
    holds_long = half != early
    tokens = rank_ref[...]
    rows, lanes = tokens.shape
    per_dev = rows * lanes // ranks

    token = lanes * lax.broadcasted_iota(jnp.int32, tokens.shape, 0) + lax.broadcasted_iota(
        jnp.int32, tokens.shape, 1
    )
    hots = [jnp.where(tokens == rank, 1.0, 0.0) for rank in range(ranks)]
    earlier = count_earlier(jnp.stack(hots))
    within = sum(hots[rank] * earlier[rank] for rank in range(ranks))
    before = jnp.where(token < start, 1.0, 0.0)
    upto = jnp.where(token < start + half_rows, 1.0, 0.0)
    lane = lax.broadcasted_iota(jnp.int32, (1, lanes), 1)
    target = jnp.bitwise_xor(rank_here, 2 * jnp.bitwise_and(lane, 3))
    lane_long = jnp.where(lane < 4, jnp.where(holds_long, 1.0, 0.0), jnp.where(holds_long, 0.0, 1.0))
    lane_own = jnp.where(lane < 4, 1.0, 0.0)
    lows, longs, long_first, rest_first = [], [], [], []
    long_count, rest_count = [[0.0, 0.0], [0.0, 0.0]], [[0.0, 0.0], [0.0, 0.0]]
    for rank, hot in enumerate(hots):
        low = jnp.sum(hot * before, keepdims=True)
        long_rows = jnp.sum(hot * upto, keepdims=True) - low
        group, parity = rank // (ranks // 2), rank % 2
        lows.append(low)
        longs.append(long_rows)
        long_first.append(long_count[group][parity])
        rest_first.append(rest_count[group][parity])
        long_count[group][parity] = long_first[rank] + long_rows
        rest_count[group][parity] = rest_first[rank] + (per_dev - long_rows)
    long_base = rest_base = low_of = long_of = 0.0
    runs = [0.0] * 5
    for rank, hot in enumerate(hots):
        low, high, long_rows = lows[rank], lows[rank] + longs[rank], longs[rank]
        group, parity = rank // (ranks // 2), rank % 2
        own_group = jnp.where(half == group, 1.0, 0.0)
        long_after = own_group * long_count[1 - group][parity]
        rest_after = own_group * rest_count[1 - group][parity]
        long_base += hot * (long_first[rank] + long_after - low)
        rest_base += hot * (rest_first[rank] + rest_after)
        low_of += hot * low
        long_of += hot * long_rows
        first = long_first[rank] + lane_own * long_after
        rest = rest_first[rank] + lane_own * rest_after
        here = jnp.where(target == rank, 1.0, 0.0)
        values = (
            (0.0, low),
            (low, high),
            (high, float(per_dev)),
            (0.0, rest),
            (first - low, rest - long_rows),
        )
        runs = [
            run + here * (lane_long * if_long + (1.0 - lane_long) * if_rest)
            for run, (if_long, if_rest) in zip(runs, values)
        ]
    furthest = rows * lanes // 4 + per_dev // 2
    for index, run in enumerate(runs):
        run = run.astype(jnp.int32)
        runs_ref[index : index + 1, :] = (
            run if index < 3 else jnp.clip(run, -per_dev, furthest)
        )
    sorted_at = within + jnp.where(
        upto - before == 1.0, long_base, rest_base - jnp.where(within < low_of, 0.0, long_of)
    )
    held[...] = jnp.where(jnp.bitwise_and(tokens, 1) == core, sorted_at.astype(jnp.int32), -1)
    half_lines = rows // 2
    spots = lanes * lax.broadcasted_iota(
        jnp.int32, (half_lines, lanes), 0
    ) + lax.broadcasted_iota(jnp.int32, (half_lines, lanes), 1)
    later = packed_rows(place_ref, spots) >= half_rows
    held[:half_lines, :] = jnp.where(later, held[half_lines:, :], held[:half_lines, :])
    lines = half_lines // 4
    for d in range(4):
        line = lines * jnp.bitwise_xor(chip, d)
        order_ref[lines * d : lines * (d + 1), :] = held[pl.ds(line, lines), :]

    column = lax.broadcasted_iota(jnp.int32, (1, HEAD_DIM), 1)
    chip_rows = query_ref.shape[0] // 4
    for d in range(4):
        local = lax.broadcasted_iota(jnp.int32, (chip_rows, 1), 0)
        spots = chip_rows * jnp.bitwise_xor(chip, d) + local
        inside, leading = clip_flags(packed_rows(place_ref, spots), bounds_ref)
        spot = slice(d * chip_rows, (d + 1) * chip_rows)
        inside = jnp.where(inside, 1.0, 0.0)
        prefix = jnp.sum(jnp.where(leading, 1.0, 0.0), axis=1, keepdims=True)
        query_ref[spot, :] = jnp.where(column == clips, prefix, inside).astype(jnp.bfloat16)
        outside = jnp.where(column < clips, NEG * (1.0 - inside), 0.0)
        key_ref[spot, :] = jnp.where(column == clips, NEG * (1.0 - prefix), outside).astype(
            jnp.bfloat16
        )


def make_tables(place, bounds, token_rank, ranks, keys):
    vmem = pl.BlockSpec(memory_space=pltpu.VMEM)
    tokens = token_rank.reshape(-1, HEAD_DIM)
    features = jax.ShapeDtypeStruct((keys, HEAD_DIM), jnp.bfloat16)
    return pl.pallas_call(
        functools.partial(table_kernel, ranks),
        in_specs=[pl.BlockSpec(memory_space=pltpu.SMEM), vmem, vmem],
        out_specs=(vmem,) * 4,
        out_shape=(
            jax.ShapeDtypeStruct((tokens.shape[0] // 2, HEAD_DIM), jnp.int32),
            jax.ShapeDtypeStruct((8, HEAD_DIM), jnp.int32),
            features,
            features,
        ),
        scratch_shapes=[pltpu.VMEM(tokens.shape, jnp.int32)],
        compiler_params=pltpu.CompilerParams(vmem_limit_bytes=26 * MIB),
        cost_estimate=pl.CostEstimate(flops=COST, bytes_accessed=COST, transcendentals=0),
    )(place, bounds, tokens)


def select_kernel(low, place_ref, own_ref, moved_ref, *rest):
    out_ref = rest[-1]
    spots = place_ref[7] + low + lax.broadcasted_iota(jnp.int32, (out_ref.shape[0], 1), 0)
    swapped = jnp.where(spots < place_ref[0], place_ref[1], 1 - place_ref[1])
    out_ref[...] = jnp.where(swapped == 1, moved_ref[...], own_ref[...])


def select_rows(place, own, moved, low, after):
    vmem = pl.BlockSpec(memory_space=pltpu.VMEM)
    return pl.pallas_call(
        functools.partial(select_kernel, low),
        in_specs=[pl.BlockSpec(memory_space=pltpu.SMEM), vmem, vmem]
        + [pl.BlockSpec(memory_space=pl.ANY)] * len(after),
        out_specs=vmem,
        out_shape=jax.ShapeDtypeStruct(moved.shape, moved.dtype),
        compiler_params=pltpu.CompilerParams(vmem_limit_bytes=8 * MIB),
        cost_estimate=pl.CostEstimate(flops=COST, bytes_accessed=COST, transcendentals=0),
    )(place, own, moved, *after)


def head_of(chip, index, group_heads):
    return 2 * group_heads * (chip // 2) + 2 * index + chip % 2


def weight_copies(place_ref, w_ref, out_ref, sems):
    columns = out_ref.shape[2]
    pair = jnp.bitwise_xor(place_ref[4] // 2, place_ref[8])
    spot = pl.ds(pl.multiple_of(pair * columns, HEAD_DIM), columns)
    depth = out_ref.shape[1] // COPY_PIECES
    copies = []
    for part in range(3):
        for piece in range(COPY_PIECES):
            rows = slice(piece * depth, (piece + 1) * depth)
            copies.append(
                pltpu.make_async_copy(
                    w_ref.at[part, rows, spot], out_ref.at[part, rows, :], sems.at[part, piece]
                )
            )
    return copies


def fetch_kernel(place_ref, w_ref, *rest):
    out_ref, sems = rest[-2:]
    copies = weight_copies(place_ref, w_ref, out_ref, sems)
    for copy in copies:
        copy.start()
    for copy in copies:
        copy.wait()


def fetch_weights(place, w_parts, after):
    parts, depth, columns = w_parts.shape
    hbm = pl.BlockSpec(memory_space=pltpu.HBM)
    return pl.pallas_call(
        fetch_kernel,
        in_specs=[pl.BlockSpec(memory_space=pltpu.SMEM), hbm]
        + [pl.BlockSpec(memory_space=pl.ANY)] * len(after),
        out_specs=pl.BlockSpec(memory_space=pltpu.VMEM),
        out_shape=jax.ShapeDtypeStruct((parts, depth, columns // 2), w_parts.dtype),
        scratch_shapes=[pltpu.SemaphoreType.DMA((parts, COPY_PIECES))],
        compiler_params=pltpu.CompilerParams(vmem_limit_bytes=20 * MIB),
        cost_estimate=pl.CostEstimate(flops=COST, bytes_accessed=COST, transcendentals=0),
    )(place, w_parts, *after)


def norm_kernel(place_ref, *refs):
    pieces = len(SWAP_ROWS)
    bounds_ref, noise_ref, level_ref, gain_ref = refs[2 * pieces : 2 * pieces + 4]
    out_ref = refs[-1]
    width = out_ref.shape[1] // 2
    side, first = place_ref[6], place_ref[7]
    clips, levels = noise_ref.shape[0], level_ref.shape[0]
    spots = [pl.ds(pl.multiple_of(s * width, 128), width) for s in (side, 1 - side)]
    level = lax.broadcasted_iota(jnp.int32, (clips, levels), 1)
    chosen = jnp.where(noise_ref[...] == level, 1.0, 0.0).astype(jnp.bfloat16)
    tables = [
        jnp.dot(chosen, level_ref[:, spot], preferred_element_type=jnp.float32).astype(
            jnp.bfloat16
        )
        for spot in spots
    ]
    low = 0
    for piece in range(pieces):
        own_ref, other_ref = refs[piece], refs[pieces + piece]
        count = own_ref.shape[0]
        rows = slice(low, low + count)
        places = first + low + lax.broadcasted_iota(jnp.int32, (count, 1), 0)
        low += count
        unused, leading = clip_flags(packed_rows(place_ref, places), bounds_ref)
        picks = jnp.where(leading, 1.0, 0.0)[:, :clips].astype(jnp.bfloat16)
        shifted = [
            ref[...].astype(jnp.float32)
            + jnp.dot(picks, table, preferred_element_type=jnp.float32)
            for ref, table in zip((own_ref, other_ref), tables)
        ]
        squares = sum(jnp.sum(part * part, axis=1, keepdims=True) for part in shifted)
        factor = lax.rsqrt(squares / (2 * width) + EPS)
        for part, spot in zip(shifted, spots):
            out_ref[rows, spot] = (part * factor * gain_ref[:, spot]).astype(jnp.bfloat16)


def normalize_rows(place, kept, other, bounds, noise_levels, level_table, norm_gain, after):
    rows, depth = sum(part.shape[0] for part in kept), 2 * kept[0].shape[1]
    vmem = pl.BlockSpec(memory_space=pltpu.VMEM)
    return pl.pallas_call(
        norm_kernel,
        in_specs=[pl.BlockSpec(memory_space=pltpu.SMEM)]
        + [vmem] * (2 * len(kept) + 4)
        + [pl.BlockSpec(memory_space=pl.ANY)] * len(after),
        out_specs=vmem,
        out_shape=jax.ShapeDtypeStruct((rows, depth), jnp.bfloat16),
        compiler_params=pltpu.CompilerParams(vmem_limit_bytes=26 * MIB),
        cost_estimate=pl.CostEstimate(flops=COST, bytes_accessed=COST, transcendentals=0),
    )(place, *kept, *other, bounds, noise_levels, level_table, norm_gain.reshape(1, -1), *after)


def project_kernel(indices, place_ref, own_ref, pair_ref, weights_ref, *rest):
    first_ref, second_ref = rest[-2:]
    rows = jnp.concatenate([own_ref[...], pair_ref[...]], axis=0)
    count = own_ref.shape[0]
    same = place_ref[4] % 2 == place_ref[8]

    def store(outcome, base, even_ref, odd_ref):
        for index, core in enumerate((place_ref[8], 1 - place_ref[8])):
            spot = pl.ds(pl.multiple_of(core * count, count), count)
            half = outcome[index * count : (index + 1) * count]
            for part in range(3):
                to = slice(base + part * HEAD_DIM, base + (part + 1) * HEAD_DIM)
                even_ref[spot, to] = half[:, 2 * part * HEAD_DIM : (2 * part + 1) * HEAD_DIM]
                odd_ref[spot, to] = half[:, (2 * part + 1) * HEAD_DIM : 2 * (part + 1) * HEAD_DIM]

    for position, index in enumerate(indices):
        spot = slice(2 * index * HEAD_DIM, 2 * (index + 1) * HEAD_DIM)
        weights = jnp.concatenate([weights_ref[part, :, spot] for part in range(3)], axis=1)
        outcome = jnp.dot(rows, weights, preferred_element_type=jnp.float32).astype(jnp.bfloat16)
        base = 3 * position * HEAD_DIM

        @pl.when(same)
        def _():
            store(outcome, base, first_ref, second_ref)

        @pl.when(jnp.logical_not(same))
        def _():
            store(outcome, base, second_ref, first_ref)


def project_heads(place, own, pair, weights, indices, after):
    rows = own.shape[0]
    vmem = pl.BlockSpec(memory_space=pltpu.VMEM)
    shape = jax.ShapeDtypeStruct((2 * rows, 3 * len(indices) * HEAD_DIM), jnp.bfloat16)
    return pl.pallas_call(
        functools.partial(project_kernel, indices),
        in_specs=[pl.BlockSpec(memory_space=pltpu.SMEM), vmem, vmem, vmem]
        + [pl.BlockSpec(memory_space=pl.ANY)] * len(after),
        out_specs=(vmem, vmem),
        out_shape=(shape, shape),
        compiler_params=pltpu.CompilerParams(vmem_limit_bytes=26 * MIB),
        cost_estimate=pl.CostEstimate(flops=COST, bytes_accessed=COST, transcendentals=0),
    )(place, own, pair, weights, *after)


def attend_kernel(base, place_ref, runs_ref, *refs):
    mine, near, far, pair_first, pair_far, pair_near = refs[:6]
    order_ref, query_mask_ref, key_mask_ref = refs[6:9]
    stay_ref, cross_ref, q_all, k_all, v_all, sorted_out = refs[-6:]
    chip_rows = mine.shape[0]
    rows = chip_rows // 2
    queries = sorted_out.shape[0] - 2 * rows

    def hold(sources):
        for index, source in enumerate(sources):
            spot = slice(index * chip_rows, (index + 1) * chip_rows)
            for part, held in enumerate((q_all, k_all, v_all)):
                low = base + part * HEAD_DIM
                held[spot, :HEAD_DIM] = source[:, low : low + HEAD_DIM]

    @pl.when(place_ref[8] == 0)
    def _():
        hold((mine, near, pair_near, pair_far))

    @pl.when(place_ref[8] == 1)
    def _():
        hold((pair_first, pair_near, near, far))

    q_all[:, HEAD_DIM:] = query_mask_ref[...]
    k_all[:, HEAD_DIM:] = key_mask_ref[...]
    v_all[:, HEAD_DIM:] = jnp.ones((4 * chip_rows, HEAD_DIM), jnp.bfloat16)
    tile = queries // ATTEND_TILES

    def score(step):
        wanted = step * tile + lax.broadcasted_iota(jnp.int32, (tile, 1), 0)
        picks = jnp.concatenate(
            [
                jnp.where(order_ref[line : line + 1, :] == wanted, 1.0, 0.0).astype(jnp.bfloat16)
                for line in range(order_ref.shape[0])
            ],
            axis=1,
        )
        sorted_queries = jnp.dot(picks, q_all[...], preferred_element_type=jnp.float32)
        return lax.dot_general(
            sorted_queries.astype(jnp.bfloat16),
            k_all[...],
            (((1,), (1,)), ((), ())),
            preferred_element_type=jnp.float32,
        )

    coming = score(0)
    for step in range(ATTEND_TILES):
        scores = coming
        if step + 1 < ATTEND_TILES:
            coming = score(step + 1)
        top = jnp.max(scores, axis=1, keepdims=True)
        weights = jnp.exp2((scores - top) * (HEAD_DIM ** (-0.5) * LOG2E))
        summed = jnp.dot(
            weights.astype(jnp.bfloat16), v_all[...], preferred_element_type=jnp.float32
        )
        sorted_out[rows + step * tile : rows + (step + 1) * tile, :] = (
            summed[:, :HEAD_DIM] / summed[:, HEAD_DIM:]
        )

    cross_ref[...] = sorted_out[rows : rows + cross_ref.shape[0], :].astype(jnp.bfloat16)
    for d in range(4):
        stay_ref[d] = spread_run(sorted_out, runs_ref, d, rows).astype(jnp.bfloat16)


def spread_run(sorted_ref, runs_ref, lane, rows):
    furthest = sorted_ref.shape[0] - 2 * rows
    row = lax.broadcasted_iota(jnp.int32, (rows, 1), 0)
    parts = [
        sorted_ref[pl.ds(rows + jnp.clip(runs_ref[line, lane], -rows, furthest), rows), :]
        for line in (3, 4)
    ]
    in_second = (row >= runs_ref[1, lane]) & (row < runs_ref[2, lane])
    return jnp.where(row < runs_ref[0, lane], parts[0], jnp.where(in_second, parts[1], 0.0))


def attend(place, runs, blocks, position, order, query_mask, key_mask, cap, after):
    chip_rows = blocks[0].shape[0]
    rows, keys = chip_rows // 2, 4 * chip_rows
    queries = keys // 2 + rows // 2
    vmem, smem = pl.BlockSpec(memory_space=pltpu.VMEM), pl.BlockSpec(memory_space=pltpu.SMEM)
    shape = jax.ShapeDtypeStruct((4, rows, HEAD_DIM), jnp.bfloat16)
    return pl.pallas_call(
        functools.partial(attend_kernel, 3 * position * HEAD_DIM),
        in_specs=[smem, smem]
        + [vmem] * (len(blocks) + 3)
        + [pl.BlockSpec(memory_space=pl.ANY)] * len(after),
        out_specs=(vmem, vmem),
        out_shape=(shape, jax.ShapeDtypeStruct((cap, HEAD_DIM), jnp.bfloat16)),
        scratch_shapes=[
            pltpu.VMEM((keys, 2 * HEAD_DIM), jnp.bfloat16),
            pltpu.VMEM((keys, 2 * HEAD_DIM), jnp.bfloat16),
            pltpu.VMEM((keys, 2 * HEAD_DIM), jnp.bfloat16),
            pltpu.VMEM((queries + 2 * rows, HEAD_DIM), jnp.float32),
        ],
        compiler_params=pltpu.CompilerParams(vmem_limit_bytes=32 * MIB),
        cost_estimate=pl.CostEstimate(
            flops=COST, bytes_accessed=COST, transcendentals=0
        ),
    )(place, runs, *blocks, order, query_mask, key_mask, *after)


def join_kernel(heads, runs_ref, *refs):
    outs, held = refs[-5:-1], refs[-1]
    rows = outs[0].shape[0]
    for head in range(heads):
        stay_ref, arrived_ref = refs[2 * head], refs[2 * head + 1]
        held[rows : rows + arrived_ref.shape[0], :] = arrived_ref[...].astype(jnp.float32)
        spot = slice(head * HEAD_DIM, (head + 1) * HEAD_DIM)
        for d in range(4):
            arrived = spread_run(held, runs_ref, 4 + d, rows).astype(jnp.bfloat16)
            outs[d][:, spot] = stay_ref[d] + arrived


def join_halves(runs, stays, arrivals, after, cost):
    heads, (slots, rows, width) = len(stays), stays[0].shape
    vmem = pl.BlockSpec(memory_space=pltpu.VMEM)
    pairs = [part for both in zip(stays, arrivals) for part in both]
    shape = jax.ShapeDtypeStruct((rows, heads * width), jnp.bfloat16)
    return pl.pallas_call(
        functools.partial(join_kernel, heads),
        in_specs=[pl.BlockSpec(memory_space=pltpu.SMEM)]
        + [vmem] * len(pairs)
        + [pl.BlockSpec(memory_space=pl.ANY)] * len(after),
        out_specs=(vmem,) * slots,
        out_shape=(shape,) * slots,
        scratch_shapes=[pltpu.VMEM((arrivals[0].shape[0] + 2 * rows, width), jnp.float32)],
        compiler_params=pltpu.CompilerParams(vmem_limit_bytes=16 * MIB),
        cost_estimate=pl.CostEstimate(flops=cost, bytes_accessed=COST, transcendentals=0),
    )(runs, *pairs, *after)


def gather_kernel(first_heads, last_heads, place_ref, w_ref, held_ref, pair_ref, *rest):
    own_first, own_last, far_first, far_last, sems = rest[-5:]
    chip, columns = place_ref[4], own_first.shape[1]
    heads = w_ref.shape[0] // HEAD_DIM // 4
    spot = pl.ds(pl.multiple_of(place_ref[6] * columns, HEAD_DIM), columns)

    def rows_at(block):
        return pl.ds(pl.multiple_of(block * HEAD_DIM, HEAD_DIM), HEAD_DIM)

    def transfers(near_ref, far_ref):
        copies = []
        for indices, own, far in ((first_heads, own_first, far_first), (last_heads, own_last, far_last)):
            for d in range(4):
                for position, index in enumerate(indices):
                    head = head_of(jnp.bitwise_xor(chip, d), index, heads)
                    there = 2 * index + jnp.bitwise_xor(chip, d) % 2
                    to = slice(
                        (len(indices) * d + position) * HEAD_DIM,
                        (len(indices) * d + position + 1) * HEAD_DIM,
                    )
                    source = near_ref if d < 2 else far_ref
                    slot = heads * d + index
                    copies.append(
                        pltpu.make_async_copy(
                            w_ref.at[rows_at(head), spot], own.at[to, :], sems.at[0, slot]
                        )
                    )
                    copies.append(
                        pltpu.make_async_copy(
                            source.at[rows_at(there), :], far.at[to, :], sems.at[1, slot]
                        )
                    )
        for copy in copies:
            copy.start()
        for copy in copies:
            copy.wait()

    @pl.when(chip // 2 == place_ref[8])
    def _():
        transfers(held_ref, pair_ref)

    @pl.when(chip // 2 != place_ref[8])
    def _():
        transfers(pair_ref, held_ref)


def gather_out_weights(place, w_out, held, pair, first_heads, last_heads, after):
    columns = w_out.shape[1] // 2
    vmem, hbm = pl.BlockSpec(memory_space=pltpu.VMEM), pl.BlockSpec(memory_space=pltpu.HBM)
    any_space = pl.BlockSpec(memory_space=pl.ANY)
    shapes = [
        jax.ShapeDtypeStruct((4 * len(indices) * HEAD_DIM, columns), w_out.dtype)
        for indices in (first_heads, last_heads)
    ]
    return pl.pallas_call(
        functools.partial(gather_kernel, first_heads, last_heads),
        in_specs=[pl.BlockSpec(memory_space=pltpu.SMEM), hbm]
        + [any_space] * (2 + len(after)),
        out_specs=(vmem,) * 4,
        out_shape=(*shapes, *shapes),
        scratch_shapes=[pltpu.SemaphoreType.DMA((2, w_out.shape[0] // HEAD_DIM))],
        compiler_params=pltpu.CompilerParams(vmem_limit_bytes=16 * MIB),
        cost_estimate=pl.CostEstimate(flops=COST, bytes_accessed=COST, transcendentals=0),
    )(place, w_out, held, pair, *after)


def out_rows_kernel(*refs):
    refs[-1][...] = jnp.concatenate([ref[...] for ref in refs[:-1]], axis=1)


def out_kernel(rows_ref, weights_ref, *refs):
    product = jnp.dot(rows_ref[...], weights_ref[...], preferred_element_type=jnp.float32)
    if len(refs) > 1:
        product = refs[0][...] + product
    refs[-1][...] = product.astype(refs[-1].dtype)


def out_call(kernel, arrays, shape, dtype):
    vmem = pl.BlockSpec(memory_space=pltpu.VMEM)
    return pl.pallas_call(
        kernel,
        in_specs=[vmem] * len(arrays),
        out_specs=vmem,
        out_shape=jax.ShapeDtypeStruct(shape, dtype),
        compiler_params=pltpu.CompilerParams(vmem_limit_bytes=16 * MIB),
        cost_estimate=pl.CostEstimate(flops=COST, bytes_accessed=COST, transcendentals=0),
    )(*arrays)


SWAP_ROWS = (112, 112, 96)
PACKED_ROWS = 768
ATTEND_TILES = 3
HEAD_CHUNKS = ((0,), (1, 2))
COPY_PIECES = 4


def halved_body(
    inputs,
    norm_gain,
    level_table,
    w_qkv,
    w_out,
    clip_lengths,
    prefix_lengths,
    noise_levels,
    token_rank,
):
    ranks, per_dev = 16, inputs.shape[0]
    half_rows = 8 * per_dev
    clips = clip_lengths.shape[0]
    index = jnp.arange(clips, dtype=jnp.int32)

    ahead = (index[None, :] < index[:, None]) & (clip_lengths == MAXCLIP)[:, None]
    start = jnp.sum(jnp.where(ahead, clip_lengths[None, :], 0))
    early = start <= half_rows // 2

    row = jnp.arange(ranks * per_dev, dtype=jnp.int32)
    in_long = (row >= start) & (row < start + half_rows)
    home = jnp.where(in_long == early, 0, 1)
    crosses = token_rank // (ranks // 2) != home
    kind = jnp.where(crosses, 2 * home + token_rank % 2, 4)
    counts = jnp.sum((kind[:, None] == jnp.arange(4)[None, :]).astype(jnp.int32), axis=0)
    fits = jnp.max(counts) <= PACKED_ROWS
    choice = jnp.where(early, 0, 1) + jnp.where(fits, 0, 2)
    most = half_rows // 2 + per_dev // 2
    return lax.switch(
        choice,
        [
            functools.partial(halved_program, blocks, cap)
            for cap in (PACKED_ROWS, most)
            for blocks in (range(4), range(4, 8))
        ],
        start,
        inputs,
        norm_gain,
        level_table,
        w_qkv,
        w_out,
        clip_lengths,
        prefix_lengths,
        noise_levels,
        token_rank,
    )


def halved_program(
    swapping,
    cap,
    start,
    inputs,
    norm_gain,
    level_table,
    w_qkv,
    w_out,
    clip_lengths,
    prefix_lengths,
    noise_levels,
    token_rank,
):
    rank_here = lax.axis_index("ctx")
    side = lax.axis_index("head")
    per_dev, columns = inputs.shape
    ranks = 16
    half_rows = 8 * per_dev
    group_heads = w_qkv.shape[2] // HEAD_DIM // 4
    clips = clip_lengths.shape[0]
    half, block, core = rank_here // 8, rank_here % 8, rank_here % 2
    chip = block // 2
    swap_sides = [(0, 1), (1, 0)]

    def exchange(array, flip, only=lambda r: True):
        pairs = [(r, r ^ flip) for r in range(ranks) if only(r)]
        return lax.ppermute(array, "ctx", pairs)

    place = jnp.stack(
        [
            start,
            jnp.int32(1 if 0 in swapping else 0),
            half,
            jnp.int32(half_rows),
            chip,
            jnp.int32(clips),
            side,
            block * per_dev,
            core,
            rank_here,
        ]
    )
    index = jnp.arange(clips, dtype=jnp.int32)
    earlier = index[None, :] < index[:, None]
    begins = jnp.sum(jnp.where(earlier, clip_lengths[None, :], 0), axis=1)
    leads = begins + jnp.minimum(prefix_lengths, clip_lengths)
    bounds = jnp.pad(
        jnp.stack([begins, begins + clip_lengths, leads]), ((0, 5), (0, HEAD_DIM - clips))
    )

    cuts = [sum(SWAP_ROWS[:i]) for i in range(len(SWAP_ROWS) + 1)]
    kept = []
    for low, high in zip(cuts[:-1], cuts[1:]):
        own = inputs[low:high]
        sent = own
        if len(kept) > 0 and high == per_dev:
            sent, unused = lax.optimization_barrier((own, kept[0]))
        moved = exchange(sent, 8, lambda r: r % 8 in swapping)
        kept.append(select_rows(place, own, moved, low, kept[-1:]))
    other = [lax.ppermute(part, "head", swap_sides) for part in kept]
    w_parts = jnp.transpose(w_qkv, (1, 0, 2))
    weights = fetch_weights(place, w_parts, kept[-1:])
    depth = w_out.shape[0] // 2
    sent = lax.dynamic_slice(w_out, (core * depth, (1 - side) * columns), (depth, columns))
    far_held = lax.ppermute(sent, "head", swap_sides)
    normed = normalize_rows(
        place,
        kept,
        other,
        bounds,
        noise_levels.reshape(-1, 1),
        level_table,
        norm_gain,
        [weights, sent],
    )
    pair = exchange(normed, 1)
    query_order, runs, query_mask, key_mask = make_tables(
        place, bounds, token_rank, ranks, half_rows
    )

    blocks, after = [], [query_order]
    for heads in HEAD_CHUNKS:
        first, second = project_heads(place, normed, pair, weights, heads, after)
        near = lax.ppermute(
            second, "ctx", [(r, r ^ (2 if r % 2 == 0 else 4)) for r in range(ranks)]
        )
        far = exchange(first, 6, lambda r: r % 2 == 1)
        blocks.append((first, near, far))
        after = [first]

    def share(block, after):
        first, near, far = block
        shared, near, far, *unused = lax.optimization_barrier((first, near, far, *after))
        return [
            first,
            near,
            far,
            exchange(shared, 1, lambda r: r % 2 == 0),
            exchange(far, 1, lambda r: r % 2 == 1),
            exchange(near, 1),
        ]

    stays, arrivals, after = [], [], [blocks[-1][0]]
    for block, heads in zip(blocks, HEAD_CHUNKS):
        block = share(block, after)
        for position, head in enumerate(heads):
            stay, cross = attend(
                place, runs, block, position, query_order, query_mask, key_mask, cap, after
            )
            stays.append(stay)
            arrivals.append(exchange(cross, 8))
            after = [cross] + (arrivals[head - 1 : head] if head else [])

    first_heads, last_head = list(range(group_heads - 1)), [group_heads - 1]

    def across(heads, after, cost):
        joined = join_halves(runs, stays[heads], arrivals[heads], after, cost)
        pieces = [exchange(part, 2 * d) if d else part for d, part in enumerate(joined)]
        width = sum(piece.shape[1] for piece in pieces)
        rows = out_call(out_rows_kernel, pieces, (per_dev, width), jnp.bfloat16)
        return rows, lax.ppermute(rows, "head", swap_sides)

    first_rows, first_far = across(slice(0, -1), [cross], COST)
    far_pair = exchange(lax.optimization_barrier((far_held, first_rows))[0], 1)
    w_first, w_last, w_far_first, w_far_last = gather_out_weights(
        place, w_out, far_held, far_pair, first_heads, last_head, [first_rows]
    )
    last_rows, last_far = across(slice(-1, None), [], LONG_COST)
    shape = (per_dev, columns)
    total = out_call(out_kernel, [first_rows, w_first], shape, jnp.float32)
    total = out_call(out_kernel, [last_rows, w_last, total], shape, jnp.float32)
    total = out_call(out_kernel, [first_far, w_far_first, total], shape, jnp.float32)
    return out_call(out_kernel, [last_far, w_far_last, total], shape, jnp.bfloat16)


def solution(mesh):
    in_specs = (
        P("ctx", "head"),
        P(),
        P(),
        P(None, None, "head"),
        P("head", None),
        P(),
        P(),
        P(),
        P(),
    )
    out_specs = P("ctx", "head")

    def body(inputs, norm_gain, level_table, w_qkv, *rest):
        ranks, sides = mesh.shape["ctx"], mesh.shape["head"]
        heads_here = w_qkv.shape[2] // HEAD_DIM
        halved = (
            ranks == 16
            and sides == 2
            and ranks * inputs.shape[0] == 2 * MAXCLIP
            and heads_here == 4 * sum(len(heads) for heads in HEAD_CHUNKS)
        )
        run = halved_body if halved else gathered_body
        return run(inputs, norm_gain, level_table, w_qkv, *rest)

    return jax.shard_map(body, mesh=mesh, in_specs=in_specs, out_specs=out_specs, check_vma=False)
```

```python
import functools

import jax
import jax.numpy as jnp
from jax import lax
from jax.experimental import pallas as pl
from jax.experimental.pallas import tpu as pltpu
from jax.sharding import PartitionSpec as P

HEAD_DIM = 128


NEG = -1e30
EPS = 1e-06
MAXCLIP = 2560
LOG2E = 1.4426950408889634
MIB = 1024 * 1024
COST = 1000000
LONG_COST = 200000000000


def clip_tables(total_rows, clip_lengths, prefix_lengths, noise_levels):
    rows = jnp.arange(total_rows, dtype=jnp.int32)
    ends = jnp.cumsum(clip_lengths)
    begins = ends - clip_lengths
    clip_of = jnp.sum((rows[:, None] >= ends[None, :]).astype(jnp.int32), axis=1)
    member = clip_of[:, None] == jnp.arange(clip_lengths.shape[0], dtype=jnp.int32)[None, :]
    begin_row = jnp.sum(jnp.where(member, begins[None, :], 0), axis=1)
    lead = jnp.minimum(prefix_lengths, clip_lengths)
    lead_row = jnp.sum(jnp.where(member, lead[None, :], 0), axis=1)
    level_row = jnp.sum(jnp.where(member, noise_levels[None, :], 0), axis=1)
    in_prefix = rows - begin_row < lead_row
    return (clip_of, in_prefix, level_row)


def rank_tables(token_rank, ranks, per_rank):
    onehot = (token_rank[:, None] == jnp.arange(ranks, dtype=jnp.int32)[None, :]).astype(jnp.int32)
    earlier = jnp.cumsum(onehot, axis=0) - onehot
    within = jnp.sum(earlier * onehot, axis=1)
    counts = jnp.sum(onehot.reshape(ranks, per_rank, ranks), axis=1)
    starts = jnp.cumsum(counts, axis=0) - counts
    return (within, counts, starts)


def normalize(rows, in_prefix, level_row, level_table, norm_gain):
    picks = (
        level_row[:, None] == jnp.arange(level_table.shape[0], dtype=jnp.int32)[None, :]
    ) & in_prefix[:, None]
    added = jnp.dot(picks.astype(jnp.bfloat16), level_table, preferred_element_type=jnp.float32)
    shifted = rows.astype(jnp.float32) + added
    factor = lax.rsqrt(jnp.mean(shifted * shifted, axis=-1, keepdims=True) + EPS)
    return (shifted * factor * norm_gain).astype(jnp.bfloat16)


def fold_keys(state, queries, query_clip, query_prefix, pairs, key_clip, key_prefix):
    width = queries.shape[1]
    heads_here = width // HEAD_DIM
    factor = HEAD_DIM ** (-0.5)
    allowed_query = jnp.logical_not(query_prefix)

    def absorb(carry, block):
        block_pairs, block_clip, block_prefix = block
        allowed = (query_clip[:, None] == block_clip[None, :]) & (
            allowed_query[:, None] | block_prefix[None, :]
        )
        updated = []
        for head in range(heads_here):
            top, total, summed = carry[head]
            low = head * HEAD_DIM
            q_head = queries[:, low : low + HEAD_DIM]
            k_head = block_pairs[:, low : low + HEAD_DIM]
            v_head = block_pairs[:, width + low : width + low + HEAD_DIM]
            scores = (
                lax.dot_general(
                    q_head, k_head, (((1,), (1,)), ((), ())), preferred_element_type=jnp.float32
                )
                * factor
            )
            masked = jnp.where(allowed, scores, NEG)
            new_top = jnp.maximum(top, jnp.max(masked, axis=1, keepdims=True))
            fade = jnp.exp(top - new_top)
            weights = jnp.where(allowed, jnp.exp(scores - new_top), 0.0)
            total = total * fade + jnp.sum(weights, axis=1, keepdims=True)
            summed = summed * fade + jnp.dot(
                weights.astype(jnp.bfloat16), v_head, preferred_element_type=jnp.float32
            )
            updated.append((new_top, total, summed))
        return (tuple(updated), None)

    count = pairs.shape[0]
    step = 2048 if count > 2048 and count % 2048 == 0 else count
    if step == count:
        result, unused = absorb(state, (pairs, key_clip, key_prefix))
        return result
    stacked = (
        pairs.reshape(count // step, step, pairs.shape[1]),
        key_clip.reshape(count // step, step),
        key_prefix.reshape(count // step, step),
    )
    result, unused = lax.scan(absorb, state, stacked)
    return result


def gathered_body(
    inputs,
    norm_gain,
    level_table,
    w_qkv,
    w_out,
    clip_lengths,
    prefix_lengths,
    noise_levels,
    token_rank,
):
    ranks = lax.axis_size("ctx")
    rank_here = lax.axis_index("ctx")
    per_dev = inputs.shape[0]
    slots = 2 * per_dev // ranks
    local_width = w_qkv.shape[2]
    heads_here = local_width // HEAD_DIM
    total_rows = per_dev * ranks
    clip_of, in_prefix, level_row = clip_tables(
        total_rows, clip_lengths, prefix_lengths, noise_levels
    )
    within, counts, starts = rank_tables(token_rank, ranks, per_dev)
    place = token_rank * per_dev + within
    order = (
        jnp.zeros((total_rows,), jnp.int32).at[place].set(jnp.arange(total_rows, dtype=jnp.int32))
    )
    first = rank_here * per_dev
    own_rank = lax.dynamic_slice_in_dim(token_rank, first, per_dev, 0)
    own_within = lax.dynamic_slice_in_dim(within, first, per_dev, 0)
    send_starts = lax.dynamic_slice_in_dim(starts, rank_here, 1, 0)[0]
    recv_counts = lax.dynamic_slice_in_dim(counts, rank_here, 1, 1)[:, 0]
    recv_starts = lax.dynamic_slice_in_dim(starts, rank_here, 1, 1)[:, 0]
    balanced_rows = lax.dynamic_slice_in_dim(order, first, per_dev, 0)
    target = own_rank * slots + own_within - send_starts[own_rank]
    buffer = jnp.zeros((ranks * slots, inputs.shape[1]), inputs.dtype).at[target].set(inputs)
    received = lax.all_to_all(
        buffer.reshape(ranks, slots, inputs.shape[1]),
        "ctx",
        split_axis=0,
        concat_axis=0,
        tiled=True,
    )
    spots = jnp.arange(slots, dtype=jnp.int32)[None, :]
    index = jnp.where(spots < recv_counts[:, None], recv_starts[:, None] + spots, per_dev).reshape(
        -1
    )
    flat = received.reshape(ranks * slots, received.shape[2])
    rows = jnp.zeros((per_dev, received.shape[2]), received.dtype).at[index].set(flat, mode="drop")
    full_rows = lax.all_gather(rows, "head", axis=1, tiled=True)
    normed = normalize(
        full_rows, in_prefix[balanced_rows], level_row[balanced_rows], level_table, norm_gain
    )
    qkv = jnp.dot(
        normed, w_qkv.reshape(w_qkv.shape[0], 3 * local_width), preferred_element_type=jnp.float32
    ).astype(jnp.bfloat16)
    start_state = tuple(
        (
            (
                jnp.full((per_dev, 1), NEG, jnp.float32),
                jnp.zeros((per_dev, 1), jnp.float32),
                jnp.zeros((per_dev, HEAD_DIM), jnp.float32),
            )
            for head in range(heads_here)
        )
    )
    key_clip = clip_of[order]
    key_prefix = in_prefix[order]
    query_clip = lax.dynamic_slice_in_dim(key_clip, first, per_dev, 0)
    query_prefix = lax.dynamic_slice_in_dim(key_prefix, first, per_dev, 0)
    queries = qkv[:, :local_width]
    pairs = qkv[:, local_width:]
    state = fold_keys(
        start_state,
        queries,
        query_clip,
        query_prefix,
        lax.all_gather(pairs, "ctx", axis=0, tiled=True),
        key_clip,
        key_prefix,
    )
    parts = [state[head][2] / state[head][1] for head in range(heads_here)]
    attention = jnp.concatenate(parts, axis=1).astype(jnp.bfloat16)
    terms = jnp.dot(attention, w_out, preferred_element_type=jnp.float32)
    return lax.psum_scatter(terms.astype(jnp.bfloat16), "head", scatter_dimension=1, tiled=True)


def packed_rows(place_ref, spots):
    start, early, half = place_ref[0], place_ref[1], place_ref[2]
    total = place_ref[3]
    before = jnp.where(spots < start, early, 1 - early)
    return spots + total * (half + before * (1 - 2 * half))


def clip_flags(rows, bounds_ref):
    begins, ends, leads = bounds_ref[0:1, :], bounds_ref[1:2, :], bounds_ref[2:3, :]
    inside = (rows >= begins) & (rows < ends)
    return inside, inside & (rows < leads)


def count_earlier(hot):
    ranks, rows, lanes = hot.shape
    flat = hot.reshape(ranks * rows, lanes).astype(jnp.bfloat16)

    def numbers(shape, axis):
        return lax.broadcasted_iota(jnp.int32, shape, axis)

    def group(index):
        return sum(jnp.where(index >= rows * k, 1, 0) for k in range(1, ranks))

    def ones(flags):
        return jnp.where(flags, 1.0, 0.0).astype(jnp.bfloat16)

    total = ranks * rows
    in_row = ones(numbers((lanes, lanes), 0) < numbers((lanes, lanes), 1))
    below, across = numbers((total, 1), 0), numbers((1, total), 1)
    in_rank = ones((group(below) == group(across)) & (across < below))
    row_sums = jnp.dot(
        flat, jnp.ones((lanes, lanes), jnp.bfloat16), preferred_element_type=jnp.float32
    )
    earlier = jnp.dot(flat, in_row, preferred_element_type=jnp.float32) + jnp.dot(
        in_rank, row_sums.astype(jnp.bfloat16), preferred_element_type=jnp.float32
    )
    return earlier.reshape(ranks, rows, lanes)


def table_kernel(ranks, indices, group_heads, place_ref, bounds_ref, rank_ref, w_ref, *refs):
    order_ref, runs_ref, query_ref, key_ref, weights_ref, held, sems = refs
    copies = weight_copies(place_ref, indices, group_heads, w_ref, weights_ref, sems)
    for copy in copies:
        copy.start()
    start, early, half, half_rows = (place_ref[k] for k in range(4))
    chip, clips, core, rank_here = (place_ref[k] for k in (4, 5, 8, 9))
    holds_long = half != early
    tokens = rank_ref[...]
    rows, lanes = tokens.shape
    per_dev = rows * lanes // ranks

    token = lanes * lax.broadcasted_iota(jnp.int32, tokens.shape, 0) + lax.broadcasted_iota(
        jnp.int32, tokens.shape, 1
    )
    hots = [jnp.where(tokens == rank, 1.0, 0.0) for rank in range(ranks)]
    earlier = count_earlier(jnp.stack(hots))
    within = sum(hots[rank] * earlier[rank] for rank in range(ranks))
    before = jnp.where(token < start, 1.0, 0.0)
    upto = jnp.where(token < start + half_rows, 1.0, 0.0)
    lane = lax.broadcasted_iota(jnp.int32, (1, lanes), 1)
    target = jnp.bitwise_xor(rank_here, 2 * jnp.bitwise_and(lane, 3))
    lane_long = jnp.where(lane < 4, jnp.where(holds_long, 1.0, 0.0), jnp.where(holds_long, 0.0, 1.0))
    lane_own = jnp.where(lane < 4, 1.0, 0.0)
    lows, longs, long_first, rest_first = [], [], [], []
    long_count, rest_count = [[0.0, 0.0], [0.0, 0.0]], [[0.0, 0.0], [0.0, 0.0]]
    for rank, hot in enumerate(hots):
        low = jnp.sum(hot * before, keepdims=True)
        long_rows = jnp.sum(hot * upto, keepdims=True) - low
        group, parity = rank // (ranks // 2), rank % 2
        lows.append(low)
        longs.append(long_rows)
        long_first.append(long_count[group][parity])
        rest_first.append(rest_count[group][parity])
        long_count[group][parity] = long_first[rank] + long_rows
        rest_count[group][parity] = rest_first[rank] + (per_dev - long_rows)
    long_base = rest_base = low_of = long_of = 0.0
    runs = [0.0] * 5
    for rank, hot in enumerate(hots):
        low, high, long_rows = lows[rank], lows[rank] + longs[rank], longs[rank]
        group, parity = rank // (ranks // 2), rank % 2
        own_group = jnp.where(half == group, 1.0, 0.0)
        long_after = own_group * long_count[1 - group][parity]
        rest_after = own_group * rest_count[1 - group][parity]
        long_base += hot * (long_first[rank] + long_after - low)
        rest_base += hot * (rest_first[rank] + rest_after)
        low_of += hot * low
        long_of += hot * long_rows
        first = long_first[rank] + lane_own * long_after
        rest = rest_first[rank] + lane_own * rest_after
        here = jnp.where(target == rank, 1.0, 0.0)
        values = (
            (0.0, low),
            (low, high),
            (high, float(per_dev)),
            (0.0, rest),
            (first - low, rest - long_rows),
        )
        runs = [
            run + here * (lane_long * if_long + (1.0 - lane_long) * if_rest)
            for run, (if_long, if_rest) in zip(runs, values)
        ]
    furthest = rows * lanes // 4 + per_dev // 2
    for index, run in enumerate(runs):
        run = run.astype(jnp.int32)
        runs_ref[index : index + 1, :] = (
            run if index < 3 else jnp.clip(run, -per_dev, furthest)
        )
    sorted_at = within + jnp.where(
        upto - before == 1.0, long_base, rest_base - jnp.where(within < low_of, 0.0, long_of)
    )
    held[...] = jnp.where(jnp.bitwise_and(tokens, 1) == core, sorted_at.astype(jnp.int32), -1)
    half_lines = rows // 2
    spots = lanes * lax.broadcasted_iota(
        jnp.int32, (half_lines, lanes), 0
    ) + lax.broadcasted_iota(jnp.int32, (half_lines, lanes), 1)
    later = packed_rows(place_ref, spots) >= half_rows
    held[:half_lines, :] = jnp.where(later, held[half_lines:, :], held[:half_lines, :])
    lines = half_lines // 4
    for d in range(4):
        line = lines * jnp.bitwise_xor(chip, d)
        order_ref[lines * d : lines * (d + 1), :] = held[pl.ds(line, lines), :]

    column = lax.broadcasted_iota(jnp.int32, (1, HEAD_DIM), 1)
    chip_rows = query_ref.shape[0] // 4
    for d in range(4):
        local = lax.broadcasted_iota(jnp.int32, (chip_rows, 1), 0)
        spots = chip_rows * jnp.bitwise_xor(chip, d) + local
        inside, leading = clip_flags(packed_rows(place_ref, spots), bounds_ref)
        spot = slice(d * chip_rows, (d + 1) * chip_rows)
        inside = jnp.where(inside, 1.0, 0.0)
        prefix = jnp.sum(jnp.where(leading, 1.0, 0.0), axis=1, keepdims=True)
        query_ref[spot, :] = jnp.where(column == clips, prefix, inside).astype(jnp.bfloat16)
        outside = jnp.where(column < clips, NEG * (1.0 - inside), 0.0)
        key_ref[spot, :] = jnp.where(column == clips, NEG * (1.0 - prefix), outside).astype(
            jnp.bfloat16
        )
    for copy in copies:
        copy.wait()


def make_tables(place, bounds, token_rank, ranks, keys, w_parts, indices, group_heads):
    vmem = pl.BlockSpec(memory_space=pltpu.VMEM)
    tokens = token_rank.reshape(-1, HEAD_DIM)
    features = jax.ShapeDtypeStruct((keys, HEAD_DIM), jnp.bfloat16)
    return pl.pallas_call(
        functools.partial(table_kernel, ranks, indices, group_heads),
        in_specs=[
            pl.BlockSpec(memory_space=pltpu.SMEM),
            vmem,
            vmem,
            pl.BlockSpec(memory_space=pltpu.HBM),
        ],
        out_specs=(vmem,) * 5,
        out_shape=(
            jax.ShapeDtypeStruct((tokens.shape[0] // 2, HEAD_DIM), jnp.int32),
            jax.ShapeDtypeStruct((8, HEAD_DIM), jnp.int32),
            features,
            features,
            weight_shape(w_parts, indices),
        ),
        scratch_shapes=[
            pltpu.VMEM(tokens.shape, jnp.int32),
            pltpu.SemaphoreType.DMA((3, COPY_PIECES)),
        ],
        compiler_params=pltpu.CompilerParams(vmem_limit_bytes=26 * MIB),
        cost_estimate=pl.CostEstimate(flops=COST, bytes_accessed=COST, transcendentals=0),
    )(place, bounds, tokens, w_parts)


def select_kernel(low, place_ref, own_ref, moved_ref, *rest):
    out_ref = rest[-1]
    spots = place_ref[7] + low + lax.broadcasted_iota(jnp.int32, (out_ref.shape[0], 1), 0)
    swapped = jnp.where(spots < place_ref[0], place_ref[1], 1 - place_ref[1])
    out_ref[...] = jnp.where(swapped == 1, moved_ref[...], own_ref[...])


def select_rows(place, own, moved, low, after):
    vmem = pl.BlockSpec(memory_space=pltpu.VMEM)
    return pl.pallas_call(
        functools.partial(select_kernel, low),
        in_specs=[pl.BlockSpec(memory_space=pltpu.SMEM), vmem, vmem]
        + [pl.BlockSpec(memory_space=pl.ANY)] * len(after),
        out_specs=vmem,
        out_shape=jax.ShapeDtypeStruct(moved.shape, moved.dtype),
        compiler_params=pltpu.CompilerParams(vmem_limit_bytes=8 * MIB),
        cost_estimate=pl.CostEstimate(flops=COST, bytes_accessed=COST, transcendentals=0),
    )(place, own, moved, *after)


def head_of(chip, index, group_heads):
    return 2 * group_heads * (chip // 2) + 2 * index + chip % 2


def weight_copies(place_ref, indices, group_heads, w_ref, out_ref, sems):
    pair = jnp.bitwise_xor(place_ref[4] // 2, place_ref[8])
    first = head_of(2 * pair, indices[0], group_heads)
    columns = pl.ds(pl.multiple_of(first * HEAD_DIM, HEAD_DIM), out_ref.shape[2])
    depth = out_ref.shape[1] // COPY_PIECES
    copies = []
    for part in range(3):
        for piece in range(COPY_PIECES):
            rows = slice(piece * depth, (piece + 1) * depth)
            copies.append(
                pltpu.make_async_copy(
                    w_ref.at[part, rows, columns], out_ref.at[part, rows, :], sems.at[part, piece]
                )
            )
    return copies


def weight_shape(w_parts, indices):
    return jax.ShapeDtypeStruct(
        (*w_parts.shape[:2], 2 * len(indices) * HEAD_DIM), w_parts.dtype
    )


def norm_kernel(place_ref, *refs):
    pieces = len(SWAP_ROWS)
    bounds_ref, noise_ref, level_ref, gain_ref = refs[2 * pieces : 2 * pieces + 4]
    out_ref = refs[-1]
    width = out_ref.shape[1] // 2
    side, first = place_ref[6], place_ref[7]
    clips, levels = noise_ref.shape[0], level_ref.shape[0]
    spots = [pl.ds(pl.multiple_of(s * width, 128), width) for s in (side, 1 - side)]
    level = lax.broadcasted_iota(jnp.int32, (clips, levels), 1)
    chosen = jnp.where(noise_ref[...] == level, 1.0, 0.0).astype(jnp.bfloat16)
    tables = [
        jnp.dot(chosen, level_ref[:, spot], preferred_element_type=jnp.float32).astype(
            jnp.bfloat16
        )
        for spot in spots
    ]
    low = 0
    for piece in range(pieces):
        own_ref, other_ref = refs[piece], refs[pieces + piece]
        count = own_ref.shape[0]
        rows = slice(low, low + count)
        places = first + low + lax.broadcasted_iota(jnp.int32, (count, 1), 0)
        low += count
        unused, leading = clip_flags(packed_rows(place_ref, places), bounds_ref)
        picks = jnp.where(leading, 1.0, 0.0)[:, :clips].astype(jnp.bfloat16)
        shifted = [
            ref[...].astype(jnp.float32)
            + jnp.dot(picks, table, preferred_element_type=jnp.float32)
            for ref, table in zip((own_ref, other_ref), tables)
        ]
        squares = sum(jnp.sum(part * part, axis=1, keepdims=True) for part in shifted)
        factor = lax.rsqrt(squares / (2 * width) + EPS)
        for part, spot in zip(shifted, spots):
            out_ref[rows, spot] = (part * factor * gain_ref[:, spot]).astype(jnp.bfloat16)


def normalize_rows(place, kept, other, bounds, noise_levels, level_table, norm_gain):
    rows, depth = sum(part.shape[0] for part in kept), 2 * kept[0].shape[1]
    vmem = pl.BlockSpec(memory_space=pltpu.VMEM)
    return pl.pallas_call(
        norm_kernel,
        in_specs=[pl.BlockSpec(memory_space=pltpu.SMEM)] + [vmem] * (2 * len(kept) + 4),
        out_specs=vmem,
        out_shape=jax.ShapeDtypeStruct((rows, depth), jnp.bfloat16),
        compiler_params=pltpu.CompilerParams(vmem_limit_bytes=26 * MIB),
        cost_estimate=pl.CostEstimate(flops=COST, bytes_accessed=COST, transcendentals=0),
    )(place, *kept, *other, bounds, noise_levels, level_table, norm_gain.reshape(1, -1))


def project_kernel(upcoming, group_heads, place_ref, own_ref, pair_ref, weights_ref, w_ref, *rest):
    copies = []
    if upcoming:
        first_ref, second_ref, next_ref, sems = rest[-4:]
        copies = weight_copies(place_ref, upcoming, group_heads, w_ref, next_ref, sems)
    else:
        first_ref, second_ref = rest[-2:]
    for copy in copies:
        copy.start()
    rows = jnp.concatenate([own_ref[...], pair_ref[...]], axis=0)
    count = own_ref.shape[0]
    same = place_ref[4] % 2 == place_ref[8]

    def store(outcome, base, even_ref, odd_ref):
        for index, core in enumerate((place_ref[8], 1 - place_ref[8])):
            spot = pl.ds(pl.multiple_of(core * count, count), count)
            half = outcome[index * count : (index + 1) * count]
            for part in range(3):
                to = slice(base + part * HEAD_DIM, base + (part + 1) * HEAD_DIM)
                even_ref[spot, to] = half[:, 2 * part * HEAD_DIM : (2 * part + 1) * HEAD_DIM]
                odd_ref[spot, to] = half[:, (2 * part + 1) * HEAD_DIM : 2 * (part + 1) * HEAD_DIM]

    for position in range(weights_ref.shape[2] // (2 * HEAD_DIM)):
        spot = slice(2 * position * HEAD_DIM, 2 * (position + 1) * HEAD_DIM)
        weights = jnp.concatenate([weights_ref[part, :, spot] for part in range(3)], axis=1)
        outcome = jnp.dot(rows, weights, preferred_element_type=jnp.float32).astype(jnp.bfloat16)
        base = 3 * position * HEAD_DIM

        @pl.when(same)
        def _():
            store(outcome, base, first_ref, second_ref)

        @pl.when(jnp.logical_not(same))
        def _():
            store(outcome, base, second_ref, first_ref)

    for copy in copies:
        copy.wait()


def project_heads(place, own, pair, weights, w_parts, upcoming, group_heads, after):
    rows = own.shape[0]
    vmem = pl.BlockSpec(memory_space=pltpu.VMEM)
    shape = jax.ShapeDtypeStruct((2 * rows, 3 * weights.shape[2] // 2), jnp.bfloat16)
    more = len(upcoming) > 0
    return pl.pallas_call(
        functools.partial(project_kernel, upcoming, group_heads),
        in_specs=[
            pl.BlockSpec(memory_space=pltpu.SMEM),
            vmem,
            vmem,
            vmem,
            pl.BlockSpec(memory_space=pltpu.HBM),
        ]
        + [pl.BlockSpec(memory_space=pl.ANY)] * len(after),
        out_specs=(vmem,) * (2 + more),
        out_shape=(shape, shape) + (weight_shape(w_parts, upcoming),) * more,
        scratch_shapes=[pltpu.SemaphoreType.DMA((3, COPY_PIECES))] * more,
        compiler_params=pltpu.CompilerParams(vmem_limit_bytes=26 * MIB),
        cost_estimate=pl.CostEstimate(flops=COST, bytes_accessed=COST, transcendentals=0),
    )(place, own, pair, weights, w_parts, *after)


def attend_kernel(base, place_ref, runs_ref, *refs):
    mine, near, far, pair_first, pair_far, pair_near = refs[:6]
    order_ref, query_mask_ref, key_mask_ref = refs[6:9]
    stay_ref, cross_ref, more_ref, q_all, k_all, v_all, sorted_out = refs[-7:]
    chip_rows = mine.shape[0]
    rows = chip_rows // 2
    queries = sorted_out.shape[0] - 2 * rows

    def hold(sources):
        for index, source in enumerate(sources):
            spot = slice(index * chip_rows, (index + 1) * chip_rows)
            for part, held in enumerate((q_all, k_all, v_all)):
                low = base + part * HEAD_DIM
                held[spot, :HEAD_DIM] = source[:, low : low + HEAD_DIM]

    @pl.when(place_ref[8] == 0)
    def _():
        hold((mine, near, pair_near, pair_far))

    @pl.when(place_ref[8] == 1)
    def _():
        hold((pair_first, pair_near, near, far))

    q_all[:, HEAD_DIM:] = query_mask_ref[...]
    k_all[:, HEAD_DIM:] = key_mask_ref[...]
    v_all[:, HEAD_DIM:] = jnp.ones((4 * chip_rows, HEAD_DIM), jnp.bfloat16)
    tile = queries // ATTEND_TILES

    def score(step):
        wanted = step * tile + lax.broadcasted_iota(jnp.int32, (tile, 1), 0)
        picks = jnp.concatenate(
            [
                jnp.where(order_ref[line : line + 1, :] == wanted, 1.0, 0.0).astype(jnp.bfloat16)
                for line in range(order_ref.shape[0])
            ],
            axis=1,
        )
        sorted_queries = jnp.dot(picks, q_all[...], preferred_element_type=jnp.float32)
        return lax.dot_general(
            sorted_queries.astype(jnp.bfloat16),
            k_all[...],
            (((1,), (1,)), ((), ())),
            preferred_element_type=jnp.float32,
        )

    coming = score(0)
    for step in range(ATTEND_TILES):
        scores = coming
        if step + 1 < ATTEND_TILES:
            coming = score(step + 1)
        top = jnp.max(scores, axis=1, keepdims=True)
        weights = jnp.exp2((scores - top) * (HEAD_DIM ** (-0.5) * LOG2E))
        summed = jnp.dot(
            weights.astype(jnp.bfloat16), v_all[...], preferred_element_type=jnp.float32
        )
        sorted_out[rows + step * tile : rows + (step + 1) * tile, :] = (
            summed[:, :HEAD_DIM] / summed[:, HEAD_DIM:]
        )

    low = rows
    for ref in (cross_ref, more_ref):
        ref[...] = sorted_out[low : low + ref.shape[0], :].astype(jnp.bfloat16)
        low += ref.shape[0]
    for d in range(4):
        stay_ref[d] = spread_run(sorted_out, runs_ref, d, rows).astype(jnp.bfloat16)


def spread_run(sorted_ref, runs_ref, lane, rows):
    furthest = sorted_ref.shape[0] - 2 * rows
    row = lax.broadcasted_iota(jnp.int32, (rows, 1), 0)
    parts = [
        sorted_ref[pl.ds(rows + jnp.clip(runs_ref[line, lane], -rows, furthest), rows), :]
        for line in (3, 4)
    ]
    in_second = (row >= runs_ref[1, lane]) & (row < runs_ref[2, lane])
    return jnp.where(row < runs_ref[0, lane], parts[0], jnp.where(in_second, parts[1], 0.0))


def attend(place, runs, blocks, position, order, query_mask, key_mask, after):
    chip_rows = blocks[0].shape[0]
    rows, keys = chip_rows // 2, 4 * chip_rows
    queries = keys // 2 + rows // 2
    vmem, smem = pl.BlockSpec(memory_space=pltpu.VMEM), pl.BlockSpec(memory_space=pltpu.SMEM)
    shape = jax.ShapeDtypeStruct((4, rows, HEAD_DIM), jnp.bfloat16)
    return pl.pallas_call(
        functools.partial(attend_kernel, 3 * position * HEAD_DIM),
        in_specs=[smem, smem]
        + [vmem] * (len(blocks) + 3)
        + [pl.BlockSpec(memory_space=pl.ANY)] * len(after),
        out_specs=(vmem, vmem, vmem),
        out_shape=(shape,)
        + tuple(
            jax.ShapeDtypeStruct((count, HEAD_DIM), jnp.bfloat16)
            for count in (PACKED_ROWS, queries - PACKED_ROWS)
        ),
        scratch_shapes=[
            pltpu.VMEM((keys, 2 * HEAD_DIM), jnp.bfloat16),
            pltpu.VMEM((keys, 2 * HEAD_DIM), jnp.bfloat16),
            pltpu.VMEM((keys, 2 * HEAD_DIM), jnp.bfloat16),
            pltpu.VMEM((queries + 2 * rows, HEAD_DIM), jnp.float32),
        ],
        compiler_params=pltpu.CompilerParams(vmem_limit_bytes=32 * MIB),
        cost_estimate=pl.CostEstimate(
            flops=COST, bytes_accessed=COST, transcendentals=0
        ),
    )(place, runs, *blocks, order, query_mask, key_mask, *after)


def join_kernel(heads, runs_ref, *refs):
    outs, held = refs[-5:-1], refs[-1]
    rows = outs[0].shape[0]
    for head in range(heads):
        stay_ref, low = refs[3 * head], rows
        for ref in refs[3 * head + 1 : 3 * head + 3]:
            held[low : low + ref.shape[0], :] = ref[...].astype(jnp.float32)
            low += ref.shape[0]
        spot = slice(head * HEAD_DIM, (head + 1) * HEAD_DIM)
        for d in range(4):
            arrived = spread_run(held, runs_ref, 4 + d, rows).astype(jnp.bfloat16)
            outs[d][:, spot] = stay_ref[d] + arrived


def join_halves(runs, stays, arrivals, others, after, cost):
    heads, (slots, rows, width) = len(stays), stays[0].shape
    vmem = pl.BlockSpec(memory_space=pltpu.VMEM)
    parts = [part for three in zip(stays, arrivals, others) for part in three]
    shape = jax.ShapeDtypeStruct((rows, heads * width), jnp.bfloat16)
    return pl.pallas_call(
        functools.partial(join_kernel, heads),
        in_specs=[pl.BlockSpec(memory_space=pltpu.SMEM)]
        + [vmem] * len(parts)
        + [pl.BlockSpec(memory_space=pl.ANY)] * len(after),
        out_specs=(vmem,) * slots,
        out_shape=(shape,) * slots,
        scratch_shapes=[
            pltpu.VMEM((arrivals[0].shape[0] + others[0].shape[0] + 2 * rows, width), jnp.float32)
        ],
        compiler_params=pltpu.CompilerParams(vmem_limit_bytes=16 * MIB),
        cost_estimate=pl.CostEstimate(flops=cost, bytes_accessed=COST, transcendentals=0),
    )(runs, *parts, *after)


def gather_kernel(first_heads, last_heads, place_ref, w_ref, held_ref, pair_ref, *rest):
    own_first, own_last, far_first, far_last, sems = rest[-5:]
    chip, columns = place_ref[4], own_first.shape[1]
    heads = w_ref.shape[0] // HEAD_DIM // 4
    spot = pl.ds(pl.multiple_of(place_ref[6] * columns, HEAD_DIM), columns)

    def rows_at(block):
        return pl.ds(pl.multiple_of(block * HEAD_DIM, HEAD_DIM), HEAD_DIM)

    def transfers(near_ref, far_ref):
        copies = []
        for indices, own, far in ((first_heads, own_first, far_first), (last_heads, own_last, far_last)):
            for d in range(4):
                for position, index in enumerate(indices):
                    head = head_of(jnp.bitwise_xor(chip, d), index, heads)
                    there = 2 * index + jnp.bitwise_xor(chip, d) % 2
                    to = slice(
                        (len(indices) * d + position) * HEAD_DIM,
                        (len(indices) * d + position + 1) * HEAD_DIM,
                    )
                    source = near_ref if d < 2 else far_ref
                    slot = heads * d + index
                    copies.append(
                        pltpu.make_async_copy(
                            w_ref.at[rows_at(head), spot], own.at[to, :], sems.at[0, slot]
                        )
                    )
                    copies.append(
                        pltpu.make_async_copy(
                            source.at[rows_at(there), :], far.at[to, :], sems.at[1, slot]
                        )
                    )
        for copy in copies:
            copy.start()
        for copy in copies:
            copy.wait()

    @pl.when(chip // 2 == place_ref[8])
    def _():
        transfers(held_ref, pair_ref)

    @pl.when(chip // 2 != place_ref[8])
    def _():
        transfers(pair_ref, held_ref)


def gather_out_weights(place, w_out, held, pair, first_heads, last_heads, after):
    columns = w_out.shape[1] // 2
    vmem, hbm = pl.BlockSpec(memory_space=pltpu.VMEM), pl.BlockSpec(memory_space=pltpu.HBM)
    any_space = pl.BlockSpec(memory_space=pl.ANY)
    shapes = [
        jax.ShapeDtypeStruct((4 * len(indices) * HEAD_DIM, columns), w_out.dtype)
        for indices in (first_heads, last_heads)
    ]
    return pl.pallas_call(
        functools.partial(gather_kernel, first_heads, last_heads),
        in_specs=[pl.BlockSpec(memory_space=pltpu.SMEM), hbm]
        + [any_space] * (2 + len(after)),
        out_specs=(vmem,) * 4,
        out_shape=(*shapes, *shapes),
        scratch_shapes=[pltpu.SemaphoreType.DMA((2, w_out.shape[0] // HEAD_DIM))],
        compiler_params=pltpu.CompilerParams(vmem_limit_bytes=16 * MIB),
        cost_estimate=pl.CostEstimate(flops=COST, bytes_accessed=COST, transcendentals=0),
    )(place, w_out, held, pair, *after)


def out_rows_kernel(*refs):
    refs[-1][...] = jnp.concatenate([ref[...] for ref in refs[:-1]], axis=1)


def out_kernel(rows_ref, weights_ref, *refs):
    product = jnp.dot(rows_ref[...], weights_ref[...], preferred_element_type=jnp.float32)
    if len(refs) > 1:
        product = refs[0][...] + product
    refs[-1][...] = product.astype(refs[-1].dtype)


def out_call(kernel, arrays, shape, dtype):
    vmem = pl.BlockSpec(memory_space=pltpu.VMEM)
    return pl.pallas_call(
        kernel,
        in_specs=[vmem] * len(arrays),
        out_specs=vmem,
        out_shape=jax.ShapeDtypeStruct(shape, dtype),
        compiler_params=pltpu.CompilerParams(vmem_limit_bytes=16 * MIB),
        cost_estimate=pl.CostEstimate(flops=COST, bytes_accessed=COST, transcendentals=0),
    )(*arrays)


SWAP_ROWS = (112, 112, 96)
PACKED_ROWS = 768
ATTEND_TILES = 3
HEAD_CHUNKS = ((0,), (1, 2))
COPY_PIECES = 4


def halved_body(
    inputs,
    norm_gain,
    level_table,
    w_qkv,
    w_out,
    clip_lengths,
    prefix_lengths,
    noise_levels,
    token_rank,
):
    ranks, per_dev = 16, inputs.shape[0]
    half_rows = 8 * per_dev
    clips = clip_lengths.shape[0]
    index = jnp.arange(clips, dtype=jnp.int32)

    ahead = (index[None, :] < index[:, None]) & (clip_lengths == MAXCLIP)[:, None]
    start = jnp.sum(jnp.where(ahead, clip_lengths[None, :], 0))
    early = start <= half_rows // 2

    rank_here = lax.axis_index("ctx")
    side = lax.axis_index("head")
    columns = inputs.shape[1]
    group_heads = w_qkv.shape[2] // HEAD_DIM // 4
    half, block, core = rank_here // 8, rank_here % 8, rank_here % 2
    chip = block // 2
    swap_sides = [(0, 1), (1, 0)]

    def exchange(array, flip, only=lambda r: True):
        pairs = [(r, r ^ flip) for r in range(ranks) if only(r)]
        return lax.ppermute(array, "ctx", pairs)

    def move_rows(swapping):
        return functools.partial(moved_rows, swapping)

    def moved_rows(
        swapping, start, inputs, clip_lengths, prefix_lengths, noise_levels, w_out
    ):
        place = jnp.stack(
            [
                start,
                jnp.int32(1 if 0 in swapping else 0),
                half,
                jnp.int32(half_rows),
                chip,
                jnp.int32(clips),
                side,
                block * per_dev,
                core,
                rank_here,
            ]
        )
        earlier = index[None, :] < index[:, None]
        begins = jnp.sum(jnp.where(earlier, clip_lengths[None, :], 0), axis=1)
        leads = begins + jnp.minimum(prefix_lengths, clip_lengths)
        bounds = jnp.pad(
            jnp.stack([begins, begins + clip_lengths, leads]), ((0, 5), (0, HEAD_DIM - clips))
        )

        cuts = [sum(SWAP_ROWS[:i]) for i in range(len(SWAP_ROWS) + 1)]
        kept = []
        for low, high in zip(cuts[:-1], cuts[1:]):
            own = inputs[low:high]
            sent = own
            if len(kept) > 0 and high == per_dev:
                sent, unused = lax.optimization_barrier((own, kept[0]))
            moved = exchange(sent, 8, lambda r: r % 8 in swapping)
            kept.append(select_rows(place, own, moved, low, kept[-1:]))
        other = [lax.ppermute(part, "head", swap_sides) for part in kept]
        depth = w_out.shape[0] // 2
        sent = lax.dynamic_slice(w_out, (core * depth, (1 - side) * columns), (depth, columns))
        return tuple(kept), tuple(other), place, bounds, noise_levels.reshape(-1, 1), sent

    kept, other, place, bounds, noise_column, sent = lax.cond(
        early,
        move_rows(range(4)),
        move_rows(range(4, 8)),
        start,
        inputs,
        clip_lengths,
        prefix_lengths,
        noise_levels,
        w_out,
    )
    far_held = lax.ppermute(sent, "head", swap_sides)
    normed = normalize_rows(place, kept, other, bounds, noise_column, level_table, norm_gain)
    pair = exchange(normed, 1)
    w_parts = jnp.transpose(w_qkv, (1, 0, 2))
    query_order, runs, query_mask, key_mask, weights = make_tables(
        place, bounds, token_rank, ranks, half_rows, w_parts, HEAD_CHUNKS[0], group_heads
    )

    blocks, after = [], []
    for upcoming in (*HEAD_CHUNKS[1:], ()):
        first, second, *more = project_heads(
            place, normed, pair, weights, w_parts, upcoming, group_heads, after
        )
        weights = more[0] if more else None
        near = lax.ppermute(
            second, "ctx", [(r, r ^ (2 if r % 2 == 0 else 4)) for r in range(ranks)]
        )
        far = exchange(first, 6, lambda r: r % 2 == 1)
        blocks.append((first, near, far))
        if not after:
            after = [exchange(first, 1, lambda r: r % 2 == 0)]
    pair_firsts = [after[0]]

    def share(block, after):
        first, near, far = block
        near, far, *unused = lax.optimization_barrier((near, far, *after))
        if len(pair_firsts) == 0:
            first_after, *unused = lax.optimization_barrier((first, *after))
            pair_firsts.append(exchange(first_after, 1, lambda r: r % 2 == 0))
        return [
            first,
            near,
            far,
            pair_firsts.pop(),
            exchange(far, 1, lambda r: r % 2 == 1),
            exchange(near, 1),
        ]

    stays, arrivals, others, after = [], [], [], [blocks[-1][0]]
    for block, heads in zip(blocks, HEAD_CHUNKS):
        block = share(block, after)
        for position, head in enumerate(heads):
            stay, cross, more = attend(
                place, runs, block, position, query_order, query_mask, key_mask, after
            )
            stays.append(stay)
            arrivals.append(exchange(cross, 8))
            others.append(more)
            after = [cross] + (arrivals[head - 1 : head] if head else [])

    row = jnp.arange(ranks * per_dev, dtype=jnp.int32)
    in_long = (row >= start) & (row < start + half_rows)
    home = jnp.where(in_long == early, 0, 1)
    crosses = token_rank // (ranks // 2) != home
    kind = jnp.where(crosses, 2 * home + token_rank % 2, 4)
    counts = jnp.sum((kind[:, None] == jnp.arange(4)[None, :]).astype(jnp.int32), axis=0)
    fits = jnp.max(counts) <= PACKED_ROWS
    others = lax.cond(
        fits, lambda parts: parts, lambda parts: tuple(exchange(p, 8) for p in parts), tuple(others)
    )

    first_heads, last_head = list(range(group_heads - 1)), [group_heads - 1]

    def across(heads, after, cost):
        joined = join_halves(runs, stays[heads], arrivals[heads], others[heads], after, cost)
        pieces = [exchange(part, 2 * d) if d else part for d, part in enumerate(joined)]
        width = sum(piece.shape[1] for piece in pieces)
        rows = out_call(out_rows_kernel, pieces, (per_dev, width), jnp.bfloat16)
        return rows, lax.ppermute(rows, "head", swap_sides)

    first_rows, first_far = across(slice(0, -1), [cross], COST)
    far_pair = exchange(lax.optimization_barrier((far_held, first_rows))[0], 1)
    w_first, w_last, w_far_first, w_far_last = gather_out_weights(
        place, w_out, far_held, far_pair, first_heads, last_head, [first_rows]
    )
    last_rows, last_far = across(slice(-1, None), [], LONG_COST)
    shape = (per_dev, columns)
    total = out_call(out_kernel, [first_rows, w_first], shape, jnp.float32)
    total = out_call(out_kernel, [last_rows, w_last, total], shape, jnp.float32)
    total = out_call(out_kernel, [first_far, w_far_first, total], shape, jnp.float32)
    return out_call(out_kernel, [last_far, w_far_last, total], shape, jnp.bfloat16)


def solution(mesh):
    in_specs = (
        P("ctx", "head"),
        P(),
        P(),
        P(None, None, "head"),
        P("head", None),
        P(),
        P(),
        P(),
        P(),
    )
    out_specs = P("ctx", "head")

    def body(inputs, norm_gain, level_table, w_qkv, *rest):
        ranks, sides = mesh.shape["ctx"], mesh.shape["head"]
        heads_here = w_qkv.shape[2] // HEAD_DIM
        halved = (
            ranks == 16
            and sides == 2
            and ranks * inputs.shape[0] == 2 * MAXCLIP
            and heads_here == 4 * sum(len(heads) for heads in HEAD_CHUNKS)
        )
        run = halved_body if halved else gathered_body
        return run(inputs, norm_gain, level_table, w_qkv, *rest)

    return jax.shard_map(body, mesh=mesh, in_specs=in_specs, out_specs=out_specs, check_vma=False)
```

```python
import functools

import jax
import jax.numpy as jnp
from jax import lax
from jax.experimental import pallas as pl
from jax.experimental.pallas import tpu as pltpu
from jax.sharding import PartitionSpec as P

HEAD_DIM = 128


NEG = -1e30
EPS = 1e-06
MAXCLIP = 2560
LOG2E = 1.4426950408889634
MIB = 1024 * 1024
COST = 1000000
LONG_COST = 200000000000


def clip_tables(total_rows, clip_lengths, prefix_lengths, noise_levels):
    rows = jnp.arange(total_rows, dtype=jnp.int32)
    ends = jnp.cumsum(clip_lengths)
    begins = ends - clip_lengths
    clip_of = jnp.sum((rows[:, None] >= ends[None, :]).astype(jnp.int32), axis=1)
    member = clip_of[:, None] == jnp.arange(clip_lengths.shape[0], dtype=jnp.int32)[None, :]
    begin_row = jnp.sum(jnp.where(member, begins[None, :], 0), axis=1)
    lead = jnp.minimum(prefix_lengths, clip_lengths)
    lead_row = jnp.sum(jnp.where(member, lead[None, :], 0), axis=1)
    level_row = jnp.sum(jnp.where(member, noise_levels[None, :], 0), axis=1)
    in_prefix = rows - begin_row < lead_row
    return (clip_of, in_prefix, level_row)


def rank_tables(token_rank, ranks, per_rank):
    onehot = (token_rank[:, None] == jnp.arange(ranks, dtype=jnp.int32)[None, :]).astype(jnp.int32)
    earlier = jnp.cumsum(onehot, axis=0) - onehot
    within = jnp.sum(earlier * onehot, axis=1)
    counts = jnp.sum(onehot.reshape(ranks, per_rank, ranks), axis=1)
    starts = jnp.cumsum(counts, axis=0) - counts
    return (within, counts, starts)


def normalize(rows, in_prefix, level_row, level_table, norm_gain):
    picks = (
        level_row[:, None] == jnp.arange(level_table.shape[0], dtype=jnp.int32)[None, :]
    ) & in_prefix[:, None]
    added = jnp.dot(picks.astype(jnp.bfloat16), level_table, preferred_element_type=jnp.float32)
    shifted = rows.astype(jnp.float32) + added
    factor = lax.rsqrt(jnp.mean(shifted * shifted, axis=-1, keepdims=True) + EPS)
    return (shifted * factor * norm_gain).astype(jnp.bfloat16)


def fold_keys(state, queries, query_clip, query_prefix, pairs, key_clip, key_prefix):
    width = queries.shape[1]
    heads_here = width // HEAD_DIM
    factor = HEAD_DIM ** (-0.5)
    allowed_query = jnp.logical_not(query_prefix)

    def absorb(carry, block):
        block_pairs, block_clip, block_prefix = block
        allowed = (query_clip[:, None] == block_clip[None, :]) & (
            allowed_query[:, None] | block_prefix[None, :]
        )
        updated = []
        for head in range(heads_here):
            top, total, summed = carry[head]
            low = head * HEAD_DIM
            q_head = queries[:, low : low + HEAD_DIM]
            k_head = block_pairs[:, low : low + HEAD_DIM]
            v_head = block_pairs[:, width + low : width + low + HEAD_DIM]
            scores = (
                lax.dot_general(
                    q_head, k_head, (((1,), (1,)), ((), ())), preferred_element_type=jnp.float32
                )
                * factor
            )
            masked = jnp.where(allowed, scores, NEG)
            new_top = jnp.maximum(top, jnp.max(masked, axis=1, keepdims=True))
            fade = jnp.exp(top - new_top)
            weights = jnp.where(allowed, jnp.exp(scores - new_top), 0.0)
            total = total * fade + jnp.sum(weights, axis=1, keepdims=True)
            summed = summed * fade + jnp.dot(
                weights.astype(jnp.bfloat16), v_head, preferred_element_type=jnp.float32
            )
            updated.append((new_top, total, summed))
        return (tuple(updated), None)

    count = pairs.shape[0]
    step = 2048 if count > 2048 and count % 2048 == 0 else count
    if step == count:
        result, unused = absorb(state, (pairs, key_clip, key_prefix))
        return result
    stacked = (
        pairs.reshape(count // step, step, pairs.shape[1]),
        key_clip.reshape(count // step, step),
        key_prefix.reshape(count // step, step),
    )
    result, unused = lax.scan(absorb, state, stacked)
    return result


def gathered_body(
    inputs,
    norm_gain,
    level_table,
    w_qkv,
    w_out,
    clip_lengths,
    prefix_lengths,
    noise_levels,
    token_rank,
):
    ranks = lax.axis_size("ctx")
    rank_here = lax.axis_index("ctx")
    per_dev = inputs.shape[0]
    slots = 2 * per_dev // ranks
    local_width = w_qkv.shape[2]
    heads_here = local_width // HEAD_DIM
    total_rows = per_dev * ranks
    clip_of, in_prefix, level_row = clip_tables(
        total_rows, clip_lengths, prefix_lengths, noise_levels
    )
    within, counts, starts = rank_tables(token_rank, ranks, per_dev)
    place = token_rank * per_dev + within
    order = (
        jnp.zeros((total_rows,), jnp.int32).at[place].set(jnp.arange(total_rows, dtype=jnp.int32))
    )
    first = rank_here * per_dev
    own_rank = lax.dynamic_slice_in_dim(token_rank, first, per_dev, 0)
    own_within = lax.dynamic_slice_in_dim(within, first, per_dev, 0)
    send_starts = lax.dynamic_slice_in_dim(starts, rank_here, 1, 0)[0]
    recv_counts = lax.dynamic_slice_in_dim(counts, rank_here, 1, 1)[:, 0]
    recv_starts = lax.dynamic_slice_in_dim(starts, rank_here, 1, 1)[:, 0]
    balanced_rows = lax.dynamic_slice_in_dim(order, first, per_dev, 0)
    target = own_rank * slots + own_within - send_starts[own_rank]
    buffer = jnp.zeros((ranks * slots, inputs.shape[1]), inputs.dtype).at[target].set(inputs)
    received = lax.all_to_all(
        buffer.reshape(ranks, slots, inputs.shape[1]),
        "ctx",
        split_axis=0,
        concat_axis=0,
        tiled=True,
    )
    spots = jnp.arange(slots, dtype=jnp.int32)[None, :]
    index = jnp.where(spots < recv_counts[:, None], recv_starts[:, None] + spots, per_dev).reshape(
        -1
    )
    flat = received.reshape(ranks * slots, received.shape[2])
    rows = jnp.zeros((per_dev, received.shape[2]), received.dtype).at[index].set(flat, mode="drop")
    full_rows = lax.all_gather(rows, "head", axis=1, tiled=True)
    normed = normalize(
        full_rows, in_prefix[balanced_rows], level_row[balanced_rows], level_table, norm_gain
    )
    qkv = jnp.dot(
        normed, w_qkv.reshape(w_qkv.shape[0], 3 * local_width), preferred_element_type=jnp.float32
    ).astype(jnp.bfloat16)
    start_state = tuple(
        (
            (
                jnp.full((per_dev, 1), NEG, jnp.float32),
                jnp.zeros((per_dev, 1), jnp.float32),
                jnp.zeros((per_dev, HEAD_DIM), jnp.float32),
            )
            for head in range(heads_here)
        )
    )
    key_clip = clip_of[order]
    key_prefix = in_prefix[order]
    query_clip = lax.dynamic_slice_in_dim(key_clip, first, per_dev, 0)
    query_prefix = lax.dynamic_slice_in_dim(key_prefix, first, per_dev, 0)
    queries = qkv[:, :local_width]
    pairs = qkv[:, local_width:]
    state = fold_keys(
        start_state,
        queries,
        query_clip,
        query_prefix,
        lax.all_gather(pairs, "ctx", axis=0, tiled=True),
        key_clip,
        key_prefix,
    )
    parts = [state[head][2] / state[head][1] for head in range(heads_here)]
    attention = jnp.concatenate(parts, axis=1).astype(jnp.bfloat16)
    terms = jnp.dot(attention, w_out, preferred_element_type=jnp.float32)
    return lax.psum_scatter(terms.astype(jnp.bfloat16), "head", scatter_dimension=1, tiled=True)


def packed_rows(place_ref, spots):
    start, early, half = place_ref[0], place_ref[1], place_ref[2]
    total = place_ref[3]
    before = jnp.where(spots < start, early, 1 - early)
    return spots + total * (half + before * (1 - 2 * half))


def clip_flags(rows, bounds_ref):
    begins, ends, leads = bounds_ref[0:1, :], bounds_ref[1:2, :], bounds_ref[2:3, :]
    inside = (rows >= begins) & (rows < ends)
    return inside, inside & (rows < leads)


def count_earlier(hot):
    ranks, rows, lanes = hot.shape
    flat = hot.reshape(ranks * rows, lanes).astype(jnp.bfloat16)

    def numbers(shape, axis):
        return lax.broadcasted_iota(jnp.int32, shape, axis)

    def group(index):
        return sum(jnp.where(index >= rows * k, 1, 0) for k in range(1, ranks))

    def ones(flags):
        return jnp.where(flags, 1.0, 0.0).astype(jnp.bfloat16)

    total = ranks * rows
    in_row = ones(numbers((lanes, lanes), 0) < numbers((lanes, lanes), 1))
    below, across = numbers((total, 1), 0), numbers((1, total), 1)
    in_rank = ones((group(below) == group(across)) & (across < below))
    row_sums = jnp.dot(
        flat, jnp.ones((lanes, lanes), jnp.bfloat16), preferred_element_type=jnp.float32
    )
    earlier = jnp.dot(flat, in_row, preferred_element_type=jnp.float32) + jnp.dot(
        in_rank, row_sums.astype(jnp.bfloat16), preferred_element_type=jnp.float32
    )
    return earlier.reshape(ranks, rows, lanes)


def table_kernel(ranks, place_ref, bounds_ref, rank_ref, w_ref, *refs):
    order_ref, runs_ref, query_ref, key_ref, weights_ref, held, sems = refs
    copies = weight_copies(place_ref, w_ref, weights_ref, sems)
    for copy in copies:
        copy.start()
    start, early, half, half_rows = (place_ref[k] for k in range(4))
    chip, clips, core, rank_here = (place_ref[k] for k in (4, 5, 8, 9))
    holds_long = half != early
    tokens = rank_ref[...]
    rows, lanes = tokens.shape
    per_dev = rows * lanes // ranks

    token = lanes * lax.broadcasted_iota(jnp.int32, tokens.shape, 0) + lax.broadcasted_iota(
        jnp.int32, tokens.shape, 1
    )
    hots = [jnp.where(tokens == rank, 1.0, 0.0) for rank in range(ranks)]
    earlier = count_earlier(jnp.stack(hots))
    within = sum(hots[rank] * earlier[rank] for rank in range(ranks))
    before = jnp.where(token < start, 1.0, 0.0)
    upto = jnp.where(token < start + half_rows, 1.0, 0.0)
    lane = lax.broadcasted_iota(jnp.int32, (1, lanes), 1)
    target = jnp.bitwise_xor(rank_here, 2 * jnp.bitwise_and(lane, 3))
    lane_long = jnp.where(lane < 4, jnp.where(holds_long, 1.0, 0.0), jnp.where(holds_long, 0.0, 1.0))
    lane_own = jnp.where(lane < 4, 1.0, 0.0)
    lows, longs, long_first, rest_first = [], [], [], []
    long_count, rest_count = [[0.0, 0.0], [0.0, 0.0]], [[0.0, 0.0], [0.0, 0.0]]
    for rank, hot in enumerate(hots):
        low = jnp.sum(hot * before, keepdims=True)
        long_rows = jnp.sum(hot * upto, keepdims=True) - low
        group, parity = rank // (ranks // 2), rank % 2
        lows.append(low)
        longs.append(long_rows)
        long_first.append(long_count[group][parity])
        rest_first.append(rest_count[group][parity])
        long_count[group][parity] = long_first[rank] + long_rows
        rest_count[group][parity] = rest_first[rank] + (per_dev - long_rows)
    long_base = rest_base = low_of = long_of = 0.0
    runs = [0.0] * 5
    for rank, hot in enumerate(hots):
        low, high, long_rows = lows[rank], lows[rank] + longs[rank], longs[rank]
        group, parity = rank // (ranks // 2), rank % 2
        own_group = jnp.where(half == group, 1.0, 0.0)
        long_after = own_group * long_count[1 - group][parity]
        rest_after = own_group * rest_count[1 - group][parity]
        long_base += hot * (long_first[rank] + long_after - low)
        rest_base += hot * (rest_first[rank] + rest_after)
        low_of += hot * low
        long_of += hot * long_rows
        first = long_first[rank] + lane_own * long_after
        rest = rest_first[rank] + lane_own * rest_after
        here = jnp.where(target == rank, 1.0, 0.0)
        values = (
            (0.0, low),
            (low, high),
            (high, float(per_dev)),
            (0.0, rest),
            (first - low, rest - long_rows),
        )
        runs = [
            run + here * (lane_long * if_long + (1.0 - lane_long) * if_rest)
            for run, (if_long, if_rest) in zip(runs, values)
        ]
    furthest = rows * lanes // 4 + per_dev // 2
    for index, run in enumerate(runs):
        run = run.astype(jnp.int32)
        runs_ref[index : index + 1, :] = (
            run if index < 3 else jnp.clip(run, -per_dev, furthest)
        )
    sorted_at = within + jnp.where(
        upto - before == 1.0, long_base, rest_base - jnp.where(within < low_of, 0.0, long_of)
    )
    held[...] = jnp.where(jnp.bitwise_and(tokens, 1) == core, sorted_at.astype(jnp.int32), -1)
    half_lines = rows // 2
    spots = lanes * lax.broadcasted_iota(
        jnp.int32, (half_lines, lanes), 0
    ) + lax.broadcasted_iota(jnp.int32, (half_lines, lanes), 1)
    later = packed_rows(place_ref, spots) >= half_rows
    held[:half_lines, :] = jnp.where(later, held[half_lines:, :], held[:half_lines, :])
    lines = half_lines // 4
    for d in range(4):
        line = lines * jnp.bitwise_xor(chip, d)
        order_ref[lines * d : lines * (d + 1), :] = held[pl.ds(line, lines), :]

    column = lax.broadcasted_iota(jnp.int32, (1, HEAD_DIM), 1)
    chip_rows = query_ref.shape[0] // 4
    for d in range(4):
        local = lax.broadcasted_iota(jnp.int32, (chip_rows, 1), 0)
        spots = chip_rows * jnp.bitwise_xor(chip, d) + local
        inside, leading = clip_flags(packed_rows(place_ref, spots), bounds_ref)
        spot = slice(d * chip_rows, (d + 1) * chip_rows)
        inside = jnp.where(inside, 1.0, 0.0)
        prefix = jnp.sum(jnp.where(leading, 1.0, 0.0), axis=1, keepdims=True)
        query_ref[spot, :] = jnp.where(column == clips, prefix, inside).astype(jnp.bfloat16)
        outside = jnp.where(column < clips, NEG * (1.0 - inside), 0.0)
        key_ref[spot, :] = jnp.where(column == clips, NEG * (1.0 - prefix), outside).astype(
            jnp.bfloat16
        )
    for copy in copies:
        copy.wait()


def make_tables(place, bounds, token_rank, ranks, keys, w_parts):
    vmem = pl.BlockSpec(memory_space=pltpu.VMEM)
    tokens = token_rank.reshape(-1, HEAD_DIM)
    features = jax.ShapeDtypeStruct((keys, HEAD_DIM), jnp.bfloat16)
    return pl.pallas_call(
        functools.partial(table_kernel, ranks),
        in_specs=[
            pl.BlockSpec(memory_space=pltpu.SMEM),
            vmem,
            vmem,
            pl.BlockSpec(memory_space=pltpu.HBM),
        ],
        out_specs=(vmem,) * 5,
        out_shape=(
            jax.ShapeDtypeStruct((tokens.shape[0] // 2, HEAD_DIM), jnp.int32),
            jax.ShapeDtypeStruct((8, HEAD_DIM), jnp.int32),
            features,
            features,
            jax.ShapeDtypeStruct((*w_parts.shape[:2], w_parts.shape[2] // 2), w_parts.dtype),
        ),
        scratch_shapes=[
            pltpu.VMEM(tokens.shape, jnp.int32),
            pltpu.SemaphoreType.DMA((3, COPY_PIECES)),
        ],
        compiler_params=pltpu.CompilerParams(vmem_limit_bytes=26 * MIB),
        cost_estimate=pl.CostEstimate(flops=COST, bytes_accessed=COST, transcendentals=0),
    )(place, bounds, tokens, w_parts)


def select_kernel(low, place_ref, own_ref, moved_ref, *rest):
    out_ref = rest[-1]
    spots = place_ref[7] + low + lax.broadcasted_iota(jnp.int32, (out_ref.shape[0], 1), 0)
    swapped = jnp.where(spots < place_ref[0], place_ref[1], 1 - place_ref[1])
    out_ref[...] = jnp.where(swapped == 1, moved_ref[...], own_ref[...])


def select_rows(place, own, moved, low, after):
    vmem = pl.BlockSpec(memory_space=pltpu.VMEM)
    return pl.pallas_call(
        functools.partial(select_kernel, low),
        in_specs=[pl.BlockSpec(memory_space=pltpu.SMEM), vmem, vmem]
        + [pl.BlockSpec(memory_space=pl.ANY)] * len(after),
        out_specs=vmem,
        out_shape=jax.ShapeDtypeStruct(moved.shape, moved.dtype),
        compiler_params=pltpu.CompilerParams(vmem_limit_bytes=8 * MIB),
        cost_estimate=pl.CostEstimate(flops=COST, bytes_accessed=COST, transcendentals=0),
    )(place, own, moved, *after)


def head_of(chip, index, group_heads):
    return 2 * group_heads * (chip // 2) + 2 * index + chip % 2


def weight_copies(place_ref, w_ref, out_ref, sems):
    pair = jnp.bitwise_xor(place_ref[4] // 2, place_ref[8])
    columns = pl.ds(pl.multiple_of(pair * out_ref.shape[2], HEAD_DIM), out_ref.shape[2])
    depth = out_ref.shape[1] // COPY_PIECES
    copies = []
    for part in range(3):
        for piece in range(COPY_PIECES):
            rows = slice(piece * depth, (piece + 1) * depth)
            copies.append(
                pltpu.make_async_copy(
                    w_ref.at[part, rows, columns], out_ref.at[part, rows, :], sems.at[part, piece]
                )
            )
    return copies


def norm_kernel(place_ref, *refs):
    pieces = len(SWAP_ROWS)
    bounds_ref, noise_ref, level_ref, gain_ref = refs[2 * pieces : 2 * pieces + 4]
    out_ref = refs[-1]
    width = out_ref.shape[1] // 2
    side, first = place_ref[6], place_ref[7]
    clips, levels = noise_ref.shape[0], level_ref.shape[0]
    spots = [pl.ds(pl.multiple_of(s * width, 128), width) for s in (side, 1 - side)]
    level = lax.broadcasted_iota(jnp.int32, (clips, levels), 1)
    chosen = jnp.where(noise_ref[...] == level, 1.0, 0.0).astype(jnp.bfloat16)
    tables = [
        jnp.dot(chosen, level_ref[:, spot], preferred_element_type=jnp.float32).astype(
            jnp.bfloat16
        )
        for spot in spots
    ]
    low = 0
    for piece in range(pieces):
        own_ref, other_ref = refs[piece], refs[pieces + piece]
        count = own_ref.shape[0]
        rows = slice(low, low + count)
        places = first + low + lax.broadcasted_iota(jnp.int32, (count, 1), 0)
        low += count
        unused, leading = clip_flags(packed_rows(place_ref, places), bounds_ref)
        picks = jnp.where(leading, 1.0, 0.0)[:, :clips].astype(jnp.bfloat16)
        shifted = [
            ref[...].astype(jnp.float32)
            + jnp.dot(picks, table, preferred_element_type=jnp.float32)
            for ref, table in zip((own_ref, other_ref), tables)
        ]
        squares = sum(jnp.sum(part * part, axis=1, keepdims=True) for part in shifted)
        factor = lax.rsqrt(squares / (2 * width) + EPS)
        for part, spot in zip(shifted, spots):
            out_ref[rows, spot] = (part * factor * gain_ref[:, spot]).astype(jnp.bfloat16)


def normalize_rows(place, kept, other, bounds, noise_levels, level_table, norm_gain):
    rows, depth = sum(part.shape[0] for part in kept), 2 * kept[0].shape[1]
    vmem = pl.BlockSpec(memory_space=pltpu.VMEM)
    return pl.pallas_call(
        norm_kernel,
        in_specs=[pl.BlockSpec(memory_space=pltpu.SMEM)] + [vmem] * (2 * len(kept) + 4),
        out_specs=vmem,
        out_shape=jax.ShapeDtypeStruct((rows, depth), jnp.bfloat16),
        compiler_params=pltpu.CompilerParams(vmem_limit_bytes=26 * MIB),
        cost_estimate=pl.CostEstimate(flops=COST, bytes_accessed=COST, transcendentals=0),
    )(place, *kept, *other, bounds, noise_levels, level_table, norm_gain.reshape(1, -1))


def project_kernel(indices, place_ref, own_ref, pair_ref, weights_ref, *rest):
    first_ref, second_ref = rest[-2:]
    rows = jnp.concatenate([own_ref[...], pair_ref[...]], axis=0)
    count = own_ref.shape[0]
    same = place_ref[4] % 2 == place_ref[8]

    def store(outcome, base, even_ref, odd_ref):
        for index, core in enumerate((place_ref[8], 1 - place_ref[8])):
            spot = pl.ds(pl.multiple_of(core * count, count), count)
            half = outcome[index * count : (index + 1) * count]
            for part in range(3):
                to = slice(base + part * HEAD_DIM, base + (part + 1) * HEAD_DIM)
                even_ref[spot, to] = half[:, 2 * part * HEAD_DIM : (2 * part + 1) * HEAD_DIM]
                odd_ref[spot, to] = half[:, (2 * part + 1) * HEAD_DIM : 2 * (part + 1) * HEAD_DIM]

    for position, index in enumerate(indices):
        spot = slice(2 * index * HEAD_DIM, 2 * (index + 1) * HEAD_DIM)
        weights = jnp.concatenate([weights_ref[part, :, spot] for part in range(3)], axis=1)
        outcome = jnp.dot(rows, weights, preferred_element_type=jnp.float32).astype(jnp.bfloat16)
        base = 3 * position * HEAD_DIM

        @pl.when(same)
        def _():
            store(outcome, base, first_ref, second_ref)

        @pl.when(jnp.logical_not(same))
        def _():
            store(outcome, base, second_ref, first_ref)


def project_heads(place, own, pair, weights, indices, after):
    rows = own.shape[0]
    vmem = pl.BlockSpec(memory_space=pltpu.VMEM)
    shape = jax.ShapeDtypeStruct((2 * rows, 3 * len(indices) * HEAD_DIM), jnp.bfloat16)
    return pl.pallas_call(
        functools.partial(project_kernel, indices),
        in_specs=[pl.BlockSpec(memory_space=pltpu.SMEM), vmem, vmem, vmem]
        + [pl.BlockSpec(memory_space=pl.ANY)] * len(after),
        out_specs=(vmem, vmem),
        out_shape=(shape, shape),
        compiler_params=pltpu.CompilerParams(vmem_limit_bytes=20 * MIB),
        cost_estimate=pl.CostEstimate(flops=COST, bytes_accessed=COST, transcendentals=0),
    )(place, own, pair, weights, *after)


def attend_kernel(base, place_ref, runs_ref, *refs):
    mine, near, far, pair_first, pair_far, pair_near = refs[:6]
    order_ref, query_mask_ref, key_mask_ref = refs[6:9]
    stay_ref, cross_ref, more_ref, q_all, k_all, v_all, sorted_out = refs[-7:]
    chip_rows = mine.shape[0]
    rows = chip_rows // 2
    queries = sorted_out.shape[0] - 2 * rows

    def hold(sources):
        for index, source in enumerate(sources):
            spot = slice(index * chip_rows, (index + 1) * chip_rows)
            for part, held in enumerate((q_all, k_all, v_all)):
                low = base + part * HEAD_DIM
                held[spot, :HEAD_DIM] = source[:, low : low + HEAD_DIM]

    @pl.when(place_ref[8] == 0)
    def _():
        hold((mine, near, pair_near, pair_far))

    @pl.when(place_ref[8] == 1)
    def _():
        hold((pair_first, pair_near, near, far))

    q_all[:, HEAD_DIM:] = query_mask_ref[...]
    k_all[:, HEAD_DIM:] = key_mask_ref[...]
    v_all[:, HEAD_DIM:] = jnp.ones((4 * chip_rows, HEAD_DIM), jnp.bfloat16)
    tile = queries // ATTEND_TILES

    def score(step):
        wanted = step * tile + lax.broadcasted_iota(jnp.int32, (tile, 1), 0)
        picks = jnp.concatenate(
            [
                jnp.where(order_ref[line : line + 1, :] == wanted, 1.0, 0.0).astype(jnp.bfloat16)
                for line in range(order_ref.shape[0])
            ],
            axis=1,
        )
        sorted_queries = jnp.dot(picks, q_all[...], preferred_element_type=jnp.float32)
        return lax.dot_general(
            sorted_queries.astype(jnp.bfloat16),
            k_all[...],
            (((1,), (1,)), ((), ())),
            preferred_element_type=jnp.float32,
        )

    coming = score(0)
    for step in range(ATTEND_TILES):
        scores = coming
        if step + 1 < ATTEND_TILES:
            coming = score(step + 1)
        top = jnp.max(scores, axis=1, keepdims=True)
        weights = jnp.exp2((scores - top) * (HEAD_DIM ** (-0.5) * LOG2E))
        summed = jnp.dot(
            weights.astype(jnp.bfloat16), v_all[...], preferred_element_type=jnp.float32
        )
        sorted_out[rows + step * tile : rows + (step + 1) * tile, :] = (
            summed[:, :HEAD_DIM] / summed[:, HEAD_DIM:]
        )

    low = rows
    for ref in (cross_ref, more_ref):
        ref[...] = sorted_out[low : low + ref.shape[0], :].astype(jnp.bfloat16)
        low += ref.shape[0]
    for d in range(4):
        stay_ref[d] = spread_run(sorted_out, runs_ref, d, rows).astype(jnp.bfloat16)


def spread_run(sorted_ref, runs_ref, lane, rows):
    furthest = sorted_ref.shape[0] - 2 * rows
    row = lax.broadcasted_iota(jnp.int32, (rows, 1), 0)
    parts = [
        sorted_ref[pl.ds(rows + jnp.clip(runs_ref[line, lane], -rows, furthest), rows), :]
        for line in (3, 4)
    ]
    in_second = (row >= runs_ref[1, lane]) & (row < runs_ref[2, lane])
    return jnp.where(row < runs_ref[0, lane], parts[0], jnp.where(in_second, parts[1], 0.0))


def attend(place, runs, blocks, position, order, query_mask, key_mask, after):
    chip_rows = blocks[0].shape[0]
    rows, keys = chip_rows // 2, 4 * chip_rows
    queries = keys // 2 + rows // 2
    vmem, smem = pl.BlockSpec(memory_space=pltpu.VMEM), pl.BlockSpec(memory_space=pltpu.SMEM)
    shape = jax.ShapeDtypeStruct((4, rows, HEAD_DIM), jnp.bfloat16)
    return pl.pallas_call(
        functools.partial(attend_kernel, 3 * position * HEAD_DIM),
        in_specs=[smem, smem]
        + [vmem] * (len(blocks) + 3)
        + [pl.BlockSpec(memory_space=pl.ANY)] * len(after),
        out_specs=(vmem, vmem, vmem),
        out_shape=(shape,)
        + tuple(
            jax.ShapeDtypeStruct((count, HEAD_DIM), jnp.bfloat16)
            for count in (PACKED_ROWS, queries - PACKED_ROWS)
        ),
        scratch_shapes=[
            pltpu.VMEM((keys, 2 * HEAD_DIM), jnp.bfloat16),
            pltpu.VMEM((keys, 2 * HEAD_DIM), jnp.bfloat16),
            pltpu.VMEM((keys, 2 * HEAD_DIM), jnp.bfloat16),
            pltpu.VMEM((queries + 2 * rows, HEAD_DIM), jnp.float32),
        ],
        compiler_params=pltpu.CompilerParams(vmem_limit_bytes=24 * MIB),
        cost_estimate=pl.CostEstimate(
            flops=COST, bytes_accessed=COST, transcendentals=0
        ),
    )(place, runs, *blocks, order, query_mask, key_mask, *after)


def join_kernel(heads, runs_ref, *refs):
    outs, held = refs[-5:-1], refs[-1]
    rows = outs[0].shape[0]
    for head in range(heads):
        stay_ref, low = refs[3 * head], rows
        for ref in refs[3 * head + 1 : 3 * head + 3]:
            held[low : low + ref.shape[0], :] = ref[...].astype(jnp.float32)
            low += ref.shape[0]
        spot = slice(head * HEAD_DIM, (head + 1) * HEAD_DIM)
        for d in range(4):
            arrived = spread_run(held, runs_ref, 4 + d, rows).astype(jnp.bfloat16)
            outs[d][:, spot] = stay_ref[d] + arrived


def join_halves(runs, stays, arrivals, others, after, cost):
    heads, (slots, rows, width) = len(stays), stays[0].shape
    vmem = pl.BlockSpec(memory_space=pltpu.VMEM)
    parts = [part for three in zip(stays, arrivals, others) for part in three]
    shape = jax.ShapeDtypeStruct((rows, heads * width), jnp.bfloat16)
    return pl.pallas_call(
        functools.partial(join_kernel, heads),
        in_specs=[pl.BlockSpec(memory_space=pltpu.SMEM)]
        + [vmem] * len(parts)
        + [pl.BlockSpec(memory_space=pl.ANY)] * len(after),
        out_specs=(vmem,) * slots,
        out_shape=(shape,) * slots,
        scratch_shapes=[
            pltpu.VMEM((arrivals[0].shape[0] + others[0].shape[0] + 2 * rows, width), jnp.float32)
        ],
        compiler_params=pltpu.CompilerParams(vmem_limit_bytes=16 * MIB),
        cost_estimate=pl.CostEstimate(flops=cost, bytes_accessed=COST, transcendentals=0),
    )(runs, *parts, *after)


def gather_kernel(place_ref, w_ref, held_ref, pair_ref, *rest):
    outs, sems = rest[-5:-1], rest[-1]
    chip, columns = place_ref[4], outs[0].shape[1]
    heads = w_ref.shape[0] // HEAD_DIM // 4
    spot = pl.ds(pl.multiple_of(place_ref[6] * columns, HEAD_DIM), columns)

    def rows_at(block):
        return pl.ds(pl.multiple_of(block * HEAD_DIM, HEAD_DIM), HEAD_DIM)

    def transfers(near_ref, far_ref):
        copies = []
        for d in range(4):
            for index in range(heads):
                last = index + 1 == heads
                group = 1 if last else 0
                to = d if last else d * (heads - 1) + index
                to = slice(to * HEAD_DIM, (to + 1) * HEAD_DIM)
                head = head_of(jnp.bitwise_xor(chip, d), index, heads)
                there = 2 * index + jnp.bitwise_xor(chip, d) % 2
                sources = (
                    w_ref.at[rows_at(head), spot],
                    (near_ref if d < 2 else far_ref).at[rows_at(there), :],
                )
                for side, source in enumerate(sources):
                    copies.append(
                        pltpu.make_async_copy(
                            source, outs[2 * side + group].at[to, :], sems.at[side, index, d]
                        )
                    )
        for copy in copies:
            copy.start()
        for copy in copies:
            copy.wait()

    @pl.when(chip // 2 == place_ref[8])
    def _():
        transfers(held_ref, pair_ref)

    @pl.when(chip // 2 != place_ref[8])
    def _():
        transfers(pair_ref, held_ref)


def gather_out_weights(place, w_out, held, pair, group_heads, after):
    vmem, hbm = pl.BlockSpec(memory_space=pltpu.VMEM), pl.BlockSpec(memory_space=pltpu.HBM)
    any_space = pl.BlockSpec(memory_space=pl.ANY)
    shapes = tuple(
        jax.ShapeDtypeStruct((count * HEAD_DIM, w_out.shape[1] // 2), w_out.dtype)
        for count in (4 * (group_heads - 1), 4)
    )
    return pl.pallas_call(
        gather_kernel,
        in_specs=[pl.BlockSpec(memory_space=pltpu.SMEM), hbm] + [any_space] * (2 + len(after)),
        out_specs=(vmem,) * 4,
        out_shape=shapes + shapes,
        scratch_shapes=[pltpu.SemaphoreType.DMA((2, group_heads, 4))],
        compiler_params=pltpu.CompilerParams(vmem_limit_bytes=16 * MIB),
        cost_estimate=pl.CostEstimate(flops=COST, bytes_accessed=COST, transcendentals=0),
    )(place, w_out, held, pair, *after)


def out_rows_kernel(*refs):
    refs[-1][...] = jnp.concatenate([ref[...] for ref in refs[:-1]], axis=1)


def out_kernel(pairs, *refs):
    total = refs[2 * pairs][...] if len(refs) > 2 * pairs + 1 else None
    for pair in range(pairs):
        product = jnp.dot(
            refs[2 * pair][...], refs[2 * pair + 1][...], preferred_element_type=jnp.float32
        )
        total = product if total is None else total + product
    refs[-1][...] = total.astype(refs[-1].dtype)


def out_call(kernel, arrays, shape, dtype):
    vmem = pl.BlockSpec(memory_space=pltpu.VMEM)
    return pl.pallas_call(
        kernel,
        in_specs=[vmem] * len(arrays),
        out_specs=vmem,
        out_shape=jax.ShapeDtypeStruct(shape, dtype),
        compiler_params=pltpu.CompilerParams(vmem_limit_bytes=16 * MIB),
        cost_estimate=pl.CostEstimate(flops=COST, bytes_accessed=COST, transcendentals=0),
    )(*arrays)


SWAP_ROWS = (128, 112, 80)
PACKED_ROWS = 768
ATTEND_TILES = 3
HEAD_CHUNKS = ((0,), (1, 2))
COPY_PIECES = 4


def halved_body(
    inputs,
    norm_gain,
    level_table,
    w_qkv,
    w_out,
    clip_lengths,
    prefix_lengths,
    noise_levels,
    token_rank,
):
    ranks, per_dev = 16, inputs.shape[0]
    half_rows = 8 * per_dev
    clips = clip_lengths.shape[0]
    index = jnp.arange(clips, dtype=jnp.int32)

    ahead = (index[None, :] < index[:, None]) & (clip_lengths == MAXCLIP)[:, None]
    start = jnp.sum(jnp.where(ahead, clip_lengths[None, :], 0))
    early = start <= half_rows // 2

    rank_here = lax.axis_index("ctx")
    side = lax.axis_index("head")
    columns = inputs.shape[1]
    group_heads = w_qkv.shape[2] // HEAD_DIM // 4
    half, block, core = rank_here // 8, rank_here % 8, rank_here % 2
    chip = block // 2
    swap_sides = [(0, 1), (1, 0)]

    def exchange(array, flip, only=lambda r: True):
        pairs = [(r, r ^ flip) for r in range(ranks) if only(r)]
        return lax.ppermute(array, "ctx", pairs)

    def move_rows(swapping):
        return functools.partial(moved_rows, swapping)

    def moved_rows(
        swapping, start, inputs, clip_lengths, prefix_lengths, noise_levels, w_out
    ):
        place = jnp.stack(
            [
                start,
                jnp.int32(1 if 0 in swapping else 0),
                half,
                jnp.int32(half_rows),
                chip,
                jnp.int32(clips),
                side,
                block * per_dev,
                core,
                rank_here,
            ]
        )
        earlier = index[None, :] < index[:, None]
        begins = jnp.sum(jnp.where(earlier, clip_lengths[None, :], 0), axis=1)
        leads = begins + jnp.minimum(prefix_lengths, clip_lengths)
        bounds = jnp.pad(
            jnp.stack([begins, begins + clip_lengths, leads]), ((0, 5), (0, HEAD_DIM - clips))
        )

        cuts = [sum(SWAP_ROWS[:i]) for i in range(len(SWAP_ROWS) + 1)]
        kept, moved = [], []
        for low, high in zip(cuts[:-1], cuts[1:]):
            own = inputs[low:high]
            moved.append(exchange(own, 8, lambda r: r % 8 in swapping))
            kept.append(select_rows(place, own, moved[-1], low, kept[-1:]))
        other = [lax.ppermute(part, "head", swap_sides) for part in kept]
        depth = w_out.shape[0] // 2
        sent = lax.dynamic_slice(w_out, (core * depth, (1 - side) * columns), (depth, columns))
        return tuple(kept), tuple(other), place, bounds, noise_levels.reshape(-1, 1), sent

    kept, other, place, bounds, noise_column, sent = lax.cond(
        early,
        move_rows(range(4)),
        move_rows(range(4, 8)),
        start,
        inputs,
        clip_lengths,
        prefix_lengths,
        noise_levels,
        w_out,
    )
    far_held = lax.ppermute(sent, "head", swap_sides)
    normed = normalize_rows(place, kept, other, bounds, noise_column, level_table, norm_gain)
    pair = exchange(normed, 1)
    w_parts = jnp.transpose(w_qkv, (1, 0, 2))
    query_order, runs, query_mask, key_mask, weights = make_tables(
        place, bounds, token_rank, ranks, half_rows, w_parts
    )

    row = jnp.arange(ranks * per_dev, dtype=jnp.int32)
    in_long = (row >= start) & (row < start + half_rows)
    home = jnp.where(in_long == early, 0, 1)
    crosses = token_rank // (ranks // 2) != home
    kind = jnp.where(crosses, 2 * home + token_rank % 2, 4)
    counts = jnp.sum((kind[:, None] == jnp.arange(4)[None, :]).astype(jnp.int32), axis=0)
    fits = jnp.max(counts) <= PACKED_ROWS

    def cross_rest(parts):
        return lax.cond(
            fits,
            lambda parts: parts,
            lambda parts: tuple(exchange(part, 8) for part in parts),
            tuple(parts),
        )

    blocks, after = [], [query_order]
    for heads in HEAD_CHUNKS:
        first, second = project_heads(place, normed, pair, weights, heads, after)
        near = lax.ppermute(
            second, "ctx", [(r, r ^ (2 if r % 2 == 0 else 4)) for r in range(ranks)]
        )
        far = exchange(first, 6, lambda r: r % 2 == 1)
        blocks.append((first, near, far))
        after = [first]

    def share(block, after):
        first, near, far = block
        shared, *unused = lax.optimization_barrier((first, *after))
        near, far, *unused = lax.optimization_barrier((near, far, *after))
        return [
            first,
            near,
            far,
            exchange(shared, 1, lambda r: r % 2 == 0),
            exchange(far, 1, lambda r: r % 2 == 1),
            exchange(near, 1),
        ]

    def join(heads, after, cost):
        joined = join_halves(runs, stays[heads], arrivals[heads], others[heads], after, cost)
        return [exchange(part, 2 * d) if d else part for d, part in enumerate(joined)]

    stays, arrivals, others = [], [], []
    after = [blocks[-1][0]]
    for block, heads in zip(blocks, HEAD_CHUNKS):
        block = share(block, after)
        for position, head in enumerate(heads):
            stay, cross, more = attend(
                place, runs, block, position, query_order, query_mask, key_mask, after
            )
            stays.append(stay)
            arrivals.append(exchange(cross, 8))
            others.append(more)
            after = [cross] + (arrivals[head - 1 : head] if head else [])
            if head == 1:
                far_pair = exchange(lax.optimization_barrier((far_held, cross))[0], 1)

    others = cross_rest(others)
    w_all = gather_out_weights(place, w_out, far_held, far_pair, group_heads, [cross])

    def side_by_side(parts):
        width = sum(part.shape[1] for part in parts)
        return out_call(out_rows_kernel, parts, (per_dev, width), jnp.bfloat16)

    pieces = join(slice(0, -1), [cross], COST)
    rows = [side_by_side(pieces), side_by_side(join(slice(-1, None), [], LONG_COST))]
    far_rows = [lax.ppermute(part, "head", swap_sides) for part in rows]
    w_own, w_far = w_all[:2], w_all[2:]

    def add(terms, total, dtype):
        arrays = [array for term in terms for array in term] + total
        return out_call(functools.partial(out_kernel, len(terms)), arrays, (per_dev, columns), dtype)

    own, far = list(zip(rows, w_own)), list(zip(far_rows, w_far))
    total = add(own[:1], [], jnp.float32)
    total = add(own[1:] + far[:1], [total], jnp.float32)
    return add(far[1:], [total], jnp.bfloat16)


def solution(mesh):
    in_specs = (
        P("ctx", "head"),
        P(),
        P(),
        P(None, None, "head"),
        P("head", None),
        P(),
        P(),
        P(),
        P(),
    )
    out_specs = P("ctx", "head")

    def body(inputs, norm_gain, level_table, w_qkv, *rest):
        ranks, sides = mesh.shape["ctx"], mesh.shape["head"]
        heads_here = w_qkv.shape[2] // HEAD_DIM
        halved = (
            ranks == 16
            and sides == 2
            and ranks * inputs.shape[0] == 2 * MAXCLIP
            and heads_here == 4 * sum(len(heads) for heads in HEAD_CHUNKS)
        )
        run = halved_body if halved else gathered_body
        return run(inputs, norm_gain, level_table, w_qkv, *rest)

    return jax.shard_map(body, mesh=mesh, in_specs=in_specs, out_specs=out_specs, check_vma=False)
```

```python
import functools

import jax
import jax.numpy as jnp
from jax import lax
from jax.experimental import pallas as pl
from jax.experimental.pallas import tpu as pltpu
from jax.sharding import PartitionSpec as P

HEAD_DIM = 128


NEG = -1e30
EPS = 1e-06
MAXCLIP = 2560
LOG2E = 1.4426950408889634
MIB = 1024 * 1024
COST = 1000000
LONG_COST = 200000000000


def clip_tables(total_rows, clip_lengths, prefix_lengths, noise_levels):
    rows = jnp.arange(total_rows, dtype=jnp.int32)
    ends = jnp.cumsum(clip_lengths)
    begins = ends - clip_lengths
    clip_of = jnp.sum((rows[:, None] >= ends[None, :]).astype(jnp.int32), axis=1)
    member = clip_of[:, None] == jnp.arange(clip_lengths.shape[0], dtype=jnp.int32)[None, :]
    begin_row = jnp.sum(jnp.where(member, begins[None, :], 0), axis=1)
    lead = jnp.minimum(prefix_lengths, clip_lengths)
    lead_row = jnp.sum(jnp.where(member, lead[None, :], 0), axis=1)
    level_row = jnp.sum(jnp.where(member, noise_levels[None, :], 0), axis=1)
    in_prefix = rows - begin_row < lead_row
    return (clip_of, in_prefix, level_row)


def rank_tables(token_rank, ranks, per_rank):
    onehot = (token_rank[:, None] == jnp.arange(ranks, dtype=jnp.int32)[None, :]).astype(jnp.int32)
    earlier = jnp.cumsum(onehot, axis=0) - onehot
    within = jnp.sum(earlier * onehot, axis=1)
    counts = jnp.sum(onehot.reshape(ranks, per_rank, ranks), axis=1)
    starts = jnp.cumsum(counts, axis=0) - counts
    return (within, counts, starts)


def normalize(rows, in_prefix, level_row, level_table, norm_gain):
    picks = (
        level_row[:, None] == jnp.arange(level_table.shape[0], dtype=jnp.int32)[None, :]
    ) & in_prefix[:, None]
    added = jnp.dot(picks.astype(jnp.bfloat16), level_table, preferred_element_type=jnp.float32)
    shifted = rows.astype(jnp.float32) + added
    factor = lax.rsqrt(jnp.mean(shifted * shifted, axis=-1, keepdims=True) + EPS)
    return (shifted * factor * norm_gain).astype(jnp.bfloat16)


def fold_keys(state, queries, query_clip, query_prefix, pairs, key_clip, key_prefix):
    width = queries.shape[1]
    heads_here = width // HEAD_DIM
    factor = HEAD_DIM ** (-0.5)
    allowed_query = jnp.logical_not(query_prefix)

    def absorb(carry, block):
        block_pairs, block_clip, block_prefix = block
        allowed = (query_clip[:, None] == block_clip[None, :]) & (
            allowed_query[:, None] | block_prefix[None, :]
        )
        updated = []
        for head in range(heads_here):
            top, total, summed = carry[head]
            low = head * HEAD_DIM
            q_head = queries[:, low : low + HEAD_DIM]
            k_head = block_pairs[:, low : low + HEAD_DIM]
            v_head = block_pairs[:, width + low : width + low + HEAD_DIM]
            scores = (
                lax.dot_general(
                    q_head, k_head, (((1,), (1,)), ((), ())), preferred_element_type=jnp.float32
                )
                * factor
            )
            masked = jnp.where(allowed, scores, NEG)
            new_top = jnp.maximum(top, jnp.max(masked, axis=1, keepdims=True))
            fade = jnp.exp(top - new_top)
            weights = jnp.where(allowed, jnp.exp(scores - new_top), 0.0)
            total = total * fade + jnp.sum(weights, axis=1, keepdims=True)
            summed = summed * fade + jnp.dot(
                weights.astype(jnp.bfloat16), v_head, preferred_element_type=jnp.float32
            )
            updated.append((new_top, total, summed))
        return (tuple(updated), None)

    count = pairs.shape[0]
    step = 2048 if count > 2048 and count % 2048 == 0 else count
    if step == count:
        result, unused = absorb(state, (pairs, key_clip, key_prefix))
        return result
    stacked = (
        pairs.reshape(count // step, step, pairs.shape[1]),
        key_clip.reshape(count // step, step),
        key_prefix.reshape(count // step, step),
    )
    result, unused = lax.scan(absorb, state, stacked)
    return result


def gathered_body(
    inputs,
    norm_gain,
    level_table,
    w_qkv,
    w_out,
    clip_lengths,
    prefix_lengths,
    noise_levels,
    token_rank,
):
    ranks = lax.axis_size("ctx")
    rank_here = lax.axis_index("ctx")
    per_dev = inputs.shape[0]
    slots = 2 * per_dev // ranks
    local_width = w_qkv.shape[2]
    heads_here = local_width // HEAD_DIM
    total_rows = per_dev * ranks
    clip_of, in_prefix, level_row = clip_tables(
        total_rows, clip_lengths, prefix_lengths, noise_levels
    )
    within, counts, starts = rank_tables(token_rank, ranks, per_dev)
    place = token_rank * per_dev + within
    order = (
        jnp.zeros((total_rows,), jnp.int32).at[place].set(jnp.arange(total_rows, dtype=jnp.int32))
    )
    first = rank_here * per_dev
    own_rank = lax.dynamic_slice_in_dim(token_rank, first, per_dev, 0)
    own_within = lax.dynamic_slice_in_dim(within, first, per_dev, 0)
    send_starts = lax.dynamic_slice_in_dim(starts, rank_here, 1, 0)[0]
    recv_counts = lax.dynamic_slice_in_dim(counts, rank_here, 1, 1)[:, 0]
    recv_starts = lax.dynamic_slice_in_dim(starts, rank_here, 1, 1)[:, 0]
    balanced_rows = lax.dynamic_slice_in_dim(order, first, per_dev, 0)
    target = own_rank * slots + own_within - send_starts[own_rank]
    buffer = jnp.zeros((ranks * slots, inputs.shape[1]), inputs.dtype).at[target].set(inputs)
    received = lax.all_to_all(
        buffer.reshape(ranks, slots, inputs.shape[1]),
        "ctx",
        split_axis=0,
        concat_axis=0,
        tiled=True,
    )
    spots = jnp.arange(slots, dtype=jnp.int32)[None, :]
    index = jnp.where(spots < recv_counts[:, None], recv_starts[:, None] + spots, per_dev).reshape(
        -1
    )
    flat = received.reshape(ranks * slots, received.shape[2])
    rows = jnp.zeros((per_dev, received.shape[2]), received.dtype).at[index].set(flat, mode="drop")
    full_rows = lax.all_gather(rows, "head", axis=1, tiled=True)
    normed = normalize(
        full_rows, in_prefix[balanced_rows], level_row[balanced_rows], level_table, norm_gain
    )
    qkv = jnp.dot(
        normed, w_qkv.reshape(w_qkv.shape[0], 3 * local_width), preferred_element_type=jnp.float32
    ).astype(jnp.bfloat16)
    start_state = tuple(
        (
            (
                jnp.full((per_dev, 1), NEG, jnp.float32),
                jnp.zeros((per_dev, 1), jnp.float32),
                jnp.zeros((per_dev, HEAD_DIM), jnp.float32),
            )
            for head in range(heads_here)
        )
    )
    key_clip = clip_of[order]
    key_prefix = in_prefix[order]
    query_clip = lax.dynamic_slice_in_dim(key_clip, first, per_dev, 0)
    query_prefix = lax.dynamic_slice_in_dim(key_prefix, first, per_dev, 0)
    queries = qkv[:, :local_width]
    pairs = qkv[:, local_width:]
    state = fold_keys(
        start_state,
        queries,
        query_clip,
        query_prefix,
        lax.all_gather(pairs, "ctx", axis=0, tiled=True),
        key_clip,
        key_prefix,
    )
    parts = [state[head][2] / state[head][1] for head in range(heads_here)]
    attention = jnp.concatenate(parts, axis=1).astype(jnp.bfloat16)
    terms = jnp.dot(attention, w_out, preferred_element_type=jnp.float32)
    return lax.psum_scatter(terms.astype(jnp.bfloat16), "head", scatter_dimension=1, tiled=True)


def packed_rows(place_ref, spots):
    start, early, half = place_ref[0], place_ref[1], place_ref[2]
    total = place_ref[3]
    before = jnp.where(spots < start, early, 1 - early)
    return spots + total * (half + before * (1 - 2 * half))


def clip_flags(rows, bounds_ref):
    begins, ends, leads = bounds_ref[0:1, :], bounds_ref[1:2, :], bounds_ref[2:3, :]
    inside = (rows >= begins) & (rows < ends)
    return inside, inside & (rows < leads)


def count_earlier(hot):
    ranks, rows, lanes = hot.shape
    flat = hot.reshape(ranks * rows, lanes).astype(jnp.bfloat16)

    def numbers(shape, axis):
        return lax.broadcasted_iota(jnp.int32, shape, axis)

    def group(index):
        return sum(jnp.where(index >= rows * k, 1, 0) for k in range(1, ranks))

    def ones(flags):
        return jnp.where(flags, 1.0, 0.0).astype(jnp.bfloat16)

    total = ranks * rows
    in_row = ones(numbers((lanes, lanes), 0) < numbers((lanes, lanes), 1))
    below, across = numbers((total, 1), 0), numbers((1, total), 1)
    in_rank = ones((group(below) == group(across)) & (across < below))
    row_sums = jnp.dot(
        flat, jnp.ones((lanes, lanes), jnp.bfloat16), preferred_element_type=jnp.float32
    )
    earlier = jnp.dot(flat, in_row, preferred_element_type=jnp.float32) + jnp.dot(
        in_rank, row_sums.astype(jnp.bfloat16), preferred_element_type=jnp.float32
    )
    return earlier.reshape(ranks, rows, lanes)


def table_kernel(ranks, place_ref, bounds_ref, rank_ref, w_ref, *refs):
    order_ref, runs_ref, query_ref, key_ref, weights_ref, held, sems = refs
    copies = weight_copies(place_ref, w_ref, weights_ref, sems)
    for copy in copies:
        copy.start()
    start, early, half, half_rows = (place_ref[k] for k in range(4))
    chip, clips, core, rank_here = (place_ref[k] for k in (4, 5, 8, 9))
    holds_long = half != early
    tokens = rank_ref[...]
    rows, lanes = tokens.shape
    per_dev = rows * lanes // ranks

    token = lanes * lax.broadcasted_iota(jnp.int32, tokens.shape, 0) + lax.broadcasted_iota(
        jnp.int32, tokens.shape, 1
    )
    hots = [jnp.where(tokens == rank, 1.0, 0.0) for rank in range(ranks)]
    earlier = count_earlier(jnp.stack(hots))
    within = sum(hots[rank] * earlier[rank] for rank in range(ranks))
    before = jnp.where(token < start, 1.0, 0.0)
    upto = jnp.where(token < start + half_rows, 1.0, 0.0)
    lane = lax.broadcasted_iota(jnp.int32, (1, lanes), 1)
    target = jnp.bitwise_xor(rank_here, 2 * jnp.bitwise_and(lane, 3))
    lane_long = jnp.where(lane < 4, jnp.where(holds_long, 1.0, 0.0), jnp.where(holds_long, 0.0, 1.0))
    lane_own = jnp.where(lane < 4, 1.0, 0.0)
    lows, longs, long_first, rest_first = [], [], [], []
    long_count, rest_count = [[0.0, 0.0], [0.0, 0.0]], [[0.0, 0.0], [0.0, 0.0]]
    for rank, hot in enumerate(hots):
        low = jnp.sum(hot * before, keepdims=True)
        long_rows = jnp.sum(hot * upto, keepdims=True) - low
        group, parity = rank // (ranks // 2), rank % 2
        lows.append(low)
        longs.append(long_rows)
        long_first.append(long_count[group][parity])
        rest_first.append(rest_count[group][parity])
        long_count[group][parity] = long_first[rank] + long_rows
        rest_count[group][parity] = rest_first[rank] + (per_dev - long_rows)
    long_base = rest_base = low_of = long_of = 0.0
    runs = [0.0] * 5
    for rank, hot in enumerate(hots):
        low, high, long_rows = lows[rank], lows[rank] + longs[rank], longs[rank]
        group, parity = rank // (ranks // 2), rank % 2
        own_group = jnp.where(half == group, 1.0, 0.0)
        long_after = own_group * long_count[1 - group][parity]
        rest_after = own_group * rest_count[1 - group][parity]
        long_base += hot * (long_first[rank] + long_after - low)
        rest_base += hot * (rest_first[rank] + rest_after)
        low_of += hot * low
        long_of += hot * long_rows
        first = long_first[rank] + lane_own * long_after
        rest = rest_first[rank] + lane_own * rest_after
        here = jnp.where(target == rank, 1.0, 0.0)
        values = (
            (0.0, low),
            (low, high),
            (high, float(per_dev)),
            (0.0, rest),
            (first - low, rest - long_rows),
        )
        runs = [
            run + here * (lane_long * if_long + (1.0 - lane_long) * if_rest)
            for run, (if_long, if_rest) in zip(runs, values)
        ]
    furthest = rows * lanes // 4 + per_dev // 2
    for index, run in enumerate(runs):
        run = run.astype(jnp.int32)
        runs_ref[index : index + 1, :] = (
            run if index < 3 else jnp.clip(run, -per_dev, furthest)
        )
    sorted_at = within + jnp.where(
        upto - before == 1.0, long_base, rest_base - jnp.where(within < low_of, 0.0, long_of)
    )
    held[...] = jnp.where(jnp.bitwise_and(tokens, 1) == core, sorted_at.astype(jnp.int32), -1)
    half_lines = rows // 2
    spots = lanes * lax.broadcasted_iota(
        jnp.int32, (half_lines, lanes), 0
    ) + lax.broadcasted_iota(jnp.int32, (half_lines, lanes), 1)
    later = packed_rows(place_ref, spots) >= half_rows
    held[:half_lines, :] = jnp.where(later, held[half_lines:, :], held[:half_lines, :])
    lines = half_lines // 4
    for d in range(4):
        line = lines * jnp.bitwise_xor(chip, d)
        order_ref[lines * d : lines * (d + 1), :] = held[pl.ds(line, lines), :]

    column = lax.broadcasted_iota(jnp.int32, (1, HEAD_DIM), 1)
    chip_rows = query_ref.shape[0] // 4
    for d in range(4):
        local = lax.broadcasted_iota(jnp.int32, (chip_rows, 1), 0)
        spots = chip_rows * jnp.bitwise_xor(chip, d) + local
        inside, leading = clip_flags(packed_rows(place_ref, spots), bounds_ref)
        spot = slice(d * chip_rows, (d + 1) * chip_rows)
        inside = jnp.where(inside, 1.0, 0.0)
        prefix = jnp.sum(jnp.where(leading, 1.0, 0.0), axis=1, keepdims=True)
        query_ref[spot, :] = jnp.where(column == clips, prefix, inside).astype(jnp.bfloat16)
        outside = jnp.where(column < clips, NEG * (1.0 - inside), 0.0)
        key_ref[spot, :] = jnp.where(column == clips, NEG * (1.0 - prefix), outside).astype(
            jnp.bfloat16
        )
    for copy in copies:
        copy.wait()


def make_tables(place, bounds, token_rank, ranks, keys, w_parts):
    vmem = pl.BlockSpec(memory_space=pltpu.VMEM)
    tokens = token_rank.reshape(-1, HEAD_DIM)
    features = jax.ShapeDtypeStruct((keys, HEAD_DIM), jnp.bfloat16)
    return pl.pallas_call(
        functools.partial(table_kernel, ranks),
        in_specs=[
            pl.BlockSpec(memory_space=pltpu.SMEM),
            vmem,
            vmem,
            pl.BlockSpec(memory_space=pltpu.HBM),
        ],
        out_specs=(vmem,) * 5,
        out_shape=(
            jax.ShapeDtypeStruct((tokens.shape[0] // 2, HEAD_DIM), jnp.int32),
            jax.ShapeDtypeStruct((8, HEAD_DIM), jnp.int32),
            features,
            features,
            jax.ShapeDtypeStruct((*w_parts.shape[:2], w_parts.shape[2] // 2), w_parts.dtype),
        ),
        scratch_shapes=[
            pltpu.VMEM(tokens.shape, jnp.int32),
            pltpu.SemaphoreType.DMA((3, COPY_PIECES)),
        ],
        compiler_params=pltpu.CompilerParams(vmem_limit_bytes=26 * MIB),
        cost_estimate=pl.CostEstimate(flops=COST, bytes_accessed=COST, transcendentals=0),
    )(place, bounds, tokens, w_parts)


def select_kernel(low, place_ref, own_ref, moved_ref, *rest):
    out_ref = rest[-1]
    spots = place_ref[7] + low + lax.broadcasted_iota(jnp.int32, (out_ref.shape[0], 1), 0)
    swapped = jnp.where(spots < place_ref[0], place_ref[1], 1 - place_ref[1])
    out_ref[...] = jnp.where(swapped == 1, moved_ref[...], own_ref[...])


def select_rows(place, own, moved, low, after):
    vmem = pl.BlockSpec(memory_space=pltpu.VMEM)
    return pl.pallas_call(
        functools.partial(select_kernel, low),
        in_specs=[pl.BlockSpec(memory_space=pltpu.SMEM), vmem, vmem]
        + [pl.BlockSpec(memory_space=pl.ANY)] * len(after),
        out_specs=vmem,
        out_shape=jax.ShapeDtypeStruct(moved.shape, moved.dtype),
        compiler_params=pltpu.CompilerParams(vmem_limit_bytes=8 * MIB),
        cost_estimate=pl.CostEstimate(flops=COST, bytes_accessed=COST, transcendentals=0),
    )(place, own, moved, *after)


def head_of(chip, index, group_heads):
    return 2 * group_heads * (chip // 2) + 2 * index + chip % 2


def weight_copies(place_ref, w_ref, out_ref, sems):
    pair = jnp.bitwise_xor(place_ref[4] // 2, place_ref[8])
    columns = pl.ds(pl.multiple_of(pair * out_ref.shape[2], HEAD_DIM), out_ref.shape[2])
    depth = out_ref.shape[1] // COPY_PIECES
    copies = []
    for part in range(3):
        for piece in range(COPY_PIECES):
            rows = slice(piece * depth, (piece + 1) * depth)
            copies.append(
                pltpu.make_async_copy(
                    w_ref.at[part, rows, columns], out_ref.at[part, rows, :], sems.at[part, piece]
                )
            )
    return copies


def norm_kernel(place_ref, *refs):
    pieces = len(SWAP_ROWS)
    bounds_ref, noise_ref, level_ref, gain_ref = refs[2 * pieces : 2 * pieces + 4]
    out_ref = refs[-1]
    width = out_ref.shape[1] // 2
    side, first = place_ref[6], place_ref[7]
    clips, levels = noise_ref.shape[0], level_ref.shape[0]
    spots = [pl.ds(pl.multiple_of(s * width, 128), width) for s in (side, 1 - side)]
    level = lax.broadcasted_iota(jnp.int32, (clips, levels), 1)
    chosen = jnp.where(noise_ref[...] == level, 1.0, 0.0).astype(jnp.bfloat16)
    tables = [
        jnp.dot(chosen, level_ref[:, spot], preferred_element_type=jnp.float32).astype(
            jnp.bfloat16
        )
        for spot in spots
    ]
    low = 0
    for piece in range(pieces):
        own_ref, other_ref = refs[piece], refs[pieces + piece]
        count = own_ref.shape[0]
        rows = slice(low, low + count)
        places = first + low + lax.broadcasted_iota(jnp.int32, (count, 1), 0)
        low += count
        unused, leading = clip_flags(packed_rows(place_ref, places), bounds_ref)
        picks = jnp.where(leading, 1.0, 0.0)[:, :clips].astype(jnp.bfloat16)
        shifted = [
            ref[...].astype(jnp.float32)
            + jnp.dot(picks, table, preferred_element_type=jnp.float32)
            for ref, table in zip((own_ref, other_ref), tables)
        ]
        squares = sum(jnp.sum(part * part, axis=1, keepdims=True) for part in shifted)
        factor = lax.rsqrt(squares / (2 * width) + EPS)
        for part, spot in zip(shifted, spots):
            out_ref[rows, spot] = (part * factor * gain_ref[:, spot]).astype(jnp.bfloat16)


def normalize_rows(place, kept, other, bounds, noise_levels, level_table, norm_gain):
    rows, depth = sum(part.shape[0] for part in kept), 2 * kept[0].shape[1]
    vmem = pl.BlockSpec(memory_space=pltpu.VMEM)
    return pl.pallas_call(
        norm_kernel,
        in_specs=[pl.BlockSpec(memory_space=pltpu.SMEM)] + [vmem] * (2 * len(kept) + 4),
        out_specs=vmem,
        out_shape=jax.ShapeDtypeStruct((rows, depth), jnp.bfloat16),
        compiler_params=pltpu.CompilerParams(vmem_limit_bytes=26 * MIB),
        cost_estimate=pl.CostEstimate(flops=COST, bytes_accessed=COST, transcendentals=0),
    )(place, *kept, *other, bounds, noise_levels, level_table, norm_gain.reshape(1, -1))


def project_kernel(indices, place_ref, own_ref, pair_ref, weights_ref, *rest):
    first_ref, second_ref = rest[-2:]
    rows = jnp.concatenate([own_ref[...], pair_ref[...]], axis=0)
    count = own_ref.shape[0]
    same = place_ref[4] % 2 == place_ref[8]

    def store(outcome, base, even_ref, odd_ref):
        for index, core in enumerate((place_ref[8], 1 - place_ref[8])):
            spot = pl.ds(pl.multiple_of(core * count, count), count)
            half = outcome[index * count : (index + 1) * count]
            for part in range(3):
                to = slice(base + part * HEAD_DIM, base + (part + 1) * HEAD_DIM)
                even_ref[spot, to] = half[:, 2 * part * HEAD_DIM : (2 * part + 1) * HEAD_DIM]
                odd_ref[spot, to] = half[:, (2 * part + 1) * HEAD_DIM : 2 * (part + 1) * HEAD_DIM]

    for position, index in enumerate(indices):
        spot = slice(2 * index * HEAD_DIM, 2 * (index + 1) * HEAD_DIM)
        weights = jnp.concatenate([weights_ref[part, :, spot] for part in range(3)], axis=1)
        outcome = jnp.dot(rows, weights, preferred_element_type=jnp.float32).astype(jnp.bfloat16)
        base = 3 * position * HEAD_DIM

        @pl.when(same)
        def _():
            store(outcome, base, first_ref, second_ref)

        @pl.when(jnp.logical_not(same))
        def _():
            store(outcome, base, second_ref, first_ref)


def project_heads(place, own, pair, weights, indices, after):
    rows = own.shape[0]
    vmem = pl.BlockSpec(memory_space=pltpu.VMEM)
    shape = jax.ShapeDtypeStruct((2 * rows, 3 * len(indices) * HEAD_DIM), jnp.bfloat16)
    return pl.pallas_call(
        functools.partial(project_kernel, indices),
        in_specs=[pl.BlockSpec(memory_space=pltpu.SMEM), vmem, vmem, vmem]
        + [pl.BlockSpec(memory_space=pl.ANY)] * len(after),
        out_specs=(vmem, vmem),
        out_shape=(shape, shape),
        compiler_params=pltpu.CompilerParams(vmem_limit_bytes=20 * MIB),
        cost_estimate=pl.CostEstimate(flops=COST, bytes_accessed=COST, transcendentals=0),
    )(place, own, pair, weights, *after)


def attend_kernel(base, place_ref, runs_ref, *refs):
    mine, near, far, pair_first, pair_far, pair_near = refs[:6]
    order_ref, query_mask_ref, key_mask_ref = refs[6:9]
    stay_ref, cross_ref, more_ref, q_all, k_all, v_all, sorted_out = refs[-7:]
    chip_rows = mine.shape[0]
    rows = chip_rows // 2
    queries = sorted_out.shape[0] - 2 * rows

    def hold(sources):
        for index, source in enumerate(sources):
            spot = slice(index * chip_rows, (index + 1) * chip_rows)
            for part, held in enumerate((q_all, k_all, v_all)):
                low = base + part * HEAD_DIM
                held[spot, :HEAD_DIM] = source[:, low : low + HEAD_DIM]

    @pl.when(place_ref[8] == 0)
    def _():
        hold((mine, near, pair_near, pair_far))

    @pl.when(place_ref[8] == 1)
    def _():
        hold((pair_first, pair_near, near, far))

    q_all[:, HEAD_DIM:] = query_mask_ref[...]
    k_all[:, HEAD_DIM:] = key_mask_ref[...]
    v_all[:, HEAD_DIM:] = jnp.ones((4 * chip_rows, HEAD_DIM), jnp.bfloat16)
    tile = queries // ATTEND_TILES

    def score(step):
        wanted = step * tile + lax.broadcasted_iota(jnp.int32, (tile, 1), 0)
        picks = jnp.concatenate(
            [
                jnp.where(order_ref[line : line + 1, :] == wanted, 1.0, 0.0).astype(jnp.bfloat16)
                for line in range(order_ref.shape[0])
            ],
            axis=1,
        )
        sorted_queries = jnp.dot(picks, q_all[...], preferred_element_type=jnp.float32)
        return lax.dot_general(
            sorted_queries.astype(jnp.bfloat16),
            k_all[...],
            (((1,), (1,)), ((), ())),
            preferred_element_type=jnp.float32,
        )

    coming = score(0)
    for step in range(ATTEND_TILES):
        scores = coming
        if step + 1 < ATTEND_TILES:
            coming = score(step + 1)
        top = jnp.max(scores, axis=1, keepdims=True)
        weights = jnp.exp2((scores - top) * (HEAD_DIM ** (-0.5) * LOG2E))
        summed = jnp.dot(
            weights.astype(jnp.bfloat16), v_all[...], preferred_element_type=jnp.float32
        )
        sorted_out[rows + step * tile : rows + (step + 1) * tile, :] = (
            summed[:, :HEAD_DIM] / summed[:, HEAD_DIM:]
        )

    low = rows
    for ref in (cross_ref, more_ref):
        ref[...] = sorted_out[low : low + ref.shape[0], :].astype(jnp.bfloat16)
        low += ref.shape[0]
    for d in range(4):
        stay_ref[d] = spread_run(sorted_out, runs_ref, d, rows).astype(jnp.bfloat16)


def spread_run(sorted_ref, runs_ref, lane, rows):
    furthest = sorted_ref.shape[0] - 2 * rows
    row = lax.broadcasted_iota(jnp.int32, (rows, 1), 0)
    parts = [
        sorted_ref[pl.ds(rows + jnp.clip(runs_ref[line, lane], -rows, furthest), rows), :]
        for line in (3, 4)
    ]
    in_second = (row >= runs_ref[1, lane]) & (row < runs_ref[2, lane])
    return jnp.where(row < runs_ref[0, lane], parts[0], jnp.where(in_second, parts[1], 0.0))


def attend(place, runs, blocks, position, order, query_mask, key_mask, after):
    chip_rows = blocks[0].shape[0]
    rows, keys = chip_rows // 2, 4 * chip_rows
    queries = keys // 2 + rows // 2
    vmem, smem = pl.BlockSpec(memory_space=pltpu.VMEM), pl.BlockSpec(memory_space=pltpu.SMEM)
    shape = jax.ShapeDtypeStruct((4, rows, HEAD_DIM), jnp.bfloat16)
    return pl.pallas_call(
        functools.partial(attend_kernel, 3 * position * HEAD_DIM),
        in_specs=[smem, smem]
        + [vmem] * (len(blocks) + 3)
        + [pl.BlockSpec(memory_space=pl.ANY)] * len(after),
        out_specs=(vmem, vmem, vmem),
        out_shape=(shape,)
        + tuple(
            jax.ShapeDtypeStruct((count, HEAD_DIM), jnp.bfloat16)
            for count in (PACKED_ROWS, queries - PACKED_ROWS)
        ),
        scratch_shapes=[
            pltpu.VMEM((keys, 2 * HEAD_DIM), jnp.bfloat16),
            pltpu.VMEM((keys, 2 * HEAD_DIM), jnp.bfloat16),
            pltpu.VMEM((keys, 2 * HEAD_DIM), jnp.bfloat16),
            pltpu.VMEM((queries + 2 * rows, HEAD_DIM), jnp.float32),
        ],
        compiler_params=pltpu.CompilerParams(vmem_limit_bytes=24 * MIB),
        cost_estimate=pl.CostEstimate(
            flops=COST, bytes_accessed=COST, transcendentals=0
        ),
    )(place, runs, *blocks, order, query_mask, key_mask, *after)


def join_kernel(heads, runs_ref, *refs):
    outs, held = refs[-5:-1], refs[-1]
    rows = outs[0].shape[0]
    for head in range(heads):
        stay_ref, low = refs[3 * head], rows
        for ref in refs[3 * head + 1 : 3 * head + 3]:
            held[low : low + ref.shape[0], :] = ref[...].astype(jnp.float32)
            low += ref.shape[0]
        spot = slice(head * HEAD_DIM, (head + 1) * HEAD_DIM)
        for d in range(4):
            arrived = spread_run(held, runs_ref, 4 + d, rows).astype(jnp.bfloat16)
            outs[d][:, spot] = stay_ref[d] + arrived


def join_halves(runs, stays, arrivals, others, after, cost):
    heads, (slots, rows, width) = len(stays), stays[0].shape
    vmem = pl.BlockSpec(memory_space=pltpu.VMEM)
    parts = [part for three in zip(stays, arrivals, others) for part in three]
    shape = jax.ShapeDtypeStruct((rows, heads * width), jnp.bfloat16)
    return pl.pallas_call(
        functools.partial(join_kernel, heads),
        in_specs=[pl.BlockSpec(memory_space=pltpu.SMEM)]
        + [vmem] * len(parts)
        + [pl.BlockSpec(memory_space=pl.ANY)] * len(after),
        out_specs=(vmem,) * slots,
        out_shape=(shape,) * slots,
        scratch_shapes=[
            pltpu.VMEM((arrivals[0].shape[0] + others[0].shape[0] + 2 * rows, width), jnp.float32)
        ],
        compiler_params=pltpu.CompilerParams(vmem_limit_bytes=16 * MIB),
        cost_estimate=pl.CostEstimate(flops=cost, bytes_accessed=COST, transcendentals=0),
    )(runs, *parts, *after)


def gather_kernel(place_ref, w_ref, held_ref, pair_ref, *rest):
    outs, sems = rest[-5:-1], rest[-1]
    chip, columns = place_ref[4], outs[0].shape[1]
    heads = w_ref.shape[0] // HEAD_DIM // 4
    spot = pl.ds(pl.multiple_of(place_ref[6] * columns, HEAD_DIM), columns)

    def rows_at(block):
        return pl.ds(pl.multiple_of(block * HEAD_DIM, HEAD_DIM), HEAD_DIM)

    def transfers(near_ref, far_ref):
        copies = []
        for d in range(4):
            for index in range(heads):
                last = index + 1 == heads
                group = 1 if last else 0
                to = d if last else d * (heads - 1) + index
                to = slice(to * HEAD_DIM, (to + 1) * HEAD_DIM)
                head = head_of(jnp.bitwise_xor(chip, d), index, heads)
                there = 2 * index + jnp.bitwise_xor(chip, d) % 2
                sources = (
                    w_ref.at[rows_at(head), spot],
                    (near_ref if d < 2 else far_ref).at[rows_at(there), :],
                )
                for side, source in enumerate(sources):
                    copies.append(
                        pltpu.make_async_copy(
                            source, outs[2 * side + group].at[to, :], sems.at[side, index, d]
                        )
                    )
        for copy in copies:
            copy.start()
        for copy in copies:
            copy.wait()

    @pl.when(chip // 2 == place_ref[8])
    def _():
        transfers(held_ref, pair_ref)

    @pl.when(chip // 2 != place_ref[8])
    def _():
        transfers(pair_ref, held_ref)


def gather_out_weights(place, w_out, held, pair, group_heads, after):
    vmem, hbm = pl.BlockSpec(memory_space=pltpu.VMEM), pl.BlockSpec(memory_space=pltpu.HBM)
    any_space = pl.BlockSpec(memory_space=pl.ANY)
    shapes = tuple(
        jax.ShapeDtypeStruct((count * HEAD_DIM, w_out.shape[1] // 2), w_out.dtype)
        for count in (4 * (group_heads - 1), 4)
    )
    return pl.pallas_call(
        gather_kernel,
        in_specs=[pl.BlockSpec(memory_space=pltpu.SMEM), hbm] + [any_space] * (2 + len(after)),
        out_specs=(vmem,) * 4,
        out_shape=shapes + shapes,
        scratch_shapes=[pltpu.SemaphoreType.DMA((2, group_heads, 4))],
        compiler_params=pltpu.CompilerParams(vmem_limit_bytes=16 * MIB),
        cost_estimate=pl.CostEstimate(flops=COST, bytes_accessed=COST, transcendentals=0),
    )(place, w_out, held, pair, *after)


def out_rows_kernel(*refs):
    refs[-1][...] = jnp.concatenate([ref[...] for ref in refs[:-1]], axis=1)


def out_kernel(pairs, *refs):
    total = refs[2 * pairs][...] if len(refs) > 2 * pairs + 1 else None
    for pair in range(pairs):
        product = jnp.dot(
            refs[2 * pair][...], refs[2 * pair + 1][...], preferred_element_type=jnp.float32
        )
        total = product if total is None else total + product
    refs[-1][...] = total.astype(refs[-1].dtype)


def out_call(kernel, arrays, shape, dtype):
    vmem = pl.BlockSpec(memory_space=pltpu.VMEM)
    return pl.pallas_call(
        kernel,
        in_specs=[vmem] * len(arrays),
        out_specs=vmem,
        out_shape=jax.ShapeDtypeStruct(shape, dtype),
        compiler_params=pltpu.CompilerParams(vmem_limit_bytes=16 * MIB),
        cost_estimate=pl.CostEstimate(flops=COST, bytes_accessed=COST, transcendentals=0),
    )(*arrays)


SWAP_ROWS = (128, 112, 80)
PACKED_ROWS = 768
ATTEND_TILES = 3
HEAD_CHUNKS = ((0,), (1, 2))
COPY_PIECES = 4


def halved_body(
    inputs,
    norm_gain,
    level_table,
    w_qkv,
    w_out,
    clip_lengths,
    prefix_lengths,
    noise_levels,
    token_rank,
):
    ranks, per_dev = 16, inputs.shape[0]
    half_rows = 8 * per_dev
    clips = clip_lengths.shape[0]
    index = jnp.arange(clips, dtype=jnp.int32)

    ahead = (index[None, :] < index[:, None]) & (clip_lengths == MAXCLIP)[:, None]
    start = jnp.sum(jnp.where(ahead, clip_lengths[None, :], 0))
    early = start <= half_rows // 2

    rank_here = lax.axis_index("ctx")
    side = lax.axis_index("head")
    columns = inputs.shape[1]
    group_heads = w_qkv.shape[2] // HEAD_DIM // 4
    half, block, core = rank_here // 8, rank_here % 8, rank_here % 2
    chip = block // 2
    swap_sides = [(0, 1), (1, 0)]

    def exchange(array, flip, only=lambda r: True):
        pairs = [(r, r ^ flip) for r in range(ranks) if only(r)]
        return lax.ppermute(array, "ctx", pairs)

    def move_rows(swapping):
        return functools.partial(moved_rows, swapping)

    def moved_rows(
        swapping, start, inputs, clip_lengths, prefix_lengths, noise_levels, w_out
    ):
        place = jnp.stack(
            [
                start,
                jnp.int32(1 if 0 in swapping else 0),
                half,
                jnp.int32(half_rows),
                chip,
                jnp.int32(clips),
                side,
                block * per_dev,
                core,
                rank_here,
            ]
        )
        earlier = index[None, :] < index[:, None]
        begins = jnp.sum(jnp.where(earlier, clip_lengths[None, :], 0), axis=1)
        leads = begins + jnp.minimum(prefix_lengths, clip_lengths)
        bounds = jnp.pad(
            jnp.stack([begins, begins + clip_lengths, leads]), ((0, 5), (0, HEAD_DIM - clips))
        )

        cuts = [sum(SWAP_ROWS[:i]) for i in range(len(SWAP_ROWS) + 1)]
        kept, moved = [], []
        for low, high in zip(cuts[:-1], cuts[1:]):
            own = inputs[low:high]
            moved.append(exchange(own, 8, lambda r: r % 8 in swapping))
            kept.append(select_rows(place, own, moved[-1], low, kept[-1:]))
        other = [lax.ppermute(part, "head", swap_sides) for part in kept]
        depth = w_out.shape[0] // 2
        sent = lax.dynamic_slice(w_out, (core * depth, (1 - side) * columns), (depth, columns))
        return tuple(kept), tuple(other), place, bounds, noise_levels.reshape(-1, 1), sent

    kept, other, place, bounds, noise_column, sent = lax.cond(
        early,
        move_rows(range(4)),
        move_rows(range(4, 8)),
        start,
        inputs,
        clip_lengths,
        prefix_lengths,
        noise_levels,
        w_out,
    )
    far_held = lax.ppermute(sent, "head", swap_sides)
    normed = normalize_rows(place, kept, other, bounds, noise_column, level_table, norm_gain)
    pair = exchange(normed, 1)
    w_parts = jnp.transpose(w_qkv, (1, 0, 2))
    query_order, runs, query_mask, key_mask, weights = make_tables(
        place, bounds, token_rank, ranks, half_rows, w_parts
    )

    row = jnp.arange(ranks * per_dev, dtype=jnp.int32)
    in_long = (row >= start) & (row < start + half_rows)
    home = jnp.where(in_long == early, 0, 1)
    crosses = token_rank // (ranks // 2) != home
    kind = jnp.where(crosses, 2 * home + token_rank % 2, 4)
    counts = jnp.sum((kind[:, None] == jnp.arange(4)[None, :]).astype(jnp.int32), axis=0)
    fits = jnp.max(counts) <= PACKED_ROWS

    def cross_rest(parts):
        return lax.cond(
            fits,
            lambda parts: parts,
            lambda parts: tuple(exchange(part, 8) for part in parts),
            tuple(parts),
        )

    def held_back(array, after):
        return lax.optimization_barrier((array, *after))[0]

    blocks, pair_firsts, after = [], [], [query_order]
    for heads in HEAD_CHUNKS:
        first, second = project_heads(
            held_back(place, after), normed, pair, weights, heads, []
        )
        near = lax.ppermute(
            second, "ctx", [(r, r ^ (2 if r % 2 == 0 else 4)) for r in range(ranks)]
        )
        far = exchange(first, 6, lambda r: r % 2 == 1)
        blocks.append((first, near, far))
        if not pair_firsts:
            pair_firsts.append(exchange(first, 1, lambda r: r % 2 == 0))
            after = [pair_firsts[0]]

    def share(block, after):
        first, near, far = block
        near, far, *unused = lax.optimization_barrier((near, far, *after))
        if not pair_firsts:
            pair_firsts.append(exchange(held_back(first, after), 1, lambda r: r % 2 == 0))
        return [
            first,
            near,
            far,
            pair_firsts.pop(),
            exchange(far, 1, lambda r: r % 2 == 1),
            exchange(near, 1),
        ]

    def join(heads, after, cost):
        joined = join_halves(
            held_back(runs, after), stays[heads], arrivals[heads], others[heads], [], cost
        )
        return [exchange(part, 2 * d) if d else part for d, part in enumerate(joined)]

    stays, arrivals, others = [], [], []
    after = [blocks[-1][0]]
    for block, heads in zip(blocks, HEAD_CHUNKS):
        block = share(block, after)
        for position, head in enumerate(heads):
            stay, cross, more = attend(
                held_back(place, after),
                runs,
                block,
                position,
                query_order,
                query_mask,
                key_mask,
                [],
            )
            stays.append(stay)
            arrivals.append(exchange(cross, 8))
            others.append(more)
            after = [cross] + (arrivals[head - 1 : head] if head else [])
            if head == 1:
                far_pair = exchange(lax.optimization_barrier((far_held, cross))[0], 1)

    others = cross_rest(others)
    w_all = gather_out_weights(
        held_back(place, [cross]), w_out, far_held, far_pair, group_heads, []
    )

    def side_by_side(parts):
        width = sum(part.shape[1] for part in parts)
        return out_call(out_rows_kernel, parts, (per_dev, width), jnp.bfloat16)

    pieces = join(slice(0, -1), [cross], COST)
    rows = [side_by_side(pieces), side_by_side(join(slice(-1, None), [], LONG_COST))]
    far_rows = [lax.ppermute(part, "head", swap_sides) for part in rows]
    w_own, w_far = w_all[:2], w_all[2:]

    def add(terms, total, dtype):
        arrays = [array for term in terms for array in term] + total
        return out_call(functools.partial(out_kernel, len(terms)), arrays, (per_dev, columns), dtype)

    own, far = list(zip(rows, w_own)), list(zip(far_rows, w_far))
    total = add(own[:1], [], jnp.float32)
    total = add(own[1:] + far[:1], [total], jnp.float32)
    return add(far[1:], [total], jnp.bfloat16)


def solution(mesh):
    in_specs = (
        P("ctx", "head"),
        P(),
        P(),
        P(None, None, "head"),
        P("head", None),
        P(),
        P(),
        P(),
        P(),
    )
    out_specs = P("ctx", "head")

    def body(inputs, norm_gain, level_table, w_qkv, *rest):
        ranks, sides = mesh.shape["ctx"], mesh.shape["head"]
        heads_here = w_qkv.shape[2] // HEAD_DIM
        halved = (
            ranks == 16
            and sides == 2
            and ranks * inputs.shape[0] == 2 * MAXCLIP
            and heads_here == 4 * sum(len(heads) for heads in HEAD_CHUNKS)
        )
        run = halved_body if halved else gathered_body
        return run(inputs, norm_gain, level_table, w_qkv, *rest)

    return jax.shard_map(body, mesh=mesh, in_specs=in_specs, out_specs=out_specs, check_vma=False)
```

```python
import functools

import jax
import jax.numpy as jnp
from jax import lax
from jax.experimental import pallas as pl
from jax.experimental.pallas import tpu as pltpu
from jax.sharding import PartitionSpec as P

HEAD_DIM = 128


NEG = -1e30
EPS = 1e-06
MAXCLIP = 2560
LOG2E = 1.4426950408889634
MIB = 1024 * 1024
COST = 1000000
LONG_COST = 200000000000


def clip_tables(total_rows, clip_lengths, prefix_lengths, noise_levels):
    rows = jnp.arange(total_rows, dtype=jnp.int32)
    ends = jnp.cumsum(clip_lengths)
    begins = ends - clip_lengths
    clip_of = jnp.sum((rows[:, None] >= ends[None, :]).astype(jnp.int32), axis=1)
    member = clip_of[:, None] == jnp.arange(clip_lengths.shape[0], dtype=jnp.int32)[None, :]
    begin_row = jnp.sum(jnp.where(member, begins[None, :], 0), axis=1)
    lead = jnp.minimum(prefix_lengths, clip_lengths)
    lead_row = jnp.sum(jnp.where(member, lead[None, :], 0), axis=1)
    level_row = jnp.sum(jnp.where(member, noise_levels[None, :], 0), axis=1)
    in_prefix = rows - begin_row < lead_row
    return (clip_of, in_prefix, level_row)


def rank_tables(token_rank, ranks, per_rank):
    onehot = (token_rank[:, None] == jnp.arange(ranks, dtype=jnp.int32)[None, :]).astype(jnp.int32)
    earlier = jnp.cumsum(onehot, axis=0) - onehot
    within = jnp.sum(earlier * onehot, axis=1)
    counts = jnp.sum(onehot.reshape(ranks, per_rank, ranks), axis=1)
    starts = jnp.cumsum(counts, axis=0) - counts
    return (within, counts, starts)


def normalize(rows, in_prefix, level_row, level_table, norm_gain):
    picks = (
        level_row[:, None] == jnp.arange(level_table.shape[0], dtype=jnp.int32)[None, :]
    ) & in_prefix[:, None]
    added = jnp.dot(picks.astype(jnp.bfloat16), level_table, preferred_element_type=jnp.float32)
    shifted = rows.astype(jnp.float32) + added
    factor = lax.rsqrt(jnp.mean(shifted * shifted, axis=-1, keepdims=True) + EPS)
    return (shifted * factor * norm_gain).astype(jnp.bfloat16)


def fold_keys(state, queries, query_clip, query_prefix, pairs, key_clip, key_prefix):
    width = queries.shape[1]
    heads_here = width // HEAD_DIM
    factor = HEAD_DIM ** (-0.5)
    allowed_query = jnp.logical_not(query_prefix)

    def absorb(carry, block):
        block_pairs, block_clip, block_prefix = block
        allowed = (query_clip[:, None] == block_clip[None, :]) & (
            allowed_query[:, None] | block_prefix[None, :]
        )
        updated = []
        for head in range(heads_here):
            top, total, summed = carry[head]
            low = head * HEAD_DIM
            q_head = queries[:, low : low + HEAD_DIM]
            k_head = block_pairs[:, low : low + HEAD_DIM]
            v_head = block_pairs[:, width + low : width + low + HEAD_DIM]
            scores = (
                lax.dot_general(
                    q_head, k_head, (((1,), (1,)), ((), ())), preferred_element_type=jnp.float32
                )
                * factor
            )
            masked = jnp.where(allowed, scores, NEG)
            new_top = jnp.maximum(top, jnp.max(masked, axis=1, keepdims=True))
            fade = jnp.exp(top - new_top)
            weights = jnp.where(allowed, jnp.exp(scores - new_top), 0.0)
            total = total * fade + jnp.sum(weights, axis=1, keepdims=True)
            summed = summed * fade + jnp.dot(
                weights.astype(jnp.bfloat16), v_head, preferred_element_type=jnp.float32
            )
            updated.append((new_top, total, summed))
        return (tuple(updated), None)

    count = pairs.shape[0]
    step = 2048 if count > 2048 and count % 2048 == 0 else count
    if step == count:
        result, unused = absorb(state, (pairs, key_clip, key_prefix))
        return result
    stacked = (
        pairs.reshape(count // step, step, pairs.shape[1]),
        key_clip.reshape(count // step, step),
        key_prefix.reshape(count // step, step),
    )
    result, unused = lax.scan(absorb, state, stacked)
    return result


def gathered_body(
    inputs,
    norm_gain,
    level_table,
    w_qkv,
    w_out,
    clip_lengths,
    prefix_lengths,
    noise_levels,
    token_rank,
):
    ranks = lax.axis_size("ctx")
    rank_here = lax.axis_index("ctx")
    per_dev = inputs.shape[0]
    slots = 2 * per_dev // ranks
    local_width = w_qkv.shape[2]
    heads_here = local_width // HEAD_DIM
    total_rows = per_dev * ranks
    clip_of, in_prefix, level_row = clip_tables(
        total_rows, clip_lengths, prefix_lengths, noise_levels
    )
    within, counts, starts = rank_tables(token_rank, ranks, per_dev)
    place = token_rank * per_dev + within
    order = (
        jnp.zeros((total_rows,), jnp.int32).at[place].set(jnp.arange(total_rows, dtype=jnp.int32))
    )
    first = rank_here * per_dev
    own_rank = lax.dynamic_slice_in_dim(token_rank, first, per_dev, 0)
    own_within = lax.dynamic_slice_in_dim(within, first, per_dev, 0)
    send_starts = lax.dynamic_slice_in_dim(starts, rank_here, 1, 0)[0]
    recv_counts = lax.dynamic_slice_in_dim(counts, rank_here, 1, 1)[:, 0]
    recv_starts = lax.dynamic_slice_in_dim(starts, rank_here, 1, 1)[:, 0]
    balanced_rows = lax.dynamic_slice_in_dim(order, first, per_dev, 0)
    target = own_rank * slots + own_within - send_starts[own_rank]
    buffer = jnp.zeros((ranks * slots, inputs.shape[1]), inputs.dtype).at[target].set(inputs)
    received = lax.all_to_all(
        buffer.reshape(ranks, slots, inputs.shape[1]),
        "ctx",
        split_axis=0,
        concat_axis=0,
        tiled=True,
    )
    spots = jnp.arange(slots, dtype=jnp.int32)[None, :]
    index = jnp.where(spots < recv_counts[:, None], recv_starts[:, None] + spots, per_dev).reshape(
        -1
    )
    flat = received.reshape(ranks * slots, received.shape[2])
    rows = jnp.zeros((per_dev, received.shape[2]), received.dtype).at[index].set(flat, mode="drop")
    full_rows = lax.all_gather(rows, "head", axis=1, tiled=True)
    normed = normalize(
        full_rows, in_prefix[balanced_rows], level_row[balanced_rows], level_table, norm_gain
    )
    qkv = jnp.dot(
        normed, w_qkv.reshape(w_qkv.shape[0], 3 * local_width), preferred_element_type=jnp.float32
    ).astype(jnp.bfloat16)
    start_state = tuple(
        (
            (
                jnp.full((per_dev, 1), NEG, jnp.float32),
                jnp.zeros((per_dev, 1), jnp.float32),
                jnp.zeros((per_dev, HEAD_DIM), jnp.float32),
            )
            for head in range(heads_here)
        )
    )
    key_clip = clip_of[order]
    key_prefix = in_prefix[order]
    query_clip = lax.dynamic_slice_in_dim(key_clip, first, per_dev, 0)
    query_prefix = lax.dynamic_slice_in_dim(key_prefix, first, per_dev, 0)
    queries = qkv[:, :local_width]
    pairs = qkv[:, local_width:]
    state = fold_keys(
        start_state,
        queries,
        query_clip,
        query_prefix,
        lax.all_gather(pairs, "ctx", axis=0, tiled=True),
        key_clip,
        key_prefix,
    )
    parts = [state[head][2] / state[head][1] for head in range(heads_here)]
    attention = jnp.concatenate(parts, axis=1).astype(jnp.bfloat16)
    terms = jnp.dot(attention, w_out, preferred_element_type=jnp.float32)
    return lax.psum_scatter(terms.astype(jnp.bfloat16), "head", scatter_dimension=1, tiled=True)


def packed_rows(place_ref, spots):
    start, early, half = place_ref[0], place_ref[1], place_ref[2]
    total = place_ref[3]
    before = jnp.where(spots < start, early, 1 - early)
    return spots + total * (half + before * (1 - 2 * half))


def clip_flags(rows, bounds_ref):
    begins, ends, leads = bounds_ref[0:1, :], bounds_ref[1:2, :], bounds_ref[2:3, :]
    inside = (rows >= begins) & (rows < ends)
    return inside, inside & (rows < leads)


def count_earlier(hot):
    ranks, rows, lanes = hot.shape
    flat = hot.reshape(ranks * rows, lanes).astype(jnp.bfloat16)

    def numbers(shape, axis):
        return lax.broadcasted_iota(jnp.int32, shape, axis)

    def group(index):
        return sum(jnp.where(index >= rows * k, 1, 0) for k in range(1, ranks))

    def ones(flags):
        return jnp.where(flags, 1.0, 0.0).astype(jnp.bfloat16)

    total = ranks * rows
    in_row = ones(numbers((lanes, lanes), 0) < numbers((lanes, lanes), 1))
    below, across = numbers((total, 1), 0), numbers((1, total), 1)
    in_rank = ones((group(below) == group(across)) & (across < below))
    row_sums = jnp.dot(
        flat, jnp.ones((lanes, lanes), jnp.bfloat16), preferred_element_type=jnp.float32
    )
    earlier = jnp.dot(flat, in_row, preferred_element_type=jnp.float32) + jnp.dot(
        in_rank, row_sums.astype(jnp.bfloat16), preferred_element_type=jnp.float32
    )
    return earlier.reshape(ranks, rows, lanes)


def table_kernel(ranks, place_ref, bounds_ref, rank_ref, w_ref, *refs):
    order_ref, runs_ref, query_ref, key_ref, weights_ref, held, sems = refs
    copies = weight_copies(place_ref, w_ref, weights_ref, sems)
    for copy in copies:
        copy.start()
    start, early, half, half_rows = (place_ref[k] for k in range(4))
    chip, clips, core, rank_here = (place_ref[k] for k in (4, 5, 8, 9))
    holds_long = half != early
    tokens = rank_ref[...]
    rows, lanes = tokens.shape
    per_dev = rows * lanes // ranks

    token = lanes * lax.broadcasted_iota(jnp.int32, tokens.shape, 0) + lax.broadcasted_iota(
        jnp.int32, tokens.shape, 1
    )
    hots = [jnp.where(tokens == rank, 1.0, 0.0) for rank in range(ranks)]
    earlier = count_earlier(jnp.stack(hots))
    within = sum(hots[rank] * earlier[rank] for rank in range(ranks))
    before = jnp.where(token < start, 1.0, 0.0)
    upto = jnp.where(token < start + half_rows, 1.0, 0.0)
    lane = lax.broadcasted_iota(jnp.int32, (1, lanes), 1)
    target = jnp.bitwise_xor(rank_here, 2 * jnp.bitwise_and(lane, 3))
    lane_long = jnp.where(lane < 4, jnp.where(holds_long, 1.0, 0.0), jnp.where(holds_long, 0.0, 1.0))
    lane_own = jnp.where(lane < 4, 1.0, 0.0)
    lows, longs, long_first, rest_first = [], [], [], []
    long_count, rest_count = [[0.0, 0.0], [0.0, 0.0]], [[0.0, 0.0], [0.0, 0.0]]
    for rank, hot in enumerate(hots):
        low = jnp.sum(hot * before, keepdims=True)
        long_rows = jnp.sum(hot * upto, keepdims=True) - low
        group, parity = rank // (ranks // 2), rank % 2
        lows.append(low)
        longs.append(long_rows)
        long_first.append(long_count[group][parity])
        rest_first.append(rest_count[group][parity])
        long_count[group][parity] = long_first[rank] + long_rows
        rest_count[group][parity] = rest_first[rank] + (per_dev - long_rows)
    long_base = rest_base = low_of = long_of = 0.0
    runs = [0.0] * 5
    for rank, hot in enumerate(hots):
        low, high, long_rows = lows[rank], lows[rank] + longs[rank], longs[rank]
        group, parity = rank // (ranks // 2), rank % 2
        own_group = jnp.where(half == group, 1.0, 0.0)
        long_after = own_group * long_count[1 - group][parity]
        rest_after = own_group * rest_count[1 - group][parity]
        long_base += hot * (long_first[rank] + long_after - low)
        rest_base += hot * (rest_first[rank] + rest_after)
        low_of += hot * low
        long_of += hot * long_rows
        first = long_first[rank] + lane_own * long_after
        rest = rest_first[rank] + lane_own * rest_after
        here = jnp.where(target == rank, 1.0, 0.0)
        values = (
            (0.0, low),
            (low, high),
            (high, float(per_dev)),
            (0.0, rest),
            (first - low, rest - long_rows),
        )
        runs = [
            run + here * (lane_long * if_long + (1.0 - lane_long) * if_rest)
            for run, (if_long, if_rest) in zip(runs, values)
        ]
    furthest = rows * lanes // 4 + per_dev // 2
    for index, run in enumerate(runs):
        run = run.astype(jnp.int32)
        runs_ref[index : index + 1, :] = (
            run if index < 3 else jnp.clip(run, -per_dev, furthest)
        )
    sorted_at = within + jnp.where(
        upto - before == 1.0, long_base, rest_base - jnp.where(within < low_of, 0.0, long_of)
    )
    held[...] = jnp.where(jnp.bitwise_and(tokens, 1) == core, sorted_at.astype(jnp.int32), -1)
    half_lines = rows // 2
    spots = lanes * lax.broadcasted_iota(
        jnp.int32, (half_lines, lanes), 0
    ) + lax.broadcasted_iota(jnp.int32, (half_lines, lanes), 1)
    later = packed_rows(place_ref, spots) >= half_rows
    held[:half_lines, :] = jnp.where(later, held[half_lines:, :], held[:half_lines, :])
    lines = half_lines // 4
    for d in range(4):
        line = lines * jnp.bitwise_xor(chip, d)
        order_ref[lines * d : lines * (d + 1), :] = held[pl.ds(line, lines), :]

    column = lax.broadcasted_iota(jnp.int32, (1, HEAD_DIM), 1)
    chip_rows = query_ref.shape[0] // 4
    for d in range(4):
        local = lax.broadcasted_iota(jnp.int32, (chip_rows, 1), 0)
        spots = chip_rows * jnp.bitwise_xor(chip, d) + local
        inside, leading = clip_flags(packed_rows(place_ref, spots), bounds_ref)
        spot = slice(d * chip_rows, (d + 1) * chip_rows)
        inside = jnp.where(inside, 1.0, 0.0)
        prefix = jnp.sum(jnp.where(leading, 1.0, 0.0), axis=1, keepdims=True)
        query_ref[spot, :] = jnp.where(column == clips, prefix, inside).astype(jnp.bfloat16)
        outside = jnp.where(column < clips, NEG * (1.0 - inside), 0.0)
        key_ref[spot, :] = jnp.where(column == clips, NEG * (1.0 - prefix), outside).astype(
            jnp.bfloat16
        )
    for copy in copies:
        copy.wait()


def make_tables(place, bounds, token_rank, ranks, keys, w_parts):
    vmem = pl.BlockSpec(memory_space=pltpu.VMEM)
    tokens = token_rank.reshape(-1, HEAD_DIM)
    features = jax.ShapeDtypeStruct((keys, HEAD_DIM), jnp.bfloat16)
    return pl.pallas_call(
        functools.partial(table_kernel, ranks),
        in_specs=[
            pl.BlockSpec(memory_space=pltpu.SMEM),
            vmem,
            vmem,
            pl.BlockSpec(memory_space=pltpu.HBM),
        ],
        out_specs=(vmem,) * 5,
        out_shape=(
            jax.ShapeDtypeStruct((tokens.shape[0] // 2, HEAD_DIM), jnp.int32),
            jax.ShapeDtypeStruct((8, HEAD_DIM), jnp.int32),
            features,
            features,
            jax.ShapeDtypeStruct((*w_parts.shape[:2], w_parts.shape[2] // 2), w_parts.dtype),
        ),
        scratch_shapes=[
            pltpu.VMEM(tokens.shape, jnp.int32),
            pltpu.SemaphoreType.DMA((3, COPY_PIECES)),
        ],
        compiler_params=pltpu.CompilerParams(vmem_limit_bytes=26 * MIB),
        cost_estimate=pl.CostEstimate(flops=COST, bytes_accessed=COST, transcendentals=0),
    )(place, bounds, tokens, w_parts)


def select_kernel(low, place_ref, own_ref, moved_ref, *rest):
    out_ref = rest[-1]
    spots = place_ref[7] + low + lax.broadcasted_iota(jnp.int32, (out_ref.shape[0], 1), 0)
    swapped = jnp.where(spots < place_ref[0], place_ref[1], 1 - place_ref[1])
    out_ref[...] = jnp.where(swapped == 1, moved_ref[...], own_ref[...])


def select_rows(place, own, moved, low, after):
    vmem = pl.BlockSpec(memory_space=pltpu.VMEM)
    return pl.pallas_call(
        functools.partial(select_kernel, low),
        in_specs=[pl.BlockSpec(memory_space=pltpu.SMEM), vmem, vmem]
        + [pl.BlockSpec(memory_space=pl.ANY)] * len(after),
        out_specs=vmem,
        out_shape=jax.ShapeDtypeStruct(moved.shape, moved.dtype),
        compiler_params=pltpu.CompilerParams(vmem_limit_bytes=8 * MIB),
        cost_estimate=pl.CostEstimate(flops=COST, bytes_accessed=COST, transcendentals=0),
    )(place, own, moved, *after)


def head_of(chip, index, group_heads):
    return 2 * group_heads * (chip // 2) + 2 * index + chip % 2


def weight_copies(place_ref, w_ref, out_ref, sems):
    pair = jnp.bitwise_xor(place_ref[4] // 2, place_ref[8])
    columns = pl.ds(pl.multiple_of(pair * out_ref.shape[2], HEAD_DIM), out_ref.shape[2])
    depth = out_ref.shape[1] // COPY_PIECES
    copies = []
    for part in range(3):
        for piece in range(COPY_PIECES):
            rows = slice(piece * depth, (piece + 1) * depth)
            copies.append(
                pltpu.make_async_copy(
                    w_ref.at[part, rows, columns], out_ref.at[part, rows, :], sems.at[part, piece]
                )
            )
    return copies


def norm_kernel(place_ref, *refs):
    pieces = len(SWAP_ROWS)
    bounds_ref, noise_ref, level_ref, gain_ref = refs[2 * pieces : 2 * pieces + 4]
    out_ref = refs[-1]
    width = out_ref.shape[1] // 2
    side, first = place_ref[6], place_ref[7]
    clips, levels = noise_ref.shape[0], level_ref.shape[0]
    spots = [pl.ds(pl.multiple_of(s * width, 128), width) for s in (side, 1 - side)]
    level = lax.broadcasted_iota(jnp.int32, (clips, levels), 1)
    chosen = jnp.where(noise_ref[...] == level, 1.0, 0.0).astype(jnp.bfloat16)
    tables = [
        jnp.dot(chosen, level_ref[:, spot], preferred_element_type=jnp.float32).astype(
            jnp.bfloat16
        )
        for spot in spots
    ]
    low = 0
    for piece in range(pieces):
        own_ref, other_ref = refs[piece], refs[pieces + piece]
        count = own_ref.shape[0]
        rows = slice(low, low + count)
        places = first + low + lax.broadcasted_iota(jnp.int32, (count, 1), 0)
        low += count
        unused, leading = clip_flags(packed_rows(place_ref, places), bounds_ref)
        picks = jnp.where(leading, 1.0, 0.0)[:, :clips].astype(jnp.bfloat16)
        shifted = [
            ref[...].astype(jnp.float32)
            + jnp.dot(picks, table, preferred_element_type=jnp.float32)
            for ref, table in zip((own_ref, other_ref), tables)
        ]
        squares = sum(jnp.sum(part * part, axis=1, keepdims=True) for part in shifted)
        factor = lax.rsqrt(squares / (2 * width) + EPS)
        for part, spot in zip(shifted, spots):
            out_ref[rows, spot] = (part * factor * gain_ref[:, spot]).astype(jnp.bfloat16)


def normalize_rows(place, kept, other, bounds, noise_levels, level_table, norm_gain):
    rows, depth = sum(part.shape[0] for part in kept), 2 * kept[0].shape[1]
    vmem = pl.BlockSpec(memory_space=pltpu.VMEM)
    return pl.pallas_call(
        norm_kernel,
        in_specs=[pl.BlockSpec(memory_space=pltpu.SMEM)] + [vmem] * (2 * len(kept) + 4),
        out_specs=vmem,
        out_shape=jax.ShapeDtypeStruct((rows, depth), jnp.bfloat16),
        compiler_params=pltpu.CompilerParams(vmem_limit_bytes=26 * MIB),
        cost_estimate=pl.CostEstimate(flops=COST, bytes_accessed=COST, transcendentals=0),
    )(place, *kept, *other, bounds, noise_levels, level_table, norm_gain.reshape(1, -1))


def project_kernel(indices, place_ref, own_ref, pair_ref, weights_ref, *rest):
    first_ref, second_ref = rest[-2:]
    rows = jnp.concatenate([own_ref[...], pair_ref[...]], axis=0)
    count = own_ref.shape[0]
    same = place_ref[4] % 2 == place_ref[8]

    def store(outcome, base, even_ref, odd_ref):
        for index, core in enumerate((place_ref[8], 1 - place_ref[8])):
            spot = pl.ds(pl.multiple_of(core * count, count), count)
            half = outcome[index * count : (index + 1) * count]
            for part in range(3):
                to = slice(base + part * HEAD_DIM, base + (part + 1) * HEAD_DIM)
                even_ref[spot, to] = half[:, 2 * part * HEAD_DIM : (2 * part + 1) * HEAD_DIM]
                odd_ref[spot, to] = half[:, (2 * part + 1) * HEAD_DIM : 2 * (part + 1) * HEAD_DIM]

    for position, index in enumerate(indices):
        spot = slice(2 * index * HEAD_DIM, 2 * (index + 1) * HEAD_DIM)
        weights = jnp.concatenate([weights_ref[part, :, spot] for part in range(3)], axis=1)
        outcome = jnp.dot(rows, weights, preferred_element_type=jnp.float32).astype(jnp.bfloat16)
        base = 3 * position * HEAD_DIM

        @pl.when(same)
        def _():
            store(outcome, base, first_ref, second_ref)

        @pl.when(jnp.logical_not(same))
        def _():
            store(outcome, base, second_ref, first_ref)


def project_heads(place, own, pair, weights, indices, after):
    rows = own.shape[0]
    vmem = pl.BlockSpec(memory_space=pltpu.VMEM)
    shape = jax.ShapeDtypeStruct((2 * rows, 3 * len(indices) * HEAD_DIM), jnp.bfloat16)
    return pl.pallas_call(
        functools.partial(project_kernel, indices),
        in_specs=[pl.BlockSpec(memory_space=pltpu.SMEM), vmem, vmem, vmem]
        + [pl.BlockSpec(memory_space=pl.ANY)] * len(after),
        out_specs=(vmem, vmem),
        out_shape=(shape, shape),
        compiler_params=pltpu.CompilerParams(vmem_limit_bytes=20 * MIB),
        cost_estimate=pl.CostEstimate(flops=COST, bytes_accessed=COST, transcendentals=0),
    )(place, own, pair, weights, *after)


def attend_kernel(base, place_ref, runs_ref, *refs):
    mine, near, far, pair_first, pair_far, pair_near = refs[:6]
    order_ref, query_mask_ref, key_mask_ref = refs[6:9]
    stay_ref, cross_ref, more_ref, q_all, k_all, v_all, sorted_out = refs[-7:]
    chip_rows = mine.shape[0]
    rows = chip_rows // 2
    queries = sorted_out.shape[0] - 2 * rows

    def hold(sources):
        for index, source in enumerate(sources):
            spot = slice(index * chip_rows, (index + 1) * chip_rows)
            for part, held in enumerate((q_all, k_all, v_all)):
                low = base + part * HEAD_DIM
                held[spot, :HEAD_DIM] = source[:, low : low + HEAD_DIM]

    @pl.when(place_ref[8] == 0)
    def _():
        hold((mine, near, pair_near, pair_far))

    @pl.when(place_ref[8] == 1)
    def _():
        hold((pair_first, pair_near, near, far))

    q_all[:, HEAD_DIM:] = query_mask_ref[...]
    k_all[:, HEAD_DIM:] = key_mask_ref[...]
    v_all[:, HEAD_DIM:] = jnp.ones((4 * chip_rows, HEAD_DIM), jnp.bfloat16)
    tile = queries // ATTEND_TILES

    def score(step):
        wanted = step * tile + lax.broadcasted_iota(jnp.int32, (tile, 1), 0)
        picks = jnp.concatenate(
            [
                jnp.where(order_ref[line : line + 1, :] == wanted, 1.0, 0.0).astype(jnp.bfloat16)
                for line in range(order_ref.shape[0])
            ],
            axis=1,
        )
        sorted_queries = jnp.dot(picks, q_all[...], preferred_element_type=jnp.float32)
        return lax.dot_general(
            sorted_queries.astype(jnp.bfloat16),
            k_all[...],
            (((1,), (1,)), ((), ())),
            preferred_element_type=jnp.float32,
        )

    coming = score(0)
    for step in range(ATTEND_TILES):
        scores = coming
        if step + 1 < ATTEND_TILES:
            coming = score(step + 1)
        top = jnp.max(scores, axis=1, keepdims=True)
        weights = jnp.exp2((scores - top) * (HEAD_DIM ** (-0.5) * LOG2E))
        summed = jnp.dot(
            weights.astype(jnp.bfloat16), v_all[...], preferred_element_type=jnp.float32
        )
        sorted_out[rows + step * tile : rows + (step + 1) * tile, :] = (
            summed[:, :HEAD_DIM] / summed[:, HEAD_DIM:]
        )

    low = rows
    for ref in (cross_ref, more_ref):
        ref[...] = sorted_out[low : low + ref.shape[0], :].astype(jnp.bfloat16)
        low += ref.shape[0]
    for d in range(4):
        stay_ref[d] = spread_run(sorted_out, runs_ref, d, rows).astype(jnp.bfloat16)


def spread_run(sorted_ref, runs_ref, lane, rows):
    furthest = sorted_ref.shape[0] - 2 * rows
    row = lax.broadcasted_iota(jnp.int32, (rows, 1), 0)
    parts = [
        sorted_ref[pl.ds(rows + jnp.clip(runs_ref[line, lane], -rows, furthest), rows), :]
        for line in (3, 4)
    ]
    in_second = (row >= runs_ref[1, lane]) & (row < runs_ref[2, lane])
    return jnp.where(row < runs_ref[0, lane], parts[0], jnp.where(in_second, parts[1], 0.0))


def attend(place, runs, blocks, position, order, query_mask, key_mask, after):
    chip_rows = blocks[0].shape[0]
    rows, keys = chip_rows // 2, 4 * chip_rows
    queries = keys // 2 + rows // 2
    vmem, smem = pl.BlockSpec(memory_space=pltpu.VMEM), pl.BlockSpec(memory_space=pltpu.SMEM)
    shape = jax.ShapeDtypeStruct((4, rows, HEAD_DIM), jnp.bfloat16)
    return pl.pallas_call(
        functools.partial(attend_kernel, 3 * position * HEAD_DIM),
        in_specs=[smem, smem]
        + [vmem] * (len(blocks) + 3)
        + [pl.BlockSpec(memory_space=pl.ANY)] * len(after),
        out_specs=(vmem, vmem, vmem),
        out_shape=(shape,)
        + tuple(
            jax.ShapeDtypeStruct((count, HEAD_DIM), jnp.bfloat16)
            for count in (PACKED_ROWS, queries - PACKED_ROWS)
        ),
        scratch_shapes=[
            pltpu.VMEM((keys, 2 * HEAD_DIM), jnp.bfloat16),
            pltpu.VMEM((keys, 2 * HEAD_DIM), jnp.bfloat16),
            pltpu.VMEM((keys, 2 * HEAD_DIM), jnp.bfloat16),
            pltpu.VMEM((queries + 2 * rows, HEAD_DIM), jnp.float32),
        ],
        compiler_params=pltpu.CompilerParams(vmem_limit_bytes=24 * MIB),
        cost_estimate=pl.CostEstimate(
            flops=COST, bytes_accessed=COST, transcendentals=0
        ),
    )(place, runs, *blocks, order, query_mask, key_mask, *after)


def join_kernel(heads, runs_ref, *refs):
    outs, held = refs[-5:-1], refs[-1]
    rows = outs[0].shape[0]
    for head in range(heads):
        stay_ref, low = refs[3 * head], rows
        for ref in refs[3 * head + 1 : 3 * head + 3]:
            held[low : low + ref.shape[0], :] = ref[...].astype(jnp.float32)
            low += ref.shape[0]
        spot = slice(head * HEAD_DIM, (head + 1) * HEAD_DIM)
        for d in range(4):
            arrived = spread_run(held, runs_ref, 4 + d, rows).astype(jnp.bfloat16)
            outs[d][:, spot] = stay_ref[d] + arrived


def join_halves(runs, stays, arrivals, others, after, cost):
    heads, (slots, rows, width) = len(stays), stays[0].shape
    vmem = pl.BlockSpec(memory_space=pltpu.VMEM)
    parts = [part for three in zip(stays, arrivals, others) for part in three]
    shape = jax.ShapeDtypeStruct((rows, heads * width), jnp.bfloat16)
    return pl.pallas_call(
        functools.partial(join_kernel, heads),
        in_specs=[pl.BlockSpec(memory_space=pltpu.SMEM)]
        + [vmem] * len(parts)
        + [pl.BlockSpec(memory_space=pl.ANY)] * len(after),
        out_specs=(vmem,) * slots,
        out_shape=(shape,) * slots,
        scratch_shapes=[
            pltpu.VMEM((arrivals[0].shape[0] + others[0].shape[0] + 2 * rows, width), jnp.float32)
        ],
        compiler_params=pltpu.CompilerParams(vmem_limit_bytes=16 * MIB),
        cost_estimate=pl.CostEstimate(flops=cost, bytes_accessed=COST, transcendentals=0),
    )(runs, *parts, *after)


def gather_kernel(place_ref, w_ref, held_ref, pair_ref, *rest):
    outs, sems = rest[-5:-1], rest[-1]
    chip, columns = place_ref[4], outs[0].shape[1]
    heads = w_ref.shape[0] // HEAD_DIM // 4
    spot = pl.ds(pl.multiple_of(place_ref[6] * columns, HEAD_DIM), columns)

    def rows_at(block):
        return pl.ds(pl.multiple_of(block * HEAD_DIM, HEAD_DIM), HEAD_DIM)

    def transfers(near_ref, far_ref):
        copies = []
        for d in range(4):
            for index in range(heads):
                last = index + 1 == heads
                group = 1 if last else 0
                to = d if last else d * (heads - 1) + index
                to = slice(to * HEAD_DIM, (to + 1) * HEAD_DIM)
                head = head_of(jnp.bitwise_xor(chip, d), index, heads)
                there = 2 * index + jnp.bitwise_xor(chip, d) % 2
                sources = (
                    w_ref.at[rows_at(head), spot],
                    (near_ref if d < 2 else far_ref).at[rows_at(there), :],
                )
                for side, source in enumerate(sources):
                    copies.append(
                        pltpu.make_async_copy(
                            source, outs[2 * side + group].at[to, :], sems.at[side, index, d]
                        )
                    )
        for copy in copies:
            copy.start()
        for copy in copies:
            copy.wait()

    @pl.when(chip // 2 == place_ref[8])
    def _():
        transfers(held_ref, pair_ref)

    @pl.when(chip // 2 != place_ref[8])
    def _():
        transfers(pair_ref, held_ref)


def gather_out_weights(place, w_out, held, pair, group_heads, after):
    vmem, hbm = pl.BlockSpec(memory_space=pltpu.VMEM), pl.BlockSpec(memory_space=pltpu.HBM)
    any_space = pl.BlockSpec(memory_space=pl.ANY)
    shapes = tuple(
        jax.ShapeDtypeStruct((count * HEAD_DIM, w_out.shape[1] // 2), w_out.dtype)
        for count in (4 * (group_heads - 1), 4)
    )
    return pl.pallas_call(
        gather_kernel,
        in_specs=[pl.BlockSpec(memory_space=pltpu.SMEM), hbm] + [any_space] * (2 + len(after)),
        out_specs=(vmem,) * 4,
        out_shape=shapes + shapes,
        scratch_shapes=[pltpu.SemaphoreType.DMA((2, group_heads, 4))],
        compiler_params=pltpu.CompilerParams(vmem_limit_bytes=16 * MIB),
        cost_estimate=pl.CostEstimate(flops=COST, bytes_accessed=COST, transcendentals=0),
    )(place, w_out, held, pair, *after)


def out_rows_kernel(*refs):
    refs[-1][...] = jnp.concatenate([ref[...] for ref in refs[:-1]], axis=1)


def out_kernel(pairs, *refs):
    total = refs[2 * pairs][...] if len(refs) > 2 * pairs + 1 else None
    for pair in range(pairs):
        product = jnp.dot(
            refs[2 * pair][...], refs[2 * pair + 1][...], preferred_element_type=jnp.float32
        )
        total = product if total is None else total + product
    refs[-1][...] = total.astype(refs[-1].dtype)


def out_call(kernel, arrays, shape, dtype):
    vmem = pl.BlockSpec(memory_space=pltpu.VMEM)
    return pl.pallas_call(
        kernel,
        in_specs=[vmem] * len(arrays),
        out_specs=vmem,
        out_shape=jax.ShapeDtypeStruct(shape, dtype),
        compiler_params=pltpu.CompilerParams(vmem_limit_bytes=16 * MIB),
        cost_estimate=pl.CostEstimate(flops=COST, bytes_accessed=COST, transcendentals=0),
    )(*arrays)


SWAP_ROWS = (128, 112, 80)
PACKED_ROWS = 768
ATTEND_TILES = 3
HEAD_CHUNKS = ((0,), (1, 2))
COPY_PIECES = 4


def halved_body(
    inputs,
    norm_gain,
    level_table,
    w_qkv,
    w_out,
    clip_lengths,
    prefix_lengths,
    noise_levels,
    token_rank,
):
    ranks, per_dev = 16, inputs.shape[0]
    half_rows = 8 * per_dev
    clips = clip_lengths.shape[0]
    index = jnp.arange(clips, dtype=jnp.int32)

    ahead = (index[None, :] < index[:, None]) & (clip_lengths == MAXCLIP)[:, None]
    start = jnp.sum(jnp.where(ahead, clip_lengths[None, :], 0))
    early = start <= half_rows // 2

    rank_here = lax.axis_index("ctx")
    side = lax.axis_index("head")
    columns = inputs.shape[1]
    group_heads = w_qkv.shape[2] // HEAD_DIM // 4
    half, block, core = rank_here // 8, rank_here % 8, rank_here % 2
    chip = block // 2
    swap_sides = [(0, 1), (1, 0)]

    def exchange(array, flip, only=lambda r: True):
        pairs = [(r, r ^ flip) for r in range(ranks) if only(r)]
        return lax.ppermute(array, "ctx", pairs)

    def move_rows(swapping):
        return functools.partial(moved_rows, swapping)

    def moved_rows(
        swapping, start, inputs, clip_lengths, prefix_lengths, noise_levels, token_rank, w_out
    ):
        place = jnp.stack(
            [
                start,
                jnp.int32(1 if 0 in swapping else 0),
                half,
                jnp.int32(half_rows),
                chip,
                jnp.int32(clips),
                side,
                block * per_dev,
                core,
                rank_here,
            ]
        )
        earlier = index[None, :] < index[:, None]
        begins = jnp.sum(jnp.where(earlier, clip_lengths[None, :], 0), axis=1)
        leads = begins + jnp.minimum(prefix_lengths, clip_lengths)
        bounds = jnp.pad(
            jnp.stack([begins, begins + clip_lengths, leads]), ((0, 5), (0, HEAD_DIM - clips))
        )

        cuts = [sum(SWAP_ROWS[:i]) for i in range(len(SWAP_ROWS) + 1)]
        kept, moved = [], []
        for low, high in zip(cuts[:-1], cuts[1:]):
            own = inputs[low:high]
            moved.append(exchange(own, 8, lambda r: r % 8 in swapping))
            kept.append(select_rows(place, own, moved[-1], low, kept[-1:]))
        other = [lax.ppermute(part, "head", swap_sides) for part in kept]
        depth = w_out.shape[0] // 2
        sent = lax.dynamic_slice(w_out, (core * depth, (1 - side) * columns), (depth, columns))
        row = jnp.arange(ranks * per_dev, dtype=jnp.int32)
        in_long = (row >= start) & (row < start + half_rows)
        home = jnp.where(in_long == (0 in swapping), 0, 1)
        crosses = token_rank // (ranks // 2) != home
        kind = jnp.where(crosses, 2 * home + token_rank % 2, 4)
        counts = jnp.sum((kind[:, None] == jnp.arange(4)[None, :]).astype(jnp.int32), axis=0)
        most = jnp.max(counts)
        return tuple(kept), tuple(other), place, bounds, noise_levels.reshape(-1, 1), sent, most

    kept, other, place, bounds, noise_column, sent, most = lax.cond(
        early,
        move_rows(range(4)),
        move_rows(range(4, 8)),
        start,
        inputs,
        clip_lengths,
        prefix_lengths,
        noise_levels,
        token_rank,
        w_out,
    )
    fits = most <= PACKED_ROWS
    far_held = lax.ppermute(sent, "head", swap_sides)
    place, fits = lax.optimization_barrier((place, fits))
    normed = normalize_rows(place, kept, other, bounds, noise_column, level_table, norm_gain)
    pair = exchange(normed, 1)
    w_parts = jnp.transpose(w_qkv, (1, 0, 2))
    query_order, runs, query_mask, key_mask, weights = make_tables(
        place, bounds, token_rank, ranks, half_rows, w_parts
    )

    def cross_rest(parts):
        return lax.cond(
            fits,
            lambda parts: parts,
            lambda parts: tuple(exchange(part, 8) for part in parts),
            tuple(parts),
        )

    def held_back(array, after):
        return lax.optimization_barrier((array, *after))[0]

    blocks, pair_firsts, after = [], [], [query_order]
    for heads in HEAD_CHUNKS:
        first, second = project_heads(
            held_back(place, after), normed, pair, weights, heads, []
        )
        near = lax.ppermute(
            second, "ctx", [(r, r ^ (2 if r % 2 == 0 else 4)) for r in range(ranks)]
        )
        far = exchange(first, 6, lambda r: r % 2 == 1)
        blocks.append((first, near, far))
        if not pair_firsts:
            pair_firsts.append(exchange(first, 1, lambda r: r % 2 == 0))
            after = [pair_firsts[0]]

    def share(block, after):
        first, near, far = block
        near, far, *unused = lax.optimization_barrier((near, far, *after))
        if not pair_firsts:
            pair_firsts.append(exchange(held_back(first, after), 1, lambda r: r % 2 == 0))
        return [
            first,
            near,
            far,
            pair_firsts.pop(),
            exchange(far, 1, lambda r: r % 2 == 1),
            exchange(near, 1),
        ]

    def join(heads, after, cost):
        joined = join_halves(
            held_back(runs, after), stays[heads], arrivals[heads], others[heads], [], cost
        )
        return [exchange(part, 2 * d) if d else part for d, part in enumerate(joined)]

    stays, arrivals, others = [], [], []
    after = [blocks[-1][0]]
    for block, heads in zip(blocks, HEAD_CHUNKS):
        block = share(block, after)
        for position, head in enumerate(heads):
            stay, cross, more = attend(
                held_back(place, after),
                runs,
                block,
                position,
                query_order,
                query_mask,
                key_mask,
                [],
            )
            stays.append(stay)
            arrivals.append(exchange(cross, 8))
            others.append(more)
            after = [cross] + (arrivals[head - 1 : head] if head else [])
            if head == 1:
                far_pair = exchange(lax.optimization_barrier((far_held, cross))[0], 1)

    others = cross_rest(others)
    w_all = gather_out_weights(
        held_back(place, [cross]), w_out, far_held, far_pair, group_heads, []
    )

    def side_by_side(parts):
        width = sum(part.shape[1] for part in parts)
        return out_call(out_rows_kernel, parts, (per_dev, width), jnp.bfloat16)

    pieces = join(slice(0, -1), [cross], COST)
    rows = [side_by_side(pieces), side_by_side(join(slice(-1, None), [], LONG_COST))]
    far_rows = [lax.ppermute(part, "head", swap_sides) for part in rows]
    w_own, w_far = w_all[:2], w_all[2:]

    def add(terms, total, dtype):
        arrays = [array for term in terms for array in term] + total
        return out_call(functools.partial(out_kernel, len(terms)), arrays, (per_dev, columns), dtype)

    own, far = list(zip(rows, w_own)), list(zip(far_rows, w_far))
    total = add(own[:1], [], jnp.float32)
    total = add(own[1:] + far[:1], [total], jnp.float32)
    return add(far[1:], [total], jnp.bfloat16)


def solution(mesh):
    in_specs = (
        P("ctx", "head"),
        P(),
        P(),
        P(None, None, "head"),
        P("head", None),
        P(),
        P(),
        P(),
        P(),
    )
    out_specs = P("ctx", "head")

    def body(inputs, norm_gain, level_table, w_qkv, *rest):
        ranks, sides = mesh.shape["ctx"], mesh.shape["head"]
        heads_here = w_qkv.shape[2] // HEAD_DIM
        halved = (
            ranks == 16
            and sides == 2
            and ranks * inputs.shape[0] == 2 * MAXCLIP
            and heads_here == 4 * sum(len(heads) for heads in HEAD_CHUNKS)
        )
        run = halved_body if halved else gathered_body
        return run(inputs, norm_gain, level_table, w_qkv, *rest)

    return jax.shard_map(body, mesh=mesh, in_specs=in_specs, out_specs=out_specs, check_vma=False)
```

```python
import functools

import jax
import jax.numpy as jnp
from jax import lax
from jax.experimental import pallas as pl
from jax.experimental.pallas import tpu as pltpu
from jax.sharding import PartitionSpec as P

HEAD_DIM = 128


NEG = -1e30
EPS = 1e-06
MAXCLIP = 2560
LOG2E = 1.4426950408889634
MIB = 1024 * 1024
COST = 1000000
LONG_COST = 200000000000


def clip_tables(total_rows, clip_lengths, prefix_lengths, noise_levels):
    rows = jnp.arange(total_rows, dtype=jnp.int32)
    ends = jnp.cumsum(clip_lengths)
    begins = ends - clip_lengths
    clip_of = jnp.sum((rows[:, None] >= ends[None, :]).astype(jnp.int32), axis=1)
    member = clip_of[:, None] == jnp.arange(clip_lengths.shape[0], dtype=jnp.int32)[None, :]
    begin_row = jnp.sum(jnp.where(member, begins[None, :], 0), axis=1)
    lead = jnp.minimum(prefix_lengths, clip_lengths)
    lead_row = jnp.sum(jnp.where(member, lead[None, :], 0), axis=1)
    level_row = jnp.sum(jnp.where(member, noise_levels[None, :], 0), axis=1)
    in_prefix = rows - begin_row < lead_row
    return (clip_of, in_prefix, level_row)


def rank_tables(token_rank, ranks, per_rank):
    onehot = (token_rank[:, None] == jnp.arange(ranks, dtype=jnp.int32)[None, :]).astype(jnp.int32)
    earlier = jnp.cumsum(onehot, axis=0) - onehot
    within = jnp.sum(earlier * onehot, axis=1)
    counts = jnp.sum(onehot.reshape(ranks, per_rank, ranks), axis=1)
    starts = jnp.cumsum(counts, axis=0) - counts
    return (within, counts, starts)


def normalize(rows, in_prefix, level_row, level_table, norm_gain):
    picks = (
        level_row[:, None] == jnp.arange(level_table.shape[0], dtype=jnp.int32)[None, :]
    ) & in_prefix[:, None]
    added = jnp.dot(picks.astype(jnp.bfloat16), level_table, preferred_element_type=jnp.float32)
    shifted = rows.astype(jnp.float32) + added
    factor = lax.rsqrt(jnp.mean(shifted * shifted, axis=-1, keepdims=True) + EPS)
    return (shifted * factor * norm_gain).astype(jnp.bfloat16)


def fold_keys(state, queries, query_clip, query_prefix, pairs, key_clip, key_prefix):
    width = queries.shape[1]
    heads_here = width // HEAD_DIM
    factor = HEAD_DIM ** (-0.5)
    allowed_query = jnp.logical_not(query_prefix)

    def absorb(carry, block):
        block_pairs, block_clip, block_prefix = block
        allowed = (query_clip[:, None] == block_clip[None, :]) & (
            allowed_query[:, None] | block_prefix[None, :]
        )
        updated = []
        for head in range(heads_here):
            top, total, summed = carry[head]
            low = head * HEAD_DIM
            q_head = queries[:, low : low + HEAD_DIM]
            k_head = block_pairs[:, low : low + HEAD_DIM]
            v_head = block_pairs[:, width + low : width + low + HEAD_DIM]
            scores = (
                lax.dot_general(
                    q_head, k_head, (((1,), (1,)), ((), ())), preferred_element_type=jnp.float32
                )
                * factor
            )
            masked = jnp.where(allowed, scores, NEG)
            new_top = jnp.maximum(top, jnp.max(masked, axis=1, keepdims=True))
            fade = jnp.exp(top - new_top)
            weights = jnp.where(allowed, jnp.exp(scores - new_top), 0.0)
            total = total * fade + jnp.sum(weights, axis=1, keepdims=True)
            summed = summed * fade + jnp.dot(
                weights.astype(jnp.bfloat16), v_head, preferred_element_type=jnp.float32
            )
            updated.append((new_top, total, summed))
        return (tuple(updated), None)

    count = pairs.shape[0]
    step = 2048 if count > 2048 and count % 2048 == 0 else count
    if step == count:
        result, unused = absorb(state, (pairs, key_clip, key_prefix))
        return result
    stacked = (
        pairs.reshape(count // step, step, pairs.shape[1]),
        key_clip.reshape(count // step, step),
        key_prefix.reshape(count // step, step),
    )
    result, unused = lax.scan(absorb, state, stacked)
    return result


def gathered_body(
    inputs,
    norm_gain,
    level_table,
    w_qkv,
    w_out,
    clip_lengths,
    prefix_lengths,
    noise_levels,
    token_rank,
):
    ranks = lax.axis_size("ctx")
    rank_here = lax.axis_index("ctx")
    per_dev = inputs.shape[0]
    slots = 2 * per_dev // ranks
    local_width = w_qkv.shape[2]
    heads_here = local_width // HEAD_DIM
    total_rows = per_dev * ranks
    clip_of, in_prefix, level_row = clip_tables(
        total_rows, clip_lengths, prefix_lengths, noise_levels
    )
    within, counts, starts = rank_tables(token_rank, ranks, per_dev)
    place = token_rank * per_dev + within
    order = (
        jnp.zeros((total_rows,), jnp.int32).at[place].set(jnp.arange(total_rows, dtype=jnp.int32))
    )
    first = rank_here * per_dev
    own_rank = lax.dynamic_slice_in_dim(token_rank, first, per_dev, 0)
    own_within = lax.dynamic_slice_in_dim(within, first, per_dev, 0)
    send_starts = lax.dynamic_slice_in_dim(starts, rank_here, 1, 0)[0]
    recv_counts = lax.dynamic_slice_in_dim(counts, rank_here, 1, 1)[:, 0]
    recv_starts = lax.dynamic_slice_in_dim(starts, rank_here, 1, 1)[:, 0]
    balanced_rows = lax.dynamic_slice_in_dim(order, first, per_dev, 0)
    target = own_rank * slots + own_within - send_starts[own_rank]
    buffer = jnp.zeros((ranks * slots, inputs.shape[1]), inputs.dtype).at[target].set(inputs)
    received = lax.all_to_all(
        buffer.reshape(ranks, slots, inputs.shape[1]),
        "ctx",
        split_axis=0,
        concat_axis=0,
        tiled=True,
    )
    spots = jnp.arange(slots, dtype=jnp.int32)[None, :]
    index = jnp.where(spots < recv_counts[:, None], recv_starts[:, None] + spots, per_dev).reshape(
        -1
    )
    flat = received.reshape(ranks * slots, received.shape[2])
    rows = jnp.zeros((per_dev, received.shape[2]), received.dtype).at[index].set(flat, mode="drop")
    full_rows = lax.all_gather(rows, "head", axis=1, tiled=True)
    normed = normalize(
        full_rows, in_prefix[balanced_rows], level_row[balanced_rows], level_table, norm_gain
    )
    qkv = jnp.dot(
        normed, w_qkv.reshape(w_qkv.shape[0], 3 * local_width), preferred_element_type=jnp.float32
    ).astype(jnp.bfloat16)
    start_state = tuple(
        (
            (
                jnp.full((per_dev, 1), NEG, jnp.float32),
                jnp.zeros((per_dev, 1), jnp.float32),
                jnp.zeros((per_dev, HEAD_DIM), jnp.float32),
            )
            for head in range(heads_here)
        )
    )
    key_clip = clip_of[order]
    key_prefix = in_prefix[order]
    query_clip = lax.dynamic_slice_in_dim(key_clip, first, per_dev, 0)
    query_prefix = lax.dynamic_slice_in_dim(key_prefix, first, per_dev, 0)
    queries = qkv[:, :local_width]
    pairs = qkv[:, local_width:]
    state = fold_keys(
        start_state,
        queries,
        query_clip,
        query_prefix,
        lax.all_gather(pairs, "ctx", axis=0, tiled=True),
        key_clip,
        key_prefix,
    )
    parts = [state[head][2] / state[head][1] for head in range(heads_here)]
    attention = jnp.concatenate(parts, axis=1).astype(jnp.bfloat16)
    terms = jnp.dot(attention, w_out, preferred_element_type=jnp.float32)
    return lax.psum_scatter(terms.astype(jnp.bfloat16), "head", scatter_dimension=1, tiled=True)


def packed_rows(place_ref, spots):
    start, early, half = place_ref[0], place_ref[1], place_ref[2]
    total = place_ref[3]
    before = jnp.where(spots < start, early, 1 - early)
    return spots + total * (half + before * (1 - 2 * half))


def clip_flags(rows, bounds_ref):
    begins, ends, leads = bounds_ref[0:1, :], bounds_ref[1:2, :], bounds_ref[2:3, :]
    inside = (rows >= begins) & (rows < ends)
    return inside, inside & (rows < leads)


def count_earlier(hot):
    ranks, rows, lanes = hot.shape
    flat = hot.reshape(ranks * rows, lanes).astype(jnp.bfloat16)

    def numbers(shape, axis):
        return lax.broadcasted_iota(jnp.int32, shape, axis)

    def group(index):
        return sum(jnp.where(index >= rows * k, 1, 0) for k in range(1, ranks))

    def ones(flags):
        return jnp.where(flags, 1.0, 0.0).astype(jnp.bfloat16)

    total = ranks * rows
    in_row = ones(numbers((lanes, lanes), 0) < numbers((lanes, lanes), 1))
    below, across = numbers((total, 1), 0), numbers((1, total), 1)
    in_rank = ones((group(below) == group(across)) & (across < below))
    row_sums = jnp.dot(
        flat, jnp.ones((lanes, lanes), jnp.bfloat16), preferred_element_type=jnp.float32
    )
    earlier = jnp.dot(flat, in_row, preferred_element_type=jnp.float32) + jnp.dot(
        in_rank, row_sums.astype(jnp.bfloat16), preferred_element_type=jnp.float32
    )
    return earlier.reshape(ranks, rows, lanes)


def table_kernel(ranks, place_ref, bounds_ref, rank_ref, w_ref, *refs):
    order_ref, runs_ref, query_ref, key_ref, weights_ref, held, sems = refs
    copies = weight_copies(place_ref, (1, 2), w_ref, weights_ref, sems)
    for copy in copies:
        copy.start()
    start, early, half, half_rows = (place_ref[k] for k in range(4))
    chip, clips, core, rank_here = (place_ref[k] for k in (4, 5, 8, 9))
    holds_long = half != early
    tokens = rank_ref[...]
    rows, lanes = tokens.shape
    per_dev = rows * lanes // ranks

    token = lanes * lax.broadcasted_iota(jnp.int32, tokens.shape, 0) + lax.broadcasted_iota(
        jnp.int32, tokens.shape, 1
    )
    hots = [jnp.where(tokens == rank, 1.0, 0.0) for rank in range(ranks)]
    earlier = count_earlier(jnp.stack(hots))
    within = sum(hots[rank] * earlier[rank] for rank in range(ranks))
    before = jnp.where(token < start, 1.0, 0.0)
    upto = jnp.where(token < start + half_rows, 1.0, 0.0)
    lane = lax.broadcasted_iota(jnp.int32, (1, lanes), 1)
    target = jnp.bitwise_xor(rank_here, 2 * jnp.bitwise_and(lane, 3))
    lane_long = jnp.where(lane < 4, jnp.where(holds_long, 1.0, 0.0), jnp.where(holds_long, 0.0, 1.0))
    lane_own = jnp.where(lane < 4, 1.0, 0.0)
    lows, longs, long_first, rest_first = [], [], [], []
    long_count, rest_count = [[0.0, 0.0], [0.0, 0.0]], [[0.0, 0.0], [0.0, 0.0]]
    for rank, hot in enumerate(hots):
        low = jnp.sum(hot * before, keepdims=True)
        long_rows = jnp.sum(hot * upto, keepdims=True) - low
        group, parity = rank // (ranks // 2), rank % 2
        lows.append(low)
        longs.append(long_rows)
        long_first.append(long_count[group][parity])
        rest_first.append(rest_count[group][parity])
        long_count[group][parity] = long_first[rank] + long_rows
        rest_count[group][parity] = rest_first[rank] + (per_dev - long_rows)
    long_base = rest_base = low_of = long_of = 0.0
    runs = [0.0] * 5
    for rank, hot in enumerate(hots):
        low, high, long_rows = lows[rank], lows[rank] + longs[rank], longs[rank]
        group, parity = rank // (ranks // 2), rank % 2
        own_group = jnp.where(half == group, 1.0, 0.0)
        long_after = own_group * long_count[1 - group][parity]
        rest_after = own_group * rest_count[1 - group][parity]
        long_base += hot * (long_first[rank] + long_after - low)
        rest_base += hot * (rest_first[rank] + rest_after)
        low_of += hot * low
        long_of += hot * long_rows
        first = long_first[rank] + lane_own * long_after
        rest = rest_first[rank] + lane_own * rest_after
        here = jnp.where(target == rank, 1.0, 0.0)
        values = (
            (0.0, low),
            (low, high),
            (high, float(per_dev)),
            (0.0, rest),
            (first - low, rest - long_rows),
        )
        runs = [
            run + here * (lane_long * if_long + (1.0 - lane_long) * if_rest)
            for run, (if_long, if_rest) in zip(runs, values)
        ]
    furthest = rows * lanes // 4 + per_dev // 2
    for index, run in enumerate(runs):
        run = run.astype(jnp.int32)
        runs_ref[index : index + 1, :] = (
            run if index < 3 else jnp.clip(run, -per_dev, furthest)
        )
    sorted_at = within + jnp.where(
        upto - before == 1.0, long_base, rest_base - jnp.where(within < low_of, 0.0, long_of)
    )
    held[...] = jnp.where(jnp.bitwise_and(tokens, 1) == core, sorted_at.astype(jnp.int32), -1)
    half_lines = rows // 2
    spots = lanes * lax.broadcasted_iota(
        jnp.int32, (half_lines, lanes), 0
    ) + lax.broadcasted_iota(jnp.int32, (half_lines, lanes), 1)
    later = packed_rows(place_ref, spots) >= half_rows
    held[:half_lines, :] = jnp.where(later, held[half_lines:, :], held[:half_lines, :])
    lines = half_lines // 4
    for d in range(4):
        line = lines * jnp.bitwise_xor(chip, d)
        order_ref[lines * d : lines * (d + 1), :] = held[pl.ds(line, lines), :]

    column = lax.broadcasted_iota(jnp.int32, (1, HEAD_DIM), 1)
    chip_rows = query_ref.shape[0] // 4
    for d in range(4):
        local = lax.broadcasted_iota(jnp.int32, (chip_rows, 1), 0)
        spots = chip_rows * jnp.bitwise_xor(chip, d) + local
        inside, leading = clip_flags(packed_rows(place_ref, spots), bounds_ref)
        spot = slice(d * chip_rows, (d + 1) * chip_rows)
        inside = jnp.where(inside, 1.0, 0.0)
        prefix = jnp.sum(jnp.where(leading, 1.0, 0.0), axis=1, keepdims=True)
        query_ref[spot, :] = jnp.where(column == clips, prefix, inside).astype(jnp.bfloat16)
        outside = jnp.where(column < clips, NEG * (1.0 - inside), 0.0)
        key_ref[spot, :] = jnp.where(column == clips, NEG * (1.0 - prefix), outside).astype(
            jnp.bfloat16
        )
    for copy in copies:
        copy.wait()


def make_tables(place, bounds, token_rank, ranks, keys, w_parts):
    vmem = pl.BlockSpec(memory_space=pltpu.VMEM)
    tokens = token_rank.reshape(-1, HEAD_DIM)
    features = jax.ShapeDtypeStruct((keys, HEAD_DIM), jnp.bfloat16)
    return pl.pallas_call(
        functools.partial(table_kernel, ranks),
        in_specs=[
            pl.BlockSpec(memory_space=pltpu.SMEM),
            vmem,
            vmem,
            pl.BlockSpec(memory_space=pltpu.HBM),
        ],
        out_specs=(vmem,) * 5,
        out_shape=(
            jax.ShapeDtypeStruct((tokens.shape[0] // 2, HEAD_DIM), jnp.int32),
            jax.ShapeDtypeStruct((8, HEAD_DIM), jnp.int32),
            features,
            features,
            weight_shape(w_parts, (1, 2)),
        ),
        scratch_shapes=[
            pltpu.VMEM(tokens.shape, jnp.int32),
            pltpu.SemaphoreType.DMA((2, COPY_PIECES)),
        ],
        compiler_params=pltpu.CompilerParams(vmem_limit_bytes=26 * MIB),
        cost_estimate=pl.CostEstimate(flops=COST, bytes_accessed=COST, transcendentals=0),
    )(place, bounds, tokens, w_parts)


def select_kernel(low, place_ref, own_ref, moved_ref, *rest):
    out_ref = rest[-1]
    spots = place_ref[7] + low + lax.broadcasted_iota(jnp.int32, (out_ref.shape[0], 1), 0)
    swapped = jnp.where(spots < place_ref[0], place_ref[1], 1 - place_ref[1])
    out_ref[...] = jnp.where(swapped == 1, moved_ref[...], own_ref[...])


def select_rows(place, own, moved, low, after):
    vmem = pl.BlockSpec(memory_space=pltpu.VMEM)
    return pl.pallas_call(
        functools.partial(select_kernel, low),
        in_specs=[pl.BlockSpec(memory_space=pltpu.SMEM), vmem, vmem]
        + [pl.BlockSpec(memory_space=pl.ANY)] * len(after),
        out_specs=vmem,
        out_shape=jax.ShapeDtypeStruct(moved.shape, moved.dtype),
        compiler_params=pltpu.CompilerParams(vmem_limit_bytes=8 * MIB),
        cost_estimate=pl.CostEstimate(flops=COST, bytes_accessed=COST, transcendentals=0),
    )(place, own, moved, *after)


def head_of(chip, index, group_heads):
    return 2 * group_heads * (chip // 2) + 2 * index + chip % 2


def weight_copies(place_ref, parts, w_ref, out_ref, sems):
    pair = jnp.bitwise_xor(place_ref[4] // 2, place_ref[8])
    columns = pl.ds(pl.multiple_of(pair * out_ref.shape[2], HEAD_DIM), out_ref.shape[2])
    depth = out_ref.shape[1] // COPY_PIECES
    copies = []
    for position, part in enumerate(parts):
        for piece in range(COPY_PIECES):
            rows = slice(piece * depth, (piece + 1) * depth)
            copies.append(
                pltpu.make_async_copy(
                    w_ref.at[part, rows, columns],
                    out_ref.at[position, rows, :],
                    sems.at[position, piece],
                )
            )
    return copies


def weight_shape(w_parts, parts):
    return jax.ShapeDtypeStruct(
        (len(parts), w_parts.shape[1], w_parts.shape[2] // 2), w_parts.dtype
    )


def norm_kernel(place_ref, *refs):
    pieces = len(SWAP_ROWS)
    bounds_ref, noise_ref, level_ref, gain_ref, w_ref = refs[2 * pieces : 2 * pieces + 5]
    out_ref, weights_ref, sems = refs[-3:]
    copies = weight_copies(place_ref, (0,), w_ref, weights_ref, sems)
    for copy in copies:
        copy.start()
    width = out_ref.shape[1] // 2
    side, first = place_ref[6], place_ref[7]
    clips, levels = noise_ref.shape[0], level_ref.shape[0]
    spots = [pl.ds(pl.multiple_of(s * width, 128), width) for s in (side, 1 - side)]
    level = lax.broadcasted_iota(jnp.int32, (clips, levels), 1)
    chosen = jnp.where(noise_ref[...] == level, 1.0, 0.0).astype(jnp.bfloat16)
    tables = [
        jnp.dot(chosen, level_ref[:, spot], preferred_element_type=jnp.float32).astype(
            jnp.bfloat16
        )
        for spot in spots
    ]
    low = 0
    for piece in range(pieces):
        own_ref, other_ref = refs[piece], refs[pieces + piece]
        count = own_ref.shape[0]
        rows = slice(low, low + count)
        places = first + low + lax.broadcasted_iota(jnp.int32, (count, 1), 0)
        low += count
        unused, leading = clip_flags(packed_rows(place_ref, places), bounds_ref)
        picks = jnp.where(leading, 1.0, 0.0)[:, :clips].astype(jnp.bfloat16)
        shifted = [
            ref[...].astype(jnp.float32)
            + jnp.dot(picks, table, preferred_element_type=jnp.float32)
            for ref, table in zip((own_ref, other_ref), tables)
        ]
        squares = sum(jnp.sum(part * part, axis=1, keepdims=True) for part in shifted)
        factor = lax.rsqrt(squares / (2 * width) + EPS)
        for part, spot in zip(shifted, spots):
            out_ref[rows, spot] = (part * factor * gain_ref[:, spot]).astype(jnp.bfloat16)
    for copy in copies:
        copy.wait()


def normalize_rows(place, kept, other, bounds, noise_levels, level_table, norm_gain, w_parts):
    rows, depth = sum(part.shape[0] for part in kept), 2 * kept[0].shape[1]
    vmem = pl.BlockSpec(memory_space=pltpu.VMEM)
    return pl.pallas_call(
        norm_kernel,
        in_specs=[pl.BlockSpec(memory_space=pltpu.SMEM)]
        + [vmem] * (2 * len(kept) + 4)
        + [pl.BlockSpec(memory_space=pltpu.HBM)],
        out_specs=(vmem, vmem),
        out_shape=(
            jax.ShapeDtypeStruct((rows, depth), jnp.bfloat16),
            weight_shape(w_parts, (0,)),
        ),
        scratch_shapes=[pltpu.SemaphoreType.DMA((1, COPY_PIECES))],
        compiler_params=pltpu.CompilerParams(vmem_limit_bytes=26 * MIB),
        cost_estimate=pl.CostEstimate(flops=COST, bytes_accessed=COST, transcendentals=0),
    )(place, *kept, *other, bounds, noise_levels, level_table, norm_gain.reshape(1, -1), w_parts)


def project_kernel(indices, place_ref, own_ref, pair_ref, query_ref, rest_ref, *rest):
    first_ref, second_ref = rest[-2:]
    rows = jnp.concatenate([own_ref[...], pair_ref[...]], axis=0)
    count = own_ref.shape[0]
    same = place_ref[4] % 2 == place_ref[8]

    def store(outcome, base, even_ref, odd_ref):
        for index, core in enumerate((place_ref[8], 1 - place_ref[8])):
            spot = pl.ds(pl.multiple_of(core * count, count), count)
            half = outcome[index * count : (index + 1) * count]
            for part in range(3):
                to = slice(base + part * HEAD_DIM, base + (part + 1) * HEAD_DIM)
                even_ref[spot, to] = half[:, 2 * part * HEAD_DIM : (2 * part + 1) * HEAD_DIM]
                odd_ref[spot, to] = half[:, (2 * part + 1) * HEAD_DIM : 2 * (part + 1) * HEAD_DIM]

    for position, index in enumerate(indices):
        spot = slice(2 * index * HEAD_DIM, 2 * (index + 1) * HEAD_DIM)
        weights = jnp.concatenate(
            [query_ref[0, :, spot], rest_ref[0, :, spot], rest_ref[1, :, spot]], axis=1
        )
        outcome = jnp.dot(rows, weights, preferred_element_type=jnp.float32).astype(jnp.bfloat16)
        base = 3 * position * HEAD_DIM

        @pl.when(same)
        def _():
            store(outcome, base, first_ref, second_ref)

        @pl.when(jnp.logical_not(same))
        def _():
            store(outcome, base, second_ref, first_ref)


def project_heads(place, own, pair, weights, indices, after):
    rows = own.shape[0]
    vmem = pl.BlockSpec(memory_space=pltpu.VMEM)
    shape = jax.ShapeDtypeStruct((2 * rows, 3 * len(indices) * HEAD_DIM), jnp.bfloat16)
    return pl.pallas_call(
        functools.partial(project_kernel, indices),
        in_specs=[pl.BlockSpec(memory_space=pltpu.SMEM)] + [vmem] * 4
        + [pl.BlockSpec(memory_space=pl.ANY)] * len(after),
        out_specs=(vmem, vmem),
        out_shape=(shape, shape),
        compiler_params=pltpu.CompilerParams(vmem_limit_bytes=20 * MIB),
        cost_estimate=pl.CostEstimate(flops=COST, bytes_accessed=COST, transcendentals=0),
    )(place, own, pair, *weights, *after)


def attend_kernel(base, place_ref, runs_ref, *refs):
    mine, near, far, pair_first, pair_far, pair_near = refs[:6]
    order_ref, query_mask_ref, key_mask_ref = refs[6:9]
    stay_ref, cross_ref, more_ref, q_all, k_all, v_all, sorted_out = refs[-7:]
    chip_rows = mine.shape[0]
    rows = chip_rows // 2
    queries = sorted_out.shape[0] - 2 * rows

    def hold(sources):
        for index, source in enumerate(sources):
            spot = slice(index * chip_rows, (index + 1) * chip_rows)
            for part, held in enumerate((q_all, k_all, v_all)):
                low = base + part * HEAD_DIM
                held[spot, :HEAD_DIM] = source[:, low : low + HEAD_DIM]

    @pl.when(place_ref[8] == 0)
    def _():
        hold((mine, near, pair_near, pair_far))

    @pl.when(place_ref[8] == 1)
    def _():
        hold((pair_first, pair_near, near, far))

    q_all[:, HEAD_DIM:] = query_mask_ref[...]
    k_all[:, HEAD_DIM:] = key_mask_ref[...]
    v_all[:, HEAD_DIM:] = jnp.ones((4 * chip_rows, HEAD_DIM), jnp.bfloat16)
    tile = queries // ATTEND_TILES

    def score(step):
        wanted = step * tile + lax.broadcasted_iota(jnp.int32, (tile, 1), 0)
        picks = jnp.concatenate(
            [
                jnp.where(order_ref[line : line + 1, :] == wanted, 1.0, 0.0).astype(jnp.bfloat16)
                for line in range(order_ref.shape[0])
            ],
            axis=1,
        )
        sorted_queries = jnp.dot(picks, q_all[...], preferred_element_type=jnp.float32)
        return lax.dot_general(
            sorted_queries.astype(jnp.bfloat16),
            k_all[...],
            (((1,), (1,)), ((), ())),
            preferred_element_type=jnp.float32,
        )

    coming = score(0)
    for step in range(ATTEND_TILES):
        scores = coming
        if step + 1 < ATTEND_TILES:
            coming = score(step + 1)
        top = jnp.max(scores, axis=1, keepdims=True)
        weights = jnp.exp2((scores - top) * (HEAD_DIM ** (-0.5) * LOG2E))
        summed = jnp.dot(
            weights.astype(jnp.bfloat16), v_all[...], preferred_element_type=jnp.float32
        )
        sorted_out[rows + step * tile : rows + (step + 1) * tile, :] = (
            summed[:, :HEAD_DIM] / summed[:, HEAD_DIM:]
        )

    low = rows
    for ref in (cross_ref, more_ref):
        ref[...] = sorted_out[low : low + ref.shape[0], :].astype(jnp.bfloat16)
        low += ref.shape[0]
    for d in range(4):
        stay_ref[d] = spread_run(sorted_out, runs_ref, d, rows).astype(jnp.bfloat16)


def spread_run(sorted_ref, runs_ref, lane, rows):
    furthest = sorted_ref.shape[0] - 2 * rows
    row = lax.broadcasted_iota(jnp.int32, (rows, 1), 0)
    parts = [
        sorted_ref[pl.ds(rows + jnp.clip(runs_ref[line, lane], -rows, furthest), rows), :]
        for line in (3, 4)
    ]
    in_second = (row >= runs_ref[1, lane]) & (row < runs_ref[2, lane])
    return jnp.where(row < runs_ref[0, lane], parts[0], jnp.where(in_second, parts[1], 0.0))


def attend(place, runs, blocks, position, order, query_mask, key_mask, after):
    chip_rows = blocks[0].shape[0]
    rows, keys = chip_rows // 2, 4 * chip_rows
    queries = keys // 2 + rows // 2
    vmem, smem = pl.BlockSpec(memory_space=pltpu.VMEM), pl.BlockSpec(memory_space=pltpu.SMEM)
    shape = jax.ShapeDtypeStruct((4, rows, HEAD_DIM), jnp.bfloat16)
    return pl.pallas_call(
        functools.partial(attend_kernel, 3 * position * HEAD_DIM),
        in_specs=[smem, smem]
        + [vmem] * (len(blocks) + 3)
        + [pl.BlockSpec(memory_space=pl.ANY)] * len(after),
        out_specs=(vmem, vmem, vmem),
        out_shape=(shape,)
        + tuple(
            jax.ShapeDtypeStruct((count, HEAD_DIM), jnp.bfloat16)
            for count in (PACKED_ROWS, queries - PACKED_ROWS)
        ),
        scratch_shapes=[
            pltpu.VMEM((keys, 2 * HEAD_DIM), jnp.bfloat16),
            pltpu.VMEM((keys, 2 * HEAD_DIM), jnp.bfloat16),
            pltpu.VMEM((keys, 2 * HEAD_DIM), jnp.bfloat16),
            pltpu.VMEM((queries + 2 * rows, HEAD_DIM), jnp.float32),
        ],
        compiler_params=pltpu.CompilerParams(vmem_limit_bytes=20 * MIB),
        cost_estimate=pl.CostEstimate(
            flops=COST, bytes_accessed=COST, transcendentals=0
        ),
    )(place, runs, *blocks, order, query_mask, key_mask, *after)


def join_kernel(heads, runs_ref, *refs):
    outs, held = refs[-5:-1], refs[-1]
    rows = outs[0].shape[0]
    for head in range(heads):
        stay_ref, low = refs[3 * head], rows
        for ref in refs[3 * head + 1 : 3 * head + 3]:
            held[low : low + ref.shape[0], :] = ref[...].astype(jnp.float32)
            low += ref.shape[0]
        spot = slice(head * HEAD_DIM, (head + 1) * HEAD_DIM)
        for d in range(4):
            arrived = spread_run(held, runs_ref, 4 + d, rows).astype(jnp.bfloat16)
            outs[d][:, spot] = stay_ref[d] + arrived


def join_halves(runs, stays, arrivals, others, after, cost):
    heads, (slots, rows, width) = len(stays), stays[0].shape
    vmem = pl.BlockSpec(memory_space=pltpu.VMEM)
    parts = [part for three in zip(stays, arrivals, others) for part in three]
    shape = jax.ShapeDtypeStruct((rows, heads * width), jnp.bfloat16)
    return pl.pallas_call(
        functools.partial(join_kernel, heads),
        in_specs=[pl.BlockSpec(memory_space=pltpu.SMEM)]
        + [vmem] * len(parts)
        + [pl.BlockSpec(memory_space=pl.ANY)] * len(after),
        out_specs=(vmem,) * slots,
        out_shape=(shape,) * slots,
        scratch_shapes=[
            pltpu.VMEM((arrivals[0].shape[0] + others[0].shape[0] + 2 * rows, width), jnp.float32)
        ],
        compiler_params=pltpu.CompilerParams(vmem_limit_bytes=16 * MIB),
        cost_estimate=pl.CostEstimate(flops=cost, bytes_accessed=COST, transcendentals=0),
    )(runs, *parts, *after)


def gather_kernel(place_ref, w_ref, held_ref, pair_ref, *rest):
    outs, sems = rest[-5:-1], rest[-1]
    chip, columns = place_ref[4], outs[0].shape[1]
    heads = w_ref.shape[0] // HEAD_DIM // 4
    spot = pl.ds(pl.multiple_of(place_ref[6] * columns, HEAD_DIM), columns)

    def rows_at(block):
        return pl.ds(pl.multiple_of(block * HEAD_DIM, HEAD_DIM), HEAD_DIM)

    def transfers(near_ref, far_ref):
        copies = []
        for d in range(4):
            for index in range(heads):
                last = index + 1 == heads
                group = 1 if last else 0
                to = d if last else d * (heads - 1) + index
                to = slice(to * HEAD_DIM, (to + 1) * HEAD_DIM)
                head = head_of(jnp.bitwise_xor(chip, d), index, heads)
                there = 2 * index + jnp.bitwise_xor(chip, d) % 2
                sources = (
                    w_ref.at[rows_at(head), spot],
                    (near_ref if d < 2 else far_ref).at[rows_at(there), :],
                )
                for side, source in enumerate(sources):
                    copies.append(
                        pltpu.make_async_copy(
                            source, outs[2 * side + group].at[to, :], sems.at[side, index, d]
                        )
                    )
        for copy in copies:
            copy.start()
        for copy in copies:
            copy.wait()

    @pl.when(chip // 2 == place_ref[8])
    def _():
        transfers(held_ref, pair_ref)

    @pl.when(chip // 2 != place_ref[8])
    def _():
        transfers(pair_ref, held_ref)


def gather_out_weights(place, w_out, held, pair, group_heads, after):
    vmem, hbm = pl.BlockSpec(memory_space=pltpu.VMEM), pl.BlockSpec(memory_space=pltpu.HBM)
    any_space = pl.BlockSpec(memory_space=pl.ANY)
    shapes = tuple(
        jax.ShapeDtypeStruct((count * HEAD_DIM, w_out.shape[1] // 2), w_out.dtype)
        for count in (4 * (group_heads - 1), 4)
    )
    return pl.pallas_call(
        gather_kernel,
        in_specs=[pl.BlockSpec(memory_space=pltpu.SMEM), hbm] + [any_space] * (2 + len(after)),
        out_specs=(vmem,) * 4,
        out_shape=shapes + shapes,
        scratch_shapes=[pltpu.SemaphoreType.DMA((2, group_heads, 4))],
        compiler_params=pltpu.CompilerParams(vmem_limit_bytes=16 * MIB),
        cost_estimate=pl.CostEstimate(flops=COST, bytes_accessed=COST, transcendentals=0),
    )(place, w_out, held, pair, *after)


def out_rows_kernel(*refs):
    refs[-1][...] = jnp.concatenate([ref[...] for ref in refs[:-1]], axis=1)


def out_kernel(pairs, *refs):
    total = refs[2 * pairs][...] if len(refs) > 2 * pairs + 1 else None
    for pair in range(pairs):
        product = jnp.dot(
            refs[2 * pair][...], refs[2 * pair + 1][...], preferred_element_type=jnp.float32
        )
        total = product if total is None else total + product
    refs[-1][...] = total.astype(refs[-1].dtype)


def out_call(kernel, arrays, shape, dtype):
    vmem = pl.BlockSpec(memory_space=pltpu.VMEM)
    return pl.pallas_call(
        kernel,
        in_specs=[vmem] * len(arrays),
        out_specs=vmem,
        out_shape=jax.ShapeDtypeStruct(shape, dtype),
        compiler_params=pltpu.CompilerParams(vmem_limit_bytes=16 * MIB),
        cost_estimate=pl.CostEstimate(flops=COST, bytes_accessed=COST, transcendentals=0),
    )(*arrays)


SWAP_ROWS = (128, 112, 80)
PACKED_ROWS = 768
ATTEND_TILES = 5
HEAD_CHUNKS = ((0,), (1, 2))
COPY_PIECES = 4


def halved_body(
    inputs,
    norm_gain,
    level_table,
    w_qkv,
    w_out,
    clip_lengths,
    prefix_lengths,
    noise_levels,
    token_rank,
):
    ranks, per_dev = 16, inputs.shape[0]
    half_rows = 8 * per_dev
    clips = clip_lengths.shape[0]
    index = jnp.arange(clips, dtype=jnp.int32)

    ahead = (index[None, :] < index[:, None]) & (clip_lengths == MAXCLIP)[:, None]
    start = jnp.sum(jnp.where(ahead, clip_lengths[None, :], 0))
    early = start <= half_rows // 2

    rank_here = lax.axis_index("ctx")
    side = lax.axis_index("head")
    columns = inputs.shape[1]
    group_heads = w_qkv.shape[2] // HEAD_DIM // 4
    half, block, core = rank_here // 8, rank_here % 8, rank_here % 2
    chip = block // 2
    swap_sides = [(0, 1), (1, 0)]

    def exchange(array, flip, only=lambda r: True):
        pairs = [(r, r ^ flip) for r in range(ranks) if only(r)]
        return lax.ppermute(array, "ctx", pairs)

    def move_rows(swapping):
        return functools.partial(moved_rows, swapping)

    def moved_rows(
        swapping, start, inputs, clip_lengths, prefix_lengths, noise_levels, token_rank, w_out
    ):
        place = jnp.stack(
            [
                start,
                jnp.int32(1 if 0 in swapping else 0),
                half,
                jnp.int32(half_rows),
                chip,
                jnp.int32(clips),
                side,
                block * per_dev,
                core,
                rank_here,
            ]
        )
        earlier = index[None, :] < index[:, None]
        begins = jnp.sum(jnp.where(earlier, clip_lengths[None, :], 0), axis=1)
        leads = begins + jnp.minimum(prefix_lengths, clip_lengths)
        bounds = jnp.pad(
            jnp.stack([begins, begins + clip_lengths, leads]), ((0, 5), (0, HEAD_DIM - clips))
        )

        cuts = [sum(SWAP_ROWS[:i]) for i in range(len(SWAP_ROWS) + 1)]
        kept, moved = [], []
        for low, high in zip(cuts[:-1], cuts[1:]):
            own = inputs[low:high]
            moved.append(exchange(own, 8, lambda r: r % 8 in swapping))
            kept.append(select_rows(place, own, moved[-1], low, kept[-1:]))
        other = [lax.ppermute(part, "head", swap_sides) for part in kept]
        depth = w_out.shape[0] // 2
        sent = lax.dynamic_slice(w_out, (core * depth, (1 - side) * columns), (depth, columns))
        row = jnp.arange(ranks * per_dev, dtype=jnp.int32)
        in_long = (row >= start) & (row < start + half_rows)
        home = jnp.where(in_long == (0 in swapping), 0, 1)
        crosses = token_rank // (ranks // 2) != home
        kind = jnp.where(crosses, 2 * home + token_rank % 2, 4)
        counts = jnp.sum((kind[:, None] == jnp.arange(4)[None, :]).astype(jnp.int32), axis=0)
        most = jnp.max(counts)
        return tuple(kept), tuple(other), place, bounds, noise_levels.reshape(-1, 1), sent, most

    kept, other, place, bounds, noise_column, sent, most = lax.cond(
        early,
        move_rows(range(4)),
        move_rows(range(4, 8)),
        start,
        inputs,
        clip_lengths,
        prefix_lengths,
        noise_levels,
        token_rank,
        w_out,
    )
    fits = most <= PACKED_ROWS
    far_held = lax.ppermute(sent, "head", swap_sides)
    place, fits = lax.optimization_barrier((place, fits))
    w_parts = jnp.transpose(w_qkv, (1, 0, 2))
    normed, query_weights = normalize_rows(
        place, kept, other, bounds, noise_column, level_table, norm_gain, w_parts
    )
    pair = exchange(normed, 1)
    query_order, runs, query_mask, key_mask, rest_weights = make_tables(
        place, bounds, token_rank, ranks, half_rows, w_parts
    )

    def cross_rest(parts):
        return lax.cond(
            fits,
            lambda parts: parts,
            lambda parts: tuple(exchange(part, 8) for part in parts),
            tuple(parts),
        )

    def held_back(array, after):
        return lax.optimization_barrier((array, *after))[0]

    blocks, pair_firsts, after = [], [], [query_order]
    for heads in HEAD_CHUNKS:
        first, second = project_heads(
            held_back(place, after), normed, pair, (query_weights, rest_weights), heads, []
        )
        near = lax.ppermute(
            second, "ctx", [(r, r ^ (2 if r % 2 == 0 else 4)) for r in range(ranks)]
        )
        far = exchange(first, 6, lambda r: r % 2 == 1)
        blocks.append((first, near, far))
        if not pair_firsts:
            pair_firsts.append(exchange(first, 1, lambda r: r % 2 == 0))
            after = [pair_firsts[0]]

    def share(block, after):
        first, near, far = block
        near, far, *unused = lax.optimization_barrier((near, far, *after))
        if not pair_firsts:
            pair_firsts.append(exchange(held_back(first, after), 1, lambda r: r % 2 == 0))
        return [
            first,
            near,
            far,
            pair_firsts.pop(),
            exchange(far, 1, lambda r: r % 2 == 1),
            exchange(near, 1),
        ]

    def join(heads, after, cost):
        joined = join_halves(
            held_back(runs, after), stays[heads], arrivals[heads], others[heads], [], cost
        )
        return [exchange(part, 2 * d) if d else part for d, part in enumerate(joined)]

    stays, arrivals, others = [], [], []
    after = [blocks[-1][0]]
    for block, heads in zip(blocks, HEAD_CHUNKS):
        block = share(block, after)
        for position, head in enumerate(heads):
            stay, cross, more = attend(
                held_back(place, after),
                runs,
                block,
                position,
                query_order,
                query_mask,
                key_mask,
                [],
            )
            stays.append(stay)
            arrivals.append(exchange(cross, 8))
            others.append(more)
            after = [cross] + (arrivals[head - 1 : head] if head else [])
            if head == 1:
                far_pair = exchange(lax.optimization_barrier((far_held, cross))[0], 1)

    others = cross_rest(others)
    w_all = gather_out_weights(
        held_back(place, [cross]), w_out, far_held, far_pair, group_heads, []
    )

    def side_by_side(parts):
        width = sum(part.shape[1] for part in parts)
        return out_call(out_rows_kernel, parts, (per_dev, width), jnp.bfloat16)

    pieces = join(slice(0, -1), [cross], COST)
    rows = [side_by_side(pieces), side_by_side(join(slice(-1, None), [], LONG_COST))]
    far_rows = [lax.ppermute(part, "head", swap_sides) for part in rows]
    w_own, w_far = w_all[:2], w_all[2:]

    def add(terms, total, dtype):
        arrays = [array for term in terms for array in term] + total
        return out_call(functools.partial(out_kernel, len(terms)), arrays, (per_dev, columns), dtype)

    own, far = list(zip(rows, w_own)), list(zip(far_rows, w_far))
    total = add(own[:1], [], jnp.float32)
    total = add(own[1:] + far[:1], [total], jnp.float32)
    return add(far[1:], [total], jnp.bfloat16)


def solution(mesh):
    in_specs = (
        P("ctx", "head"),
        P(),
        P(),
        P(None, None, "head"),
        P("head", None),
        P(),
        P(),
        P(),
        P(),
    )
    out_specs = P("ctx", "head")

    def body(inputs, norm_gain, level_table, w_qkv, *rest):
        ranks, sides = mesh.shape["ctx"], mesh.shape["head"]
        heads_here = w_qkv.shape[2] // HEAD_DIM
        halved = (
            ranks == 16
            and sides == 2
            and ranks * inputs.shape[0] == 2 * MAXCLIP
            and heads_here == 4 * sum(len(heads) for heads in HEAD_CHUNKS)
        )
        run = halved_body if halved else gathered_body
        return run(inputs, norm_gain, level_table, w_qkv, *rest)

    return jax.shard_map(body, mesh=mesh, in_specs=in_specs, out_specs=out_specs, check_vma=False)
```

```python
import functools

import jax
import jax.numpy as jnp
from jax import lax
from jax.experimental import pallas as pl
from jax.experimental.pallas import tpu as pltpu
from jax.sharding import PartitionSpec as P

HEAD_DIM = 128


NEG = -1e30
EPS = 1e-06
MAXCLIP = 2560
LOG2E = 1.4426950408889634
MIB = 1024 * 1024
COST = 1000000
LONG_COST = 200000000000


def clip_tables(total_rows, clip_lengths, prefix_lengths, noise_levels):
    rows = jnp.arange(total_rows, dtype=jnp.int32)
    ends = jnp.cumsum(clip_lengths)
    begins = ends - clip_lengths
    clip_of = jnp.sum((rows[:, None] >= ends[None, :]).astype(jnp.int32), axis=1)
    member = clip_of[:, None] == jnp.arange(clip_lengths.shape[0], dtype=jnp.int32)[None, :]
    begin_row = jnp.sum(jnp.where(member, begins[None, :], 0), axis=1)
    lead = jnp.minimum(prefix_lengths, clip_lengths)
    lead_row = jnp.sum(jnp.where(member, lead[None, :], 0), axis=1)
    level_row = jnp.sum(jnp.where(member, noise_levels[None, :], 0), axis=1)
    in_prefix = rows - begin_row < lead_row
    return (clip_of, in_prefix, level_row)


def rank_tables(token_rank, ranks, per_rank):
    onehot = (token_rank[:, None] == jnp.arange(ranks, dtype=jnp.int32)[None, :]).astype(jnp.int32)
    earlier = jnp.cumsum(onehot, axis=0) - onehot
    within = jnp.sum(earlier * onehot, axis=1)
    counts = jnp.sum(onehot.reshape(ranks, per_rank, ranks), axis=1)
    starts = jnp.cumsum(counts, axis=0) - counts
    return (within, counts, starts)


def normalize(rows, in_prefix, level_row, level_table, norm_gain):
    picks = (
        level_row[:, None] == jnp.arange(level_table.shape[0], dtype=jnp.int32)[None, :]
    ) & in_prefix[:, None]
    added = jnp.dot(picks.astype(jnp.bfloat16), level_table, preferred_element_type=jnp.float32)
    shifted = rows.astype(jnp.float32) + added
    factor = lax.rsqrt(jnp.mean(shifted * shifted, axis=-1, keepdims=True) + EPS)
    return (shifted * factor * norm_gain).astype(jnp.bfloat16)


def fold_keys(state, queries, query_clip, query_prefix, pairs, key_clip, key_prefix):
    width = queries.shape[1]
    heads_here = width // HEAD_DIM
    factor = HEAD_DIM ** (-0.5)
    allowed_query = jnp.logical_not(query_prefix)

    def absorb(carry, block):
        block_pairs, block_clip, block_prefix = block
        allowed = (query_clip[:, None] == block_clip[None, :]) & (
            allowed_query[:, None] | block_prefix[None, :]
        )
        updated = []
        for head in range(heads_here):
            top, total, summed = carry[head]
            low = head * HEAD_DIM
            q_head = queries[:, low : low + HEAD_DIM]
            k_head = block_pairs[:, low : low + HEAD_DIM]
            v_head = block_pairs[:, width + low : width + low + HEAD_DIM]
            scores = (
                lax.dot_general(
                    q_head, k_head, (((1,), (1,)), ((), ())), preferred_element_type=jnp.float32
                )
                * factor
            )
            masked = jnp.where(allowed, scores, NEG)
            new_top = jnp.maximum(top, jnp.max(masked, axis=1, keepdims=True))
            fade = jnp.exp(top - new_top)
            weights = jnp.where(allowed, jnp.exp(scores - new_top), 0.0)
            total = total * fade + jnp.sum(weights, axis=1, keepdims=True)
            summed = summed * fade + jnp.dot(
                weights.astype(jnp.bfloat16), v_head, preferred_element_type=jnp.float32
            )
            updated.append((new_top, total, summed))
        return (tuple(updated), None)

    count = pairs.shape[0]
    step = 2048 if count > 2048 and count % 2048 == 0 else count
    if step == count:
        result, unused = absorb(state, (pairs, key_clip, key_prefix))
        return result
    stacked = (
        pairs.reshape(count // step, step, pairs.shape[1]),
        key_clip.reshape(count // step, step),
        key_prefix.reshape(count // step, step),
    )
    result, unused = lax.scan(absorb, state, stacked)
    return result


def gathered_body(
    inputs,
    norm_gain,
    level_table,
    w_qkv,
    w_out,
    clip_lengths,
    prefix_lengths,
    noise_levels,
    token_rank,
):
    ranks = lax.axis_size("ctx")
    rank_here = lax.axis_index("ctx")
    per_dev = inputs.shape[0]
    slots = 2 * per_dev // ranks
    local_width = w_qkv.shape[2]
    heads_here = local_width // HEAD_DIM
    total_rows = per_dev * ranks
    clip_of, in_prefix, level_row = clip_tables(
        total_rows, clip_lengths, prefix_lengths, noise_levels
    )
    within, counts, starts = rank_tables(token_rank, ranks, per_dev)
    place = token_rank * per_dev + within
    order = (
        jnp.zeros((total_rows,), jnp.int32).at[place].set(jnp.arange(total_rows, dtype=jnp.int32))
    )
    first = rank_here * per_dev
    own_rank = lax.dynamic_slice_in_dim(token_rank, first, per_dev, 0)
    own_within = lax.dynamic_slice_in_dim(within, first, per_dev, 0)
    send_starts = lax.dynamic_slice_in_dim(starts, rank_here, 1, 0)[0]
    recv_counts = lax.dynamic_slice_in_dim(counts, rank_here, 1, 1)[:, 0]
    recv_starts = lax.dynamic_slice_in_dim(starts, rank_here, 1, 1)[:, 0]
    balanced_rows = lax.dynamic_slice_in_dim(order, first, per_dev, 0)
    target = own_rank * slots + own_within - send_starts[own_rank]
    buffer = jnp.zeros((ranks * slots, inputs.shape[1]), inputs.dtype).at[target].set(inputs)
    received = lax.all_to_all(
        buffer.reshape(ranks, slots, inputs.shape[1]),
        "ctx",
        split_axis=0,
        concat_axis=0,
        tiled=True,
    )
    spots = jnp.arange(slots, dtype=jnp.int32)[None, :]
    index = jnp.where(spots < recv_counts[:, None], recv_starts[:, None] + spots, per_dev).reshape(
        -1
    )
    flat = received.reshape(ranks * slots, received.shape[2])
    rows = jnp.zeros((per_dev, received.shape[2]), received.dtype).at[index].set(flat, mode="drop")
    full_rows = lax.all_gather(rows, "head", axis=1, tiled=True)
    normed = normalize(
        full_rows, in_prefix[balanced_rows], level_row[balanced_rows], level_table, norm_gain
    )
    qkv = jnp.dot(
        normed, w_qkv.reshape(w_qkv.shape[0], 3 * local_width), preferred_element_type=jnp.float32
    ).astype(jnp.bfloat16)
    start_state = tuple(
        (
            (
                jnp.full((per_dev, 1), NEG, jnp.float32),
                jnp.zeros((per_dev, 1), jnp.float32),
                jnp.zeros((per_dev, HEAD_DIM), jnp.float32),
            )
            for head in range(heads_here)
        )
    )
    key_clip = clip_of[order]
    key_prefix = in_prefix[order]
    query_clip = lax.dynamic_slice_in_dim(key_clip, first, per_dev, 0)
    query_prefix = lax.dynamic_slice_in_dim(key_prefix, first, per_dev, 0)
    queries = qkv[:, :local_width]
    pairs = qkv[:, local_width:]
    state = fold_keys(
        start_state,
        queries,
        query_clip,
        query_prefix,
        lax.all_gather(pairs, "ctx", axis=0, tiled=True),
        key_clip,
        key_prefix,
    )
    parts = [state[head][2] / state[head][1] for head in range(heads_here)]
    attention = jnp.concatenate(parts, axis=1).astype(jnp.bfloat16)
    terms = jnp.dot(attention, w_out, preferred_element_type=jnp.float32)
    return lax.psum_scatter(terms.astype(jnp.bfloat16), "head", scatter_dimension=1, tiled=True)


def packed_rows(place_ref, spots):
    start, early, half = place_ref[0], place_ref[1], place_ref[2]
    total = place_ref[3]
    before = jnp.where(spots < start, early, 1 - early)
    return spots + total * (half + before * (1 - 2 * half))


def clip_flags(rows, bounds_ref):
    begins, ends, leads = bounds_ref[0:1, :], bounds_ref[1:2, :], bounds_ref[2:3, :]
    inside = (rows >= begins) & (rows < ends)
    return inside, inside & (rows < leads)


def count_earlier(hot):
    ranks, rows, lanes = hot.shape
    flat = hot.reshape(ranks * rows, lanes).astype(jnp.bfloat16)

    def numbers(shape, axis):
        return lax.broadcasted_iota(jnp.int32, shape, axis)

    def group(index):
        return sum(jnp.where(index >= rows * k, 1, 0) for k in range(1, ranks))

    def ones(flags):
        return jnp.where(flags, 1.0, 0.0).astype(jnp.bfloat16)

    total = ranks * rows
    in_row = ones(numbers((lanes, lanes), 0) < numbers((lanes, lanes), 1))
    below, across = numbers((total, 1), 0), numbers((1, total), 1)
    in_rank = ones((group(below) == group(across)) & (across < below))
    row_sums = jnp.dot(
        flat, jnp.ones((lanes, lanes), jnp.bfloat16), preferred_element_type=jnp.float32
    )
    earlier = jnp.dot(flat, in_row, preferred_element_type=jnp.float32) + jnp.dot(
        in_rank, row_sums.astype(jnp.bfloat16), preferred_element_type=jnp.float32
    )
    return earlier.reshape(ranks, rows, lanes)


def table_kernel(ranks, place_ref, bounds_ref, rank_ref, w_ref, *refs):
    order_ref, runs_ref, query_ref, key_ref, weights_ref, held, sems = refs
    copies = weight_copies(place_ref, w_ref, weights_ref, sems)
    for copy in copies:
        copy.start()
    start, early, half, half_rows = (place_ref[k] for k in range(4))
    chip, clips, core, rank_here = (place_ref[k] for k in (4, 5, 8, 9))
    holds_long = half != early
    tokens = rank_ref[...]
    rows, lanes = tokens.shape
    per_dev = rows * lanes // ranks

    token = lanes * lax.broadcasted_iota(jnp.int32, tokens.shape, 0) + lax.broadcasted_iota(
        jnp.int32, tokens.shape, 1
    )
    hots = [jnp.where(tokens == rank, 1.0, 0.0) for rank in range(ranks)]
    earlier = count_earlier(jnp.stack(hots))
    within = sum(hots[rank] * earlier[rank] for rank in range(ranks))
    before = jnp.where(token < start, 1.0, 0.0)
    upto = jnp.where(token < start + half_rows, 1.0, 0.0)
    lane = lax.broadcasted_iota(jnp.int32, (1, lanes), 1)
    target = jnp.bitwise_xor(rank_here, 2 * jnp.bitwise_and(lane, 3))
    lane_long = jnp.where(lane < 4, jnp.where(holds_long, 1.0, 0.0), jnp.where(holds_long, 0.0, 1.0))
    lane_own = jnp.where(lane < 4, 1.0, 0.0)
    lows, longs, long_first, rest_first = [], [], [], []
    long_count, rest_count = [[0.0, 0.0], [0.0, 0.0]], [[0.0, 0.0], [0.0, 0.0]]
    for rank, hot in enumerate(hots):
        low = jnp.sum(hot * before, keepdims=True)
        long_rows = jnp.sum(hot * upto, keepdims=True) - low
        group, parity = rank // (ranks // 2), rank % 2
        lows.append(low)
        longs.append(long_rows)
        long_first.append(long_count[group][parity])
        rest_first.append(rest_count[group][parity])
        long_count[group][parity] = long_first[rank] + long_rows
        rest_count[group][parity] = rest_first[rank] + (per_dev - long_rows)
    long_base = rest_base = low_of = long_of = 0.0
    runs = [0.0] * 5
    for rank, hot in enumerate(hots):
        low, high, long_rows = lows[rank], lows[rank] + longs[rank], longs[rank]
        group, parity = rank // (ranks // 2), rank % 2
        own_group = jnp.where(half == group, 1.0, 0.0)
        long_after = own_group * long_count[1 - group][parity]
        rest_after = own_group * rest_count[1 - group][parity]
        long_base += hot * (long_first[rank] + long_after - low)
        rest_base += hot * (rest_first[rank] + rest_after)
        low_of += hot * low
        long_of += hot * long_rows
        first = long_first[rank] + lane_own * long_after
        rest = rest_first[rank] + lane_own * rest_after
        here = jnp.where(target == rank, 1.0, 0.0)
        values = (
            (0.0, low),
            (low, high),
            (high, float(per_dev)),
            (0.0, rest),
            (first - low, rest - long_rows),
        )
        runs = [
            run + here * (lane_long * if_long + (1.0 - lane_long) * if_rest)
            for run, (if_long, if_rest) in zip(runs, values)
        ]
    furthest = rows * lanes // 4 + per_dev // 2
    for index, run in enumerate(runs):
        run = run.astype(jnp.int32)
        runs_ref[index : index + 1, :] = (
            run if index < 3 else jnp.clip(run, -per_dev, furthest)
        )
    sorted_at = within + jnp.where(
        upto - before == 1.0, long_base, rest_base - jnp.where(within < low_of, 0.0, long_of)
    )
    held[...] = jnp.where(jnp.bitwise_and(tokens, 1) == core, sorted_at.astype(jnp.int32), -1)
    half_lines = rows // 2
    spots = lanes * lax.broadcasted_iota(
        jnp.int32, (half_lines, lanes), 0
    ) + lax.broadcasted_iota(jnp.int32, (half_lines, lanes), 1)
    later = packed_rows(place_ref, spots) >= half_rows
    held[:half_lines, :] = jnp.where(later, held[half_lines:, :], held[:half_lines, :])
    lines = half_lines // 4
    for d in range(4):
        line = lines * jnp.bitwise_xor(chip, d)
        order_ref[lines * d : lines * (d + 1), :] = held[pl.ds(line, lines), :]

    column = lax.broadcasted_iota(jnp.int32, (1, HEAD_DIM), 1)
    chip_rows = query_ref.shape[0] // 4
    for d in range(4):
        local = lax.broadcasted_iota(jnp.int32, (chip_rows, 1), 0)
        spots = chip_rows * jnp.bitwise_xor(chip, d) + local
        inside, leading = clip_flags(packed_rows(place_ref, spots), bounds_ref)
        spot = slice(d * chip_rows, (d + 1) * chip_rows)
        inside = jnp.where(inside, 1.0, 0.0)
        prefix = jnp.sum(jnp.where(leading, 1.0, 0.0), axis=1, keepdims=True)
        query_ref[spot, :] = jnp.where(column == clips, prefix, inside).astype(jnp.bfloat16)
        outside = jnp.where(column < clips, NEG * (1.0 - inside), 0.0)
        key_ref[spot, :] = jnp.where(column == clips, NEG * (1.0 - prefix), outside).astype(
            jnp.bfloat16
        )
    for copy in copies:
        copy.wait()


def make_tables(place, bounds, token_rank, ranks, keys, w_parts):
    vmem = pl.BlockSpec(memory_space=pltpu.VMEM)
    tokens = token_rank.reshape(-1, HEAD_DIM)
    features = jax.ShapeDtypeStruct((keys, HEAD_DIM), jnp.bfloat16)
    return pl.pallas_call(
        functools.partial(table_kernel, ranks),
        in_specs=[
            pl.BlockSpec(memory_space=pltpu.SMEM),
            vmem,
            vmem,
            pl.BlockSpec(memory_space=pltpu.HBM),
        ],
        out_specs=(vmem,) * 5,
        out_shape=(
            jax.ShapeDtypeStruct((tokens.shape[0] // 2, HEAD_DIM), jnp.int32),
            jax.ShapeDtypeStruct((8, HEAD_DIM), jnp.int32),
            features,
            features,
            jax.ShapeDtypeStruct((*w_parts.shape[:2], w_parts.shape[2] // 2), w_parts.dtype),
        ),
        scratch_shapes=[
            pltpu.VMEM(tokens.shape, jnp.int32),
            pltpu.SemaphoreType.DMA((3, COPY_PIECES)),
        ],
        compiler_params=pltpu.CompilerParams(vmem_limit_bytes=26 * MIB),
        cost_estimate=pl.CostEstimate(flops=COST, bytes_accessed=COST, transcendentals=0),
    )(place, bounds, tokens, w_parts)


def select_kernel(low, place_ref, own_ref, moved_ref, *rest):
    out_ref = rest[-1]
    spots = place_ref[7] + low + lax.broadcasted_iota(jnp.int32, (out_ref.shape[0], 1), 0)
    swapped = jnp.where(spots < place_ref[0], place_ref[1], 1 - place_ref[1])
    out_ref[...] = jnp.where(swapped == 1, moved_ref[...], own_ref[...])


def select_rows(place, own, moved, low, after):
    vmem = pl.BlockSpec(memory_space=pltpu.VMEM)
    return pl.pallas_call(
        functools.partial(select_kernel, low),
        in_specs=[pl.BlockSpec(memory_space=pltpu.SMEM), vmem, vmem]
        + [pl.BlockSpec(memory_space=pl.ANY)] * len(after),
        out_specs=vmem,
        out_shape=jax.ShapeDtypeStruct(moved.shape, moved.dtype),
        compiler_params=pltpu.CompilerParams(vmem_limit_bytes=8 * MIB),
        cost_estimate=pl.CostEstimate(flops=COST, bytes_accessed=COST, transcendentals=0),
    )(place, own, moved, *after)


def head_of(chip, index, group_heads):
    return 2 * group_heads * (chip // 2) + 2 * index + chip % 2


def weight_copies(place_ref, w_ref, out_ref, sems):
    pair = jnp.bitwise_xor(place_ref[4] // 2, place_ref[8])
    columns = pl.ds(pl.multiple_of(pair * out_ref.shape[2], HEAD_DIM), out_ref.shape[2])
    depth = out_ref.shape[1] // COPY_PIECES
    copies = []
    for part in range(3):
        for piece in range(COPY_PIECES):
            rows = slice(piece * depth, (piece + 1) * depth)
            copies.append(
                pltpu.make_async_copy(
                    w_ref.at[part, rows, columns], out_ref.at[part, rows, :], sems.at[part, piece]
                )
            )
    return copies


def norm_kernel(place_ref, *refs):
    pieces = len(SWAP_ROWS)
    bounds_ref, noise_ref, level_ref, gain_ref = refs[2 * pieces : 2 * pieces + 4]
    out_ref = refs[-1]
    width = out_ref.shape[1] // 2
    side, first = place_ref[6], place_ref[7]
    clips, levels = noise_ref.shape[0], level_ref.shape[0]
    spots = [pl.ds(pl.multiple_of(s * width, 128), width) for s in (side, 1 - side)]
    level = lax.broadcasted_iota(jnp.int32, (clips, levels), 1)
    chosen = jnp.where(noise_ref[...] == level, 1.0, 0.0).astype(jnp.bfloat16)
    tables = [
        jnp.dot(chosen, level_ref[:, spot], preferred_element_type=jnp.float32).astype(
            jnp.bfloat16
        )
        for spot in spots
    ]
    low = 0
    for piece in range(pieces):
        own_ref, other_ref = refs[piece], refs[pieces + piece]
        count = own_ref.shape[0]
        rows = slice(low, low + count)
        places = first + low + lax.broadcasted_iota(jnp.int32, (count, 1), 0)
        low += count
        unused, leading = clip_flags(packed_rows(place_ref, places), bounds_ref)
        picks = jnp.where(leading, 1.0, 0.0)[:, :clips].astype(jnp.bfloat16)
        shifted = [
            ref[...].astype(jnp.float32)
            + jnp.dot(picks, table, preferred_element_type=jnp.float32)
            for ref, table in zip((own_ref, other_ref), tables)
        ]
        squares = sum(jnp.sum(part * part, axis=1, keepdims=True) for part in shifted)
        factor = lax.rsqrt(squares / (2 * width) + EPS)
        for part, spot in zip(shifted, spots):
            out_ref[rows, spot] = (part * factor * gain_ref[:, spot]).astype(jnp.bfloat16)


def normalize_rows(place, kept, other, bounds, noise_levels, level_table, norm_gain):
    rows, depth = sum(part.shape[0] for part in kept), 2 * kept[0].shape[1]
    vmem = pl.BlockSpec(memory_space=pltpu.VMEM)
    return pl.pallas_call(
        norm_kernel,
        in_specs=[pl.BlockSpec(memory_space=pltpu.SMEM)] + [vmem] * (2 * len(kept) + 4),
        out_specs=vmem,
        out_shape=jax.ShapeDtypeStruct((rows, depth), jnp.bfloat16),
        compiler_params=pltpu.CompilerParams(vmem_limit_bytes=26 * MIB),
        cost_estimate=pl.CostEstimate(flops=COST, bytes_accessed=COST, transcendentals=0),
    )(place, *kept, *other, bounds, noise_levels, level_table, norm_gain.reshape(1, -1))


def project_kernel(indices, place_ref, own_ref, pair_ref, weights_ref, *rest):
    first_ref, second_ref = rest[-2:]
    rows = jnp.concatenate([own_ref[...], pair_ref[...]], axis=0)
    count = own_ref.shape[0]
    same = place_ref[4] % 2 == place_ref[8]

    def store(outcome, base, even_ref, odd_ref):
        for index, core in enumerate((place_ref[8], 1 - place_ref[8])):
            spot = pl.ds(pl.multiple_of(core * count, count), count)
            half = outcome[index * count : (index + 1) * count]
            for part in range(3):
                to = slice(base + part * HEAD_DIM, base + (part + 1) * HEAD_DIM)
                even_ref[spot, to] = half[:, 2 * part * HEAD_DIM : (2 * part + 1) * HEAD_DIM]
                odd_ref[spot, to] = half[:, (2 * part + 1) * HEAD_DIM : 2 * (part + 1) * HEAD_DIM]

    for position, index in enumerate(indices):
        spot = slice(2 * index * HEAD_DIM, 2 * (index + 1) * HEAD_DIM)
        weights = jnp.concatenate([weights_ref[part, :, spot] for part in range(3)], axis=1)
        outcome = jnp.dot(rows, weights, preferred_element_type=jnp.float32).astype(jnp.bfloat16)
        base = 3 * position * HEAD_DIM

        @pl.when(same)
        def _():
            store(outcome, base, first_ref, second_ref)

        @pl.when(jnp.logical_not(same))
        def _():
            store(outcome, base, second_ref, first_ref)


def project_heads(place, own, pair, weights, indices, after):
    rows = own.shape[0]
    vmem = pl.BlockSpec(memory_space=pltpu.VMEM)
    shape = jax.ShapeDtypeStruct((2 * rows, 3 * len(indices) * HEAD_DIM), jnp.bfloat16)
    return pl.pallas_call(
        functools.partial(project_kernel, indices),
        in_specs=[pl.BlockSpec(memory_space=pltpu.SMEM), vmem, vmem, vmem]
        + [pl.BlockSpec(memory_space=pl.ANY)] * len(after),
        out_specs=(vmem, vmem),
        out_shape=(shape, shape),
        compiler_params=pltpu.CompilerParams(vmem_limit_bytes=20 * MIB),
        cost_estimate=pl.CostEstimate(flops=COST, bytes_accessed=COST, transcendentals=0),
    )(place, own, pair, weights, *after)


def attend_kernel(base, place_ref, runs_ref, *refs):
    mine, near, far, pair_first, pair_far, pair_near = refs[:6]
    order_ref, query_mask_ref, key_mask_ref = refs[6:9]
    stay_ref, cross_ref, q_all, k_all, v_all, sorted_out = refs[-6:]
    chip_rows = mine.shape[0]
    rows = chip_rows // 2
    queries = sorted_out.shape[0] - 2 * rows

    def hold(sources):
        for index, source in enumerate(sources):
            spot = slice(index * chip_rows, (index + 1) * chip_rows)
            for part, held in enumerate((q_all, k_all, v_all)):
                low = base + part * HEAD_DIM
                held[spot, :HEAD_DIM] = source[:, low : low + HEAD_DIM]

    @pl.when(place_ref[8] == 0)
    def _():
        hold((mine, near, pair_near, pair_far))

    @pl.when(place_ref[8] == 1)
    def _():
        hold((pair_first, pair_near, near, far))

    q_all[:, HEAD_DIM:] = query_mask_ref[...]
    k_all[:, HEAD_DIM:] = key_mask_ref[...]
    v_all[:, HEAD_DIM:] = jnp.ones((4 * chip_rows, HEAD_DIM), jnp.bfloat16)
    tile = queries // ATTEND_TILES

    def score(step):
        wanted = step * tile + lax.broadcasted_iota(jnp.int32, (tile, 1), 0)
        picks = jnp.concatenate(
            [
                jnp.where(order_ref[line : line + 1, :] == wanted, 1.0, 0.0).astype(jnp.bfloat16)
                for line in range(order_ref.shape[0])
            ],
            axis=1,
        )
        sorted_queries = jnp.dot(picks, q_all[...], preferred_element_type=jnp.float32)
        return lax.dot_general(
            sorted_queries.astype(jnp.bfloat16),
            k_all[...],
            (((1,), (1,)), ((), ())),
            preferred_element_type=jnp.float32,
        )

    coming = score(0)
    for step in range(ATTEND_TILES):
        scores = coming
        if step + 1 < ATTEND_TILES:
            coming = score(step + 1)
        top = jnp.max(scores, axis=1, keepdims=True)
        weights = jnp.exp2((scores - top) * (HEAD_DIM ** (-0.5) * LOG2E))
        summed = jnp.dot(
            weights.astype(jnp.bfloat16), v_all[...], preferred_element_type=jnp.float32
        )
        sorted_out[rows + step * tile : rows + (step + 1) * tile, :] = (
            summed[:, :HEAD_DIM] / summed[:, HEAD_DIM:]
        )

    cross_ref[...] = sorted_out[rows : rows + cross_ref.shape[0], :].astype(jnp.bfloat16)
    for d in range(4):
        stay_ref[d] = spread_run(sorted_out, runs_ref, d, rows).astype(jnp.bfloat16)


def spread_run(sorted_ref, runs_ref, lane, rows):
    furthest = sorted_ref.shape[0] - 2 * rows
    row = lax.broadcasted_iota(jnp.int32, (rows, 1), 0)
    parts = [
        sorted_ref[pl.ds(rows + jnp.clip(runs_ref[line, lane], -rows, furthest), rows), :]
        for line in (3, 4)
    ]
    in_second = (row >= runs_ref[1, lane]) & (row < runs_ref[2, lane])
    return jnp.where(row < runs_ref[0, lane], parts[0], jnp.where(in_second, parts[1], 0.0))


def attend(place, runs, blocks, position, order, query_mask, key_mask, after):
    chip_rows = blocks[0].shape[0]
    rows, keys = chip_rows // 2, 4 * chip_rows
    queries = keys // 2 + rows // 2
    vmem, smem = pl.BlockSpec(memory_space=pltpu.VMEM), pl.BlockSpec(memory_space=pltpu.SMEM)
    shape = jax.ShapeDtypeStruct((4, rows, HEAD_DIM), jnp.bfloat16)
    return pl.pallas_call(
        functools.partial(attend_kernel, 3 * position * HEAD_DIM),
        in_specs=[smem, smem]
        + [vmem] * (len(blocks) + 3)
        + [pl.BlockSpec(memory_space=pl.ANY)] * len(after),
        out_specs=(vmem, vmem),
        out_shape=(shape, jax.ShapeDtypeStruct((CROSSING_ROWS, HEAD_DIM), jnp.bfloat16)),
        scratch_shapes=[
            pltpu.VMEM((keys, 2 * HEAD_DIM), jnp.bfloat16),
            pltpu.VMEM((keys, 2 * HEAD_DIM), jnp.bfloat16),
            pltpu.VMEM((keys, 2 * HEAD_DIM), jnp.bfloat16),
            pltpu.VMEM((queries + 2 * rows, HEAD_DIM), jnp.float32),
        ],
        compiler_params=pltpu.CompilerParams(vmem_limit_bytes=20 * MIB),
        cost_estimate=pl.CostEstimate(
            flops=COST, bytes_accessed=COST, transcendentals=0
        ),
    )(place, runs, *blocks, order, query_mask, key_mask, *after)


def join_kernel(heads, runs_ref, *refs):
    outs, held = refs[-5:-1], refs[-1]
    rows = outs[0].shape[0]
    for head in range(heads):
        stay_ref, arrived_ref = refs[2 * head], refs[2 * head + 1]
        held[rows : rows + arrived_ref.shape[0], :] = arrived_ref[...].astype(jnp.float32)
        spot = slice(head * HEAD_DIM, (head + 1) * HEAD_DIM)
        for d in range(4):
            arrived = spread_run(held, runs_ref, 4 + d, rows).astype(jnp.bfloat16)
            outs[d][:, spot] = stay_ref[d] + arrived


def join_halves(runs, stays, arrivals, after, cost):
    heads, (slots, rows, width) = len(stays), stays[0].shape
    vmem = pl.BlockSpec(memory_space=pltpu.VMEM)
    parts = [part for both in zip(stays, arrivals) for part in both]
    shape = jax.ShapeDtypeStruct((rows, heads * width), jnp.bfloat16)
    return pl.pallas_call(
        functools.partial(join_kernel, heads),
        in_specs=[pl.BlockSpec(memory_space=pltpu.SMEM)]
        + [vmem] * len(parts)
        + [pl.BlockSpec(memory_space=pl.ANY)] * len(after),
        out_specs=(vmem,) * slots,
        out_shape=(shape,) * slots,
        scratch_shapes=[pltpu.VMEM((arrivals[0].shape[0] + 2 * rows, width), jnp.float32)],
        compiler_params=pltpu.CompilerParams(vmem_limit_bytes=16 * MIB),
        cost_estimate=pl.CostEstimate(flops=cost, bytes_accessed=COST, transcendentals=0),
    )(runs, *parts, *after)


def gather_kernel(place_ref, w_ref, held_ref, pair_ref, *rest):
    outs, sems = rest[-5:-1], rest[-1]
    chip, columns = place_ref[4], outs[0].shape[1]
    heads = w_ref.shape[0] // HEAD_DIM // 4
    spot = pl.ds(pl.multiple_of(place_ref[6] * columns, HEAD_DIM), columns)

    def rows_at(block):
        return pl.ds(pl.multiple_of(block * HEAD_DIM, HEAD_DIM), HEAD_DIM)

    def transfers(near_ref, far_ref):
        copies = []
        for d in range(4):
            for index in range(heads):
                last = index + 1 == heads
                group = 1 if last else 0
                to = d if last else d * (heads - 1) + index
                to = slice(to * HEAD_DIM, (to + 1) * HEAD_DIM)
                head = head_of(jnp.bitwise_xor(chip, d), index, heads)
                there = 2 * index + jnp.bitwise_xor(chip, d) % 2
                sources = (
                    w_ref.at[rows_at(head), spot],
                    (near_ref if d < 2 else far_ref).at[rows_at(there), :],
                )
                for side, source in enumerate(sources):
                    copies.append(
                        pltpu.make_async_copy(
                            source, outs[2 * side + group].at[to, :], sems.at[side, index, d]
                        )
                    )
        for copy in copies:
            copy.start()
        for copy in copies:
            copy.wait()

    @pl.when(chip // 2 == place_ref[8])
    def _():
        transfers(held_ref, pair_ref)

    @pl.when(chip // 2 != place_ref[8])
    def _():
        transfers(pair_ref, held_ref)


def gather_out_weights(place, w_out, held, pair, group_heads, after):
    vmem, hbm = pl.BlockSpec(memory_space=pltpu.VMEM), pl.BlockSpec(memory_space=pltpu.HBM)
    any_space = pl.BlockSpec(memory_space=pl.ANY)
    shapes = tuple(
        jax.ShapeDtypeStruct((count * HEAD_DIM, w_out.shape[1] // 2), w_out.dtype)
        for count in (4 * (group_heads - 1), 4)
    )
    return pl.pallas_call(
        gather_kernel,
        in_specs=[pl.BlockSpec(memory_space=pltpu.SMEM), hbm] + [any_space] * (2 + len(after)),
        out_specs=(vmem,) * 4,
        out_shape=shapes + shapes,
        scratch_shapes=[pltpu.SemaphoreType.DMA((2, group_heads, 4))],
        compiler_params=pltpu.CompilerParams(vmem_limit_bytes=16 * MIB),
        cost_estimate=pl.CostEstimate(flops=COST, bytes_accessed=COST, transcendentals=0),
    )(place, w_out, held, pair, *after)


def out_rows_kernel(*refs):
    refs[-1][...] = jnp.concatenate([ref[...] for ref in refs[:-1]], axis=1)


def out_kernel(pairs, *refs):
    total = refs[2 * pairs][...] if len(refs) > 2 * pairs + 1 else None
    for pair in range(pairs):
        product = jnp.dot(
            refs[2 * pair][...], refs[2 * pair + 1][...], preferred_element_type=jnp.float32
        )
        total = product if total is None else total + product
    refs[-1][...] = total.astype(refs[-1].dtype)


def out_call(kernel, arrays, shape, dtype):
    vmem = pl.BlockSpec(memory_space=pltpu.VMEM)
    return pl.pallas_call(
        kernel,
        in_specs=[vmem] * len(arrays),
        out_specs=vmem,
        out_shape=jax.ShapeDtypeStruct(shape, dtype),
        compiler_params=pltpu.CompilerParams(vmem_limit_bytes=16 * MIB),
        cost_estimate=pl.CostEstimate(flops=COST, bytes_accessed=COST, transcendentals=0),
    )(*arrays)


SWAP_ROWS = (128, 112, 80)
CROSSING_ROWS = 1040
ATTEND_TILES = 5
HEAD_CHUNKS = ((0,), (1, 2))
COPY_PIECES = 4


def halved_body(
    inputs,
    norm_gain,
    level_table,
    w_qkv,
    w_out,
    clip_lengths,
    prefix_lengths,
    noise_levels,
    token_rank,
):
    ranks, per_dev = 16, inputs.shape[0]
    half_rows = 8 * per_dev
    clips = clip_lengths.shape[0]
    index = jnp.arange(clips, dtype=jnp.int32)

    ahead = (index[None, :] < index[:, None]) & (clip_lengths == MAXCLIP)[:, None]
    start = jnp.sum(jnp.where(ahead, clip_lengths[None, :], 0))
    early = start <= half_rows // 2

    rank_here = lax.axis_index("ctx")
    side = lax.axis_index("head")
    columns = inputs.shape[1]
    group_heads = w_qkv.shape[2] // HEAD_DIM // 4
    half, block, core = rank_here // 8, rank_here % 8, rank_here % 2
    chip = block // 2
    swap_sides = [(0, 1), (1, 0)]

    def exchange(array, flip, only=lambda r: True):
        pairs = [(r, r ^ flip) for r in range(ranks) if only(r)]
        return lax.ppermute(array, "ctx", pairs)

    def move_rows(swapping):
        return functools.partial(moved_rows, swapping)

    def moved_rows(
        swapping, start, inputs, clip_lengths, prefix_lengths, noise_levels, w_out
    ):
        place = jnp.stack(
            [
                start,
                jnp.int32(1 if 0 in swapping else 0),
                half,
                jnp.int32(half_rows),
                chip,
                jnp.int32(clips),
                side,
                block * per_dev,
                core,
                rank_here,
            ]
        )
        earlier = index[None, :] < index[:, None]
        begins = jnp.sum(jnp.where(earlier, clip_lengths[None, :], 0), axis=1)
        leads = begins + jnp.minimum(prefix_lengths, clip_lengths)
        bounds = jnp.pad(
            jnp.stack([begins, begins + clip_lengths, leads]), ((0, 5), (0, HEAD_DIM - clips))
        )

        cuts = [sum(SWAP_ROWS[:i]) for i in range(len(SWAP_ROWS) + 1)]
        kept, moved = [], []
        for low, high in zip(cuts[:-1], cuts[1:]):
            own = inputs[low:high]
            moved.append(exchange(own, 8, lambda r: r % 8 in swapping))
            kept.append(select_rows(place, own, moved[-1], low, kept[-1:]))
        other = [lax.ppermute(part, "head", swap_sides) for part in kept]
        depth = w_out.shape[0] // 2
        sent = lax.dynamic_slice(w_out, (core * depth, (1 - side) * columns), (depth, columns))
        return tuple(kept), tuple(other), place, bounds, noise_levels.reshape(-1, 1), sent

    kept, other, place, bounds, noise_column, sent = lax.cond(
        early,
        move_rows(range(4)),
        move_rows(range(4, 8)),
        start,
        inputs,
        clip_lengths,
        prefix_lengths,
        noise_levels,
        w_out,
    )
    far_held = lax.ppermute(sent, "head", swap_sides)
    normed = normalize_rows(place, kept, other, bounds, noise_column, level_table, norm_gain)
    pair = exchange(normed, 1)
    w_parts = jnp.transpose(w_qkv, (1, 0, 2))
    query_order, runs, query_mask, key_mask, weights = make_tables(
        place, bounds, token_rank, ranks, half_rows, w_parts
    )

    def held_back(array, after):
        return lax.optimization_barrier((array, *after))[0]

    blocks, pair_firsts, after = [], [], [query_order]
    for heads in HEAD_CHUNKS:
        first, second = project_heads(
            held_back(place, after), normed, pair, weights, heads, []
        )
        near = lax.ppermute(
            second, "ctx", [(r, r ^ (2 if r % 2 == 0 else 4)) for r in range(ranks)]
        )
        far = exchange(first, 6, lambda r: r % 2 == 1)
        blocks.append((first, near, far))
        if not pair_firsts:
            pair_firsts.append(exchange(first, 1, lambda r: r % 2 == 0))
            after = [pair_firsts[0]]

    def share(block, after):
        first, near, far = block
        near, far, *unused = lax.optimization_barrier((near, far, *after))
        if not pair_firsts:
            pair_firsts.append(exchange(held_back(first, after), 1, lambda r: r % 2 == 0))
        return [
            first,
            near,
            far,
            pair_firsts.pop(),
            exchange(far, 1, lambda r: r % 2 == 1),
            exchange(near, 1),
        ]

    def join(heads, after, cost):
        joined = join_halves(
            held_back(runs, after), stays[heads], arrivals[heads], [], cost
        )
        return [exchange(part, 2 * d) if d else part for d, part in enumerate(joined)]

    stays, arrivals = [], []
    after = [blocks[-1][0]]
    for block, heads in zip(blocks, HEAD_CHUNKS):
        block = share(block, after)
        for position, head in enumerate(heads):
            stay, cross = attend(
                held_back(place, after),
                runs,
                block,
                position,
                query_order,
                query_mask,
                key_mask,
                [],
            )
            stays.append(stay)
            arrivals.append(exchange(cross, 8))
            after = [cross] + (arrivals[head - 1 : head] if head else [])
            if head == 1:
                far_pair = exchange(lax.optimization_barrier((far_held, cross))[0], 1)

    w_all = gather_out_weights(
        held_back(place, [cross]), w_out, far_held, far_pair, group_heads, []
    )

    def side_by_side(parts):
        width = sum(part.shape[1] for part in parts)
        return out_call(out_rows_kernel, parts, (per_dev, width), jnp.bfloat16)

    pieces = join(slice(0, -1), [cross], COST)
    rows = [side_by_side(pieces), side_by_side(join(slice(-1, None), [], LONG_COST))]
    far_rows = [lax.ppermute(part, "head", swap_sides) for part in rows]
    w_own, w_far = w_all[:2], w_all[2:]

    def add(terms, total, dtype):
        arrays = [array for term in terms for array in term] + total
        return out_call(functools.partial(out_kernel, len(terms)), arrays, (per_dev, columns), dtype)

    own, far = list(zip(rows, w_own)), list(zip(far_rows, w_far))
    total = add(own[:1], [], jnp.float32)
    total = add(own[1:] + far[:1], [total], jnp.float32)
    return add(far[1:], [total], jnp.bfloat16)


def solution(mesh):
    in_specs = (
        P("ctx", "head"),
        P(),
        P(),
        P(None, None, "head"),
        P("head", None),
        P(),
        P(),
        P(),
        P(),
    )
    out_specs = P("ctx", "head")

    def body(inputs, norm_gain, level_table, w_qkv, *rest):
        ranks, sides = mesh.shape["ctx"], mesh.shape["head"]
        heads_here = w_qkv.shape[2] // HEAD_DIM
        halved = (
            ranks == 16
            and sides == 2
            and ranks * inputs.shape[0] == 2 * MAXCLIP
            and heads_here == 4 * sum(len(heads) for heads in HEAD_CHUNKS)
        )
        run = halved_body if halved else gathered_body
        return run(inputs, norm_gain, level_table, w_qkv, *rest)

    return jax.shard_map(body, mesh=mesh, in_specs=in_specs, out_specs=out_specs, check_vma=False)
```

```python
import functools

import jax
import jax.numpy as jnp
from jax import lax
from jax.experimental import pallas as pl
from jax.experimental.pallas import tpu as pltpu
from jax.sharding import PartitionSpec as P

HEAD_DIM = 128


NEG = -1e30
EPS = 1e-06
MAXCLIP = 2560
LOG2E = 1.4426950408889634
MIB = 1024 * 1024
COST = 1000000
LONG_COST = 200000000000


def clip_tables(total_rows, clip_lengths, prefix_lengths, noise_levels):
    rows = jnp.arange(total_rows, dtype=jnp.int32)
    ends = jnp.cumsum(clip_lengths)
    begins = ends - clip_lengths
    clip_of = jnp.sum((rows[:, None] >= ends[None, :]).astype(jnp.int32), axis=1)
    member = clip_of[:, None] == jnp.arange(clip_lengths.shape[0], dtype=jnp.int32)[None, :]
    begin_row = jnp.sum(jnp.where(member, begins[None, :], 0), axis=1)
    lead = jnp.minimum(prefix_lengths, clip_lengths)
    lead_row = jnp.sum(jnp.where(member, lead[None, :], 0), axis=1)
    level_row = jnp.sum(jnp.where(member, noise_levels[None, :], 0), axis=1)
    in_prefix = rows - begin_row < lead_row
    return (clip_of, in_prefix, level_row)


def rank_tables(token_rank, ranks, per_rank):
    onehot = (token_rank[:, None] == jnp.arange(ranks, dtype=jnp.int32)[None, :]).astype(jnp.int32)
    earlier = jnp.cumsum(onehot, axis=0) - onehot
    within = jnp.sum(earlier * onehot, axis=1)
    counts = jnp.sum(onehot.reshape(ranks, per_rank, ranks), axis=1)
    starts = jnp.cumsum(counts, axis=0) - counts
    return (within, counts, starts)


def normalize(rows, in_prefix, level_row, level_table, norm_gain):
    picks = (
        level_row[:, None] == jnp.arange(level_table.shape[0], dtype=jnp.int32)[None, :]
    ) & in_prefix[:, None]
    added = jnp.dot(picks.astype(jnp.bfloat16), level_table, preferred_element_type=jnp.float32)
    shifted = rows.astype(jnp.float32) + added
    factor = lax.rsqrt(jnp.mean(shifted * shifted, axis=-1, keepdims=True) + EPS)
    return (shifted * factor * norm_gain).astype(jnp.bfloat16)


def fold_keys(state, queries, query_clip, query_prefix, pairs, key_clip, key_prefix):
    width = queries.shape[1]
    heads_here = width // HEAD_DIM
    factor = HEAD_DIM ** (-0.5)
    allowed_query = jnp.logical_not(query_prefix)

    def absorb(carry, block):
        block_pairs, block_clip, block_prefix = block
        allowed = (query_clip[:, None] == block_clip[None, :]) & (
            allowed_query[:, None] | block_prefix[None, :]
        )
        updated = []
        for head in range(heads_here):
            top, total, summed = carry[head]
            low = head * HEAD_DIM
            q_head = queries[:, low : low + HEAD_DIM]
            k_head = block_pairs[:, low : low + HEAD_DIM]
            v_head = block_pairs[:, width + low : width + low + HEAD_DIM]
            scores = (
                lax.dot_general(
                    q_head, k_head, (((1,), (1,)), ((), ())), preferred_element_type=jnp.float32
                )
                * factor
            )
            masked = jnp.where(allowed, scores, NEG)
            new_top = jnp.maximum(top, jnp.max(masked, axis=1, keepdims=True))
            fade = jnp.exp(top - new_top)
            weights = jnp.where(allowed, jnp.exp(scores - new_top), 0.0)
            total = total * fade + jnp.sum(weights, axis=1, keepdims=True)
            summed = summed * fade + jnp.dot(
                weights.astype(jnp.bfloat16), v_head, preferred_element_type=jnp.float32
            )
            updated.append((new_top, total, summed))
        return (tuple(updated), None)

    count = pairs.shape[0]
    step = 2048 if count > 2048 and count % 2048 == 0 else count
    if step == count:
        result, unused = absorb(state, (pairs, key_clip, key_prefix))
        return result
    stacked = (
        pairs.reshape(count // step, step, pairs.shape[1]),
        key_clip.reshape(count // step, step),
        key_prefix.reshape(count // step, step),
    )
    result, unused = lax.scan(absorb, state, stacked)
    return result


def gathered_body(
    inputs,
    norm_gain,
    level_table,
    w_qkv,
    w_out,
    clip_lengths,
    prefix_lengths,
    noise_levels,
    token_rank,
):
    ranks = lax.axis_size("ctx")
    rank_here = lax.axis_index("ctx")
    per_dev = inputs.shape[0]
    slots = 2 * per_dev // ranks
    local_width = w_qkv.shape[2]
    heads_here = local_width // HEAD_DIM
    total_rows = per_dev * ranks
    clip_of, in_prefix, level_row = clip_tables(
        total_rows, clip_lengths, prefix_lengths, noise_levels
    )
    within, counts, starts = rank_tables(token_rank, ranks, per_dev)
    place = token_rank * per_dev + within
    order = (
        jnp.zeros((total_rows,), jnp.int32).at[place].set(jnp.arange(total_rows, dtype=jnp.int32))
    )
    first = rank_here * per_dev
    own_rank = lax.dynamic_slice_in_dim(token_rank, first, per_dev, 0)
    own_within = lax.dynamic_slice_in_dim(within, first, per_dev, 0)
    send_starts = lax.dynamic_slice_in_dim(starts, rank_here, 1, 0)[0]
    recv_counts = lax.dynamic_slice_in_dim(counts, rank_here, 1, 1)[:, 0]
    recv_starts = lax.dynamic_slice_in_dim(starts, rank_here, 1, 1)[:, 0]
    balanced_rows = lax.dynamic_slice_in_dim(order, first, per_dev, 0)
    target = own_rank * slots + own_within - send_starts[own_rank]
    buffer = jnp.zeros((ranks * slots, inputs.shape[1]), inputs.dtype).at[target].set(inputs)
    received = lax.all_to_all(
        buffer.reshape(ranks, slots, inputs.shape[1]),
        "ctx",
        split_axis=0,
        concat_axis=0,
        tiled=True,
    )
    spots = jnp.arange(slots, dtype=jnp.int32)[None, :]
    index = jnp.where(spots < recv_counts[:, None], recv_starts[:, None] + spots, per_dev).reshape(
        -1
    )
    flat = received.reshape(ranks * slots, received.shape[2])
    rows = jnp.zeros((per_dev, received.shape[2]), received.dtype).at[index].set(flat, mode="drop")
    full_rows = lax.all_gather(rows, "head", axis=1, tiled=True)
    normed = normalize(
        full_rows, in_prefix[balanced_rows], level_row[balanced_rows], level_table, norm_gain
    )
    qkv = jnp.dot(
        normed, w_qkv.reshape(w_qkv.shape[0], 3 * local_width), preferred_element_type=jnp.float32
    ).astype(jnp.bfloat16)
    start_state = tuple(
        (
            (
                jnp.full((per_dev, 1), NEG, jnp.float32),
                jnp.zeros((per_dev, 1), jnp.float32),
                jnp.zeros((per_dev, HEAD_DIM), jnp.float32),
            )
            for head in range(heads_here)
        )
    )
    key_clip = clip_of[order]
    key_prefix = in_prefix[order]
    query_clip = lax.dynamic_slice_in_dim(key_clip, first, per_dev, 0)
    query_prefix = lax.dynamic_slice_in_dim(key_prefix, first, per_dev, 0)
    queries = qkv[:, :local_width]
    pairs = qkv[:, local_width:]
    state = fold_keys(
        start_state,
        queries,
        query_clip,
        query_prefix,
        lax.all_gather(pairs, "ctx", axis=0, tiled=True),
        key_clip,
        key_prefix,
    )
    parts = [state[head][2] / state[head][1] for head in range(heads_here)]
    attention = jnp.concatenate(parts, axis=1).astype(jnp.bfloat16)
    terms = jnp.dot(attention, w_out, preferred_element_type=jnp.float32)
    return lax.psum_scatter(terms.astype(jnp.bfloat16), "head", scatter_dimension=1, tiled=True)


def packed_rows(place_ref, spots):
    start, early, half = place_ref[0], place_ref[1], place_ref[2]
    total = place_ref[3]
    before = jnp.where(spots < start, early, 1 - early)
    return spots + total * (half + before * (1 - 2 * half))


def clip_flags(rows, bounds_ref):
    begins, ends, leads = bounds_ref[0:1, :], bounds_ref[1:2, :], bounds_ref[2:3, :]
    inside = (rows >= begins) & (rows < ends)
    return inside, inside & (rows < leads)


def count_earlier(hot):
    ranks, rows, lanes = hot.shape
    flat = hot.reshape(ranks * rows, lanes).astype(jnp.bfloat16)

    def numbers(shape, axis):
        return lax.broadcasted_iota(jnp.int32, shape, axis)

    def group(index):
        return sum(jnp.where(index >= rows * k, 1, 0) for k in range(1, ranks))

    def ones(flags):
        return jnp.where(flags, 1.0, 0.0).astype(jnp.bfloat16)

    total = ranks * rows
    in_row = ones(numbers((lanes, lanes), 0) < numbers((lanes, lanes), 1))
    below, across = numbers((total, 1), 0), numbers((1, total), 1)
    in_rank = ones((group(below) == group(across)) & (across < below))
    row_sums = jnp.dot(
        flat, jnp.ones((lanes, lanes), jnp.bfloat16), preferred_element_type=jnp.float32
    )
    earlier = jnp.dot(flat, in_row, preferred_element_type=jnp.float32) + jnp.dot(
        in_rank, row_sums.astype(jnp.bfloat16), preferred_element_type=jnp.float32
    )
    return earlier.reshape(ranks, rows, lanes)


def table_kernel(ranks, place_ref, bounds_ref, rank_ref, w_ref, *refs):
    order_ref, runs_ref, query_ref, key_ref, weights_ref, held, sems = refs
    copies = weight_copies(place_ref, w_ref, weights_ref, sems)
    for copy in copies:
        copy.start()
    start, early, half, half_rows = (place_ref[k] for k in range(4))
    chip, clips, core, rank_here = (place_ref[k] for k in (4, 5, 8, 9))
    holds_long = half != early
    tokens = rank_ref[...]
    rows, lanes = tokens.shape
    per_dev = rows * lanes // ranks

    token = lanes * lax.broadcasted_iota(jnp.int32, tokens.shape, 0) + lax.broadcasted_iota(
        jnp.int32, tokens.shape, 1
    )
    hots = [jnp.where(tokens == rank, 1.0, 0.0) for rank in range(ranks)]
    earlier = count_earlier(jnp.stack(hots))
    within = sum(hots[rank] * earlier[rank] for rank in range(ranks))
    before = jnp.where(token < start, 1.0, 0.0)
    upto = jnp.where(token < start + half_rows, 1.0, 0.0)
    lane = lax.broadcasted_iota(jnp.int32, (1, lanes), 1)
    target = jnp.bitwise_xor(rank_here, 2 * jnp.bitwise_and(lane, 3))
    lane_long = jnp.where(lane < 4, jnp.where(holds_long, 1.0, 0.0), jnp.where(holds_long, 0.0, 1.0))
    lane_own = jnp.where(lane < 4, 1.0, 0.0)
    lows, longs, long_first, rest_first = [], [], [], []
    long_count, rest_count = [[0.0, 0.0], [0.0, 0.0]], [[0.0, 0.0], [0.0, 0.0]]
    for rank, hot in enumerate(hots):
        low = jnp.sum(hot * before, keepdims=True)
        long_rows = jnp.sum(hot * upto, keepdims=True) - low
        group, parity = rank // (ranks // 2), rank % 2
        lows.append(low)
        longs.append(long_rows)
        long_first.append(long_count[group][parity])
        rest_first.append(rest_count[group][parity])
        long_count[group][parity] = long_first[rank] + long_rows
        rest_count[group][parity] = rest_first[rank] + (per_dev - long_rows)
    long_base = rest_base = low_of = long_of = 0.0
    runs = [0.0] * 5
    for rank, hot in enumerate(hots):
        low, high, long_rows = lows[rank], lows[rank] + longs[rank], longs[rank]
        group, parity = rank // (ranks // 2), rank % 2
        own_group = jnp.where(half == group, 1.0, 0.0)
        long_after = own_group * long_count[1 - group][parity]
        rest_after = own_group * rest_count[1 - group][parity]
        long_base += hot * (long_first[rank] + long_after - low)
        rest_base += hot * (rest_first[rank] + rest_after)
        low_of += hot * low
        long_of += hot * long_rows
        first = long_first[rank] + lane_own * long_after
        rest = rest_first[rank] + lane_own * rest_after
        here = jnp.where(target == rank, 1.0, 0.0)
        values = (
            (0.0, low),
            (low, high),
            (high, float(per_dev)),
            (0.0, rest),
            (first - low, rest - long_rows),
        )
        runs = [
            run + here * (lane_long * if_long + (1.0 - lane_long) * if_rest)
            for run, (if_long, if_rest) in zip(runs, values)
        ]
    furthest = rows * lanes // 4 + per_dev // 2
    for index, run in enumerate(runs):
        run = run.astype(jnp.int32)
        runs_ref[index : index + 1, :] = (
            run if index < 3 else jnp.clip(run, -per_dev, furthest)
        )
    sorted_at = within + jnp.where(
        upto - before == 1.0, long_base, rest_base - jnp.where(within < low_of, 0.0, long_of)
    )
    held[...] = jnp.where(jnp.bitwise_and(tokens, 1) == core, sorted_at.astype(jnp.int32), -1)
    half_lines = rows // 2
    spots = lanes * lax.broadcasted_iota(
        jnp.int32, (half_lines, lanes), 0
    ) + lax.broadcasted_iota(jnp.int32, (half_lines, lanes), 1)
    later = packed_rows(place_ref, spots) >= half_rows
    held[:half_lines, :] = jnp.where(later, held[half_lines:, :], held[:half_lines, :])
    lines = half_lines // 4
    for d in range(4):
        line = lines * jnp.bitwise_xor(chip, d)
        order_ref[lines * d : lines * (d + 1), :] = held[pl.ds(line, lines), :]

    column = lax.broadcasted_iota(jnp.int32, (1, HEAD_DIM), 1)
    chip_rows = query_ref.shape[0] // 4
    for d in range(4):
        local = lax.broadcasted_iota(jnp.int32, (chip_rows, 1), 0)
        spots = chip_rows * jnp.bitwise_xor(chip, d) + local
        inside, leading = clip_flags(packed_rows(place_ref, spots), bounds_ref)
        spot = slice(d * chip_rows, (d + 1) * chip_rows)
        inside = jnp.where(inside, 1.0, 0.0)
        prefix = jnp.sum(jnp.where(leading, 1.0, 0.0), axis=1, keepdims=True)
        query_ref[spot, :] = jnp.where(column == clips, prefix, inside).astype(jnp.bfloat16)
        outside = jnp.where(column < clips, NEG * (1.0 - inside), 0.0)
        key_ref[spot, :] = jnp.where(column == clips, NEG * (1.0 - prefix), outside).astype(
            jnp.bfloat16
        )
    for copy in copies:
        copy.wait()


def make_tables(place, bounds, token_rank, ranks, keys, w_parts):
    vmem = pl.BlockSpec(memory_space=pltpu.VMEM)
    tokens = token_rank.reshape(-1, HEAD_DIM)
    features = jax.ShapeDtypeStruct((keys, HEAD_DIM), jnp.bfloat16)
    return pl.pallas_call(
        functools.partial(table_kernel, ranks),
        in_specs=[
            pl.BlockSpec(memory_space=pltpu.SMEM),
            vmem,
            vmem,
            pl.BlockSpec(memory_space=pltpu.HBM),
        ],
        out_specs=(vmem,) * 5,
        out_shape=(
            jax.ShapeDtypeStruct((tokens.shape[0] // 2, HEAD_DIM), jnp.int32),
            jax.ShapeDtypeStruct((8, HEAD_DIM), jnp.int32),
            features,
            features,
            jax.ShapeDtypeStruct((*w_parts.shape[:2], w_parts.shape[2] // 2), w_parts.dtype),
        ),
        scratch_shapes=[
            pltpu.VMEM(tokens.shape, jnp.int32),
            pltpu.SemaphoreType.DMA((3, COPY_PIECES)),
        ],
        compiler_params=pltpu.CompilerParams(vmem_limit_bytes=26 * MIB),
        cost_estimate=pl.CostEstimate(flops=COST, bytes_accessed=COST, transcendentals=0),
    )(place, bounds, tokens, w_parts)


def select_kernel(low, place_ref, own_ref, moved_ref, *rest):
    out_ref = rest[-1]
    spots = place_ref[7] + low + lax.broadcasted_iota(jnp.int32, (out_ref.shape[0], 1), 0)
    swapped = jnp.where(spots < place_ref[0], place_ref[1], 1 - place_ref[1])
    out_ref[...] = jnp.where(swapped == 1, moved_ref[...], own_ref[...])


def select_rows(place, own, moved, low, after):
    vmem = pl.BlockSpec(memory_space=pltpu.VMEM)
    return pl.pallas_call(
        functools.partial(select_kernel, low),
        in_specs=[pl.BlockSpec(memory_space=pltpu.SMEM), vmem, vmem]
        + [pl.BlockSpec(memory_space=pl.ANY)] * len(after),
        out_specs=vmem,
        out_shape=jax.ShapeDtypeStruct(moved.shape, moved.dtype),
        compiler_params=pltpu.CompilerParams(vmem_limit_bytes=8 * MIB),
        cost_estimate=pl.CostEstimate(flops=COST, bytes_accessed=COST, transcendentals=0),
    )(place, own, moved, *after)


def head_of(chip, index, group_heads):
    return 2 * group_heads * (chip // 2) + 2 * index + chip % 2


def weight_copies(place_ref, w_ref, out_ref, sems):
    pair = jnp.bitwise_xor(place_ref[4] // 2, place_ref[8])
    columns = pl.ds(pl.multiple_of(pair * out_ref.shape[2], HEAD_DIM), out_ref.shape[2])
    depth = out_ref.shape[1] // COPY_PIECES
    copies = []
    for part in range(3):
        for piece in range(COPY_PIECES):
            rows = slice(piece * depth, (piece + 1) * depth)
            copies.append(
                pltpu.make_async_copy(
                    w_ref.at[part, rows, columns], out_ref.at[part, rows, :], sems.at[part, piece]
                )
            )
    return copies


def norm_kernel(place_ref, *refs):
    pieces = len(SWAP_ROWS)
    bounds_ref, noise_ref, level_ref, gain_ref = refs[2 * pieces : 2 * pieces + 4]
    out_ref = refs[-1]
    width = out_ref.shape[1] // 2
    side, first = place_ref[6], place_ref[7]
    clips, levels = noise_ref.shape[0], level_ref.shape[0]
    spots = [pl.ds(pl.multiple_of(s * width, 128), width) for s in (side, 1 - side)]
    level = lax.broadcasted_iota(jnp.int32, (clips, levels), 1)
    chosen = jnp.where(noise_ref[...] == level, 1.0, 0.0).astype(jnp.bfloat16)
    tables = [
        jnp.dot(chosen, level_ref[:, spot], preferred_element_type=jnp.float32).astype(
            jnp.bfloat16
        )
        for spot in spots
    ]
    low = 0
    for piece in range(pieces):
        own_ref, other_ref = refs[piece], refs[pieces + piece]
        count = own_ref.shape[0]
        rows = slice(low, low + count)
        places = first + low + lax.broadcasted_iota(jnp.int32, (count, 1), 0)
        low += count
        unused, leading = clip_flags(packed_rows(place_ref, places), bounds_ref)
        picks = jnp.where(leading, 1.0, 0.0)[:, :clips].astype(jnp.bfloat16)
        shifted = [
            ref[...].astype(jnp.float32)
            + jnp.dot(picks, table, preferred_element_type=jnp.float32)
            for ref, table in zip((own_ref, other_ref), tables)
        ]
        squares = sum(jnp.sum(part * part, axis=1, keepdims=True) for part in shifted)
        factor = lax.rsqrt(squares / (2 * width) + EPS)
        for part, spot in zip(shifted, spots):
            out_ref[rows, spot] = (part * factor * gain_ref[:, spot]).astype(jnp.bfloat16)


def normalize_rows(place, kept, other, bounds, noise_levels, level_table, norm_gain):
    rows, depth = sum(part.shape[0] for part in kept), 2 * kept[0].shape[1]
    vmem = pl.BlockSpec(memory_space=pltpu.VMEM)
    return pl.pallas_call(
        norm_kernel,
        in_specs=[pl.BlockSpec(memory_space=pltpu.SMEM)] + [vmem] * (2 * len(kept) + 4),
        out_specs=vmem,
        out_shape=jax.ShapeDtypeStruct((rows, depth), jnp.bfloat16),
        compiler_params=pltpu.CompilerParams(vmem_limit_bytes=26 * MIB),
        cost_estimate=pl.CostEstimate(flops=COST, bytes_accessed=COST, transcendentals=0),
    )(place, *kept, *other, bounds, noise_levels, level_table, norm_gain.reshape(1, -1))


def project_kernel(indices, place_ref, own_ref, pair_ref, weights_ref, *rest):
    first_ref, second_ref = rest[-2:]
    rows = jnp.concatenate([own_ref[...], pair_ref[...]], axis=0)
    count = own_ref.shape[0]
    same = place_ref[4] % 2 == place_ref[8]

    def store(outcome, base, even_ref, odd_ref):
        for index, core in enumerate((place_ref[8], 1 - place_ref[8])):
            spot = pl.ds(pl.multiple_of(core * count, count), count)
            half = outcome[index * count : (index + 1) * count]
            for part in range(3):
                to = slice(base + part * HEAD_DIM, base + (part + 1) * HEAD_DIM)
                even_ref[spot, to] = half[:, 2 * part * HEAD_DIM : (2 * part + 1) * HEAD_DIM]
                odd_ref[spot, to] = half[:, (2 * part + 1) * HEAD_DIM : 2 * (part + 1) * HEAD_DIM]

    for position, index in enumerate(indices):
        spot = slice(2 * index * HEAD_DIM, 2 * (index + 1) * HEAD_DIM)
        weights = jnp.concatenate([weights_ref[part, :, spot] for part in range(3)], axis=1)
        outcome = jnp.dot(rows, weights, preferred_element_type=jnp.float32).astype(jnp.bfloat16)
        base = 3 * position * HEAD_DIM

        @pl.when(same)
        def _():
            store(outcome, base, first_ref, second_ref)

        @pl.when(jnp.logical_not(same))
        def _():
            store(outcome, base, second_ref, first_ref)


def project_heads(place, own, pair, weights, indices, after):
    rows = own.shape[0]
    vmem = pl.BlockSpec(memory_space=pltpu.VMEM)
    shape = jax.ShapeDtypeStruct((2 * rows, 3 * len(indices) * HEAD_DIM), jnp.bfloat16)
    return pl.pallas_call(
        functools.partial(project_kernel, indices),
        in_specs=[pl.BlockSpec(memory_space=pltpu.SMEM), vmem, vmem, vmem]
        + [pl.BlockSpec(memory_space=pl.ANY)] * len(after),
        out_specs=(vmem, vmem),
        out_shape=(shape, shape),
        compiler_params=pltpu.CompilerParams(vmem_limit_bytes=20 * MIB),
        cost_estimate=pl.CostEstimate(flops=COST, bytes_accessed=COST, transcendentals=0),
    )(place, own, pair, weights, *after)


def attend_kernel(base, place_ref, runs_ref, *refs):
    mine, near, far, pair_first, pair_far, pair_near = refs[:6]
    order_ref, query_mask_ref, key_mask_ref = refs[6:9]
    stay_ref, cross_ref, q_all, k_all, v_all, sorted_out = refs[-6:]
    chip_rows = mine.shape[0]
    rows = chip_rows // 2
    queries = sorted_out.shape[0] - 2 * rows

    def hold(sources):
        for index, source in enumerate(sources):
            spot = slice(index * chip_rows, (index + 1) * chip_rows)
            for part, held in enumerate((q_all, k_all, v_all)):
                low = base + part * HEAD_DIM
                held[spot, :HEAD_DIM] = source[:, low : low + HEAD_DIM]

    @pl.when(place_ref[8] == 0)
    def _():
        hold((mine, near, pair_near, pair_far))

    @pl.when(place_ref[8] == 1)
    def _():
        hold((pair_first, pair_near, near, far))

    q_all[:, HEAD_DIM:] = query_mask_ref[...]
    k_all[:, HEAD_DIM:] = key_mask_ref[...]
    v_all[:, HEAD_DIM:] = jnp.ones((4 * chip_rows, HEAD_DIM), jnp.bfloat16)
    tile = queries // ATTEND_TILES

    def score(step):
        wanted = step * tile + lax.broadcasted_iota(jnp.int32, (tile, 1), 0)
        picks = jnp.concatenate(
            [
                jnp.where(order_ref[line : line + 1, :] == wanted, 1.0, 0.0).astype(jnp.bfloat16)
                for line in range(order_ref.shape[0])
            ],
            axis=1,
        )
        sorted_queries = jnp.dot(picks, q_all[...], preferred_element_type=jnp.float32)
        return lax.dot_general(
            sorted_queries.astype(jnp.bfloat16),
            k_all[...],
            (((1,), (1,)), ((), ())),
            preferred_element_type=jnp.float32,
        )

    coming = score(0)
    for step in range(ATTEND_TILES):
        scores = coming
        if step + 1 < ATTEND_TILES:
            coming = score(step + 1)
        top = jnp.max(scores, axis=1, keepdims=True)
        weights = jnp.exp2((scores - top) * (HEAD_DIM ** (-0.5) * LOG2E))
        summed = jnp.dot(
            weights.astype(jnp.bfloat16), v_all[...], preferred_element_type=jnp.float32
        )
        sorted_out[rows + step * tile : rows + (step + 1) * tile, :] = (
            summed[:, :HEAD_DIM] / summed[:, HEAD_DIM:]
        )

    cross_ref[...] = sorted_out[rows : rows + cross_ref.shape[0], :].astype(jnp.bfloat16)
    for d in range(4):
        stay_ref[d] = spread_run(sorted_out, runs_ref, d, rows).astype(jnp.bfloat16)


def spread_run(sorted_ref, runs_ref, lane, rows):
    furthest = sorted_ref.shape[0] - 2 * rows
    row = lax.broadcasted_iota(jnp.int32, (rows, 1), 0)
    parts = [
        sorted_ref[pl.ds(rows + jnp.clip(runs_ref[line, lane], -rows, furthest), rows), :]
        for line in (3, 4)
    ]
    in_second = (row >= runs_ref[1, lane]) & (row < runs_ref[2, lane])
    return jnp.where(row < runs_ref[0, lane], parts[0], jnp.where(in_second, parts[1], 0.0))


def attend(place, runs, blocks, position, order, query_mask, key_mask, after):
    chip_rows = blocks[0].shape[0]
    rows, keys = chip_rows // 2, 4 * chip_rows
    queries = keys // 2 + rows // 2
    vmem, smem = pl.BlockSpec(memory_space=pltpu.VMEM), pl.BlockSpec(memory_space=pltpu.SMEM)
    shape = jax.ShapeDtypeStruct((4, rows, HEAD_DIM), jnp.bfloat16)
    return pl.pallas_call(
        functools.partial(attend_kernel, 3 * position * HEAD_DIM),
        in_specs=[smem, smem]
        + [vmem] * (len(blocks) + 3)
        + [pl.BlockSpec(memory_space=pl.ANY)] * len(after),
        out_specs=(vmem, vmem),
        out_shape=(shape, jax.ShapeDtypeStruct((CROSSING_ROWS, HEAD_DIM), jnp.bfloat16)),
        scratch_shapes=[
            pltpu.VMEM((keys, 2 * HEAD_DIM), jnp.bfloat16),
            pltpu.VMEM((keys, 2 * HEAD_DIM), jnp.bfloat16),
            pltpu.VMEM((keys, 2 * HEAD_DIM), jnp.bfloat16),
            pltpu.VMEM((queries + 2 * rows, HEAD_DIM), jnp.float32),
        ],
        compiler_params=pltpu.CompilerParams(vmem_limit_bytes=20 * MIB),
        cost_estimate=pl.CostEstimate(
            flops=COST, bytes_accessed=COST, transcendentals=0
        ),
    )(place, runs, *blocks, order, query_mask, key_mask, *after)


def join_kernel(heads, runs_ref, *refs):
    outs, held = refs[-5:-1], refs[-1]
    rows = outs[0].shape[0]
    for head in range(heads):
        stay_ref, arrived_ref = refs[2 * head], refs[2 * head + 1]
        held[rows : rows + arrived_ref.shape[0], :] = arrived_ref[...].astype(jnp.float32)
        spot = slice(head * HEAD_DIM, (head + 1) * HEAD_DIM)
        for d in range(4):
            arrived = spread_run(held, runs_ref, 4 + d, rows).astype(jnp.bfloat16)
            outs[d][:, spot] = stay_ref[d] + arrived


def join_halves(runs, stays, arrivals, after, cost):
    heads, (slots, rows, width) = len(stays), stays[0].shape
    vmem = pl.BlockSpec(memory_space=pltpu.VMEM)
    parts = [part for both in zip(stays, arrivals) for part in both]
    shape = jax.ShapeDtypeStruct((rows, heads * width), jnp.bfloat16)
    return pl.pallas_call(
        functools.partial(join_kernel, heads),
        in_specs=[pl.BlockSpec(memory_space=pltpu.SMEM)]
        + [vmem] * len(parts)
        + [pl.BlockSpec(memory_space=pl.ANY)] * len(after),
        out_specs=(vmem,) * slots,
        out_shape=(shape,) * slots,
        scratch_shapes=[pltpu.VMEM((arrivals[0].shape[0] + 2 * rows, width), jnp.float32)],
        compiler_params=pltpu.CompilerParams(vmem_limit_bytes=16 * MIB),
        cost_estimate=pl.CostEstimate(flops=cost, bytes_accessed=COST, transcendentals=0),
    )(runs, *parts, *after)


def gather_kernel(place_ref, w_ref, held_ref, pair_ref, *rest):
    outs, sems = rest[-5:-1], rest[-1]
    chip, columns = place_ref[4], outs[0].shape[1]
    heads = w_ref.shape[0] // HEAD_DIM // 4
    spot = pl.ds(pl.multiple_of(place_ref[6] * columns, HEAD_DIM), columns)

    def rows_at(block):
        return pl.ds(pl.multiple_of(block * HEAD_DIM, HEAD_DIM), HEAD_DIM)

    def transfers(near_ref, far_ref):
        copies = []
        for d in range(4):
            for index in range(heads):
                last = index + 1 == heads
                group = 1 if last else 0
                to = d if last else d * (heads - 1) + index
                to = slice(to * HEAD_DIM, (to + 1) * HEAD_DIM)
                head = head_of(jnp.bitwise_xor(chip, d), index, heads)
                there = 2 * index + jnp.bitwise_xor(chip, d) % 2
                sources = (
                    w_ref.at[rows_at(head), spot],
                    (near_ref if d < 2 else far_ref).at[rows_at(there), :],
                )
                for side, source in enumerate(sources):
                    copies.append(
                        pltpu.make_async_copy(
                            source, outs[2 * side + group].at[to, :], sems.at[side, index, d]
                        )
                    )
        for copy in copies:
            copy.start()
        for copy in copies:
            copy.wait()

    @pl.when(chip // 2 == place_ref[8])
    def _():
        transfers(held_ref, pair_ref)

    @pl.when(chip // 2 != place_ref[8])
    def _():
        transfers(pair_ref, held_ref)


def gather_out_weights(place, w_out, held, pair, group_heads, after):
    vmem, hbm = pl.BlockSpec(memory_space=pltpu.VMEM), pl.BlockSpec(memory_space=pltpu.HBM)
    any_space = pl.BlockSpec(memory_space=pl.ANY)
    shapes = tuple(
        jax.ShapeDtypeStruct((count * HEAD_DIM, w_out.shape[1] // 2), w_out.dtype)
        for count in (4 * (group_heads - 1), 4)
    )
    return pl.pallas_call(
        gather_kernel,
        in_specs=[pl.BlockSpec(memory_space=pltpu.SMEM), hbm] + [any_space] * (2 + len(after)),
        out_specs=(vmem,) * 4,
        out_shape=shapes + shapes,
        scratch_shapes=[pltpu.SemaphoreType.DMA((2, group_heads, 4))],
        compiler_params=pltpu.CompilerParams(vmem_limit_bytes=16 * MIB),
        cost_estimate=pl.CostEstimate(flops=COST, bytes_accessed=COST, transcendentals=0),
    )(place, w_out, held, pair, *after)


def out_rows_kernel(*refs):
    refs[-1][...] = jnp.concatenate([ref[...] for ref in refs[:-1]], axis=1)


def out_kernel(pairs, *refs):
    total = refs[2 * pairs][...] if len(refs) > 2 * pairs + 1 else None
    for pair in range(pairs):
        product = jnp.dot(
            refs[2 * pair][...], refs[2 * pair + 1][...], preferred_element_type=jnp.float32
        )
        total = product if total is None else total + product
    refs[-1][...] = total.astype(refs[-1].dtype)


def out_call(kernel, arrays, shape, dtype):
    vmem = pl.BlockSpec(memory_space=pltpu.VMEM)
    return pl.pallas_call(
        kernel,
        in_specs=[vmem] * len(arrays),
        out_specs=vmem,
        out_shape=jax.ShapeDtypeStruct(shape, dtype),
        compiler_params=pltpu.CompilerParams(vmem_limit_bytes=16 * MIB),
        cost_estimate=pl.CostEstimate(flops=COST, bytes_accessed=COST, transcendentals=0),
    )(*arrays)


SWAP_ROWS = (128, 112, 80)
CROSSING_ROWS = 1040
ATTEND_TILES = 5
HEAD_CHUNKS = ((0,), (1, 2))
COPY_PIECES = 4


def halved_body(
    inputs,
    norm_gain,
    level_table,
    w_qkv,
    w_out,
    clip_lengths,
    prefix_lengths,
    noise_levels,
    token_rank,
):
    ranks, per_dev = 16, inputs.shape[0]
    half_rows = 8 * per_dev
    clips = clip_lengths.shape[0]
    index = jnp.arange(clips, dtype=jnp.int32)

    ahead = (index[None, :] < index[:, None]) & (clip_lengths == MAXCLIP)[:, None]
    start = jnp.sum(jnp.where(ahead, clip_lengths[None, :], 0))
    early = start <= half_rows // 2

    rank_here = lax.axis_index("ctx")
    side = lax.axis_index("head")
    columns = inputs.shape[1]
    group_heads = w_qkv.shape[2] // HEAD_DIM // 4
    half, block, core = rank_here // 8, rank_here % 8, rank_here % 2
    chip = block // 2
    swap_sides = [(0, 1), (1, 0)]

    def exchange(array, flip, only=lambda r: True):
        pairs = [(r, r ^ flip) for r in range(ranks) if only(r)]
        return lax.ppermute(array, "ctx", pairs)

    def move_rows(swapping):
        return functools.partial(moved_rows, swapping)

    def moved_rows(
        swapping, start, inputs, clip_lengths, prefix_lengths, noise_levels, w_out
    ):
        place = jnp.stack(
            [
                start,
                jnp.int32(1 if 0 in swapping else 0),
                half,
                jnp.int32(half_rows),
                chip,
                jnp.int32(clips),
                side,
                block * per_dev,
                core,
                rank_here,
            ]
        )
        earlier = index[None, :] < index[:, None]
        begins = jnp.sum(jnp.where(earlier, clip_lengths[None, :], 0), axis=1)
        leads = begins + jnp.minimum(prefix_lengths, clip_lengths)
        bounds = jnp.pad(
            jnp.stack([begins, begins + clip_lengths, leads]), ((0, 5), (0, HEAD_DIM - clips))
        )

        cuts = [sum(SWAP_ROWS[:i]) for i in range(len(SWAP_ROWS) + 1)]
        kept, moved = [], []
        for low, high in zip(cuts[:-1], cuts[1:]):
            own = inputs[low:high]
            moved.append(exchange(own, 8, lambda r: r % 8 in swapping))
            kept.append(select_rows(place, own, moved[-1], low, kept[-1:]))
        other = [lax.ppermute(part, "head", swap_sides) for part in kept]
        depth = w_out.shape[0] // 2
        sent = lax.dynamic_slice(w_out, (core * depth, (1 - side) * columns), (depth, columns))
        return tuple(kept), tuple(other), place, bounds, noise_levels.reshape(-1, 1), sent

    kept, other, place, bounds, noise_column, sent = lax.cond(
        early,
        move_rows(range(4)),
        move_rows(range(4, 8)),
        start,
        inputs,
        clip_lengths,
        prefix_lengths,
        noise_levels,
        w_out,
    )
    far_held = lax.ppermute(sent, "head", swap_sides)
    normed = normalize_rows(place, kept, other, bounds, noise_column, level_table, norm_gain)
    pair = exchange(normed, 1)
    w_parts = jnp.transpose(w_qkv, (1, 0, 2))
    query_order, runs, query_mask, key_mask, weights = make_tables(
        place, bounds, token_rank, ranks, half_rows, w_parts
    )

    def held_back(array, after):
        return lax.optimization_barrier((array, *after))[0]

    blocks, pair_firsts, after = [], [], [query_order]
    for heads in HEAD_CHUNKS:
        first, second = project_heads(
            held_back(place, after), normed, pair, weights, heads, []
        )
        near = lax.ppermute(
            second, "ctx", [(r, r ^ (2 if r % 2 == 0 else 4)) for r in range(ranks)]
        )
        far = exchange(first, 6, lambda r: r % 2 == 1)
        blocks.append((first, near, far))
        if not pair_firsts:
            pair_firsts.append(exchange(first, 1, lambda r: r % 2 == 0))
            after = [pair_firsts[0]]

    def share(block, after):
        first, near, far = block
        near, far, *unused = lax.optimization_barrier((near, far, *after))
        if not pair_firsts:
            pair_firsts.append(exchange(held_back(first, after), 1, lambda r: r % 2 == 0))
        return [
            first,
            near,
            far,
            pair_firsts.pop(),
            exchange(far, 1, lambda r: r % 2 == 1),
            exchange(near, 1),
        ]

    def join(heads, after, cost):
        joined = join_halves(
            held_back(runs, after), stays[heads], arrivals[heads], [], cost
        )
        return [exchange(part, 2 * d) if d else part for d, part in enumerate(joined)]

    stays, arrivals = [], []
    after = [blocks[-1][0]]
    for block, heads in zip(blocks, HEAD_CHUNKS):
        block = share(block, after)
        for position, head in enumerate(heads):
            stay, cross = attend(
                held_back(place, after),
                runs,
                block,
                position,
                query_order,
                query_mask,
                key_mask,
                [],
            )
            stays.append(stay)
            if head + 1 < group_heads:
                arrivals.append(exchange(cross, 8))
            after = [cross] + (arrivals[head - 1 : head] if head == 1 else [])
            if head == 1:
                far_pair = exchange(lax.optimization_barrier((far_held, cross))[0], 1)

    w_all = gather_out_weights(
        held_back(place, [cross]), w_out, far_held, far_pair, group_heads, []
    )

    def side_by_side(parts):
        width = sum(part.shape[1] for part in parts)
        return out_call(out_rows_kernel, parts, (per_dev, width), jnp.bfloat16)

    pieces = join(slice(0, group_heads - 1), [cross], COST)
    arrivals.append(exchange(held_back(cross, pieces[1:2]), 8))
    rows = [side_by_side(pieces), side_by_side(join(slice(-1, None), [], LONG_COST))]
    far_rows = [lax.ppermute(part, "head", swap_sides) for part in rows]
    w_own, w_far = w_all[:2], w_all[2:]

    def add(terms, total, dtype):
        arrays = [array for term in terms for array in term] + total
        return out_call(functools.partial(out_kernel, len(terms)), arrays, (per_dev, columns), dtype)

    own, far = list(zip(rows, w_own)), list(zip(far_rows, w_far))
    total = add(own[:1], [], jnp.float32)
    total = add(own[1:] + far[:1], [total], jnp.float32)
    return add(far[1:], [total], jnp.bfloat16)


def solution(mesh):
    in_specs = (
        P("ctx", "head"),
        P(),
        P(),
        P(None, None, "head"),
        P("head", None),
        P(),
        P(),
        P(),
        P(),
    )
    out_specs = P("ctx", "head")

    def body(inputs, norm_gain, level_table, w_qkv, *rest):
        ranks, sides = mesh.shape["ctx"], mesh.shape["head"]
        heads_here = w_qkv.shape[2] // HEAD_DIM
        halved = (
            ranks == 16
            and sides == 2
            and ranks * inputs.shape[0] == 2 * MAXCLIP
            and heads_here == 4 * sum(len(heads) for heads in HEAD_CHUNKS)
        )
        run = halved_body if halved else gathered_body
        return run(inputs, norm_gain, level_table, w_qkv, *rest)

    return jax.shard_map(body, mesh=mesh, in_specs=in_specs, out_specs=out_specs, check_vma=False)
```

```python
import functools

import jax
import jax.numpy as jnp
from jax import lax
from jax.experimental import pallas as pl
from jax.experimental.pallas import tpu as pltpu
from jax.sharding import PartitionSpec as P

HEAD_DIM = 128


NEG = -1e30
EPS = 1e-06
MAXCLIP = 2560
LOG2E = 1.4426950408889634
MIB = 1024 * 1024
COST = 1000000
LONG_COST = 200000000000


def clip_tables(total_rows, clip_lengths, prefix_lengths, noise_levels):
    rows = jnp.arange(total_rows, dtype=jnp.int32)
    ends = jnp.cumsum(clip_lengths)
    begins = ends - clip_lengths
    clip_of = jnp.sum((rows[:, None] >= ends[None, :]).astype(jnp.int32), axis=1)
    member = clip_of[:, None] == jnp.arange(clip_lengths.shape[0], dtype=jnp.int32)[None, :]
    begin_row = jnp.sum(jnp.where(member, begins[None, :], 0), axis=1)
    lead = jnp.minimum(prefix_lengths, clip_lengths)
    lead_row = jnp.sum(jnp.where(member, lead[None, :], 0), axis=1)
    level_row = jnp.sum(jnp.where(member, noise_levels[None, :], 0), axis=1)
    in_prefix = rows - begin_row < lead_row
    return (clip_of, in_prefix, level_row)


def rank_tables(token_rank, ranks, per_rank):
    onehot = (token_rank[:, None] == jnp.arange(ranks, dtype=jnp.int32)[None, :]).astype(jnp.int32)
    earlier = jnp.cumsum(onehot, axis=0) - onehot
    within = jnp.sum(earlier * onehot, axis=1)
    counts = jnp.sum(onehot.reshape(ranks, per_rank, ranks), axis=1)
    starts = jnp.cumsum(counts, axis=0) - counts
    return (within, counts, starts)


def normalize(rows, in_prefix, level_row, level_table, norm_gain):
    picks = (
        level_row[:, None] == jnp.arange(level_table.shape[0], dtype=jnp.int32)[None, :]
    ) & in_prefix[:, None]
    added = jnp.dot(picks.astype(jnp.bfloat16), level_table, preferred_element_type=jnp.float32)
    shifted = rows.astype(jnp.float32) + added
    factor = lax.rsqrt(jnp.mean(shifted * shifted, axis=-1, keepdims=True) + EPS)
    return (shifted * factor * norm_gain).astype(jnp.bfloat16)


def fold_keys(state, queries, query_clip, query_prefix, pairs, key_clip, key_prefix):
    width = queries.shape[1]
    heads_here = width // HEAD_DIM
    factor = HEAD_DIM ** (-0.5)
    allowed_query = jnp.logical_not(query_prefix)

    def absorb(carry, block):
        block_pairs, block_clip, block_prefix = block
        allowed = (query_clip[:, None] == block_clip[None, :]) & (
            allowed_query[:, None] | block_prefix[None, :]
        )
        updated = []
        for head in range(heads_here):
            top, total, summed = carry[head]
            low = head * HEAD_DIM
            q_head = queries[:, low : low + HEAD_DIM]
            k_head = block_pairs[:, low : low + HEAD_DIM]
            v_head = block_pairs[:, width + low : width + low + HEAD_DIM]
            scores = (
                lax.dot_general(
                    q_head, k_head, (((1,), (1,)), ((), ())), preferred_element_type=jnp.float32
                )
                * factor
            )
            masked = jnp.where(allowed, scores, NEG)
            new_top = jnp.maximum(top, jnp.max(masked, axis=1, keepdims=True))
            fade = jnp.exp(top - new_top)
            weights = jnp.where(allowed, jnp.exp(scores - new_top), 0.0)
            total = total * fade + jnp.sum(weights, axis=1, keepdims=True)
            summed = summed * fade + jnp.dot(
                weights.astype(jnp.bfloat16), v_head, preferred_element_type=jnp.float32
            )
            updated.append((new_top, total, summed))
        return (tuple(updated), None)

    count = pairs.shape[0]
    step = 2048 if count > 2048 and count % 2048 == 0 else count
    if step == count:
        result, unused = absorb(state, (pairs, key_clip, key_prefix))
        return result
    stacked = (
        pairs.reshape(count // step, step, pairs.shape[1]),
        key_clip.reshape(count // step, step),
        key_prefix.reshape(count // step, step),
    )
    result, unused = lax.scan(absorb, state, stacked)
    return result


def gathered_body(
    inputs,
    norm_gain,
    level_table,
    w_qkv,
    w_out,
    clip_lengths,
    prefix_lengths,
    noise_levels,
    token_rank,
):
    ranks = lax.axis_size("ctx")
    rank_here = lax.axis_index("ctx")
    per_dev = inputs.shape[0]
    slots = 2 * per_dev // ranks
    local_width = w_qkv.shape[2]
    heads_here = local_width // HEAD_DIM
    total_rows = per_dev * ranks
    clip_of, in_prefix, level_row = clip_tables(
        total_rows, clip_lengths, prefix_lengths, noise_levels
    )
    within, counts, starts = rank_tables(token_rank, ranks, per_dev)
    place = token_rank * per_dev + within
    order = (
        jnp.zeros((total_rows,), jnp.int32).at[place].set(jnp.arange(total_rows, dtype=jnp.int32))
    )
    first = rank_here * per_dev
    own_rank = lax.dynamic_slice_in_dim(token_rank, first, per_dev, 0)
    own_within = lax.dynamic_slice_in_dim(within, first, per_dev, 0)
    send_starts = lax.dynamic_slice_in_dim(starts, rank_here, 1, 0)[0]
    recv_counts = lax.dynamic_slice_in_dim(counts, rank_here, 1, 1)[:, 0]
    recv_starts = lax.dynamic_slice_in_dim(starts, rank_here, 1, 1)[:, 0]
    balanced_rows = lax.dynamic_slice_in_dim(order, first, per_dev, 0)
    target = own_rank * slots + own_within - send_starts[own_rank]
    buffer = jnp.zeros((ranks * slots, inputs.shape[1]), inputs.dtype).at[target].set(inputs)
    received = lax.all_to_all(
        buffer.reshape(ranks, slots, inputs.shape[1]),
        "ctx",
        split_axis=0,
        concat_axis=0,
        tiled=True,
    )
    spots = jnp.arange(slots, dtype=jnp.int32)[None, :]
    index = jnp.where(spots < recv_counts[:, None], recv_starts[:, None] + spots, per_dev).reshape(
        -1
    )
    flat = received.reshape(ranks * slots, received.shape[2])
    rows = jnp.zeros((per_dev, received.shape[2]), received.dtype).at[index].set(flat, mode="drop")
    full_rows = lax.all_gather(rows, "head", axis=1, tiled=True)
    normed = normalize(
        full_rows, in_prefix[balanced_rows], level_row[balanced_rows], level_table, norm_gain
    )
    qkv = jnp.dot(
        normed, w_qkv.reshape(w_qkv.shape[0], 3 * local_width), preferred_element_type=jnp.float32
    ).astype(jnp.bfloat16)
    start_state = tuple(
        (
            (
                jnp.full((per_dev, 1), NEG, jnp.float32),
                jnp.zeros((per_dev, 1), jnp.float32),
                jnp.zeros((per_dev, HEAD_DIM), jnp.float32),
            )
            for head in range(heads_here)
        )
    )
    key_clip = clip_of[order]
    key_prefix = in_prefix[order]
    query_clip = lax.dynamic_slice_in_dim(key_clip, first, per_dev, 0)
    query_prefix = lax.dynamic_slice_in_dim(key_prefix, first, per_dev, 0)
    queries = qkv[:, :local_width]
    pairs = qkv[:, local_width:]
    state = fold_keys(
        start_state,
        queries,
        query_clip,
        query_prefix,
        lax.all_gather(pairs, "ctx", axis=0, tiled=True),
        key_clip,
        key_prefix,
    )
    parts = [state[head][2] / state[head][1] for head in range(heads_here)]
    attention = jnp.concatenate(parts, axis=1).astype(jnp.bfloat16)
    terms = jnp.dot(attention, w_out, preferred_element_type=jnp.float32)
    return lax.psum_scatter(terms.astype(jnp.bfloat16), "head", scatter_dimension=1, tiled=True)


def packed_rows(place_ref, spots):
    start, early, half = place_ref[0], place_ref[1], place_ref[2]
    total = place_ref[3]
    before = jnp.where(spots < start, early, 1 - early)
    return spots + total * (half + before * (1 - 2 * half))


def clip_flags(rows, bounds_ref):
    begins, ends, leads = bounds_ref[0:1, :], bounds_ref[1:2, :], bounds_ref[2:3, :]
    inside = (rows >= begins) & (rows < ends)
    return inside, inside & (rows < leads)


def count_earlier(hot):
    ranks, rows, lanes = hot.shape
    flat = hot.reshape(ranks * rows, lanes).astype(jnp.bfloat16)

    def numbers(shape, axis):
        return lax.broadcasted_iota(jnp.int32, shape, axis)

    def group(index):
        return sum(jnp.where(index >= rows * k, 1, 0) for k in range(1, ranks))

    def ones(flags):
        return jnp.where(flags, 1.0, 0.0).astype(jnp.bfloat16)

    total = ranks * rows
    in_row = ones(numbers((lanes, lanes), 0) < numbers((lanes, lanes), 1))
    below, across = numbers((total, 1), 0), numbers((1, total), 1)
    in_rank = ones((group(below) == group(across)) & (across < below))
    row_sums = jnp.dot(
        flat, jnp.ones((lanes, lanes), jnp.bfloat16), preferred_element_type=jnp.float32
    )
    earlier = jnp.dot(flat, in_row, preferred_element_type=jnp.float32) + jnp.dot(
        in_rank, row_sums.astype(jnp.bfloat16), preferred_element_type=jnp.float32
    )
    return earlier.reshape(ranks, rows, lanes)


def table_kernel(ranks, place_ref, bounds_ref, rank_ref, w_ref, *refs):
    order_ref, runs_ref, query_ref, key_ref, weights_ref, held, sems = refs
    copies = weight_copies(place_ref, w_ref, weights_ref, sems)
    for copy in copies:
        copy.start()
    start, early, half, half_rows = (place_ref[k] for k in range(4))
    chip, clips, core, rank_here = (place_ref[k] for k in (4, 5, 8, 9))
    holds_long = half != early
    tokens = rank_ref[...]
    rows, lanes = tokens.shape
    per_dev = rows * lanes // ranks

    token = lanes * lax.broadcasted_iota(jnp.int32, tokens.shape, 0) + lax.broadcasted_iota(
        jnp.int32, tokens.shape, 1
    )
    hots = [jnp.where(tokens == rank, 1.0, 0.0) for rank in range(ranks)]
    earlier = count_earlier(jnp.stack(hots))
    within = sum(hots[rank] * earlier[rank] for rank in range(ranks))
    before = jnp.where(token < start, 1.0, 0.0)
    upto = jnp.where(token < start + half_rows, 1.0, 0.0)
    lane = lax.broadcasted_iota(jnp.int32, (1, lanes), 1)
    target = jnp.bitwise_xor(rank_here, 2 * jnp.bitwise_and(lane, 3))
    lane_long = jnp.where(lane < 4, jnp.where(holds_long, 1.0, 0.0), jnp.where(holds_long, 0.0, 1.0))
    lane_own = jnp.where(lane < 4, 1.0, 0.0)
    lows, longs, long_first, rest_first = [], [], [], []
    long_count, rest_count = [[0.0, 0.0], [0.0, 0.0]], [[0.0, 0.0], [0.0, 0.0]]
    for rank, hot in enumerate(hots):
        low = jnp.sum(hot * before, keepdims=True)
        long_rows = jnp.sum(hot * upto, keepdims=True) - low
        group, parity = rank // (ranks // 2), rank % 2
        lows.append(low)
        longs.append(long_rows)
        long_first.append(long_count[group][parity])
        rest_first.append(rest_count[group][parity])
        long_count[group][parity] = long_first[rank] + long_rows
        rest_count[group][parity] = rest_first[rank] + (per_dev - long_rows)
    long_base = rest_base = low_of = long_of = 0.0
    runs = [0.0] * 5
    for rank, hot in enumerate(hots):
        low, high, long_rows = lows[rank], lows[rank] + longs[rank], longs[rank]
        group, parity = rank // (ranks // 2), rank % 2
        own_group = jnp.where(half == group, 1.0, 0.0)
        long_after = own_group * long_count[1 - group][parity]
        rest_after = own_group * rest_count[1 - group][parity]
        long_base += hot * (long_first[rank] + long_after - low)
        rest_base += hot * (rest_first[rank] + rest_after)
        low_of += hot * low
        long_of += hot * long_rows
        first = long_first[rank] + lane_own * long_after
        rest = rest_first[rank] + lane_own * rest_after
        here = jnp.where(target == rank, 1.0, 0.0)
        values = (
            (0.0, low),
            (low, high),
            (high, float(per_dev)),
            (0.0, rest),
            (first - low, rest - long_rows),
        )
        runs = [
            run + here * (lane_long * if_long + (1.0 - lane_long) * if_rest)
            for run, (if_long, if_rest) in zip(runs, values)
        ]
    furthest = rows * lanes // 4 + per_dev // 2
    for index, run in enumerate(runs):
        run = run.astype(jnp.int32)
        runs_ref[index : index + 1, :] = (
            run if index < 3 else jnp.clip(run, -per_dev, furthest)
        )
    sorted_at = within + jnp.where(
        upto - before == 1.0, long_base, rest_base - jnp.where(within < low_of, 0.0, long_of)
    )
    held[...] = jnp.where(jnp.bitwise_and(tokens, 1) == core, sorted_at.astype(jnp.int32), -1)
    half_lines = rows // 2
    spots = lanes * lax.broadcasted_iota(
        jnp.int32, (half_lines, lanes), 0
    ) + lax.broadcasted_iota(jnp.int32, (half_lines, lanes), 1)
    later = packed_rows(place_ref, spots) >= half_rows
    held[:half_lines, :] = jnp.where(later, held[half_lines:, :], held[:half_lines, :])
    lines = half_lines // 4
    for d in range(4):
        line = lines * jnp.bitwise_xor(chip, d)
        order_ref[lines * d : lines * (d + 1), :] = held[pl.ds(line, lines), :]

    column = lax.broadcasted_iota(jnp.int32, (1, HEAD_DIM), 1)
    chip_rows = query_ref.shape[0] // 4
    for d in range(4):
        local = lax.broadcasted_iota(jnp.int32, (chip_rows, 1), 0)
        spots = chip_rows * jnp.bitwise_xor(chip, d) + local
        inside, leading = clip_flags(packed_rows(place_ref, spots), bounds_ref)
        spot = slice(d * chip_rows, (d + 1) * chip_rows)
        inside = jnp.where(inside, 1.0, 0.0)
        prefix = jnp.sum(jnp.where(leading, 1.0, 0.0), axis=1, keepdims=True)
        query_ref[spot, :] = jnp.where(column == clips, prefix, inside).astype(jnp.bfloat16)
        outside = jnp.where(column < clips, NEG * (1.0 - inside), 0.0)
        key_ref[spot, :] = jnp.where(column == clips, NEG * (1.0 - prefix), outside).astype(
            jnp.bfloat16
        )
    for copy in copies:
        copy.wait()


def make_tables(place, bounds, token_rank, ranks, keys, w_parts):
    vmem = pl.BlockSpec(memory_space=pltpu.VMEM)
    tokens = token_rank.reshape(-1, HEAD_DIM)
    features = jax.ShapeDtypeStruct((keys, HEAD_DIM), jnp.bfloat16)
    return pl.pallas_call(
        functools.partial(table_kernel, ranks),
        in_specs=[
            pl.BlockSpec(memory_space=pltpu.SMEM),
            vmem,
            vmem,
            pl.BlockSpec(memory_space=pltpu.HBM),
        ],
        out_specs=(vmem,) * 5,
        out_shape=(
            jax.ShapeDtypeStruct((tokens.shape[0] // 2, HEAD_DIM), jnp.int32),
            jax.ShapeDtypeStruct((8, HEAD_DIM), jnp.int32),
            features,
            features,
            jax.ShapeDtypeStruct((*w_parts.shape[:2], w_parts.shape[2] // 2), w_parts.dtype),
        ),
        scratch_shapes=[
            pltpu.VMEM(tokens.shape, jnp.int32),
            pltpu.SemaphoreType.DMA((3, COPY_PIECES)),
        ],
        compiler_params=pltpu.CompilerParams(vmem_limit_bytes=26 * MIB),
        cost_estimate=pl.CostEstimate(flops=COST, bytes_accessed=COST, transcendentals=0),
    )(place, bounds, tokens, w_parts)


def select_kernel(low, place_ref, own_ref, moved_ref, *rest):
    out_ref = rest[-1]
    spots = place_ref[7] + low + lax.broadcasted_iota(jnp.int32, (out_ref.shape[0], 1), 0)
    swapped = jnp.where(spots < place_ref[0], place_ref[1], 1 - place_ref[1])
    out_ref[...] = jnp.where(swapped == 1, moved_ref[...], own_ref[...])


def select_rows(place, own, moved, low, after):
    vmem = pl.BlockSpec(memory_space=pltpu.VMEM)
    return pl.pallas_call(
        functools.partial(select_kernel, low),
        in_specs=[pl.BlockSpec(memory_space=pltpu.SMEM), vmem, vmem]
        + [pl.BlockSpec(memory_space=pl.ANY)] * len(after),
        out_specs=vmem,
        out_shape=jax.ShapeDtypeStruct(moved.shape, moved.dtype),
        compiler_params=pltpu.CompilerParams(vmem_limit_bytes=8 * MIB),
        cost_estimate=pl.CostEstimate(flops=COST, bytes_accessed=COST, transcendentals=0),
    )(place, own, moved, *after)


def head_of(chip, index, group_heads):
    return 2 * group_heads * (chip // 2) + 2 * index + chip % 2


def weight_copies(place_ref, w_ref, out_ref, sems):
    pair = jnp.bitwise_xor(place_ref[4] // 2, place_ref[8])
    columns = pl.ds(pl.multiple_of(pair * out_ref.shape[2], HEAD_DIM), out_ref.shape[2])
    depth = out_ref.shape[1] // COPY_PIECES
    copies = []
    for part in range(3):
        for piece in range(COPY_PIECES):
            rows = slice(piece * depth, (piece + 1) * depth)
            copies.append(
                pltpu.make_async_copy(
                    w_ref.at[part, rows, columns], out_ref.at[part, rows, :], sems.at[part, piece]
                )
            )
    return copies


def norm_kernel(place_ref, *refs):
    pieces = len(SWAP_ROWS)
    bounds_ref, noise_ref, level_ref, gain_ref = refs[2 * pieces : 2 * pieces + 4]
    out_ref = refs[-1]
    width = out_ref.shape[1] // 2
    side, first = place_ref[6], place_ref[7]
    clips, levels = noise_ref.shape[0], level_ref.shape[0]
    spots = [pl.ds(pl.multiple_of(s * width, 128), width) for s in (side, 1 - side)]
    level = lax.broadcasted_iota(jnp.int32, (clips, levels), 1)
    chosen = jnp.where(noise_ref[...] == level, 1.0, 0.0).astype(jnp.bfloat16)
    tables = [
        jnp.dot(chosen, level_ref[:, spot], preferred_element_type=jnp.float32).astype(
            jnp.bfloat16
        )
        for spot in spots
    ]
    low = 0
    for piece in range(pieces):
        own_ref, other_ref = refs[piece], refs[pieces + piece]
        count = own_ref.shape[0]
        rows = slice(low, low + count)
        places = first + low + lax.broadcasted_iota(jnp.int32, (count, 1), 0)
        low += count
        unused, leading = clip_flags(packed_rows(place_ref, places), bounds_ref)
        picks = jnp.where(leading, 1.0, 0.0)[:, :clips].astype(jnp.bfloat16)
        shifted = [
            ref[...].astype(jnp.float32)
            + jnp.dot(picks, table, preferred_element_type=jnp.float32)
            for ref, table in zip((own_ref, other_ref), tables)
        ]
        squares = sum(jnp.sum(part * part, axis=1, keepdims=True) for part in shifted)
        factor = lax.rsqrt(squares / (2 * width) + EPS)
        for part, spot in zip(shifted, spots):
            out_ref[rows, spot] = (part * factor * gain_ref[:, spot]).astype(jnp.bfloat16)


def normalize_rows(place, kept, other, bounds, noise_levels, level_table, norm_gain):
    rows, depth = sum(part.shape[0] for part in kept), 2 * kept[0].shape[1]
    vmem = pl.BlockSpec(memory_space=pltpu.VMEM)
    return pl.pallas_call(
        norm_kernel,
        in_specs=[pl.BlockSpec(memory_space=pltpu.SMEM)] + [vmem] * (2 * len(kept) + 4),
        out_specs=vmem,
        out_shape=jax.ShapeDtypeStruct((rows, depth), jnp.bfloat16),
        compiler_params=pltpu.CompilerParams(vmem_limit_bytes=26 * MIB),
        cost_estimate=pl.CostEstimate(flops=COST, bytes_accessed=COST, transcendentals=0),
    )(place, *kept, *other, bounds, noise_levels, level_table, norm_gain.reshape(1, -1))


def project_kernel(indices, place_ref, own_ref, pair_ref, weights_ref, *rest):
    first_ref, second_ref = rest[-2:]
    rows = jnp.concatenate([own_ref[...], pair_ref[...]], axis=0)
    count = own_ref.shape[0]
    same = place_ref[4] % 2 == place_ref[8]

    def store(outcome, base, even_ref, odd_ref):
        for index, core in enumerate((place_ref[8], 1 - place_ref[8])):
            spot = pl.ds(pl.multiple_of(core * count, count), count)
            half = outcome[index * count : (index + 1) * count]
            for part in range(3):
                to = slice(base + part * HEAD_DIM, base + (part + 1) * HEAD_DIM)
                even_ref[spot, to] = half[:, 2 * part * HEAD_DIM : (2 * part + 1) * HEAD_DIM]
                odd_ref[spot, to] = half[:, (2 * part + 1) * HEAD_DIM : 2 * (part + 1) * HEAD_DIM]

    for position, index in enumerate(indices):
        spot = slice(2 * index * HEAD_DIM, 2 * (index + 1) * HEAD_DIM)
        weights = jnp.concatenate([weights_ref[part, :, spot] for part in range(3)], axis=1)
        outcome = jnp.dot(rows, weights, preferred_element_type=jnp.float32).astype(jnp.bfloat16)
        base = 3 * position * HEAD_DIM

        @pl.when(same)
        def _():
            store(outcome, base, first_ref, second_ref)

        @pl.when(jnp.logical_not(same))
        def _():
            store(outcome, base, second_ref, first_ref)


def project_heads(place, own, pair, weights, indices, after):
    rows = own.shape[0]
    vmem = pl.BlockSpec(memory_space=pltpu.VMEM)
    shape = jax.ShapeDtypeStruct((2 * rows, 3 * len(indices) * HEAD_DIM), jnp.bfloat16)
    return pl.pallas_call(
        functools.partial(project_kernel, indices),
        in_specs=[pl.BlockSpec(memory_space=pltpu.SMEM), vmem, vmem, vmem]
        + [pl.BlockSpec(memory_space=pl.ANY)] * len(after),
        out_specs=(vmem, vmem),
        out_shape=(shape, shape),
        compiler_params=pltpu.CompilerParams(vmem_limit_bytes=20 * MIB),
        cost_estimate=pl.CostEstimate(flops=COST, bytes_accessed=COST, transcendentals=0),
    )(place, own, pair, weights, *after)


def attend_kernel(base, place_ref, runs_ref, *refs):
    mine, near, far, pair_first, pair_far, pair_near = refs[:6]
    order_ref, query_mask_ref, key_mask_ref = refs[6:9]
    stay_ref, cross_ref, q_all, k_all, v_all, sorted_out = refs[-6:]
    chip_rows = mine.shape[0]
    rows = chip_rows // 2
    queries = sorted_out.shape[0] - 2 * rows

    def hold(sources):
        for index, source in enumerate(sources):
            spot = slice(index * chip_rows, (index + 1) * chip_rows)
            for part, held in enumerate((q_all, k_all, v_all)):
                low = base + part * HEAD_DIM
                held[spot, :HEAD_DIM] = source[:, low : low + HEAD_DIM]

    @pl.when(place_ref[8] == 0)
    def _():
        hold((mine, near, pair_near, pair_far))

    @pl.when(place_ref[8] == 1)
    def _():
        hold((pair_first, pair_near, near, far))

    q_all[:, HEAD_DIM:] = query_mask_ref[...]
    k_all[:, HEAD_DIM:] = key_mask_ref[...]
    v_all[:, HEAD_DIM:] = jnp.ones((4 * chip_rows, HEAD_DIM), jnp.bfloat16)
    tile = queries // ATTEND_TILES

    def score(step):
        wanted = step * tile + lax.broadcasted_iota(jnp.int32, (tile, 1), 0)
        picks = jnp.concatenate(
            [
                jnp.where(order_ref[line : line + 1, :] == wanted, 1.0, 0.0).astype(jnp.bfloat16)
                for line in range(order_ref.shape[0])
            ],
            axis=1,
        )
        sorted_queries = jnp.dot(picks, q_all[...], preferred_element_type=jnp.float32)
        return lax.dot_general(
            sorted_queries.astype(jnp.bfloat16),
            k_all[...],
            (((1,), (1,)), ((), ())),
            preferred_element_type=jnp.float32,
        )

    coming = score(0)
    for step in range(ATTEND_TILES):
        scores = coming
        if step + 1 < ATTEND_TILES:
            coming = score(step + 1)
        top = jnp.max(scores, axis=1, keepdims=True)
        weights = jnp.exp2((scores - top) * (HEAD_DIM ** (-0.5) * LOG2E))
        summed = jnp.dot(
            weights.astype(jnp.bfloat16), v_all[...], preferred_element_type=jnp.float32
        )
        sorted_out[rows + step * tile : rows + (step + 1) * tile, :] = (
            summed[:, :HEAD_DIM] / summed[:, HEAD_DIM:]
        )

    cross_ref[...] = sorted_out[rows : rows + cross_ref.shape[0], :].astype(jnp.bfloat16)
    for d in range(4):
        stay_ref[d] = spread_run(sorted_out, runs_ref, d, rows).astype(jnp.bfloat16)


def spread_run(sorted_ref, runs_ref, lane, rows):
    furthest = sorted_ref.shape[0] - 2 * rows
    row = lax.broadcasted_iota(jnp.int32, (rows, 1), 0)
    parts = [
        sorted_ref[pl.ds(rows + jnp.clip(runs_ref[line, lane], -rows, furthest), rows), :]
        for line in (3, 4)
    ]
    in_second = (row >= runs_ref[1, lane]) & (row < runs_ref[2, lane])
    return jnp.where(row < runs_ref[0, lane], parts[0], jnp.where(in_second, parts[1], 0.0))


def attend(place, runs, blocks, position, order, query_mask, key_mask, after):
    chip_rows = blocks[0].shape[0]
    rows, keys = chip_rows // 2, 4 * chip_rows
    queries = keys // 2 + rows // 2
    vmem, smem = pl.BlockSpec(memory_space=pltpu.VMEM), pl.BlockSpec(memory_space=pltpu.SMEM)
    shape = jax.ShapeDtypeStruct((4, rows, HEAD_DIM), jnp.bfloat16)
    return pl.pallas_call(
        functools.partial(attend_kernel, 3 * position * HEAD_DIM),
        in_specs=[smem, smem]
        + [vmem] * (len(blocks) + 3)
        + [pl.BlockSpec(memory_space=pl.ANY)] * len(after),
        out_specs=(vmem, vmem),
        out_shape=(shape, jax.ShapeDtypeStruct((CROSSING_ROWS, HEAD_DIM), jnp.bfloat16)),
        scratch_shapes=[
            pltpu.VMEM((keys, 2 * HEAD_DIM), jnp.bfloat16),
            pltpu.VMEM((keys, 2 * HEAD_DIM), jnp.bfloat16),
            pltpu.VMEM((keys, 2 * HEAD_DIM), jnp.bfloat16),
            pltpu.VMEM((queries + 2 * rows, HEAD_DIM), jnp.float32),
        ],
        compiler_params=pltpu.CompilerParams(vmem_limit_bytes=20 * MIB),
        cost_estimate=pl.CostEstimate(
            flops=COST, bytes_accessed=COST, transcendentals=0
        ),
    )(place, runs, *blocks, order, query_mask, key_mask, *after)


def join_kernel(heads, runs_ref, *refs):
    outs, held = refs[-5:-1], refs[-1]
    rows = outs[0].shape[0]
    for head in range(heads):
        stay_ref, arrived_ref = refs[2 * head], refs[2 * head + 1]
        held[rows : rows + arrived_ref.shape[0], :] = arrived_ref[...].astype(jnp.float32)
        spot = slice(head * HEAD_DIM, (head + 1) * HEAD_DIM)
        for d in range(4):
            arrived = spread_run(held, runs_ref, 4 + d, rows).astype(jnp.bfloat16)
            outs[d][:, spot] = stay_ref[d] + arrived


def join_halves(runs, stays, arrivals, after, cost):
    heads, (slots, rows, width) = len(stays), stays[0].shape
    vmem = pl.BlockSpec(memory_space=pltpu.VMEM)
    parts = [part for both in zip(stays, arrivals) for part in both]
    shape = jax.ShapeDtypeStruct((rows, heads * width), jnp.bfloat16)
    return pl.pallas_call(
        functools.partial(join_kernel, heads),
        in_specs=[pl.BlockSpec(memory_space=pltpu.SMEM)]
        + [vmem] * len(parts)
        + [pl.BlockSpec(memory_space=pl.ANY)] * len(after),
        out_specs=(vmem,) * slots,
        out_shape=(shape,) * slots,
        scratch_shapes=[pltpu.VMEM((arrivals[0].shape[0] + 2 * rows, width), jnp.float32)],
        compiler_params=pltpu.CompilerParams(vmem_limit_bytes=16 * MIB),
        cost_estimate=pl.CostEstimate(flops=cost, bytes_accessed=COST, transcendentals=0),
    )(runs, *parts, *after)


def gather_kernel(place_ref, w_ref, held_ref, pair_ref, *rest):
    outs, sems = rest[-5:-1], rest[-1]
    chip, columns = place_ref[4], outs[0].shape[1]
    heads = w_ref.shape[0] // HEAD_DIM // 4
    spot = pl.ds(pl.multiple_of(place_ref[6] * columns, HEAD_DIM), columns)

    def rows_at(block):
        return pl.ds(pl.multiple_of(block * HEAD_DIM, HEAD_DIM), HEAD_DIM)

    def transfers(near_ref, far_ref):
        copies = []
        for d in range(4):
            for index in range(heads):
                last = index + 1 == heads
                group = 1 if last else 0
                to = d if last else d * (heads - 1) + index
                to = slice(to * HEAD_DIM, (to + 1) * HEAD_DIM)
                head = head_of(jnp.bitwise_xor(chip, d), index, heads)
                there = 2 * index + jnp.bitwise_xor(chip, d) % 2
                sources = (
                    w_ref.at[rows_at(head), spot],
                    (near_ref if d < 2 else far_ref).at[rows_at(there), :],
                )
                for side, source in enumerate(sources):
                    copies.append(
                        pltpu.make_async_copy(
                            source, outs[2 * side + group].at[to, :], sems.at[side, index, d]
                        )
                    )
        for copy in copies:
            copy.start()
        for copy in copies:
            copy.wait()

    @pl.when(chip // 2 == place_ref[8])
    def _():
        transfers(held_ref, pair_ref)

    @pl.when(chip // 2 != place_ref[8])
    def _():
        transfers(pair_ref, held_ref)


def gather_out_weights(place, w_out, held, pair, group_heads, after):
    vmem, hbm = pl.BlockSpec(memory_space=pltpu.VMEM), pl.BlockSpec(memory_space=pltpu.HBM)
    any_space = pl.BlockSpec(memory_space=pl.ANY)
    shapes = tuple(
        jax.ShapeDtypeStruct((count * HEAD_DIM, w_out.shape[1] // 2), w_out.dtype)
        for count in (4 * (group_heads - 1), 4)
    )
    return pl.pallas_call(
        gather_kernel,
        in_specs=[pl.BlockSpec(memory_space=pltpu.SMEM), hbm] + [any_space] * (2 + len(after)),
        out_specs=(vmem,) * 4,
        out_shape=shapes + shapes,
        scratch_shapes=[pltpu.SemaphoreType.DMA((2, group_heads, 4))],
        compiler_params=pltpu.CompilerParams(vmem_limit_bytes=16 * MIB),
        cost_estimate=pl.CostEstimate(flops=COST, bytes_accessed=COST, transcendentals=0),
    )(place, w_out, held, pair, *after)


def out_rows_kernel(*refs):
    refs[-1][...] = jnp.concatenate([ref[...] for ref in refs[:-1]], axis=1)


def out_kernel(pairs, *refs):
    total = refs[2 * pairs][...] if len(refs) > 2 * pairs + 1 else None
    for pair in range(pairs):
        product = jnp.dot(
            refs[2 * pair][...], refs[2 * pair + 1][...], preferred_element_type=jnp.float32
        )
        total = product if total is None else total + product
    refs[-1][...] = total.astype(refs[-1].dtype)


def out_call(kernel, arrays, shape, dtype):
    vmem = pl.BlockSpec(memory_space=pltpu.VMEM)
    return pl.pallas_call(
        kernel,
        in_specs=[vmem] * len(arrays),
        out_specs=vmem,
        out_shape=jax.ShapeDtypeStruct(shape, dtype),
        compiler_params=pltpu.CompilerParams(vmem_limit_bytes=16 * MIB),
        cost_estimate=pl.CostEstimate(flops=COST, bytes_accessed=COST, transcendentals=0),
    )(*arrays)


SWAP_ROWS = (128, 112, 80)
CROSSING_ROWS = 1040
ATTEND_TILES = 5
HEAD_CHUNKS = ((0,), (1, 2))
COPY_PIECES = 4


def halved_body(
    inputs,
    norm_gain,
    level_table,
    w_qkv,
    w_out,
    clip_lengths,
    prefix_lengths,
    noise_levels,
    token_rank,
):
    ranks, per_dev = 16, inputs.shape[0]
    half_rows = 8 * per_dev
    clips = clip_lengths.shape[0]
    index = jnp.arange(clips, dtype=jnp.int32)

    ahead = (index[None, :] < index[:, None]) & (clip_lengths == MAXCLIP)[:, None]
    start = jnp.sum(jnp.where(ahead, clip_lengths[None, :], 0))
    early = start <= half_rows // 2

    rank_here = lax.axis_index("ctx")
    side = lax.axis_index("head")
    columns = inputs.shape[1]
    group_heads = w_qkv.shape[2] // HEAD_DIM // 4
    half, block, core = rank_here // 8, rank_here % 8, rank_here % 2
    chip = block // 2
    swap_sides = [(0, 1), (1, 0)]

    def exchange(array, flip, only=lambda r: True):
        pairs = [(r, r ^ flip) for r in range(ranks) if only(r)]
        return lax.ppermute(array, "ctx", pairs)

    def move_rows(swapping):
        return functools.partial(moved_rows, swapping)

    def moved_rows(
        swapping, start, inputs, clip_lengths, prefix_lengths, noise_levels, w_out
    ):
        place = jnp.stack(
            [
                start,
                jnp.int32(1 if 0 in swapping else 0),
                half,
                jnp.int32(half_rows),
                chip,
                jnp.int32(clips),
                side,
                block * per_dev,
                core,
                rank_here,
            ]
        )
        earlier = index[None, :] < index[:, None]
        begins = jnp.sum(jnp.where(earlier, clip_lengths[None, :], 0), axis=1)
        leads = begins + jnp.minimum(prefix_lengths, clip_lengths)
        bounds = jnp.pad(
            jnp.stack([begins, begins + clip_lengths, leads]), ((0, 5), (0, HEAD_DIM - clips))
        )

        cuts = [sum(SWAP_ROWS[:i]) for i in range(len(SWAP_ROWS) + 1)]
        kept, moved = [], []
        for low, high in zip(cuts[:-1], cuts[1:]):
            own = inputs[low:high]
            moved.append(exchange(own, 8, lambda r: r % 8 in swapping))
            kept.append(select_rows(place, own, moved[-1], low, kept[-1:]))
        other = [lax.ppermute(part, "head", swap_sides) for part in kept]
        depth = w_out.shape[0] // 2
        sent = lax.dynamic_slice(w_out, (core * depth, (1 - side) * columns), (depth, columns))
        return tuple(kept), tuple(other), place, bounds, noise_levels.reshape(-1, 1), sent

    kept, other, place, bounds, noise_column, sent = lax.cond(
        early,
        move_rows(range(4)),
        move_rows(range(4, 8)),
        start,
        inputs,
        clip_lengths,
        prefix_lengths,
        noise_levels,
        w_out,
    )
    far_held = lax.ppermute(sent, "head", swap_sides)
    normed = normalize_rows(place, kept, other, bounds, noise_column, level_table, norm_gain)
    pair = exchange(normed, 1)
    w_parts = jnp.transpose(w_qkv, (1, 0, 2))
    query_order, runs, query_mask, key_mask, weights = make_tables(
        place, bounds, token_rank, ranks, half_rows, w_parts
    )

    def held_back(array, after):
        return lax.optimization_barrier((array, *after))[0]

    blocks, pair_firsts, after = [], [], [query_order]
    for heads in HEAD_CHUNKS:
        first, second = project_heads(
            held_back(place, after), normed, pair, weights, heads, []
        )
        near = lax.ppermute(
            second, "ctx", [(r, r ^ (2 if r % 2 == 0 else 4)) for r in range(ranks)]
        )
        far = exchange(first, 6, lambda r: r % 2 == 1)
        blocks.append((first, near, far))
        if not pair_firsts:
            pair_firsts.append(exchange(first, 1, lambda r: r % 2 == 0))
            after = [pair_firsts[0]]

    def share(block, after):
        first, near, far = block
        near, far, *unused = lax.optimization_barrier((near, far, *after))
        if not pair_firsts:
            pair_firsts.append(exchange(held_back(first, after), 1, lambda r: r % 2 == 0))
        return [
            first,
            near,
            far,
            pair_firsts.pop(),
            exchange(far, 1, lambda r: r % 2 == 1),
            exchange(near, 1),
        ]

    def join(heads, after, cost):
        joined = join_halves(
            held_back(runs, after), stays[heads], arrivals[heads], [], cost
        )
        return [exchange(part, 2 * d) if d else part for d, part in enumerate(joined)]

    stays, arrivals = [], []
    after = [blocks[-1][0]]
    for block, heads in zip(blocks, HEAD_CHUNKS):
        block = share(block, after)
        for position, head in enumerate(heads):
            stay, cross = attend(
                held_back(place, after),
                runs,
                block,
                position,
                query_order,
                query_mask,
                key_mask,
                [],
            )
            stays.append(stay)
            if head + 1 < group_heads:
                arrivals.append(exchange(cross, 8))
            after = [cross] + (arrivals[head - 1 : head] if head == 1 else [])
            if head == 1:
                far_pair = exchange(lax.optimization_barrier((far_held, cross))[0], 1)

    w_all = gather_out_weights(
        held_back(place, [cross]), w_out, far_held, far_pair, group_heads, []
    )

    def side_by_side(parts):
        width = sum(part.shape[1] for part in parts)
        return out_call(out_rows_kernel, parts, (per_dev, width), jnp.bfloat16)

    pieces = join(slice(0, group_heads - 1), [cross], COST)
    arrivals.append(exchange(held_back(cross, pieces[2:3]), 8))
    rows = [side_by_side(pieces), side_by_side(join(slice(-1, None), [], LONG_COST))]
    far_rows = [lax.ppermute(part, "head", swap_sides) for part in rows]
    w_own, w_far = w_all[:2], w_all[2:]

    def add(terms, total, dtype):
        arrays = [array for term in terms for array in term] + total
        return out_call(functools.partial(out_kernel, len(terms)), arrays, (per_dev, columns), dtype)

    own, far = list(zip(rows, w_own)), list(zip(far_rows, w_far))
    total = add(own[:1], [], jnp.float32)
    total = add(own[1:] + far[:1], [total], jnp.float32)
    return add(far[1:], [total], jnp.bfloat16)


def solution(mesh):
    in_specs = (
        P("ctx", "head"),
        P(),
        P(),
        P(None, None, "head"),
        P("head", None),
        P(),
        P(),
        P(),
        P(),
    )
    out_specs = P("ctx", "head")

    def body(inputs, norm_gain, level_table, w_qkv, *rest):
        ranks, sides = mesh.shape["ctx"], mesh.shape["head"]
        heads_here = w_qkv.shape[2] // HEAD_DIM
        halved = (
            ranks == 16
            and sides == 2
            and ranks * inputs.shape[0] == 2 * MAXCLIP
            and heads_here == 4 * sum(len(heads) for heads in HEAD_CHUNKS)
        )
        run = halved_body if halved else gathered_body
        return run(inputs, norm_gain, level_table, w_qkv, *rest)

    return jax.shard_map(body, mesh=mesh, in_specs=in_specs, out_specs=out_specs, check_vma=False)
```
